128 devices in a mesh: section: 2 (over y_lo), dp: 64 (over z, y_hi, x, core).
Axes of the slice: x: 4, y: 4 (y_hi: 2, y_lo: 2; y = y_hi * 2 + y_lo), z: 4, core: 2. Of those that a mesh axis runs over, the one named last changes fastest.
Arguments:
- tokens: bfloat16 [2, 8192, 1536], P(None, 'dp'), may hold values from -6 to 6
- cotangent: bfloat16 [2, 8192, 1536], P(None, 'dp'), may hold values from -6 to 6
- starts: int32 [2, 64, 4], P(None, 'dp'), may hold values from 0 to 128, as said below
- norm_gain: bfloat16 [2, 1536], P('section', 'dp'), may hold values from 0.5 to 1.5
- w_in: bfloat16 [2, 1536, 6448], P('section', 'dp'), may hold values from -0.15625 to 0.15625
- conv_weight: bfloat16 [2, 4, 3328], P('section', None, 'dp'), may hold values from -3 to 3
- conv_bias: bfloat16 [2, 3328], P('section', 'dp'), may hold values from -1.5 to 1.5
- dt_bias: float32 [2, 48], P('section'), may hold values from -4 to -1
- a_log: float32 [2, 48], P('section'), may hold values from -10 to -1
- skip_d: float32 [2, 48], P('section'), may hold values from 0.5 to 1.5
- gate_gain: bfloat16 [2, 3072], P('section', 'dp'), may hold values from 0.5 to 1.5
- w_out: bfloat16 [2, 3072, 1536], P('section', None, 'dp'), may hold values from -0.109375 to 0.109375
Outputs:
- section_out: bfloat16 [2, 2, 8192, 1536], P('section', None, 'dp')
- in_grad: float32 [2, 2, 8192, 1536], P('section', None, 'dp')
- norm_gain_grad: float32 [2, 1536], P('section', 'dp')
- w_in_grad: float32 [2, 1536, 6448], P('section', 'dp')
- conv_weight_grad: float32 [2, 4, 3328], P('section', None, 'dp')
- conv_bias_grad: float32 [2, 3328], P('section', 'dp')
- dt_bias_grad: float32 [2, 48], P('section')
- a_log_grad: float32 [2, 48], P('section')
- skip_d_grad: float32 [2, 48], P('section')
- gate_gain_grad: float32 [2, 3072], P('section', 'dp')
- w_out_grad: float32 [2, 3072, 1536], P('section', None, 'dp')
The draws below stay inside these ranges and needn't reach their ends.
Inputs may be any that keep to these rules, and one draw needn't show every extreme that they name: starts[m, d, 0] is 0 and each row never falls. In every micro-batch one device, drawn from the seed, holds a single sequence: its other entries are 128; on the other devices the 4 entries are distinct and below 128.
All inputs are finite; a program needn't handle non-finite values.
Results may differ from the reference program's by a relative error of at most 0.018.
Values may be sent and summed in bfloat16 or wider, within the bound.
A program may use at most 320 MiB of HBM per device.

```python
import jax
import jax.numpy as jnp
from jax import lax

D = 1536
HEADS = 48
HEAD_DIM = 64
STATE = 128
KERNEL = 4
INNER = 3072
CONV_CH = 3328
PROJ = 6448
BLOCK = 64
SEQS = 4
MICRO = 2
TOK_DEV = 128
TOKENS = 8192
N_SECTION = 2
N_DP = 64


def draw_starts(key, part):
    key = jax.random.fold_in(key, 5)
    pick_key, whole_key = jax.random.split(key)
    single_dev = jax.random.randint(pick_key, (MICRO,), 0, N_DP)
    dev_places = jnp.arange(N_DP, dtype=jnp.int32)
    row_list = []
    for micro_index in range(MICRO):
        micro_key = jax.random.fold_in(whole_key, micro_index)
        dev_keys = jax.random.split(micro_key, N_DP)

        def one_device(dev_key):
            shuffled = jax.random.permutation(dev_key, TOK_DEV - 1) + 1
            cut_points = jnp.sort(shuffled[:SEQS - 1]).astype(jnp.int32)
            return jnp.concatenate([jnp.zeros((1,), jnp.int32), cut_points])
        ragged = jax.vmap(one_device)(dev_keys)
        single = jnp.concatenate([jnp.zeros((1,), jnp.int32), jnp.full((SEQS - 1,), TOK_DEV, jnp.int32)])
        chosen = (dev_places == single_dev[micro_index])[:, None]
        row_list.append(jnp.where(chosen, single[None, :], ragged))
    return jnp.stack(row_list).astype(jnp.int32)


def levels(rng, dims, cuts, low, largest):
    level, own = 1.0, jax.random.fold_in(rng, 6)
    for axis_at, shards_of in cuts:
        steps = jnp.exp(jax.random.uniform(jax.random.fold_in(own, axis_at), (shards_of,), jnp.float32, low / len(cuts), largest / len(cuts)))
        level = level * jnp.repeat(steps, dims[axis_at] // shards_of).reshape([-1 if axis == axis_at else 1 for axis in range(len(dims))])
    return level


def normal_values(own_key, extent, width, reach, cuts=(), kind=jnp.bfloat16):
    values = jax.random.normal(own_key, extent, jnp.float32) * width
    if len(cuts) > 0:
        values = levels(own_key, extent, cuts, -0.22, 0.18) * values
    return jnp.clip(values, min=-reach, max=reach).astype(kind)


def setup_inputs(seed: int = 0) -> dict:
    splits = jax.random.split(jax.random.key(seed), 13)
    tokens = normal_values(splits[0], (MICRO, TOKENS, D), 1.0, 6.0, ((1, 64),))
    cotangent = normal_values(splits[1], (MICRO, TOKENS, D), 1.0, 6.0, ((1, 64),))
    starts = draw_starts(jax.random.fold_in(splits[12], 71), 0)
    norm_gain = jnp.clip(1.0 + 0.1 * jax.random.normal(splits[3], (N_SECTION, D), jnp.float32), 0.5, 1.5).astype(jnp.bfloat16)
    w_in = normal_values(splits[4], (N_SECTION, D, PROJ), D ** -0.5, 0.15625, ((0, 2), (1, 64)))
    conv_weight = normal_values(splits[5], (N_SECTION, KERNEL, CONV_CH), KERNEL ** -0.5, 3.0, ((0, 2), (2, 64)))
    conv_bias = normal_values(splits[6], (N_SECTION, CONV_CH), 0.3, 1.5, ((0, 2), (1, 64)))
    dt_bias = jnp.clip(-4.0 + 3.0 * jax.random.uniform(splits[7], (N_SECTION, HEADS), jnp.float32) ** levels(splits[7], (N_SECTION, HEADS), ((0, 2),), -0.2, 0.2), -4.0, -1.0)
    a_log = jnp.clip(-10.0 + 9.0 * jax.random.uniform(splits[8], (N_SECTION, HEADS), jnp.float32) ** levels(splits[8], (N_SECTION, HEADS), ((0, 2),), -0.2, 0.2), -10.0, -1.0)
    skip_d = jnp.clip(0.5 + 1.0 * jax.random.uniform(splits[9], (N_SECTION, HEADS), jnp.float32) ** levels(splits[9], (N_SECTION, HEADS), ((0, 2),), -0.2, 0.2), 0.5, 1.5)
    gate_gain = jnp.clip(1.0 + 0.1 * jax.random.normal(splits[10], (N_SECTION, INNER), jnp.float32), 0.5, 1.5).astype(jnp.bfloat16)
    w_out = normal_values(splits[11], (N_SECTION, INNER, D), INNER ** -0.5, 0.109375, ((0, 2), (2, 64)))
    return dict(tokens=tokens, cotangent=cotangent, starts=starts, norm_gain=norm_gain, w_in=w_in, conv_weight=conv_weight, conv_bias=conv_bias, dt_bias=dt_bias, a_log=a_log, skip_d=skip_d, gate_gain=gate_gain, w_out=w_out)


EPS = 1e-05
HIGH = lax.Precision.HIGHEST

@jax.custom_vjp
def low(v):
    return lax.optimization_barrier(v.astype(jnp.bfloat16)).astype(jnp.float32)

@jax.custom_vjp
def low_back(v):
    return v

def low_keep(v):
    return (low(v), None)

def low_pass(kept, grad):
    return (grad,)

def back_keep(v):
    return (v, None)

def back_low(kept, grad):
    return (low(grad),)
low.defvjp(low_keep, low_pass)
low_back.defvjp(back_keep, back_low)

def segment_of(starts_dev, places):
    owner = (places // TOK_DEV).astype(jnp.int32)
    local = (places % TOK_DEV).astype(jnp.int32)
    rows_here = starts_dev[owner]
    below = (rows_here <= local[:, None]).astype(jnp.int32)
    return (owner * SEQS + lax.optimization_barrier(jnp.sum(below, axis=1)) - 1).astype(jnp.int32)

def conv_act(segment, conv_input, conv_weight, conv_bias):
    summed = jnp.zeros_like(conv_input) + conv_bias
    for tap_index in range(KERNEL):
        back_step = KERNEL - 1 - tap_index
        shifted = jnp.pad(conv_input, ((back_step, 0), (0, 0)))[:TOKENS]
        earlier = jnp.pad(segment, (back_step, 0), constant_values=-1)[:TOKENS]
        valid = (earlier == segment).astype(jnp.float32)
        summed = summed + conv_weight[tap_index] * shifted * valid[:, None]
    return jax.nn.silu(summed)

def gated_norm(mixed, gate_input, gain):
    gated = mixed * jax.nn.silu(gate_input)
    return gated * lax.rsqrt(lax.optimization_barrier(jnp.mean(gated * gated, axis=-1, keepdims=True)) + EPS) * gain

def state_mixer(x_heads, b_state, c_state, rate_input, segment, dt_bias, a_log):
    blocks = TOKENS // BLOCK
    seg_prev = jnp.pad(segment, (1, 0), constant_values=-1)[:TOKENS].reshape(blocks, BLOCK)[:, 0]
    places = jnp.arange(BLOCK, dtype=jnp.int32)
    causal = places[:, None] >= places[None, :]

    def one_block(state_in, pieces):
        x_block, b_block, c_block, rate_block, seg_block, seg_before = pieces
        step_size = jax.nn.softplus(rate_block + dt_bias)
        log_decay = jnp.cumsum(step_size * -jnp.exp(a_log), axis=0)
        keep_mask = jnp.logical_and(seg_block[:, None] == seg_block[None, :], causal)
        by_head = jnp.transpose(log_decay)
        spread = by_head[:, :, None] - by_head[:, None, :]
        kept_vals = jnp.where(keep_mask[None], jnp.exp(jnp.where(keep_mask[None], spread, 0.0)), 0.0)
        decays = kept_vals * jnp.transpose(step_size)[:, None, :]
        gram_block = low_back(jnp.einsum('in,jn->ij', c_block, b_block, precision=HIGH))
        weights_low = low(gram_block[None] * decays)
        inner_part = jnp.einsum('hij,jhp->ihp', weights_low, x_block, precision=HIGH)
        entry_scale = (seg_block == seg_before).astype(jnp.float32)[:, None] * jnp.exp(log_decay)
        state_part = entry_scale[:, :, None] * jnp.einsum('in,hpn->ihp', c_block, state_in, precision=HIGH)
        tail_mask = (seg_block == seg_block[-1]).astype(jnp.float32)[:, None]
        ending = tail_mask * jnp.exp(log_decay[-1][None, :] - log_decay) * step_size
        state_new = jnp.einsum('jh,jhp,jn->hpn', ending, x_block, b_block, precision=HIGH)
        carry_on = (seg_block[-1] == seg_before).astype(jnp.float32) * jnp.exp(log_decay[-1])
        state_out = carry_on[:, None, None] * state_in + state_new
        return (state_out, inner_part + state_part)
    pieces = (x_heads.reshape(blocks, BLOCK, HEADS, HEAD_DIM), b_state.reshape(blocks, BLOCK, STATE), c_state.reshape(blocks, BLOCK, STATE), rate_input.reshape(blocks, BLOCK, HEADS), segment.reshape(blocks, BLOCK), seg_prev)
    state_zero = jnp.zeros((HEADS, HEAD_DIM, STATE), jnp.float32)
    final_state, outputs = lax.scan(jax.checkpoint(one_block), state_zero, pieces)
    return outputs.reshape(TOKENS, HEADS, HEAD_DIM)

def layer(rows_in, starts_dev, params):
    norm_gain, w_in, conv_weight, conv_bias, dt_bias, a_log, skip_d, gate_gain, w_out = params
    places = jnp.arange(TOKENS, dtype=jnp.int32)
    segment = segment_of(starts_dev, places)
    normed = rows_in * lax.rsqrt(lax.optimization_barrier(jnp.mean(rows_in * rows_in, axis=-1, keepdims=True)) + EPS) * norm_gain
    lowered = low(normed)
    projected = low_back(jnp.dot(lowered, w_in, precision=HIGH))
    gate_input = projected[:, :INNER]
    conv_input = projected[:, INNER:INNER + CONV_CH]
    rate_input = projected[:, INNER + CONV_CH:]
    activated = low(conv_act(segment, conv_input, conv_weight, conv_bias))
    x_heads = activated[:, :INNER].reshape(TOKENS, HEADS, HEAD_DIM)
    b_state = activated[:, INNER:INNER + STATE]
    c_state = activated[:, INNER + STATE:]
    scanned = state_mixer(x_heads, b_state, c_state, rate_input, segment, dt_bias, a_log)
    mixed = low_back(scanned + skip_d[:, None] * x_heads)
    gated_low = low(gated_norm(mixed.reshape(TOKENS, INNER), gate_input, gate_gain))
    return rows_in + jnp.dot(gated_low, w_out, precision=HIGH)

def reference(tokens, cotangent, starts, norm_gain, w_in, conv_weight, conv_bias, dt_bias, a_log, skip_d, gate_gain, w_out):
    arrays = (norm_gain, w_in, conv_weight, conv_bias, dt_bias, a_log, skip_d, gate_gain, w_out)
    first_params = tuple((member[0].astype(jnp.float32) for member in arrays))
    second_params = tuple((member[1].astype(jnp.float32) for member in arrays))
    layer_in = tokens.astype(jnp.float32)
    starts_int = starts.astype(jnp.int32)

    def run_section(inputs, params):

        def one_micro(packed):
            return layer(packed[0], packed[1], params)
        return lax.map(jax.checkpoint(one_micro), (inputs, starts_int))

    def forward(first_in, delta, params_one, params_two):
        hidden = run_section(first_in, params_one)
        passed = low_back(low(hidden)) + delta
        return (hidden, run_section(passed, params_two))
    (hidden, final), pullback = jax.vjp(forward, layer_in, jnp.zeros_like(layer_in), first_params, second_params)
    grad_first, grad_delta, grads_first, grads_second = pullback((jnp.zeros_like(hidden), cotangent.astype(jnp.float32)))
    section_out = jnp.stack([hidden, final]).astype(jnp.bfloat16)
    in_grad = jnp.stack([grad_first, grad_delta])
    stacked = [jnp.stack([first_grad, second_grad]) for first_grad, second_grad in zip(grads_first, grads_second)]
    return (section_out, in_grad, stacked[0], stacked[1], stacked[2], stacked[3], stacked[4], stacked[5], stacked[6], stacked[7], stacked[8])
```

```python
import jax
import jax.numpy as jnp
from jax import lax
from jax.experimental import pallas as pl
from jax.experimental.pallas import tpu as pltpu
from jax.sharding import Mesh, PartitionSpec as P

EPS = 1e-05
BF = jnp.bfloat16
F32 = jnp.float32
HIGH = lax.Precision.HIGHEST
D = 1536
CIN = 1152
HC = 384
NH = 6
RT = 1024
PK0 = 7
PKN = 14
HEAD0 = RT + 32
HALF = 768
ANY = pl.BlockSpec(memory_space=pl.ANY)
VM = pl.BlockSpec(memory_space=pltpu.VMEM)
SM = pl.BlockSpec(memory_space=pltpu.SMEM)
VLIM = 56 * 1024 * 1024


class Net:
    def __init__(self, ssem, rsem):
        self.ssem, self.rsem, self.n, self.all = ssem, rsem, 0, []

    def send(self, src, dst, dev):
        i = self.n
        self.n += 1
        copy = pltpu.make_async_remote_copy(
            src_ref=src,
            dst_ref=dst,
            send_sem=self.ssem.at[i],
            recv_sem=self.rsem.at[i],
            device_id=dev,
            device_id_type=pl.DeviceIdType.MESH,
        )
        copy.start()
        self.all.append(copy)
        return copy

    def finish(self):
        for copy in self.all:
            copy.wait_send()


def place():
    s, z, h, x, c = (lax.axis_index(a) for a in ("s", "z", "h", "x", "c"))
    return s, z, h, x, c


def ring(i):
    return lax.rem(i + 1, 4), lax.rem(i + 3, 4), lax.rem(i + 2, 4)


def greet(devs):
    barrier = pltpu.get_barrier_semaphore()
    for dev in devs:
        pl.semaphore_signal(barrier, inc=1, device_id=dev, device_id_type=pl.DeviceIdType.MESH)
    pl.semaphore_wait(barrier, len(devs))


def zx_devs():
    s, z, h, x, c = place()
    zr, zl, _ = ring(z)
    xr, xl, _ = ring(x)
    return [{"z": zr}, {"z": zl}, {"x": xr}, {"x": xl}]


def ydev(y):
    return {"h": y // 2, "s": lax.rem(y, 2)}


def y_devs():
    s, z, h, x, c = place()
    yr, yl, _ = ring(2 * h + s)
    return [ydev(yr), ydev(yl), {"c": 1 - c}]


def group_devs():
    s, z, h, x, c = place()
    out = []
    for k in range(1, 8):
        out.append(
            {
                "s": 1 - s if k & 4 else s,
                "h": 1 - h if k & 2 else h,
                "c": 1 - c if k & 1 else c,
            }
        )
    return out


def run(gens):
    gens = list(gens)
    while gens:
        for g in list(gens):
            try:
                next(g)
            except StopIteration:
                gens.remove(g)


def g_ag(net, blk, out, lsem):
    s, z, h, x, c = place()
    zr, zl, _ = ring(z)
    xr, xl, _ = ring(x)
    a, b = pl.ds(0, HALF), pl.ds(HALF, HALF)
    local = pltpu.make_async_copy(blk, out.at[z, :, x], lsem)
    local.start()
    a1r = net.send(blk.at[:, :, a], out.at[z, :, x, :, a], {"x": xr})
    a1l = net.send(blk.at[:, :, a], out.at[z, :, x, :, a], {"x": xl})
    b1r = net.send(blk.at[:, :, b], out.at[z, :, x, :, b], {"z": zr})
    b1l = net.send(blk.at[:, :, b], out.at[z, :, x, :, b], {"z": zl})
    yield
    a1r.wait_recv()
    r = out.at[z, 0, xl, :, a]
    a2r = net.send(r, r, {"x": xr})
    a1l.wait_recv()
    r = out.at[z, 1, xr, :, a]
    a2l = net.send(r, r, {"x": xl})
    b1r.wait_recv()
    r = out.at[zl, 0, x, :, b]
    b2r = net.send(r, r, {"z": zr})
    b1l.wait_recv()
    r = out.at[zr, 1, x, :, b]
    b2l = net.send(r, r, {"z": zl})
    yield
    local.wait()
    a2r.wait_recv()
    a2l.wait_recv()
    r = out.at[z, :, :, :, a]
    a3r = net.send(r, r, {"z": zr})
    a3l = net.send(r, r, {"z": zl})
    b2r.wait_recv()
    b2l.wait_recv()
    r = out.at[:, :, x, :, b]
    b3r = net.send(r, r, {"x": xr})
    b3l = net.send(r, r, {"x": xl})
    yield
    a3r.wait_recv()
    r = out.at[zl, 0, :, :, a]
    a4r = net.send(r, r, {"z": zr})
    a3l.wait_recv()
    r = out.at[zr, 1, :, :, a]
    a4l = net.send(r, r, {"z": zl})
    b3r.wait_recv()
    r = out.at[:, 0, xl, :, b]
    b4r = net.send(r, r, {"x": xr})
    b3l.wait_recv()
    r = out.at[:, 1, xr, :, b]
    b4l = net.send(r, r, {"x": xl})
    yield
    for copy in (a4r, a4l, b4r, b4l):
        copy.wait_recv()


def g_yag(net, own, out, lsem):
    s, z, h, x, c = place()
    y = 2 * h + s
    yr, yl, yo = ring(y)
    mine = out.at[h, c, s]
    local = None
    if lsem is not None:
        local = pltpu.make_async_copy(own, mine, lsem)
        local.start()
    else:
        own = mine
    sib = {"c": 1 - c}
    c0 = net.send(own, mine, ydev(yr))
    c1 = net.send(own, mine, ydev(yl))
    c2 = net.send(own, mine, sib)
    yield
    c0.wait_recv()
    left = out.at[yl // 2, c, lax.rem(yl, 2)]
    c3 = net.send(left.at[pl.ds(0, 64)], left.at[pl.ds(0, 64)], ydev(yr))
    c4 = net.send(left, left, sib)
    c1.wait_recv()
    right = out.at[yr // 2, c, lax.rem(yr, 2)]
    c5 = net.send(right.at[pl.ds(64, 64)], right.at[pl.ds(64, 64)], ydev(yl))
    c6 = net.send(right, right, sib)
    yield
    c3.wait_recv()
    c5.wait_recv()
    far = out.at[yo // 2, c, lax.rem(yo, 2)]
    c7 = net.send(far, far, sib)
    yield
    for copy in (c2, c4, c6, c7):
        copy.wait_recv()
    if local is not None:
        local.wait()


def xrs_scratch():
    return [
        pltpu.VMEM((4, 128, D), BF),
        pltpu.VMEM((4, 128, D), BF),
        pltpu.VMEM((2, 64, D), BF),
        pltpu.VMEM((2, 128, D), BF),
    ]


def g_xrs(net, part, bufs, done):
    cb, sb, b1, b2 = bufs
    s, z, h, x, c = place()
    y = 2 * h + s
    yr, yl, yo = ring(y)
    sib = {"c": 1 - c}
    lo, hi = pl.ds(0, 64), pl.ds(64, 64)
    units = [(k // 2, lax.rem(k, 2)) for k in (yo, yr, yl, y)]
    core = [
        net.send(part.at[units[k][0], 1 - c, units[k][1]], cb.at[k], sib) for k in range(4)
    ]
    yield

    def add(k):
        core[k].wait_recv()
        sb[k] = (part[units[k][0], c, units[k][1]].astype(F32) + cb[k].astype(F32)).astype(BF)

    add(0)
    f0 = net.send(sb.at[0, lo], b1.at[0], ydev(yr))
    f1 = net.send(sb.at[0, hi], b1.at[1], ydev(yl))
    add(1)
    g1 = net.send(sb.at[1, hi], b2.at[0, hi], ydev(yr))
    add(2)
    g2 = net.send(sb.at[2, lo], b2.at[1, lo], ydev(yl))
    yield
    f0.wait_recv()
    sb[1, lo] = (sb[1, lo].astype(F32) + b1[0].astype(F32)).astype(BF)
    g3 = net.send(sb.at[1, lo], b2.at[0, lo], ydev(yr))
    f1.wait_recv()
    sb[2, hi] = (sb[2, hi].astype(F32) + b1[1].astype(F32)).astype(BF)
    g4 = net.send(sb.at[2, hi], b2.at[1, hi], ydev(yl))
    yield
    core[3].wait_recv()
    g1.wait_recv()
    g2.wait_recv()
    g3.wait_recv()
    g4.wait_recv()
    total = part[h, c, s].astype(F32) + cb[3].astype(F32)
    done(total + b2[0].astype(F32) + b2[1].astype(F32))


def rs_scratch():
    one = [
        pltpu.VMEM((2, 4, 48, HALF), BF),
        pltpu.VMEM((2, 2, 4, 48, HALF), BF),
        pltpu.VMEM((2, 4, 48, HALF), BF),
        pltpu.VMEM((2, 4, 48, HALF), BF),
        pltpu.VMEM((2, 48, HALF), BF),
        pltpu.VMEM((2, 2, 48, HALF), BF),
        pltpu.VMEM((2, 48, HALF), BF),
    ]
    return one + one


def g_rs_half(net, unit, i, axis_i, j, axis_j, bufs, done):
    b1, b2, t, sums, b3, b4, t2 = bufs
    ir, il, io = ring(i)
    jr, jl, jo = ring(j)
    right, left = {axis_i: ir}, {axis_i: il}
    f0 = net.send(unit(io, 0), b1.at[0], right)
    f1 = net.send(unit(io, 1), b1.at[1], left)
    g0 = net.send(unit(ir, 1), b2.at[0, 1], right)
    g1 = net.send(unit(il, 0), b2.at[1, 0], left)
    yield
    f0.wait_recv()
    t[0] = (unit(ir, 0)[...].astype(F32) + b1[0].astype(F32)).astype(BF)
    g2 = net.send(t.at[0], b2.at[0, 0], right)
    f1.wait_recv()
    t[1] = (unit(il, 1)[...].astype(F32) + b1[1].astype(F32)).astype(BF)
    g3 = net.send(t.at[1], b2.at[1, 1], left)
    yield
    for copy in (g0, g1, g2, g3):
        copy.wait_recv()
    for p in range(2):
        sums[p] = (
            unit(i, p)[...].astype(F32) + b2[0, p].astype(F32) + b2[1, p].astype(F32)
        ).astype(BF)
    right, left = {axis_j: jr}, {axis_j: jl}
    f0 = net.send(sums.at[0, jo], b3.at[0], right)
    f1 = net.send(sums.at[1, jo], b3.at[1], left)
    g0 = net.send(sums.at[1, jr], b4.at[0, 1], right)
    g1 = net.send(sums.at[0, jl], b4.at[1, 0], left)
    yield
    f0.wait_recv()
    t2[0] = (sums[0, jr].astype(F32) + b3[0].astype(F32)).astype(BF)
    g2 = net.send(t2.at[0], b4.at[0, 0], right)
    f1.wait_recv()
    t2[1] = (sums[1, jl].astype(F32) + b3[1].astype(F32)).astype(BF)
    g3 = net.send(t2.at[1], b4.at[1, 1], left)
    yield
    for copy in (g0, g1, g2, g3):
        copy.wait_recv()
    for p in range(2):
        done(p, sums[p, j].astype(F32) + b4[0, p].astype(F32) + b4[1, p].astype(F32))


def g_rs(net, grads, out, bufs):
    s, z, h, x, c = place()
    a, b = pl.ds(0, HALF), pl.ds(HALF, HALF)

    def put_a(p, v):
        out[p, :, 0:HALF] = v.astype(BF)

    def put_b(p, v):
        out[p, :, HALF:D] = v.astype(BF)

    ga = g_rs_half(
        net, lambda i, p: grads.at[i, p, :, :, a], z, "z", x, "x", bufs[:7], put_a
    )
    gb = g_rs_half(
        net, lambda i, p: grads.at[:, p, i, :, b], x, "x", z, "z", bufs[7:], put_b
    )
    return [ga, gb]


def g_stats(net, mine, total, sb):
    sends = [net.send(mine, sb.at[k], dev) for k, dev in enumerate(group_devs())]
    yield
    acc = mine[...]
    for k, copy in enumerate(sends):
        copy.wait_recv()
        acc = acc + sb[k]
    total[...] = acc


def class_devs():
    s, z, h, x, c = place()
    return [
        {"z": lax.rem(z + k // 4, 4), "x": lax.rem(x + k % 4, 4)} for k in range(1, 16)
    ]


def g_heads(net, mine, total, hb):
    s, z, h, x, c = place()
    sends = [net.send(mine, hb.at[z, x], dev) for dev in class_devs()]
    hb[z, x] = mine[...]
    yield
    for copy in sends:
        copy.wait_recv()
    acc = hb[0, 0]
    for k in range(1, 16):
        acc = acc + hb[k // 4, k % 4]
    total[...] = acc


def heads_scratch():
    return [pltpu.VMEM((4, 4, 8, 128), F32)]


def params(cid):
    return pltpu.CompilerParams(
        collective_id=cid, has_side_effects=True, vmem_limit_bytes=VLIM
    )


def sems(n):
    return [pltpu.SemaphoreType.DMA((n,)), pltpu.SemaphoreType.DMA((n,))]


GATHERED = jax.ShapeDtypeStruct((4, 2, 4, 48, D), BF)
CHUNKS = jax.ShapeDtypeStruct((2, 2, 2, 128, D), BF)
HEADS = jax.ShapeDtypeStruct((8, 128), F32)
CHUNK = jax.ShapeDtypeStruct((128, D), BF)


def first_gathers(blk, tok, cot):
    def kernel(blk, tok, cot, w, tall, call, lsem, ssem, rsem):
        greet(zx_devs() + y_devs())
        net = Net(ssem, rsem)
        run(
            [
                g_ag(net, blk, w, lsem.at[0]),
                g_yag(net, tok, tall, lsem.at[1]),
                g_yag(net, cot, call, lsem.at[2]),
            ]
        )
        net.finish()

    return pl.pallas_call(
        kernel,
        name="first_gathers",
        out_shape=(GATHERED, CHUNKS, CHUNKS),
        in_specs=[ANY] * 3,
        out_specs=(ANY,) * 3,
        scratch_shapes=[pltpu.SemaphoreType.DMA((3,))] + sems(40),
        compiler_params=params(0),
    )(blk, tok, cot)


def row_to_col(row):
    i = lax.broadcasted_iota(jnp.int32, (128, 128), 0)
    j = lax.broadcasted_iota(jnp.int32, (128, 128), 1)
    return jnp.sum(jnp.where(i == j, row, 0.0), axis=1, keepdims=True)


def col_to_row(col):
    i = lax.broadcasted_iota(jnp.int32, (128, 128), 0)
    j = lax.broadcasted_iota(jnp.int32, (128, 128), 1)
    return jnp.sum(jnp.where(i == j, col, 0.0), axis=0, keepdims=True)


def own_scale(total):
    s, z, h, x, c = place()
    row = total[pl.ds((2 * h + c) * 2 + s, 1), :]
    return lax.rsqrt(row_to_col(row) * (1.0 / 3072) + EPS)


def forward_sum(part, stat, x_own, blk):
    def kernel(part, stat, xo, blk, xall, w, total, fin, cb, sb, b1, b2, stb, lsem, ssem, rsem):
        greet(zx_devs() + group_devs())
        net = Net(ssem, rsem)
        s, z, h, x, c = place()

        def done(v):
            fin[...] = (xo[...].astype(F32) + own_scale(total) * v).astype(BF)

        run(
            [
                g_stats(net, stat, total, stb),
                g_xrs(net, part, (cb, sb, b1, b2), done),
                g_ag(net, blk, w, lsem.at[0]),
            ]
        )
        run([g_yag(net, fin, xall, lsem.at[1])])
        net.finish()

    return pl.pallas_call(
        kernel,
        name="forward_sum",
        out_shape=(CHUNKS, GATHERED, jax.ShapeDtypeStruct((8, 128), F32)),
        in_specs=[VM, VM, VM, ANY],
        out_specs=(ANY, ANY, VM),
        scratch_shapes=[pltpu.VMEM((128, D), BF)]
        + xrs_scratch()
        + [pltpu.VMEM((7, 8, 128), F32), pltpu.SemaphoreType.DMA((2,))]
        + sems(48),
        compiler_params=params(1),
    )(part, stat, x_own, blk)


def stats_sum(stat):
    def kernel(stat, total, stb, ssem, rsem):
        greet(group_devs())
        net = Net(ssem, rsem)
        run([g_stats(net, stat, total, stb)])
        net.finish()

    return pl.pallas_call(
        kernel,
        name="stats_sum",
        out_shape=jax.ShapeDtypeStruct((16, 128), F32),
        in_specs=[VM],
        out_specs=VM,
        scratch_shapes=[pltpu.VMEM((7, 16, 128), F32)] + sems(8),
        compiler_params=params(2),
    )(stat)


def norm_back(v, xo, eo, ng):
    xf = xo[...].astype(F32)
    vg = v * ng[...]
    r = lax.rsqrt(jnp.mean(xf * xf, axis=-1, keepdims=True) + EPS)
    dot = jnp.mean(xf * vg, axis=-1, keepdims=True)
    return eo[...].astype(F32) + r * vg - xf * (r * r * r * dot)


def backward_sum(part, x_own, e_own, ng, grads, heads):
    def kernel(part, xo, eo, ng, grads, heads, eall, out, hsum, fin, cb, sb, b1, b2, *rest):
        bufs, (hb, lsem, ssem, rsem) = rest[:14], rest[14:]
        greet(class_devs() + y_devs())
        net = Net(ssem, rsem)

        def done(v):
            fin[...] = norm_back(v, xo, eo, ng).astype(BF)

        def chain():
            yield from g_xrs(net, part, (cb, sb, b1, b2), done)
            yield from g_yag(net, fin, eall, lsem.at[0])

        run([chain()] + g_rs(net, grads, out, bufs) + [g_heads(net, heads, hsum, hb)])
        net.finish()

    return pl.pallas_call(
        kernel,
        name="backward_sum",
        out_shape=(CHUNKS, jax.ShapeDtypeStruct((2, 48, D), BF), HEADS),
        in_specs=[VM] * 6,
        out_specs=(ANY, VM, VM),
        scratch_shapes=[pltpu.VMEM((128, D), BF)]
        + xrs_scratch()
        + rs_scratch()
        + heads_scratch()
        + [pltpu.SemaphoreType.DMA((1,))]
        + sems(64),
        compiler_params=params(3),
    )(part, x_own, e_own, ng, grads, heads)


def last_sums(part0, x_own, e_own, ng, part1, x1_own, stat1, grads, heads):
    def kernel(p0, xo, eo, ng, p1, x1, st, grads, heads, ig, so, out, hsum, *rest):
        ba, bb, bufs, (hb, ssem, rsem) = rest[:4], rest[4:8], rest[8:22], rest[22:]
        greet(class_devs() + y_devs())
        net = Net(ssem, rsem)

        def done0(v):
            ig[...] = norm_back(v, xo, eo, ng).astype(BF)

        def done1(v):
            so[...] = (x1[...].astype(F32) + own_scale(st) * v).astype(BF)

        run(
            [g_xrs(net, p0, ba, done0)]
            + g_rs(net, grads, out, bufs)
            + [g_xrs(net, p1, bb, done1), g_heads(net, heads, hsum, hb)]
        )
        net.finish()

    return pl.pallas_call(
        kernel,
        name="last_sums",
        out_shape=(CHUNK, CHUNK, jax.ShapeDtypeStruct((2, 48, D), BF), HEADS),
        in_specs=[VM] * 9,
        out_specs=(VM,) * 4,
        scratch_shapes=xrs_scratch()
        + xrs_scratch()
        + rs_scratch()
        + heads_scratch()
        + sems(72),
        compiler_params=params(4),
    )(part0, x_own, e_own, ng, part1, x1_own, stat1, grads, heads)


def nt(a, b):
    return lax.dot_general(a, b, (((1,), (1,)), ((), ())), preferred_element_type=F32)


def tn(a, b):
    return lax.dot_general(a, b, (((0,), (0,)), ((), ())), preferred_element_type=F32)


def iotas():
    i = lax.broadcasted_iota(jnp.int32, (128, 128), 0)
    j = lax.broadcasted_iota(jnp.int32, (128, 128), 1)
    return i, j


def seg_of(st, chunk, places):
    seg = jnp.full(places.shape, -1, jnp.int32)
    for k in range(4):
        seg = seg + (st[chunk, k] <= places).astype(jnp.int32)
    return seg


def masks(st, chunk):
    i, j = iotas()
    seg = seg_of(st, chunk, i)
    keep = jnp.logical_and(seg == seg_of(st, chunk, j), i >= j)
    valid = [None] + [
        (seg_of(st, chunk, i - k) == seg).astype(F32) for k in range(1, 4)
    ]
    return keep, valid


def conv_tile(xt, cv, t, valid):
    lanes = slice(128 * t, 128 * t + 128)
    pre = cv[4:5, lanes] + cv[3:4, lanes] * xt
    moved = [xt]
    for k in range(1, 4):
        m = pltpu.roll(xt, k, axis=0) * valid[k]
        moved.append(m)
        pre = pre + cv[3 - k : 4 - k, lanes] * m
    return pre, moved


def rates(rt, cv):
    i, j = iotas()
    head = j < NH
    v = rt + cv[7:8, 0:128]
    dt = jnp.where(head, jnp.maximum(v, 0.0) + jnp.log1p(jnp.exp(-jnp.abs(v))), 0.0)
    lower = (i >= j).astype(F32)
    cum = jnp.dot(
        lower, -dt * cv[8:9, 0:128], precision=HIGH, preferred_element_type=F32
    )
    return v, dt, cum


def half_masks():
    _, j = iotas()
    return j < 64


def split_pair(v, low):
    zero = jnp.zeros_like(v)
    return jnp.concatenate([jnp.where(low, v, zero), jnp.where(low, zero, v)], axis=0)


def decay_of(keep, cum, cum_t, h):
    spread = jnp.where(keep, cum[:, h : h + 1] - cum_t[h : h + 1, :], -1e30)
    return jnp.exp(spread)


def load_const(cv):
    return cv[...]


def front(xb, w, ng, u_out):
    xf = xb[...].astype(F32)
    r = lax.rsqrt(jnp.mean(xf * xf, axis=-1, keepdims=True) + EPS)
    u = (xf * r * ng[...]).astype(BF)
    u_out[...] = u
    return jnp.dot(u, w[:, 0:CIN], preferred_element_type=F32)


def make_forward(with_do):
    def kernel(st, x, w, ng, cv, *rest):
        if with_do:
            e, part, stat, proj, yout, uout, doo, og = rest
        else:
            part, stat, proj, yout, uout, og = rest
        step = pl.program_id(0)
        proj[...] = front(x, w, ng, uout)
        if with_do:
            doo[...] = jnp.dot(e[...], w[:, CIN:D], preferred_element_type=F32)
        low = half_masks()
        for m in range(2):
            rows = slice(128 * m, 128 * m + 128)
            chunk = step * 2 + m
            keep, valid = masks(st, chunk)
            act = []
            for t in range(5):
                pre, _ = conv_tile(proj[rows, HC + 128 * t : HC + 128 * t + 128], cv, t, valid)
                act.append((pre * jax.nn.sigmoid(pre)).astype(BF))
            _, dt, cum = rates(proj[rows, RT:CIN], cv)
            cum_t, dt_t = jnp.transpose(cum), jnp.transpose(dt)
            gram = nt(act[4], act[3])
            gsum = jnp.zeros((128, 1), F32)
            tsum = jnp.zeros((128, 1), F32)
            for t in range(3):
                lanes = slice(128 * t, 128 * t + 128)
                mixes = []
                for h in (2 * t, 2 * t + 1):
                    dec = decay_of(keep, cum, cum_t, h)
                    mixes.append((gram * dec * dt_t[h : h + 1, :]).astype(BF))
                y = jnp.dot(
                    jnp.concatenate(mixes, axis=1),
                    split_pair(act[t], low),
                    preferred_element_type=F32,
                )
                y = y + cv[6:7, lanes] * act[t].astype(F32)
                yout[rows, lanes] = y
                zt = proj[rows, lanes]
                g = y * (zt * jax.nn.sigmoid(zt))
                gsum = gsum + jnp.sum(g * g, axis=1, keepdims=True)
                gain = cv[5:6, lanes]
                og[rows, lanes] = (g * gain).astype(BF)
                if with_do:
                    tsum = tsum + jnp.sum(g * gain * doo[rows, lanes], axis=1, keepdims=True)
            stat[pl.ds(chunk, 1), :] = col_to_row(gsum)
            if with_do:
                stat[pl.ds(chunk + 8, 1), :] = col_to_row(tsum)
        part[...] = nt(og[...], w[:, CIN:D]).astype(BF)

    return kernel


def rows_spec(cols):
    return pl.BlockSpec((256, cols), lambda i: (i, 0))


def whole(*shape):
    return pl.BlockSpec(shape, lambda i: (0,) * len(shape))


def layer_forward(st, x, w, ng, cv, e=None):
    with_do = e is not None
    n_stat = 16 if with_do else 8
    ins = [st, x, w, ng, cv] + ([e] if with_do else [])
    in_specs = [SM, rows_spec(D), whole(D, D), whole(1, D), whole(16, 640)] + (
        [rows_spec(D)] if with_do else []
    )
    outs = [
        jax.ShapeDtypeStruct((1024, D), BF),
        jax.ShapeDtypeStruct((n_stat, 128), F32),
        jax.ShapeDtypeStruct((1024, CIN), F32),
        jax.ShapeDtypeStruct((1024, HC), F32),
        jax.ShapeDtypeStruct((1024, D), BF),
    ] + ([jax.ShapeDtypeStruct((1024, HC), F32)] if with_do else [])
    out_specs = [
        rows_spec(D),
        whole(n_stat, 128),
        rows_spec(CIN),
        rows_spec(HC),
        rows_spec(D),
    ] + ([rows_spec(HC)] if with_do else [])
    return pl.pallas_call(
        make_forward(with_do),
        name="layer_forward",
        grid=(4,),
        in_specs=in_specs,
        out_specs=out_specs,
        out_shape=outs,
        scratch_shapes=[pltpu.VMEM((256, HC), BF)],
        compiler_params=pltpu.CompilerParams(vmem_limit_bytes=VLIM),
    )(*ins)


def make_backward(first):
    def kernel(st, e, w, cv, proj, yin, stat, *rest):
        if first:
            x, x1, dproj, oo, part, sm, do = rest
        else:
            do, dproj, oo, part, sm = rest
        step = pl.program_id(0)

        @pl.when(step == 0)
        def _():
            sm[...] = jnp.zeros_like(sm)

        if first:
            do[...] = jnp.dot(e[...], w[:, CIN:D], preferred_element_type=F32)
        low = half_masks()
        i, j = iotas()
        upper = (j >= i).astype(F32)

        def add(row, lanes, v):
            sm[row : row + 1, lanes] += jnp.sum(v, axis=0, keepdims=True)

        for m in range(2):
            rows = slice(128 * m, 128 * m + 128)
            chunk = step * 2 + m
            keep, valid = masks(st, chunk)
            pres, moves, act = [], [], []
            for t in range(5):
                pre, moved = conv_tile(
                    proj[rows, HC + 128 * t : HC + 128 * t + 128], cv, t, valid
                )
                pres.append(pre)
                moves.append(moved)
                act.append((pre * jax.nn.sigmoid(pre)).astype(BF))
            v, dt, cum = rates(proj[rows, RT:CIN], cv)
            cum_t, dt_t = jnp.transpose(cum), jnp.transpose(dt)
            gram = nt(act[4], act[3])
            r = lax.rsqrt(row_to_col(stat[pl.ds(chunk, 1), :]) * (1.0 / 3072) + EPS)
            if first:
                dots = jnp.sum(
                    e[rows, :].astype(F32) * (x1[rows, :].astype(F32) - x[rows, :].astype(F32)),
                    axis=1,
                    keepdims=True,
                )
                k = r * r * dots * (1.0 / 3072)
            else:
                k = r * r * r * row_to_col(stat[pl.ds(chunk + 8, 1), :]) * (1.0 / 3072)
            dact = []
            dgram = jnp.zeros((128, 128), F32)
            dcum = jnp.zeros((128, 128), F32)
            col_rows = []
            for t in range(3):
                lanes = slice(128 * t, 128 * t + 128)
                zt, y, dot_ = proj[rows, lanes], yin[rows, lanes], do[rows, lanes]
                gain = cv[5:6, lanes]
                sig = jax.nn.sigmoid(zt)
                sz = zt * sig
                g = y * sz
                oo[rows, lanes] = (g * r * gain).astype(BF)
                add(5, lanes, dot_ * g * r)
                dg = r * (dot_ * gain) - g * k
                dproj[rows, lanes] = (dg * y * (sig + sz * (1.0 - sig))).astype(BF)
                dy = (dg * sz).astype(BF)
                dyf = dy.astype(F32)
                xs = act[t]
                add(6, lanes, dyf * xs.astype(F32))
                dy2 = split_pair(dy, low)
                dmix2 = nt(dy2, xs)
                mixes = []
                for q in range(2):
                    h = 2 * t + q
                    dec = decay_of(keep, cum, cum_t, h)
                    dt_row = dt_t[h : h + 1, :]
                    pm = gram * dec
                    mixes.append((pm * dt_row).astype(BF))
                    dmix = dmix2[128 * q : 128 * q + 128]
                    dgram = dgram + dmix * (dec * dt_row)
                    vm = dmix * pm
                    col_rows.append(jnp.sum(vm, axis=0, keepdims=True))
                    rsum = jnp.sum(vm * dt_row, axis=1, keepdims=True)
                    dcum = dcum + jnp.where(j == h, rsum, 0.0)
                dxs = tn(jnp.concatenate(mixes, axis=0), dy2)
                dact.append(dxs + cv[6:7, lanes] * dyf)
            dgl = dgram.astype(BF)
            dact.append(tn(dgl, act[4]))
            dact.append(jnp.dot(dgl, act[3], preferred_element_type=F32))
            ddt = jnp.transpose(
                jnp.concatenate(col_rows + [jnp.zeros((128 - NH, 128), F32)], axis=0)
            )
            dcum = dcum - ddt * dt
            dla = jnp.dot(upper, dcum, precision=HIGH, preferred_element_type=F32)
            nexp = -cv[8:9, 0:128]
            drate = (ddt + dla * nexp) * jax.nn.sigmoid(v)
            drate = jnp.where(j < NH, drate, 0.0)
            add(7, slice(0, 128), drate)
            add(8, slice(0, 128), dla * dt * nexp)
            dproj[rows, RT:CIN] = drate.astype(BF)
            for t in range(5):
                lanes = slice(128 * t, 128 * t + 128)
                pre = pres[t]
                sp = jax.nn.sigmoid(pre)
                dpre = dact[t] * (sp + pre * sp * (1.0 - sp))
                add(4, lanes, dpre)
                add(3, lanes, dpre * moves[t][0])
                dx = cv[3:4, lanes] * dpre
                for n in range(1, 4):
                    add(3 - n, lanes, dpre * moves[t][n])
                    dx = dx + cv[3 - n : 4 - n, lanes] * pltpu.roll(
                        dpre * valid[n], 128 - n, axis=0
                    )
                dproj[rows, HC + 128 * t : HC + 128 * t + 128] = dx.astype(BF)
        part[...] = nt(dproj[...], w[:, 0:CIN]).astype(BF)

    return kernel


def layer_backward(st, e, w, cv, proj, y, stat, do=None, x=None, x1=None):
    first = do is None
    extra = [x, x1] if first else [do]
    ins = [st, e, w, cv, proj, y, stat] + extra
    in_specs = [
        SM,
        rows_spec(D),
        whole(D, D),
        whole(16, 640),
        rows_spec(CIN),
        rows_spec(HC),
        whole(*stat.shape),
    ] + ([rows_spec(D), rows_spec(D)] if first else [rows_spec(HC)])
    outs = [
        jax.ShapeDtypeStruct((1024, CIN), BF),
        jax.ShapeDtypeStruct((1024, HC), BF),
        jax.ShapeDtypeStruct((1024, D), BF),
        jax.ShapeDtypeStruct((16, 640), F32),
    ]
    return pl.pallas_call(
        make_backward(first),
        name="layer_backward",
        grid=(4,),
        in_specs=in_specs,
        out_specs=[rows_spec(CIN), rows_spec(HC), rows_spec(D), whole(16, 640)],
        out_shape=outs,
        scratch_shapes=[pltpu.VMEM((256, HC), F32)] if first else [],
        compiler_params=pltpu.CompilerParams(vmem_limit_bytes=VLIM),
    )(*ins)


def pack_shards(starts, norm_gain, w_in, conv_weight, conv_bias, gate_gain, w_out):
    small = jnp.concatenate(
        [
            conv_weight.reshape(-1),
            conv_bias,
            gate_gain,
            starts.reshape(-1).astype(BF),
            jnp.zeros((20,), BF),
        ]
    ).reshape(24, PKN)
    wide = jnp.concatenate([norm_gain[:, None], small], axis=1)

    def each(v):
        return jnp.broadcast_to(v[:, None], (24, 8, v.shape[-1]))

    rate = jnp.concatenate(
        [w_in[:, 6400:].reshape(24, 8, NH), each(wide), jnp.zeros((24, 8, 107), BF)], axis=-1
    )
    pieces = jnp.concatenate(
        [
            w_in[:, :3072].reshape(24, 8, HC),
            w_in[:, 3072:6144].reshape(24, 8, HC),
            each(w_in[:, 6144:6400]),
            rate,
            jnp.transpose(w_out).reshape(24, 8, HC),
        ],
        axis=-1,
    )
    return jnp.transpose(pieces, (1, 0, 2))


def constants(w, q, dt_bias, a_log, skip_d):
    tile = w[:, RT : RT + 128].astype(F32)
    ng = tile[:, NH][None]
    small = tile[:, PK0 : PK0 + PKN].reshape(64, 24 * PKN)
    taps = jnp.transpose(small[:, :208].reshape(64, 4, 52), (1, 0, 2)).reshape(4, 3328)
    conv = jnp.concatenate([taps, small[:, 208:260].reshape(1, 3328)], axis=0)
    gate = small[:, 260:308].reshape(1, 3072)
    conv = jnp.concatenate(
        [lax.dynamic_slice_in_dim(conv, q * HC, HC, 1), conv[:, 3072:]], axis=1
    )
    gate = lax.dynamic_slice_in_dim(gate, q * HC, HC, 1)

    def heads(v):
        return lax.dynamic_slice_in_dim(v, q * NH, NH, 0)

    skip = jnp.repeat(heads(skip_d), 64)[None]
    pad = lambda v: jnp.pad(v, ((0, 0), (0, 640 - v.shape[1])))
    rows = [
        conv,
        pad(gate),
        pad(skip),
        pad(heads(dt_bias)[None]),
        pad(heads(jnp.exp(a_log))[None]),
        jnp.zeros((7, 640), F32),
    ]
    return jnp.concatenate(rows, axis=0), ng


def pack_grads(u, dproj, e, o, sm, q):
    gin = tn(u, dproj)
    gout = tn(e, o)
    conv = jnp.zeros((5, 3328), F32)
    conv = lax.dynamic_update_slice(conv, sm[0:5, :HC], (0, q * HC))
    conv = lax.dynamic_update_slice(conv, sm[0:5, HC:640], (0, 3072))
    gate = lax.dynamic_update_slice(jnp.zeros((3072,), F32), sm[5, :HC], (q * HC,))
    heads = jnp.concatenate(
        [sm[7:9, :128], sm[6, :HC].reshape(3, 128), jnp.zeros((3, 128), F32)], axis=0
    )
    small = jnp.concatenate(
        [
            jnp.transpose(conv.reshape(5, 64, 52), (1, 0, 2)).reshape(64, 260),
            gate.reshape(64, 48),
            jnp.zeros((64, 28), F32),
        ],
        axis=1,
    ).reshape(D, PKN)
    tile = gin[:, RT:CIN] + jnp.pad(small, ((0, 0), (PK0, 128 - PK0 - PKN)))
    grads = jnp.concatenate(
        [gin[:, :RT].astype(BF), tile.astype(BF), gout.astype(BF)], axis=1
    ).reshape(4, 2, 4, 48, D)
    return grads, heads


def head_row(total):
    return jnp.concatenate(
        [total[0, :NH], total[1, :NH], jnp.sum(total[2:5].reshape(NH, 64), axis=1)]
    )


def unpack_grads(rec, w_in, norm_gain):
    rec = rec.astype(F32)
    flat = lambda v: jnp.transpose(v, (1, 0, 2)).reshape(24, -1)
    tile = rec[:, :, RT:CIN]
    w_in_grad = jnp.concatenate(
        [
            flat(rec[:, :, 0:HC]),
            flat(rec[:, :, HC : 2 * HC]),
            jnp.sum(rec[:, :, 2 * HC : RT], axis=0),
            flat(tile[:, :, :NH]),
        ],
        axis=1,
    )
    w_out_grad = jnp.transpose(flat(rec[:, :, CIN:D]))
    small = tile[:, :, PK0 : PK0 + PKN].reshape(8, 24 * PKN)
    total = jnp.sum(small, axis=0)
    heads = rec[:, 0, HEAD0 : HEAD0 + 18].reshape(8, 3, NH)
    norm_grad = jnp.sum(w_in.astype(F32) * w_in_grad, axis=1) / norm_gain.astype(F32)
    return (
        norm_grad,
        w_in_grad,
        total[:208].reshape(4, 52),
        total[208:260],
        heads[:, 0].reshape(48),
        heads[:, 1].reshape(48),
        heads[:, 2].reshape(48),
        total[260:308],
        w_out_grad,
    )


GROUP = ("s", "h", "c")


def body(
    tokens,
    cotangent,
    starts,
    norm_gain,
    w_in,
    conv_weight,
    conv_bias,
    dt_bias,
    a_log,
    skip_d,
    gate_gain,
    w_out,
):
    s, z, h, x, c = place()
    q = (s * 2 + h) * 2 + c
    mine = pack_shards(
        starts[:, 0], norm_gain[0], w_in[0], conv_weight[0], conv_bias[0], gate_gain[0], w_out[0]
    )
    rec = lax.all_to_all(mine, GROUP, 0, 0, tiled=True)
    blocks = rec.reshape(2, 2, 48, D)
    st = (
        rec[0:4, :, RT + PK0 : RT + PK0 + PKN]
        .reshape(4, 24 * PKN)[:, 308:316]
        .reshape(8, 4)
        .astype(jnp.int32)
    )
    heads = jnp.stack([dt_bias[0], a_log[0], skip_d[0]])
    other = lax.ppermute(heads, "s", [(0, 1), (1, 0)])
    heads0 = jnp.where(s == 0, heads, other)
    heads1 = jnp.where(s == 0, other, heads)

    tok_own = jnp.where(s == 0, tokens[0], tokens[1])
    cot_own = jnp.where(s == 0, cotangent[0], cotangent[1])
    w0, tall, call = first_gathers(blocks[0], tok_own, cot_own)
    w0 = w0.reshape(D, D)
    x0 = tall.reshape(1024, D)
    e1 = call.reshape(1024, D)
    cv0, ng0 = constants(w0, q, heads0[0], heads0[1], heads0[2])
    part, stat0, proj0, y0, u0 = layer_forward(st, x0, w0, ng0, cv0)
    xall, w1, stat0 = forward_sum(part.reshape(2, 2, 2, 128, D), stat0, tok_own, blocks[1])
    w1 = w1.reshape(D, D)
    x1 = xall.reshape(1024, D)
    cv1, ng1 = constants(w1, q, heads1[0], heads1[1], heads1[2])
    part1, stat1, proj1, y1, u1, do1 = layer_forward(st, x1, w1, ng1, cv1, e1)
    stat1 = stats_sum(stat1)
    dproj1, o1, dpart1, sm1 = layer_backward(st, e1, w1, cv1, proj1, y1, stat1, do=do1)
    grads1, hs1 = pack_grads(u1, dproj1, e1, o1, sm1, q)
    x1_own = jnp.where(s == 0, xall[h, c, 0], xall[h, c, 1])
    eall, gs1, hs1 = backward_sum(
        dpart1.reshape(2, 2, 2, 128, D), x1_own, cot_own, ng1, grads1, hs1
    )
    e0 = eall.reshape(1024, D)
    dproj0, o0, dpart0, sm0 = layer_backward(st, e0, w0, cv0, proj0, y0, stat0, x=x0, x1=x1)
    grads0, hs0 = pack_grads(u0, dproj0, e0, o0, sm0, q)
    e0_own = jnp.where(s == 0, eall[h, c, 0], eall[h, c, 1])
    ig0, so1, gs0, hs0 = last_sums(
        dpart0.reshape(2, 2, 2, 128, D),
        tok_own,
        e0_own,
        ng0,
        part1.reshape(2, 2, 2, 128, D),
        x1_own,
        stat1[0:8],
        grads0,
        hs0,
    )
    hrow = jnp.repeat(jnp.stack([head_row(hs0), head_row(hs1)]), 4, axis=0)
    hrow = jnp.pad(hrow[:, None], ((0, 0), (0, 23), (HEAD0, D - HEAD0 - 18)))
    back = jnp.stack([gs0, gs1]).reshape(8, 24, D) + hrow.astype(BF)
    back = lax.all_to_all(back, GROUP, 0, 0, tiled=True)
    outs = unpack_grads(back, w_in[0], norm_gain[0])

    got = lax.ppermute(jnp.where(s == 0, so1, ig0), "s", [(0, 1), (1, 0)])
    ig = jnp.where(s == 0, jnp.stack([ig0, got]), eall[h, c])
    so = jnp.where(s == 0, xall[h, c], jnp.stack([got, so1]))
    return (so[None], ig.astype(F32)[None]) + tuple(o[None] for o in outs)


def solution(mesh):
    inner = Mesh(mesh.devices.reshape(2, 4, 2, 4, 2), ("s", "z", "h", "x", "c"))
    dp = ("z", "h", "x", "c")
    in_specs = (
        P(None, dp, None),
        P(None, dp, None),
        P(None, dp, None),
        P("s", dp),
        P("s", dp, None),
        P("s", None, dp),
        P("s", dp),
        P("s", None),
        P("s", None),
        P("s", None),
        P("s", dp),
        P("s", None, dp),
    )
    out_specs = (
        P("s", None, dp, None),
        P("s", None, dp, None),
        P("s", dp),
        P("s", dp, None),
        P("s", None, dp),
        P("s", dp),
        P("s", None),
        P("s", None),
        P("s", None),
        P("s", dp),
        P("s", None, dp),
    )
    return jax.shard_map(body, mesh=inner, in_specs=in_specs, out_specs=out_specs, check_vma=False)
```

```python
import jax
import jax.numpy as jnp
from jax import lax
from jax.experimental import pallas as pl
from jax.experimental.pallas import tpu as pltpu
from jax.sharding import Mesh, PartitionSpec as P

EPS = 1e-05
BF = jnp.bfloat16
F32 = jnp.float32
HIGH = lax.Precision.HIGHEST
D = 1536
CIN = 1152
HC = 384
NH = 6
RT = 1024
PK0 = 7
PKN = 14
HEAD0 = RT + 32
HALF = 768
ANY = pl.BlockSpec(memory_space=pl.ANY)
VM = pl.BlockSpec(memory_space=pltpu.VMEM)
SM = pl.BlockSpec(memory_space=pltpu.SMEM)
VLIM = 56 * 1024 * 1024


class Net:
    def __init__(self, ssem, rsem):
        self.ssem, self.rsem, self.n, self.all = ssem, rsem, 0, []

    def send(self, src, dst, dev):
        i = self.n
        self.n += 1
        assert i < self.ssem.shape[0]
        copy = pltpu.make_async_remote_copy(
            src_ref=src,
            dst_ref=dst,
            send_sem=self.ssem.at[i],
            recv_sem=self.rsem.at[i],
            device_id=dev,
            device_id_type=pl.DeviceIdType.MESH,
        )
        copy.start()
        self.all.append(copy)
        return copy

    def finish(self):
        for copy in self.all:
            copy.wait_send()


def place():
    s, z, h, x, c = (lax.axis_index(a) for a in ("s", "z", "h", "x", "c"))
    return s, z, h, x, c


def ring(i):
    return lax.rem(i + 1, 4), lax.rem(i + 3, 4), lax.rem(i + 2, 4)


def greet(devs):
    barrier = pltpu.get_barrier_semaphore()
    for dev in devs:
        pl.semaphore_signal(barrier, inc=1, device_id=dev, device_id_type=pl.DeviceIdType.MESH)
    pl.semaphore_wait(barrier, len(devs))


def zx_devs():
    s, z, h, x, c = place()
    zr, zl, _ = ring(z)
    xr, xl, _ = ring(x)
    return [{"z": zr}, {"z": zl}, {"x": xr}, {"x": xl}]


def ydev(y):
    return {"h": y // 2, "s": lax.rem(y, 2)}


def y_devs():
    s, z, h, x, c = place()
    yr, yl, _ = ring(2 * h + s)
    return [ydev(yr), ydev(yl), {"c": 1 - c}]


def group_devs():
    s, z, h, x, c = place()
    out = []
    for k in range(1, 8):
        out.append(
            {
                "s": 1 - s if k & 4 else s,
                "h": 1 - h if k & 2 else h,
                "c": 1 - c if k & 1 else c,
            }
        )
    return out


LAT = 1.7


def inter(gens):
    gens = [[0.0, g] for g in gens]
    while gens:
        item = min(gens, key=lambda v: v[0])
        if item[0] > 0:
            yield item[0]
        try:
            item[0] = next(item[1])
        except StopIteration:
            gens.remove(item)


def run(gens):
    for _ in inter(gens):
        pass


def g_ag_part(net, blk, out, local, i, axis_i, j, axis_j, pick, lanes, times):
    ir, il, io = ring(i)
    jr, jl, jo = ring(j)
    right, left = {axis_i: ir}, {axis_i: il}
    every = slice(None)

    def at(i, j, p):
        return out.at[pick(i, j, p) + (every, lanes)]

    own = blk.at[:, :, lanes]
    a1r = net.send(own, at(i, j, every), right)
    a1l = net.send(own, at(i, j, every), left)
    yield times[0]
    a1r.wait_recv()
    r = at(il, j, 0)
    a2r = net.send(r, r, right)
    a1l.wait_recv()
    r = at(ir, j, 1)
    a2l = net.send(r, r, left)
    yield times[1]
    a2r.wait_recv()
    a2l.wait_recv()
    local.wait()
    right, left = {axis_j: jr}, {axis_j: jl}
    r = at(every, j, every)
    a3r = net.send(r, r, right)
    a3l = net.send(r, r, left)
    yield times[2]
    a3r.wait_recv()
    r = at(every, jl, 0)
    a4r = net.send(r, r, right)
    a3l.wait_recv()
    r = at(every, jr, 1)
    a4l = net.send(r, r, left)
    yield times[3]
    a4r.wait_recv()
    a4l.wait_recv()


class Once:
    def __init__(self, copy):
        self.copy, self.open = copy, True
        copy.start()

    def wait(self):
        if self.open:
            self.copy.wait()
        self.open = False


def g_ag(net, blk, out, lsem, t0=0.0):
    s, z, h, x, c = place()
    local = Once(pltpu.make_async_copy(blk, out.at[z, :, x], lsem))
    q = HALF // 2
    gens = []
    for k in range(2):
        times = [t0 + v for v in ((3.4, 6.0, 13.8, 24.0) if k == 0 else (5.2, 7.0, 20.8, 28.0))]
        gens.append(
            g_ag_part(
                net, blk, out, local, x, "x", z, "z", lambda i, j, p: (j, p, i), pl.ds(k * q, q), times
            )
        )
        gens.append(
            g_ag_part(
                net,
                blk,
                out,
                local,
                z,
                "z",
                x,
                "x",
                lambda i, j, p: (i, p, j),
                pl.ds(HALF + k * q, q),
                times,
            )
        )
    yield from inter(gens)


def g_pairs(net, own, out, lsem, t0):
    s, z, h, x, c = place()
    outer, inner, sib = {"h": 1 - h, "s": 1 - s}, {"s": 1 - s}, {"c": 1 - c}
    first = []
    for k in range(2):
        rows = pl.ds(64 * k, 64)
        first.append(net.send(own.at[s, rows], out.at[h, c, s, rows], outer))
    local = pltpu.make_async_copy(own, out.at[h, c], lsem)
    local.start()
    c0 = net.send(own, out.at[h, c], sib)
    yield t0 + 4.6 + LAT
    second = []
    for k in range(2):
        first[k].wait_recv()
        r = out.at[1 - h, c, 1 - s, pl.ds(64 * k, 64)]
        second.append(net.send(r, r, inner))
        if k == 0:
            yield t0 + 9.2 + LAT
    r = out.at[1 - h, c, 1 - s]
    c1 = net.send(r, r, sib)
    yield t0 + 14 + LAT
    for copy in second:
        copy.wait_recv()
    r = out.at[1 - h, c, s]
    c2 = net.send(r, r, sib)
    yield t0 + 16 + LAT
    for copy in (c0, c1, c2):
        copy.wait_recv()
    local.wait()


NSUB = 4
SUBT = 9.25 / NSUB
ROWS = 128 // NSUB
PART = ROWS // 2


def g_yag(net, own, out, lsem, sub, t0=0.0):
    s, z, h, x, c = place()
    y = 2 * h + s
    yr, yl, yo = ring(y)
    rows = pl.ds(sub * ROWS, ROWS)
    lo, hi = pl.ds(sub * ROWS, PART), pl.ds(sub * ROWS + PART, PART)
    own = own.at[rows]
    mine = out.at[h, c, s, rows]
    local = pltpu.make_async_copy(own, mine, lsem)
    local.start()
    sib = {"c": 1 - c}
    c0 = net.send(own, mine, ydev(yr))
    c1 = net.send(own, mine, ydev(yl))
    c2 = net.send(own, mine, sib)
    t0 = t0 + 3 + (1.5 * NSUB + 1.5 * sub + 1) * SUBT + LAT
    yield t0
    c0.wait_recv()
    left = out.at[yl // 2, c, lax.rem(yl, 2)]
    c3 = net.send(left.at[lo], left.at[lo], ydev(yr))
    c4 = net.send(left.at[rows], left.at[rows], sib)
    c1.wait_recv()
    right = out.at[yr // 2, c, lax.rem(yr, 2)]
    c5 = net.send(right.at[hi], right.at[hi], ydev(yl))
    c6 = net.send(right.at[rows], right.at[rows], sib)
    yield t0 + SUBT + LAT
    c3.wait_recv()
    c5.wait_recv()
    far = out.at[yo // 2, c, lax.rem(yo, 2), rows]
    c7 = net.send(far, far, sib)
    yield t0 + SUBT + LAT + 2.5
    for copy in (c2, c4, c6, c7):
        copy.wait_recv()
    local.wait()


def xrs_scratch():
    return [
        pltpu.VMEM((4, 128, D), BF),
        pltpu.VMEM((4, 128, D), BF),
        pltpu.VMEM((2, NSUB, PART, D), BF),
        pltpu.VMEM((2, 128, D), BF),
    ]


def g_xrs(net, part, bufs, done, sub, t0=0.0):
    cb, sb, b1, b2 = bufs
    s, z, h, x, c = place()
    y = 2 * h + s
    yr, yl, yo = ring(y)
    sib = {"c": 1 - c}
    rows = pl.ds(sub * ROWS, ROWS)
    lo, hi = pl.ds(sub * ROWS, PART), pl.ds(sub * ROWS + PART, PART)
    units = [(k // 2, lax.rem(k, 2)) for k in (yo, yr, yl, y)]
    core = [
        net.send(part.at[units[k][0], 1 - c, units[k][1], rows], cb.at[k, rows], sib)
        for k in range(4)
    ]
    yield t0 + 2 + 4.4 / NSUB * sub

    def add(k):
        core[k].wait_recv()
        sb[k, rows] = (
            part[units[k][0], c, units[k][1], rows].astype(F32) + cb[k, rows].astype(F32)
        ).astype(BF)

    add(0)
    f0 = net.send(sb.at[0, lo], b1.at[0, sub], ydev(yr))
    f1 = net.send(sb.at[0, hi], b1.at[1, sub], ydev(yl))
    add(1)
    g1 = net.send(sb.at[1, hi], b2.at[0, hi], ydev(yr))
    add(2)
    g2 = net.send(sb.at[2, lo], b2.at[1, lo], ydev(yl))
    yield t0 + 3 + (1.5 * sub + 0.5) * SUBT + LAT
    f0.wait_recv()
    sb[1, lo] = (sb[1, lo].astype(F32) + b1[0, sub].astype(F32)).astype(BF)
    g3 = net.send(sb.at[1, lo], b2.at[0, lo], ydev(yr))
    f1.wait_recv()
    sb[2, hi] = (sb[2, hi].astype(F32) + b1[1, sub].astype(F32)).astype(BF)
    g4 = net.send(sb.at[2, hi], b2.at[1, hi], ydev(yl))
    yield t0 + 3 + (1.5 * sub + 2) * SUBT + LAT
    core[3].wait_recv()
    for copy in (g1, g2, g3, g4):
        copy.wait_recv()
    total = part[h, c, s, rows].astype(F32) + cb[3, rows].astype(F32)
    done(rows, total + b2[0, rows].astype(F32) + b2[1, rows].astype(F32))


QCOL = HALF // 2


def rs_scratch():
    return [
        pltpu.VMEM((4, 2, 4, 48, QCOL), BF),
        pltpu.VMEM((4, 2, 2, 4, 48, QCOL), BF),
        pltpu.VMEM((4, 2, 4, 48, QCOL), BF),
        pltpu.VMEM((4, 2, 4, 48, QCOL), BF),
        pltpu.VMEM((4, 2, 48, QCOL), BF),
        pltpu.VMEM((4, 2, 2, 48, QCOL), BF),
        pltpu.VMEM((4, 2, 48, QCOL), BF),
    ]


def g_rs_part(net, unit, i, axis_i, j, axis_j, bufs, done, times):
    b1, b2, t, sums, b3, b4, t2 = bufs
    ir, il, io = ring(i)
    jr, jl, jo = ring(j)
    right, left = {axis_i: ir}, {axis_i: il}
    f0 = net.send(unit(io, 0), b1.at[0], right)
    f1 = net.send(unit(io, 1), b1.at[1], left)
    yield times[0]
    g0 = net.send(unit(ir, 1), b2.at[0, 1], right)
    g1 = net.send(unit(il, 0), b2.at[1, 0], left)
    yield times[1]
    f0.wait_recv()
    t[0] = (unit(ir, 0)[...].astype(F32) + b1[0].astype(F32)).astype(BF)
    g2 = net.send(t.at[0], b2.at[0, 0], right)
    f1.wait_recv()
    t[1] = (unit(il, 1)[...].astype(F32) + b1[1].astype(F32)).astype(BF)
    g3 = net.send(t.at[1], b2.at[1, 1], left)
    yield times[2]
    for copy in (g0, g1, g2, g3):
        copy.wait_recv()

    def total(p, k):
        return (
            unit(i, p)[k].astype(F32) + b2[0, p, k].astype(F32) + b2[1, p, k].astype(F32)
        )

    def put(p, k):
        sums[p, k] = total(p, k).astype(BF)

    right, left = {axis_j: jr}, {axis_j: jl}
    put(0, jo)
    f0 = net.send(sums.at[0, jo], b3.at[0], right)
    put(1, jo)
    f1 = net.send(sums.at[1, jo], b3.at[1], left)
    put(1, jr)
    g0 = net.send(sums.at[1, jr], b4.at[0, 1], right)
    put(0, jl)
    g1 = net.send(sums.at[0, jl], b4.at[1, 0], left)
    yield times[3]
    f0.wait_recv()
    t2[0] = (total(0, jr) + b3[0].astype(F32)).astype(BF)
    g2 = net.send(t2.at[0], b4.at[0, 0], right)
    f1.wait_recv()
    t2[1] = (total(1, jl) + b3[1].astype(F32)).astype(BF)
    g3 = net.send(t2.at[1], b4.at[1, 1], left)
    yield times[4]
    for copy in (g0, g1, g2, g3):
        copy.wait_recv()
    for p in range(2):
        done(p, total(p, j) + b4[0, p].astype(F32) + b4[1, p].astype(F32))


def g_rs(net, grads, out, bufs, t0=0.0):
    s, z, h, x, c = place()
    gens = []

    def one(k, first_z):
        times = [t0 + v for v in ((0.2, 5.2, 16.0, 19.5, 23.0) if k % 2 == 0 else (5.0, 8.7, 23.0, 26.0, 29.0))]
        lanes = pl.ds(k * QCOL, QCOL)
        own = [b.at[k] for b in bufs]

        def put(p, v):
            out[p, :, k * QCOL : (k + 1) * QCOL] = v.astype(BF)

        if first_z:
            unit = lambda i, p: grads.at[i, p, :, :, lanes]
            return g_rs_part(net, unit, z, "z", x, "x", own, put, times)
        unit = lambda i, p: grads.at[:, p, i, :, lanes]
        return g_rs_part(net, unit, x, "x", z, "z", own, put, times)

    return inter([one(0, True), one(2, False), one(1, True), one(3, False)])


def wgrad_scratch():
    return [
        pltpu.VMEM((1024, D), BF),
        pltpu.VMEM((1024, D), BF),
        pltpu.VMEM((1024, CIN), BF),
        pltpu.VMEM((1024, HC), BF),
        pltpu.VMEM((4, 2, 4, 48, D), BF),
        pltpu.SemaphoreType.DMA((4,)),
    ]


def g_wgrad(srcs, bufs, sem, t0=0.0):
    copies = [pltpu.make_async_copy(a, b, sem.at[k]) for k, (a, b) in enumerate(zip(srcs, bufs))]
    for copy in copies:
        copy.start()
    yield t0 + 2.0
    u, e, dproj, o, grads = bufs
    copies[0].wait()
    copies[2].wait()
    for k in range(4):
        rows = slice(384 * k, 384 * k + 384)
        grads[k, :, :, :, 0:CIN] = tn(u[:, rows], dproj[...]).astype(BF).reshape(2, 4, 48, CIN)
        if k == 0:
            copies[1].wait()
            copies[3].wait()
        grads[k, :, :, :, CIN:D] = tn(e[:, rows], o[...]).astype(BF).reshape(2, 4, 48, HC)
        yield t0 + 2.0 + 1.7 * (k + 1)


def g_stats(net, mine, total, sb):
    sends = [net.send(mine, sb.at[k], dev) for k, dev in enumerate(group_devs())]
    yield 4.0
    acc = mine[...]
    for k, copy in enumerate(sends):
        copy.wait_recv()
        acc = acc + sb[k]
    total[...] = acc


def g_small(net, mine, bz, bx, total, t0=0.0):
    s, z, h, x, c = place()
    sends = [net.send(mine, bz.at[z], {"z": lax.rem(z + k, 4)}) for k in range(1, 4)]
    bz[z] = mine[...]
    yield t0 + 4.0
    for copy in sends:
        copy.wait_recv()
    bx[x] = bz[0] + bz[1] + bz[2] + bz[3]
    r = bx.at[x]
    sends = [net.send(r, r, {"x": lax.rem(x + k, 4)}) for k in range(1, 4)]
    yield t0 + 10.0
    for copy in sends:
        copy.wait_recv()
    total[...] = bx[0] + bx[1] + bx[2] + bx[3]


def small_scratch():
    return [pltpu.VMEM((4, 8, 640), F32), pltpu.VMEM((4, 8, 640), F32)]


def small_devs():
    s, z, h, x, c = place()
    return [{"z": lax.rem(z + k, 4)} for k in range(1, 4)] + [
        {"x": lax.rem(x + k, 4)} for k in range(1, 4)
    ]


def g_share(net, sums, got, vec, heads):
    s, z, h, x, c = place()
    me = (2 * s + h) * 2 + c
    sends = []
    for dev in group_devs():
        sends.append(net.send(sums.at[dev["s"]], got.at[me], dev))
    got[me] = sums[s]
    yield 20.0
    for copy in sends:
        copy.wait_recv()
    vec[...] = jnp.zeros_like(vec)
    tail = jnp.zeros((5, 256), F32)
    for q in range(8):
        lanes = slice(q * HC, q * HC + HC)
        vec[0:5, lanes] = got[q, 0:5, 0:HC]
        vec[5:6, lanes] = got[q, 5:6, 0:HC]
        tail = tail + got[q, 0:5, HC:640]
        heads[q : q + 1, 0:256] = got[q, 5:6, HC:640]
        heads[q : q + 1, 256:640] = got[q, 6:7, 0:HC]
    vec[0:5, 3072:3328] = tail


def params(cid):
    return pltpu.CompilerParams(
        collective_id=cid, has_side_effects=True, vmem_limit_bytes=VLIM
    )


def sems(n):
    return [pltpu.SemaphoreType.DMA((n,)), pltpu.SemaphoreType.DMA((n,))]


GATHERED = jax.ShapeDtypeStruct((4, 2, 4, 48, D), BF)
CHUNKS = jax.ShapeDtypeStruct((2, 2, 2, 128, D), BF)
SMALL = jax.ShapeDtypeStruct((8, 640), F32)
CHUNK = jax.ShapeDtypeStruct((128, D), BF)


def first_gathers(blk, tok, cot):
    def kernel(blk, tok, cot, w, tall, call, lsem, ssem, rsem):
        greet(zx_devs() + y_devs())
        net = Net(ssem, rsem)
        run(
            [
                g_ag(net, blk, w, lsem.at[0]),
                g_pairs(net, tok, tall, lsem.at[1], 0.0),
                g_pairs(net, cot, call, lsem.at[2], 9.2),
            ]
        )
        net.finish()

    return pl.pallas_call(
        kernel,
        name="first_gathers",
        out_shape=(GATHERED, CHUNKS, CHUNKS),
        in_specs=[VM] * 3,
        out_specs=(ANY,) * 3,
        scratch_shapes=[pltpu.SemaphoreType.DMA((3,))] + sems(48),
        compiler_params=params(0),
    )(blk, tok, cot)


def row_to_col(row):
    i = lax.broadcasted_iota(jnp.int32, (128, 128), 0)
    j = lax.broadcasted_iota(jnp.int32, (128, 128), 1)
    return jnp.sum(jnp.where(i == j, row, 0.0), axis=1, keepdims=True)


def col_to_row(col):
    i = lax.broadcasted_iota(jnp.int32, (128, 128), 0)
    j = lax.broadcasted_iota(jnp.int32, (128, 128), 1)
    return jnp.sum(jnp.where(i == j, col, 0.0), axis=0, keepdims=True)


def own_scale(total):
    s, z, h, x, c = place()
    row = total[pl.ds((2 * h + c) * 2 + s, 1), :]
    return lax.rsqrt(row_to_col(row) * (1.0 / 3072) + EPS)


def fetch(src, dst, sem):
    copy = pltpu.make_async_copy(src, dst, sem)
    copy.start()
    return copy


def forward_sum(part, stat, tok, blk):
    def kernel(part, stat, tok, blk, xall, w, total, fin, xo, cb, sb, b1, b2, stb, lsem, ssem, rsem):
        greet(zx_devs() + group_devs())
        net = Net(ssem, rsem)
        s, z, h, x, c = place()
        own = Once(pltpu.make_async_copy(tok.at[s], xo, lsem.at[0]))

        def done(rows, v):
            own.wait()
            scale = own_scale(total)[rows.start : rows.start + rows.size]
            fin[rows] = (xo[rows].astype(F32) + scale * v).astype(BF)

        def chain(sub):
            yield from g_xrs(net, part, (cb, sb, b1, b2), done, sub)
            yield from g_yag(net, fin, xall, lsem.at[2 + sub], sub)

        run(
            [g_stats(net, stat, total, stb)]
            + [chain(sub) for sub in range(NSUB)]
            + [g_ag(net, blk, w, lsem.at[1])]
        )
        net.finish()

    return pl.pallas_call(
        kernel,
        name="forward_sum",
        out_shape=(CHUNKS, GATHERED, jax.ShapeDtypeStruct((8, 128), F32)),
        in_specs=[VM, VM, ANY, VM],
        out_specs=(ANY, ANY, VM),
        scratch_shapes=[pltpu.VMEM((128, D), BF), pltpu.VMEM((128, D), BF)]
        + xrs_scratch()
        + [pltpu.VMEM((7, 8, 128), F32), pltpu.SemaphoreType.DMA((2 + NSUB,))]
        + sems(39 + 18 * NSUB),
        compiler_params=params(1),
    )(part, stat, tok, blk)


def stats_sum(stat):
    def kernel(stat, total, stb, ssem, rsem):
        greet(group_devs())
        net = Net(ssem, rsem)
        run([g_stats(net, stat, total, stb)])
        net.finish()

    return pl.pallas_call(
        kernel,
        name="stats_sum",
        out_shape=jax.ShapeDtypeStruct((16, 128), F32),
        in_specs=[VM],
        out_specs=VM,
        scratch_shapes=[pltpu.VMEM((7, 16, 128), F32)] + sems(8),
        compiler_params=params(2),
    )(stat)


def norm_back(v, x, e, ng):
    xf = x.astype(F32)
    vg = v * ng[...]
    r = lax.rsqrt(jnp.mean(xf * xf, axis=-1, keepdims=True) + EPS)
    dot = jnp.mean(xf * vg, axis=-1, keepdims=True)
    return e.astype(F32) + r * vg - xf * (r * r * r * dot)


def backward_sum(part, xall, cot, ng, wsrc, small):
    def kernel(part, xall, cot, ng, u, e, dproj, o, small, eall, out, hsum, fin, xo, eo, *rest):
        cbs, bufs, wbufs, rest = rest[:4], rest[4:11], rest[11:17], rest[17:]
        bz, bx, lsem, ssem, rsem = rest
        greet(small_devs() + y_devs())
        net = Net(ssem, rsem)
        s, z, h, x, c = place()
        ox = Once(pltpu.make_async_copy(xall.at[h, c, s], xo, lsem.at[0]))
        oe = Once(pltpu.make_async_copy(cot.at[s], eo, lsem.at[1]))

        def done(rows, v):
            ox.wait()
            oe.wait()
            fin[rows] = norm_back(v, xo[rows], eo[rows], ng).astype(BF)

        def chain(sub):
            yield from g_xrs(net, part, cbs, done, sub)
            yield from g_yag(net, fin, eall, lsem.at[2 + sub], sub)

        def weights():
            yield from g_wgrad((u, e, dproj, o), wbufs[:5], wbufs[5])
            yield from g_rs(net, wbufs[4], out, bufs, 9.0)

        run(
            [chain(sub) for sub in range(NSUB)]
            + [weights(), g_small(net, small, bz, bx, hsum)]
        )
        net.finish()

    return pl.pallas_call(
        kernel,
        name="backward_sum",
        out_shape=(CHUNKS, jax.ShapeDtypeStruct((2, 48, D), BF), SMALL),
        in_specs=[VM, ANY, ANY, VM, ANY, ANY, ANY, ANY, VM],
        out_specs=(ANY, VM, VM),
        scratch_shapes=[pltpu.VMEM((128, D), BF)] * 3
        + xrs_scratch()
        + rs_scratch()
        + wgrad_scratch()
        + small_scratch()
        + [pltpu.SemaphoreType.DMA((2 + NSUB,))]
        + sems(54 + 18 * NSUB),
        compiler_params=params(3),
    )(part, xall, cot, ng, *wsrc, small)


def last_sums(part0, tok, eall, ng, part1, xall, stat1, wsrc, small0, small1):
    def kernel(p0, tok, eall, ng, p1, xall, st, u, e, dproj, o, sm0, sm1, ig, so, out, vec, heads, *rest):
        xo, eo, x1, ba, bb, rest = rest[0], rest[1], rest[2], rest[3:7], rest[7:11], rest[11:]
        bufs, wbufs, rest = rest[:7], rest[7:13], rest[13:]
        bz, bx, sums, got, lsem, ssem, rsem = rest
        greet(small_devs() + group_devs())
        net = Net(ssem, rsem)
        s, z, h, x, c = place()
        ox = Once(pltpu.make_async_copy(tok.at[s], xo, lsem.at[0]))
        oe = Once(pltpu.make_async_copy(eall.at[h, c, s], eo, lsem.at[1]))
        o1 = Once(pltpu.make_async_copy(xall.at[h, c, s], x1, lsem.at[2]))

        def done0(rows, v):
            ox.wait()
            oe.wait()
            ig[rows] = norm_back(v, xo[rows], eo[rows], ng).astype(BF)

        def done1(rows, v):
            o1.wait()
            scale = own_scale(st)[rows.start : rows.start + rows.size]
            so[rows] = (x1[rows].astype(F32) + scale * v).astype(BF)

        def weights():
            yield from g_wgrad((u, e, dproj, o), wbufs[:5], wbufs[5])
            yield from g_rs(net, wbufs[4], out, bufs, 9.0)

        def smalls():
            sums[1] = sm1[...]
            yield from g_small(net, sm0, bz, bx, sums.at[0])
            yield from g_share(net, sums, got, vec, heads)

        run(
            [g_xrs(net, p1, bb, done1, sub) for sub in range(NSUB)]
            + [g_xrs(net, p0, ba, done0, sub) for sub in range(NSUB)]
            + [weights(), smalls()]
        )
        net.finish()

    return pl.pallas_call(
        kernel,
        name="last_sums",
        out_shape=(
            CHUNK,
            CHUNK,
            jax.ShapeDtypeStruct((2, 48, D), BF),
            jax.ShapeDtypeStruct((8, 3328), F32),
            SMALL,
        ),
        in_specs=[VM, ANY, ANY, VM, VM, ANY, VM, ANY, ANY, ANY, ANY, VM, VM],
        out_specs=(VM,) * 5,
        scratch_shapes=[pltpu.VMEM((128, D), BF)] * 3
        + xrs_scratch()
        + xrs_scratch()
        + rs_scratch()
        + wgrad_scratch()
        + small_scratch()
        + [pltpu.VMEM((2, 8, 640), F32), pltpu.VMEM((8, 8, 640), F32)]
        + [pltpu.SemaphoreType.DMA((3,))]
        + sems(61 + 20 * NSUB),
        compiler_params=params(4),
    )(part0, tok, eall, ng, part1, xall, stat1, *wsrc, small0, small1)


def nt(a, b):
    return lax.dot_general(a, b, (((1,), (1,)), ((), ())), preferred_element_type=F32)


def tn(a, b):
    return lax.dot_general(a, b, (((0,), (0,)), ((), ())), preferred_element_type=F32)


def iotas():
    i = lax.broadcasted_iota(jnp.int32, (128, 128), 0)
    j = lax.broadcasted_iota(jnp.int32, (128, 128), 1)
    return i, j


def seg_of(st, chunk, places):
    seg = jnp.full(places.shape, -1, jnp.int32)
    for k in range(4):
        seg = seg + (st[chunk, k] <= places).astype(jnp.int32)
    return seg


def masks(st, chunk):
    i, j = iotas()
    seg = seg_of(st, chunk, i)
    keep = jnp.logical_and(seg == seg_of(st, chunk, j), i >= j)
    valid = [None] + [
        (seg_of(st, chunk, i - k) == seg).astype(F32) for k in range(1, 4)
    ]
    return keep, valid


def conv_tile(xt, cv, t, valid):
    lanes = slice(128 * t, 128 * t + 128)
    pre = cv[4:5, lanes] + cv[3:4, lanes] * xt
    moved = [xt]
    for k in range(1, 4):
        m = pltpu.roll(xt, k, axis=0) * valid[k]
        moved.append(m)
        pre = pre + cv[3 - k : 4 - k, lanes] * m
    return pre, moved


def rates(rt, cv):
    i, j = iotas()
    head = j < NH
    v = rt + cv[7:8, 0:128]
    dt = jnp.where(head, jnp.maximum(v, 0.0) + jnp.log1p(jnp.exp(-jnp.abs(v))), 0.0)
    lower = (i >= j).astype(F32)
    cum = jnp.dot(
        lower, -dt * cv[8:9, 0:128], precision=HIGH, preferred_element_type=F32
    )
    return v, dt, cum


def half_masks():
    _, j = iotas()
    return j < 64


def split_pair(v, low):
    zero = jnp.zeros_like(v)
    return jnp.concatenate([jnp.where(low, v, zero), jnp.where(low, zero, v)], axis=0)


def decay_of(keep, cum, cum_t, h):
    spread = jnp.where(keep, cum[:, h : h + 1] - cum_t[h : h + 1, :], -1e30)
    return jnp.exp(spread)


def load_const(cv):
    return cv[...]


def front(xb, w, ng, u_out):
    xf = xb[...].astype(F32)
    r = lax.rsqrt(jnp.mean(xf * xf, axis=-1, keepdims=True) + EPS)
    u = (xf * r * ng[...]).astype(BF)
    u_out[...] = u
    return jnp.dot(u, w[:, 0:CIN], preferred_element_type=F32)


def make_forward(with_do):
    def kernel(st, x, w, ng, cv, *rest):
        if with_do:
            e, part, stat, proj, yout, uout, doo, og = rest
        else:
            part, stat, proj, yout, uout, og = rest
        step = pl.program_id(0)
        proj[...] = front(x, w, ng, uout)
        if with_do:
            doo[...] = jnp.dot(e[...], w[:, CIN:D], preferred_element_type=F32)
        low = half_masks()
        for m in range(2):
            rows = slice(128 * m, 128 * m + 128)
            chunk = step * 2 + m
            keep, valid = masks(st, chunk)
            act = []
            for t in range(5):
                pre, _ = conv_tile(proj[rows, HC + 128 * t : HC + 128 * t + 128], cv, t, valid)
                act.append((pre * jax.nn.sigmoid(pre)).astype(BF))
            _, dt, cum = rates(proj[rows, RT:CIN], cv)
            cum_t, dt_t = jnp.transpose(cum), jnp.transpose(dt)
            gram = nt(act[4], act[3])
            gsum = jnp.zeros((128, 1), F32)
            tsum = jnp.zeros((128, 1), F32)
            for t in range(3):
                lanes = slice(128 * t, 128 * t + 128)
                mixes = []
                for h in (2 * t, 2 * t + 1):
                    dec = decay_of(keep, cum, cum_t, h)
                    mixes.append((gram * dec * dt_t[h : h + 1, :]).astype(BF))
                y = jnp.dot(
                    jnp.concatenate(mixes, axis=1),
                    split_pair(act[t], low),
                    preferred_element_type=F32,
                )
                y = y + cv[6:7, lanes] * act[t].astype(F32)
                yout[rows, lanes] = y
                zt = proj[rows, lanes]
                g = y * (zt * jax.nn.sigmoid(zt))
                gsum = gsum + jnp.sum(g * g, axis=1, keepdims=True)
                gain = cv[5:6, lanes]
                og[rows, lanes] = (g * gain).astype(BF)
                if with_do:
                    tsum = tsum + jnp.sum(g * gain * doo[rows, lanes], axis=1, keepdims=True)
            stat[pl.ds(chunk, 1), :] = col_to_row(gsum)
            if with_do:
                stat[pl.ds(chunk + 8, 1), :] = col_to_row(tsum)
        part[...] = nt(og[...], w[:, CIN:D]).astype(BF)

    return kernel


def rows_spec(cols):
    return pl.BlockSpec((256, cols), lambda i: (i, 0))


def whole(*shape):
    return pl.BlockSpec(shape, lambda i: (0,) * len(shape))


def layer_forward(st, x, w, ng, cv, e=None):
    with_do = e is not None
    n_stat = 16 if with_do else 8
    ins = [st, x, w, ng, cv] + ([e] if with_do else [])
    in_specs = [SM, rows_spec(D), whole(D, D), whole(1, D), whole(16, 640)] + (
        [rows_spec(D)] if with_do else []
    )
    outs = [
        jax.ShapeDtypeStruct((1024, D), BF),
        jax.ShapeDtypeStruct((n_stat, 128), F32),
        jax.ShapeDtypeStruct((1024, CIN), F32),
        jax.ShapeDtypeStruct((1024, HC), F32),
        jax.ShapeDtypeStruct((1024, D), BF),
    ] + ([jax.ShapeDtypeStruct((1024, HC), F32)] if with_do else [])
    out_specs = [
        rows_spec(D),
        whole(n_stat, 128),
        rows_spec(CIN),
        rows_spec(HC),
        rows_spec(D),
    ] + ([rows_spec(HC)] if with_do else [])
    return pl.pallas_call(
        make_forward(with_do),
        name="layer_forward",
        grid=(4,),
        in_specs=in_specs,
        out_specs=out_specs,
        out_shape=outs,
        scratch_shapes=[pltpu.VMEM((256, HC), BF)],
        compiler_params=pltpu.CompilerParams(vmem_limit_bytes=VLIM),
    )(*ins)


def make_backward(first):
    def kernel(st, e, w, cv, proj, yin, stat, *rest):
        if first:
            x, x1, dproj, oo, part, sm, do = rest
        else:
            do, dproj, oo, part, sm = rest
        step = pl.program_id(0)

        @pl.when(step == 0)
        def _():
            sm[...] = jnp.zeros_like(sm)

        if first:
            do[...] = jnp.dot(e[...], w[:, CIN:D], preferred_element_type=F32)
        low = half_masks()
        i, j = iotas()
        upper = (j >= i).astype(F32)

        def add(row, lanes, v):
            sm[row : row + 1, lanes] += jnp.sum(v, axis=0, keepdims=True)

        for m in range(2):
            rows = slice(128 * m, 128 * m + 128)
            chunk = step * 2 + m
            keep, valid = masks(st, chunk)
            pres, moves, act = [], [], []
            for t in range(5):
                pre, moved = conv_tile(
                    proj[rows, HC + 128 * t : HC + 128 * t + 128], cv, t, valid
                )
                pres.append(pre)
                moves.append(moved)
                act.append((pre * jax.nn.sigmoid(pre)).astype(BF))
            v, dt, cum = rates(proj[rows, RT:CIN], cv)
            cum_t, dt_t = jnp.transpose(cum), jnp.transpose(dt)
            gram = nt(act[4], act[3])
            r = lax.rsqrt(row_to_col(stat[pl.ds(chunk, 1), :]) * (1.0 / 3072) + EPS)
            if first:
                dots = jnp.sum(
                    e[rows, :].astype(F32) * (x1[rows, :].astype(F32) - x[rows, :].astype(F32)),
                    axis=1,
                    keepdims=True,
                )
                k = r * r * dots * (1.0 / 3072)
            else:
                k = r * r * r * row_to_col(stat[pl.ds(chunk + 8, 1), :]) * (1.0 / 3072)
            dact = []
            dgram = jnp.zeros((128, 128), F32)
            dcum = jnp.zeros((128, 128), F32)
            col_rows = []
            for t in range(3):
                lanes = slice(128 * t, 128 * t + 128)
                zt, y, dot_ = proj[rows, lanes], yin[rows, lanes], do[rows, lanes]
                gain = cv[5:6, lanes]
                sig = jax.nn.sigmoid(zt)
                sz = zt * sig
                g = y * sz
                oo[rows, lanes] = (g * r * gain).astype(BF)
                add(5, lanes, dot_ * g * r)
                dg = r * (dot_ * gain) - g * k
                dproj[rows, lanes] = (dg * y * (sig + sz * (1.0 - sig))).astype(BF)
                dy = (dg * sz).astype(BF)
                dyf = dy.astype(F32)
                xs = act[t]
                add(6, lanes, dyf * xs.astype(F32))
                dy2 = split_pair(dy, low)
                dmix2 = nt(dy2, xs)
                mixes = []
                for q in range(2):
                    h = 2 * t + q
                    dec = decay_of(keep, cum, cum_t, h)
                    dt_row = dt_t[h : h + 1, :]
                    pm = gram * dec
                    mixes.append((pm * dt_row).astype(BF))
                    dmix = dmix2[128 * q : 128 * q + 128]
                    dgram = dgram + dmix * (dec * dt_row)
                    vm = dmix * pm
                    col_rows.append(jnp.sum(vm, axis=0, keepdims=True))
                    rsum = jnp.sum(vm * dt_row, axis=1, keepdims=True)
                    dcum = dcum + jnp.where(j == h, rsum, 0.0)
                dxs = tn(jnp.concatenate(mixes, axis=0), dy2)
                dact.append(dxs + cv[6:7, lanes] * dyf)
            dgl = dgram.astype(BF)
            dact.append(tn(dgl, act[4]))
            dact.append(jnp.dot(dgl, act[3], preferred_element_type=F32))
            ddt = jnp.transpose(
                jnp.concatenate(col_rows + [jnp.zeros((128 - NH, 128), F32)], axis=0)
            )
            dcum = dcum - ddt * dt
            dla = jnp.dot(upper, dcum, precision=HIGH, preferred_element_type=F32)
            nexp = -cv[8:9, 0:128]
            drate = (ddt + dla * nexp) * jax.nn.sigmoid(v)
            drate = jnp.where(j < NH, drate, 0.0)
            add(5, slice(HC, HC + 128), drate)
            add(5, slice(HC + 128, 640), dla * dt * nexp)
            dproj[rows, RT:CIN] = drate.astype(BF)
            for t in range(5):
                lanes = slice(128 * t, 128 * t + 128)
                pre = pres[t]
                sp = jax.nn.sigmoid(pre)
                dpre = dact[t] * (sp + pre * sp * (1.0 - sp))
                add(4, lanes, dpre)
                add(3, lanes, dpre * moves[t][0])
                dx = cv[3:4, lanes] * dpre
                for n in range(1, 4):
                    add(3 - n, lanes, dpre * moves[t][n])
                    dx = dx + cv[3 - n : 4 - n, lanes] * pltpu.roll(
                        dpre * valid[n], 128 - n, axis=0
                    )
                dproj[rows, HC + 128 * t : HC + 128 * t + 128] = dx.astype(BF)
        part[...] = nt(dproj[...], w[:, 0:CIN]).astype(BF)

    return kernel


def layer_backward(st, e, w, cv, proj, y, stat, do=None, x=None, x1=None):
    first = do is None
    extra = [x, x1] if first else [do]
    ins = [st, e, w, cv, proj, y, stat] + extra
    in_specs = [
        SM,
        rows_spec(D),
        whole(D, D),
        whole(16, 640),
        rows_spec(CIN),
        rows_spec(HC),
        whole(*stat.shape),
    ] + ([rows_spec(D), rows_spec(D)] if first else [rows_spec(HC)])
    outs = [
        jax.ShapeDtypeStruct((1024, CIN), BF),
        jax.ShapeDtypeStruct((1024, HC), BF),
        jax.ShapeDtypeStruct((1024, D), BF),
        SMALL,
    ]
    return pl.pallas_call(
        make_backward(first),
        name="layer_backward",
        grid=(4,),
        in_specs=in_specs,
        out_specs=[rows_spec(CIN), rows_spec(HC), rows_spec(D), whole(8, 640)],
        out_shape=outs,
        scratch_shapes=[pltpu.VMEM((256, HC), F32)] if first else [],
        compiler_params=pltpu.CompilerParams(vmem_limit_bytes=VLIM),
    )(*ins)


def pack_shards(starts, norm_gain, w_in, conv_weight, conv_bias, gate_gain, w_out):
    small = jnp.concatenate(
        [
            conv_weight.reshape(-1),
            conv_bias,
            gate_gain,
            starts.reshape(-1).astype(BF),
            jnp.zeros((20,), BF),
        ]
    ).reshape(24, PKN)
    wide = jnp.concatenate([norm_gain[:, None], small], axis=1)

    def each(v):
        return jnp.broadcast_to(v[:, None], (24, 8, v.shape[-1]))

    rate = jnp.concatenate(
        [w_in[:, 6400:].reshape(24, 8, NH), each(wide), jnp.zeros((24, 8, 107), BF)], axis=-1
    )
    pieces = jnp.concatenate(
        [
            w_in[:, :3072].reshape(24, 8, HC),
            w_in[:, 3072:6144].reshape(24, 8, HC),
            each(w_in[:, 6144:6400]),
            rate,
            jnp.transpose(w_out).reshape(24, 8, HC),
        ],
        axis=-1,
    )
    return jnp.transpose(pieces, (1, 0, 2))


def constants(w, q, dt_bias, a_log, skip_d):
    tile = w[:, RT : RT + 128].astype(F32)
    pairs = jnp.transpose(tile[:, NH : NH + 2 * (PKN + 1)].reshape(D, 2, PKN + 1), (1, 0, 2))
    ng = pairs[:, None, :, 0]
    small = pairs[:, :, 1:].reshape(2, 64, 24 * PKN)
    taps = jnp.transpose(small[:, :, :208].reshape(2, 64, 4, 52), (0, 2, 1, 3)).reshape(2, 4, 3328)
    conv = jnp.concatenate([taps, small[:, :, 208:260].reshape(2, 1, 3328)], axis=1)
    gate = small[:, :, 260:308].reshape(2, 1, 3072)
    conv = jnp.concatenate(
        [lax.dynamic_slice_in_dim(conv, q * HC, HC, 2), conv[:, :, 3072:]], axis=2
    )
    gate = lax.dynamic_slice_in_dim(gate, q * HC, HC, 2)

    def heads(v):
        return lax.dynamic_slice_in_dim(v, q * NH, NH, 1)

    skip = jnp.repeat(heads(skip_d), 64, axis=1)[:, None]
    pad = lambda v: jnp.pad(v, ((0, 0), (0, 0), (0, 640 - v.shape[2])))
    rows = [
        conv,
        pad(gate),
        pad(skip),
        pad(heads(dt_bias)[:, None]),
        pad(heads(jnp.exp(a_log))[:, None]),
        jnp.zeros((2, 7, 640), F32),
    ]
    return jnp.concatenate(rows, axis=1), ng


def unpack_grads(rec, vec, heads, w_in, norm_gain, place_dp):
    rec = rec.astype(F32)
    flat = lambda v: jnp.transpose(v, (1, 0, 2)).reshape(24, -1)
    w_in_grad = jnp.concatenate(
        [
            flat(rec[:, :, 0:HC]),
            flat(rec[:, :, HC : 2 * HC]),
            jnp.sum(rec[:, :, 2 * HC : RT], axis=0),
            flat(rec[:, :, RT : RT + NH]),
        ],
        axis=1,
    )
    w_out_grad = jnp.transpose(flat(rec[:, :, CIN:D]))
    conv = lax.dynamic_slice_in_dim(vec[0:5], 52 * place_dp, 52, 1)
    gate = lax.dynamic_slice_in_dim(vec[5], 48 * place_dp, 48, 0)
    norm_grad = jnp.sum(w_in.astype(F32) * w_in_grad, axis=1) / norm_gain.astype(F32)
    return (
        norm_grad,
        w_in_grad,
        conv[0:4],
        conv[4],
        heads[:, 0:NH].reshape(48),
        heads[:, 128 : 128 + NH].reshape(48),
        jnp.sum(heads[:, 256:640].reshape(48, 64), axis=1),
        gate,
        w_out_grad,
    )


GROUP = ("s", "h", "c")


def body(
    tokens,
    cotangent,
    starts,
    norm_gain,
    w_in,
    conv_weight,
    conv_bias,
    dt_bias,
    a_log,
    skip_d,
    gate_gain,
    w_out,
):
    s, z, h, x, c = place()
    q = (s * 2 + h) * 2 + c
    mine = pack_shards(
        starts[:, 0], norm_gain[0], w_in[0], conv_weight[0], conv_bias[0], gate_gain[0], w_out[0]
    )
    rec = lax.all_to_all(mine, GROUP, 0, 0, tiled=True)
    blocks = rec.reshape(2, 2, 48, D)
    st = (
        rec[0:4, :, RT + PK0 : RT + PK0 + PKN]
        .reshape(4, 24 * PKN)[:, 308:316]
        .reshape(8, 4)
        .astype(jnp.int32)
    )
    gap = lambda v, n: jnp.pad(v, ((0, 0), (0, 0), (n, D - n - v.shape[2])))
    blk0 = blocks[0] + gap(blocks[1, :, :, RT + NH : RT + PK0 + PKN], RT + PK0 + PKN)
    heads = jnp.stack([dt_bias[0], a_log[0], skip_d[0]])
    other = lax.ppermute(heads, "s", [(0, 1), (1, 0)])
    heads = jnp.where(s == 0, jnp.stack([heads, other]), jnp.stack([other, heads]))

    w0, tall, call = first_gathers(blk0, tokens, cotangent)
    w0 = w0.reshape(D, D)
    x0 = tall.reshape(1024, D)
    e1 = call.reshape(1024, D)
    cv, ng = constants(w0, q, heads[:, 0], heads[:, 1], heads[:, 2])
    part, stat0, proj0, y0, u0 = layer_forward(st, x0, w0, ng[0], cv[0])
    xall, w1, stat0 = forward_sum(part.reshape(2, 2, 2, 128, D), stat0, tokens, blocks[1])
    w1 = w1.reshape(D, D)
    x1 = xall.reshape(1024, D)
    part1, stat1, proj1, y1, u1, do1 = layer_forward(st, x1, w1, ng[1], cv[1], e1)
    stat1 = stats_sum(stat1)
    dproj1, o1, dpart1, sm1 = layer_backward(st, e1, w1, cv[1], proj1, y1, stat1, do=do1)
    eall, gs1, sm1 = backward_sum(
        dpart1.reshape(2, 2, 2, 128, D), xall, cotangent, ng[1], (u1, e1, dproj1, o1), sm1
    )
    e0 = eall.reshape(1024, D)
    dproj0, o0, dpart0, sm0 = layer_backward(st, e0, w0, cv[0], proj0, y0, stat0, x=x0, x1=x1)
    ig0, so1, gs0, vec, hd = last_sums(
        dpart0.reshape(2, 2, 2, 128, D),
        tokens,
        eall,
        ng[0],
        part1.reshape(2, 2, 2, 128, D),
        xall,
        stat1[0:8],
        (u0, e0, dproj0, o0),
        sm0,
        sm1,
    )
    back = lax.all_to_all(jnp.stack([gs0, gs1]).reshape(8, 24, D), GROUP, 0, 0, tiled=True)
    place_dp = ((z * 2 + h) * 4 + x) * 2 + c
    outs = unpack_grads(back, vec, hd, w_in[0], norm_gain[0], place_dp)

    got = lax.ppermute(jnp.where(s == 0, so1, ig0), "s", [(0, 1), (1, 0)])
    ig = jnp.where(s == 0, jnp.stack([ig0, got]), eall[h, c])
    so = jnp.where(s == 0, xall[h, c], jnp.stack([got, so1]))
    return (so[None], ig.astype(F32)[None]) + tuple(o[None] for o in outs)


def solution(mesh):
    inner = Mesh(mesh.devices.reshape(2, 4, 2, 4, 2), ("s", "z", "h", "x", "c"))
    dp = ("z", "h", "x", "c")
    in_specs = (
        P(None, dp, None),
        P(None, dp, None),
        P(None, dp, None),
        P("s", dp),
        P("s", dp, None),
        P("s", None, dp),
        P("s", dp),
        P("s", None),
        P("s", None),
        P("s", None),
        P("s", dp),
        P("s", None, dp),
    )
    out_specs = (
        P("s", None, dp, None),
        P("s", None, dp, None),
        P("s", dp),
        P("s", dp, None),
        P("s", None, dp),
        P("s", dp),
        P("s", None),
        P("s", None),
        P("s", None),
        P("s", dp),
        P("s", None, dp),
    )
    return jax.shard_map(body, mesh=inner, in_specs=in_specs, out_specs=out_specs, check_vma=False)
```

```python
import jax
import jax.numpy as jnp
from jax import lax
from jax.experimental import pallas as pl
from jax.experimental.pallas import tpu as pltpu
from jax.sharding import Mesh, PartitionSpec as P

EPS = 1e-05
BF = jnp.bfloat16
F32 = jnp.float32
HIGH = lax.Precision.HIGHEST
D = 1536
CIN = 1152
HC = 384
NH = 6
RT = 1024
PK0 = 7
PKN = 14
HEAD0 = RT + 32
HALF = 768
ANY = pl.BlockSpec(memory_space=pl.ANY)
VM = pl.BlockSpec(memory_space=pltpu.VMEM)
SM = pl.BlockSpec(memory_space=pltpu.SMEM)
VLIM = 56 * 1024 * 1024


class Net:
    def __init__(self, ssem, rsem):
        self.ssem, self.rsem, self.n, self.all = ssem, rsem, 0, []

    def make(self, src, dst, dev):
        i = self.n
        self.n += 1
        assert i < self.ssem.shape[0]
        copy = pltpu.make_async_remote_copy(
            src_ref=src,
            dst_ref=dst,
            send_sem=self.ssem.at[i],
            recv_sem=self.rsem.at[i],
            device_id=dev,
            device_id_type=pl.DeviceIdType.MESH,
        )
        self.all.append(copy)
        return copy

    def send(self, src, dst, dev):
        copy = self.make(src, dst, dev)
        copy.start()
        return copy

    def finish(self):
        for copy in self.all:
            copy.wait_send()


def place():
    s, z, h, x, c = (lax.axis_index(a) for a in ("s", "z", "h", "x", "c"))
    return s, z, h, x, c


def ring(i):
    return lax.rem(i + 1, 4), lax.rem(i + 3, 4), lax.rem(i + 2, 4)


def greet(devs):
    barrier = pltpu.get_barrier_semaphore()
    for dev in devs:
        pl.semaphore_signal(barrier, inc=1, device_id=dev, device_id_type=pl.DeviceIdType.MESH)
    pl.semaphore_wait(barrier, len(devs))


def zx_devs():
    s, z, h, x, c = place()
    zr, zl, _ = ring(z)
    xr, xl, _ = ring(x)
    return [{"z": zr}, {"z": zl}, {"x": xr}, {"x": xl}]


def ydev(y):
    return {"h": y // 2, "s": lax.rem(y, 2)}


def y_devs():
    s, z, h, x, c = place()
    yr, yl, _ = ring(2 * h + s)
    return [ydev(yr), ydev(yl), {"c": 1 - c}]


def group_devs():
    s, z, h, x, c = place()
    out = []
    for k in range(1, 8):
        out.append(
            {
                "s": 1 - s if k & 4 else s,
                "h": 1 - h if k & 2 else h,
                "c": 1 - c if k & 1 else c,
            }
        )
    return out


LAT = 1.7


def inter(gens):
    gens = [[0.0, g] for g in gens]
    while gens:
        item = min(gens, key=lambda v: v[0])
        if item[0] > 0:
            yield item[0]
        try:
            item[0] = next(item[1])
        except StopIteration:
            gens.remove(item)


def run(gens):
    for _ in inter(gens):
        pass


def g_ag_part(net, blk, out, local, i, axis_i, j, axis_j, pick, lanes, times):
    ir, il, io = ring(i)
    jr, jl, jo = ring(j)
    right, left = {axis_i: ir}, {axis_i: il}
    every = slice(None)

    def at(i, j, p):
        return out.at[pick(i, j, p) + (every, lanes)]

    own = blk.at[:, :, lanes]
    a1r = net.send(own, at(i, j, every), right)
    a1l = net.send(own, at(i, j, every), left)
    yield times[0]
    a1r.wait_recv()
    r = at(il, j, 0)
    a2r = net.send(r, r, right)
    a1l.wait_recv()
    r = at(ir, j, 1)
    a2l = net.send(r, r, left)
    yield times[1]
    a2r.wait_recv()
    a2l.wait_recv()
    local.wait()
    right, left = {axis_j: jr}, {axis_j: jl}
    r = at(every, j, every)
    a3r = net.send(r, r, right)
    a3l = net.send(r, r, left)
    yield times[2]
    a3r.wait_recv()
    r = at(every, jl, 0)
    a4r = net.send(r, r, right)
    a3l.wait_recv()
    r = at(every, jr, 1)
    a4l = net.send(r, r, left)
    yield times[3]
    a4r.wait_recv()
    a4l.wait_recv()


class Once:
    def __init__(self, copy):
        self.copy, self.open = copy, True
        copy.start()

    def wait(self):
        if self.open:
            self.copy.wait()
        self.open = False


def g_ag(net, blk, out, lsem, t0=0.0):
    s, z, h, x, c = place()
    local = Once(pltpu.make_async_copy(blk, out.at[z, :, x], lsem))
    q = HALF // 2
    gens = []
    for k in range(2):
        times = [t0 + v for v in ((3.4, 6.0, 13.8, 24.0) if k == 0 else (5.2, 7.0, 20.8, 28.0))]
        gens.append(
            g_ag_part(
                net, blk, out, local, x, "x", z, "z", lambda i, j, p: (j, p, i), pl.ds(k * q, q), times
            )
        )
        gens.append(
            g_ag_part(
                net,
                blk,
                out,
                local,
                z,
                "z",
                x,
                "x",
                lambda i, j, p: (i, p, j),
                pl.ds(HALF + k * q, q),
                times,
            )
        )
    yield from inter(gens)


def g_pairs(net, own, out, lsem, t0):
    s, z, h, x, c = place()
    outer, inner, sib = {"h": 1 - h, "s": 1 - s}, {"s": 1 - s}, {"c": 1 - c}
    first = []
    for k in range(2):
        rows = pl.ds(64 * k, 64)
        first.append(net.send(own.at[s, rows], out.at[h, c, s, rows], outer))
    local = pltpu.make_async_copy(own, out.at[h, c], lsem)
    local.start()
    c0 = net.send(own, out.at[h, c], sib)
    yield t0 + 4.6 + LAT
    second = []
    for k in range(2):
        first[k].wait_recv()
        r = out.at[1 - h, c, 1 - s, pl.ds(64 * k, 64)]
        second.append(net.send(r, r, inner))
        if k == 0:
            yield t0 + 9.2 + LAT
    r = out.at[1 - h, c, 1 - s]
    c1 = net.send(r, r, sib)
    yield t0 + 14 + LAT
    for copy in second:
        copy.wait_recv()
    r = out.at[1 - h, c, s]
    c2 = net.send(r, r, sib)
    yield t0 + 16 + LAT
    for copy in (c0, c1, c2):
        copy.wait_recv()
    local.wait()


NSUB = 1
SUBT = 9.25 / NSUB
ROWS = 128 // NSUB
PART = ROWS // 2


def g_yag(net, own, out, lsem, sub, t0=0.0):
    s, z, h, x, c = place()
    y = 2 * h + s
    yr, yl, yo = ring(y)
    rows = pl.ds(sub * ROWS, ROWS)
    lo, hi = pl.ds(sub * ROWS, PART), pl.ds(sub * ROWS + PART, PART)
    own = own.at[rows]
    mine = out.at[h, c, s, rows]
    local = pltpu.make_async_copy(own, mine, lsem)
    local.start()
    sib = {"c": 1 - c}
    c0 = net.send(own, mine, ydev(yr))
    c1 = net.send(own, mine, ydev(yl))
    c2 = net.send(own, mine, sib)
    t0 = t0 + 3 + (1.5 * NSUB + 1.5 * sub + 1) * SUBT + LAT
    yield t0
    c0.wait_recv()
    left = out.at[yl // 2, c, lax.rem(yl, 2)]
    c3 = net.send(left.at[lo], left.at[lo], ydev(yr))
    c4 = net.send(left.at[rows], left.at[rows], sib)
    c1.wait_recv()
    right = out.at[yr // 2, c, lax.rem(yr, 2)]
    c5 = net.send(right.at[hi], right.at[hi], ydev(yl))
    c6 = net.send(right.at[rows], right.at[rows], sib)
    yield t0 + SUBT + LAT
    c3.wait_recv()
    c5.wait_recv()
    far = out.at[yo // 2, c, lax.rem(yo, 2), rows]
    c7 = net.send(far, far, sib)
    yield t0 + SUBT + LAT + 2.5
    for copy in (c2, c4, c6, c7):
        copy.wait_recv()
    local.wait()


def xrs_scratch():
    return [
        pltpu.VMEM((4, 128, D), BF),
        pltpu.VMEM((4, 128, D), BF),
        pltpu.VMEM((2, NSUB, PART, D), BF),
        pltpu.VMEM((2, 128, D), BF),
    ]


def g_xrs(net, part, bufs, done, sub, t0=0.0):
    cb, sb, b1, b2 = bufs
    s, z, h, x, c = place()
    y = 2 * h + s
    yr, yl, yo = ring(y)
    sib = {"c": 1 - c}
    rows = pl.ds(sub * ROWS, ROWS)
    lo, hi = pl.ds(sub * ROWS, PART), pl.ds(sub * ROWS + PART, PART)
    units = [(k // 2, lax.rem(k, 2)) for k in (yo, yr, yl, y)]
    core = [
        net.send(part.at[units[k][0], 1 - c, units[k][1], rows], cb.at[k, rows], sib)
        for k in range(4)
    ]
    yield t0 + 2 + 4.4 / NSUB * sub

    def add(k):
        core[k].wait_recv()
        sb[k, rows] = (
            part[units[k][0], c, units[k][1], rows].astype(F32) + cb[k, rows].astype(F32)
        ).astype(BF)

    add(0)
    f0 = net.send(sb.at[0, lo], b1.at[0, sub], ydev(yr))
    f1 = net.send(sb.at[0, hi], b1.at[1, sub], ydev(yl))
    add(1)
    g1 = net.send(sb.at[1, hi], b2.at[0, hi], ydev(yr))
    add(2)
    g2 = net.send(sb.at[2, lo], b2.at[1, lo], ydev(yl))
    yield t0 + 3 + (1.5 * sub + 0.5) * SUBT + LAT
    f0.wait_recv()
    sb[1, lo] = (sb[1, lo].astype(F32) + b1[0, sub].astype(F32)).astype(BF)
    g3 = net.send(sb.at[1, lo], b2.at[0, lo], ydev(yr))
    f1.wait_recv()
    sb[2, hi] = (sb[2, hi].astype(F32) + b1[1, sub].astype(F32)).astype(BF)
    g4 = net.send(sb.at[2, hi], b2.at[1, hi], ydev(yl))
    yield t0 + 3 + (1.5 * sub + 2) * SUBT + LAT
    core[3].wait_recv()
    for copy in (g1, g2, g3, g4):
        copy.wait_recv()
    total = part[h, c, s, rows].astype(F32) + cb[3, rows].astype(F32)
    done(rows, total + b2[0, rows].astype(F32) + b2[1, rows].astype(F32))


QCOL = HALF // 2


def rs_scratch():
    return [
        pltpu.VMEM((4, 2, 4, 48, QCOL), BF),
        pltpu.VMEM((4, 2, 2, 4, 48, QCOL), BF),
        pltpu.VMEM((4, 2, 4, 48, QCOL), BF),
        pltpu.VMEM((4, 2, 4, 48, QCOL), BF),
        pltpu.VMEM((4, 2, 48, QCOL), BF),
        pltpu.VMEM((4, 2, 2, 48, QCOL), BF),
        pltpu.VMEM((4, 2, 48, QCOL), BF),
    ]


def g_rs_part(net, unit, i, axis_i, j, axis_j, bufs, done, times):
    b1, b2, t, sums, b3, b4, t2 = bufs
    ir, il, io = ring(i)
    jr, jl, jo = ring(j)
    right, left = {axis_i: ir}, {axis_i: il}
    f0 = net.send(unit(io, 0), b1.at[0], right)
    f1 = net.send(unit(io, 1), b1.at[1], left)
    yield times[0]
    g0 = net.send(unit(ir, 1), b2.at[0, 1], right)
    g1 = net.send(unit(il, 0), b2.at[1, 0], left)
    yield times[1]
    f0.wait_recv()
    t[0] = (unit(ir, 0)[...].astype(F32) + b1[0].astype(F32)).astype(BF)
    g2 = net.send(t.at[0], b2.at[0, 0], right)
    f1.wait_recv()
    t[1] = (unit(il, 1)[...].astype(F32) + b1[1].astype(F32)).astype(BF)
    g3 = net.send(t.at[1], b2.at[1, 1], left)
    yield times[2]
    for copy in (g0, g1, g2, g3):
        copy.wait_recv()

    def total(p, k):
        return (
            unit(i, p)[k].astype(F32) + b2[0, p, k].astype(F32) + b2[1, p, k].astype(F32)
        )

    def put(p, k):
        sums[p, k] = total(p, k).astype(BF)

    right, left = {axis_j: jr}, {axis_j: jl}
    put(0, jo)
    f0 = net.send(sums.at[0, jo], b3.at[0], right)
    put(1, jo)
    f1 = net.send(sums.at[1, jo], b3.at[1], left)
    put(1, jr)
    g0 = net.send(sums.at[1, jr], b4.at[0, 1], right)
    put(0, jl)
    g1 = net.send(sums.at[0, jl], b4.at[1, 0], left)
    yield times[3]
    f0.wait_recv()
    t2[0] = (total(0, jr) + b3[0].astype(F32)).astype(BF)
    g2 = net.send(t2.at[0], b4.at[0, 0], right)
    f1.wait_recv()
    t2[1] = (total(1, jl) + b3[1].astype(F32)).astype(BF)
    g3 = net.send(t2.at[1], b4.at[1, 1], left)
    yield times[4]
    for copy in (g0, g1, g2, g3):
        copy.wait_recv()
    for p in range(2):
        done(p, total(p, j) + b4[0, p].astype(F32) + b4[1, p].astype(F32))


def g_rs(net, grads, out, bufs, t0=0.0):
    s, z, h, x, c = place()
    gens = []

    def one(k, first_z):
        times = [t0 + v for v in ((0.2, 5.2, 16.0, 19.5, 23.0) if k % 2 == 0 else (5.0, 8.7, 23.0, 26.0, 29.0))]
        lanes = pl.ds(k * QCOL, QCOL)
        own = [b.at[k] for b in bufs]

        def put(p, v):
            out[p, :, k * QCOL : (k + 1) * QCOL] = v.astype(BF)

        if first_z:
            unit = lambda i, p: grads.at[i, p, :, :, lanes]
            return g_rs_part(net, unit, z, "z", x, "x", own, put, times)
        unit = lambda i, p: grads.at[:, p, i, :, lanes]
        return g_rs_part(net, unit, x, "x", z, "z", own, put, times)

    return inter([one(0, True), one(2, False), one(1, True), one(3, False)])


def wgrad_scratch():
    return [
        pltpu.VMEM((1024, D), BF),
        pltpu.VMEM((1024, D), BF),
        pltpu.VMEM((1024, CIN), BF),
        pltpu.VMEM((1024, HC), BF),
        pltpu.VMEM((4, 2, 4, 48, D), BF),
        pltpu.SemaphoreType.DMA((4,)),
    ]


def g_wgrad(srcs, bufs, sem, t0=0.0):
    copies = [pltpu.make_async_copy(a, b, sem.at[k]) for k, (a, b) in enumerate(zip(srcs, bufs))]
    for copy in copies:
        copy.start()
    yield t0 + 2.0
    u, e, dproj, o, grads = bufs
    copies[0].wait()
    copies[2].wait()
    for k in range(4):
        rows = slice(384 * k, 384 * k + 384)
        grads[k, :, :, :, 0:CIN] = tn(u[:, rows], dproj[...]).astype(BF).reshape(2, 4, 48, CIN)
        if k == 0:
            copies[1].wait()
            copies[3].wait()
        grads[k, :, :, :, CIN:D] = tn(e[:, rows], o[...]).astype(BF).reshape(2, 4, 48, HC)
        yield t0 + 2.0 + 1.7 * (k + 1)


def g_stats(net, mine, total, sb):
    sends = [net.send(mine, sb.at[k], dev) for k, dev in enumerate(group_devs())]
    yield 4.0
    acc = mine[...]
    for k, copy in enumerate(sends):
        copy.wait_recv()
        acc = acc + sb[k]
    total[...] = acc


def g_small(net, mine, bz, bx, total, t0=0.0):
    s, z, h, x, c = place()
    sends = [net.send(mine, bz.at[z], {"z": lax.rem(z + k, 4)}) for k in range(1, 4)]
    bz[z] = mine[...]
    yield t0 + 4.0
    for copy in sends:
        copy.wait_recv()
    bx[x] = bz[0] + bz[1] + bz[2] + bz[3]
    r = bx.at[x]
    sends = [net.send(r, r, {"x": lax.rem(x + k, 4)}) for k in range(1, 4)]
    yield t0 + 10.0
    for copy in sends:
        copy.wait_recv()
    total[...] = bx[0] + bx[1] + bx[2] + bx[3]


def small_scratch():
    return [pltpu.VMEM((4, 8, 640), F32), pltpu.VMEM((4, 8, 640), F32)]


def small_devs():
    s, z, h, x, c = place()
    return [{"z": lax.rem(z + k, 4)} for k in range(1, 4)] + [
        {"x": lax.rem(x + k, 4)} for k in range(1, 4)
    ]


def g_share(net, sums, got, vec, heads):
    s, z, h, x, c = place()
    me = (2 * s + h) * 2 + c
    sends = []
    for dev in group_devs():
        sends.append(net.send(sums.at[dev["s"]], got.at[me], dev))
    got[me] = sums[s]
    yield 20.0
    for copy in sends:
        copy.wait_recv()
    vec[...] = jnp.zeros_like(vec)
    tail = jnp.zeros((5, 256), F32)
    for q in range(8):
        lanes = slice(q * HC, q * HC + HC)
        vec[0:5, lanes] = got[q, 0:5, 0:HC]
        vec[5:6, lanes] = got[q, 5:6, 0:HC]
        tail = tail + got[q, 0:5, HC:640]
        heads[q : q + 1, 0:256] = got[q, 5:6, HC:640]
        heads[q : q + 1, 256:640] = got[q, 6:7, 0:HC]
    vec[0:5, 3072:3328] = tail


def params(cid):
    return pltpu.CompilerParams(
        collective_id=cid, has_side_effects=True, vmem_limit_bytes=VLIM
    )


def sems(n):
    return [pltpu.SemaphoreType.DMA((n,)), pltpu.SemaphoreType.DMA((n,))]


GATHERED = jax.ShapeDtypeStruct((4, 2, 4, 48, D), BF)
CHUNKS = jax.ShapeDtypeStruct((2, 2, 2, 128, D), BF)
SMALL = jax.ShapeDtypeStruct((8, 640), F32)
CHUNK = jax.ShapeDtypeStruct((128, D), BF)


def first_gathers(blk, tok, cot):
    def kernel(blk, tok, cot, w, tall, call, lsem, ssem, rsem):
        greet(zx_devs() + y_devs())
        net = Net(ssem, rsem)
        run(
            [
                g_ag(net, blk, w, lsem.at[0]),
                g_pairs(net, tok, tall, lsem.at[1], 0.0),
                g_pairs(net, cot, call, lsem.at[2], 9.2),
            ]
        )
        net.finish()

    return pl.pallas_call(
        kernel,
        name="first_gathers",
        out_shape=(GATHERED, CHUNKS, CHUNKS),
        in_specs=[VM] * 3,
        out_specs=(ANY,) * 3,
        scratch_shapes=[pltpu.SemaphoreType.DMA((3,))] + sems(48),
        compiler_params=params(0),
    )(blk, tok, cot)


def row_to_col(row):
    i = lax.broadcasted_iota(jnp.int32, (128, 128), 0)
    j = lax.broadcasted_iota(jnp.int32, (128, 128), 1)
    return jnp.sum(jnp.where(i == j, row, 0.0), axis=1, keepdims=True)


def col_to_row(col):
    i = lax.broadcasted_iota(jnp.int32, (128, 128), 0)
    j = lax.broadcasted_iota(jnp.int32, (128, 128), 1)
    return jnp.sum(jnp.where(i == j, col, 0.0), axis=0, keepdims=True)


def own_scale(total):
    s, z, h, x, c = place()
    row = total[pl.ds((2 * h + c) * 2 + s, 1), :]
    return lax.rsqrt(row_to_col(row) * (1.0 / 3072) + EPS)


def fetch(src, dst, sem):
    copy = pltpu.make_async_copy(src, dst, sem)
    copy.start()
    return copy


def norm_back(v, x, e, ng):
    xf = x.astype(F32)
    vg = v * ng[...]
    r = lax.rsqrt(jnp.mean(xf * xf, axis=-1, keepdims=True) + EPS)
    dot = jnp.mean(xf * vg, axis=-1, keepdims=True)
    return e.astype(F32) + r * vg - xf * (r * r * r * dot)


def backward_sum(part, xall, cot, ng, wsrc, small):
    def kernel(part, xall, cot, ng, u, e, dproj, o, small, eall, out, hsum, fin, xo, eo, *rest):
        cbs, bufs, wbufs, rest = rest[:4], rest[4:11], rest[11:17], rest[17:]
        bz, bx, lsem, ssem, rsem = rest
        greet(small_devs() + y_devs())
        net = Net(ssem, rsem)
        s, z, h, x, c = place()
        ox = Once(pltpu.make_async_copy(xall.at[h, c, s], xo, lsem.at[0]))
        oe = Once(pltpu.make_async_copy(cot.at[s], eo, lsem.at[1]))

        def done(rows, v):
            ox.wait()
            oe.wait()
            fin[rows] = norm_back(v, xo[rows], eo[rows], ng).astype(BF)

        def chain(sub):
            yield from g_xrs(net, part, cbs, done, sub)
            yield from g_yag(net, fin, eall, lsem.at[2 + sub], sub)

        def weights():
            yield from g_wgrad((u, e, dproj, o), wbufs[:5], wbufs[5])
            yield from g_rs(net, wbufs[4], out, bufs, 9.0)

        run(
            [chain(sub) for sub in range(NSUB)]
            + [weights(), g_small(net, small, bz, bx, hsum)]
        )
        net.finish()

    return pl.pallas_call(
        kernel,
        name="backward_sum",
        out_shape=(CHUNKS, jax.ShapeDtypeStruct((2, 48, D), BF), SMALL),
        in_specs=[VM, ANY, ANY, VM, ANY, ANY, ANY, ANY, VM],
        out_specs=(ANY, VM, VM),
        scratch_shapes=[pltpu.VMEM((128, D), BF)] * 3
        + xrs_scratch()
        + rs_scratch()
        + wgrad_scratch()
        + small_scratch()
        + [pltpu.SemaphoreType.DMA((2 + NSUB,))]
        + sems(54 + 18 * NSUB),
        compiler_params=params(3),
    )(part, xall, cot, ng, *wsrc, small)


def last_sums(part0, tok, eall, ng, part1, xall, stat1, wsrc, small0, small1):
    def kernel(p0, tok, eall, ng, p1, xall, st, u, e, dproj, o, sm0, sm1, ig, so, out, vec, heads, *rest):
        xo, eo, x1, ba, bb, rest = rest[0], rest[1], rest[2], rest[3:7], rest[7:11], rest[11:]
        bufs, wbufs, rest = rest[:7], rest[7:13], rest[13:]
        bz, bx, sums, got, lsem, ssem, rsem = rest
        greet(small_devs() + group_devs())
        net = Net(ssem, rsem)
        s, z, h, x, c = place()
        ox = Once(pltpu.make_async_copy(tok.at[s], xo, lsem.at[0]))
        oe = Once(pltpu.make_async_copy(eall.at[h, c, s], eo, lsem.at[1]))
        o1 = Once(pltpu.make_async_copy(xall.at[h, c, s], x1, lsem.at[2]))

        def done0(rows, v):
            ox.wait()
            oe.wait()
            ig[rows] = norm_back(v, xo[rows], eo[rows], ng).astype(BF)

        def done1(rows, v):
            o1.wait()
            scale = own_scale(st)[rows.start : rows.start + rows.size]
            so[rows] = (x1[rows].astype(F32) + scale * v).astype(BF)

        def weights():
            yield from g_wgrad((u, e, dproj, o), wbufs[:5], wbufs[5])
            yield from g_rs(net, wbufs[4], out, bufs, 9.0)

        def smalls():
            sums[1] = sm1[...]
            yield from g_small(net, sm0, bz, bx, sums.at[0])
            yield from g_share(net, sums, got, vec, heads)

        run(
            [g_xrs(net, p1, bb, done1, sub) for sub in range(NSUB)]
            + [g_xrs(net, p0, ba, done0, sub) for sub in range(NSUB)]
            + [weights(), smalls()]
        )
        net.finish()

    return pl.pallas_call(
        kernel,
        name="last_sums",
        out_shape=(
            CHUNK,
            CHUNK,
            jax.ShapeDtypeStruct((2, 48, D), BF),
            jax.ShapeDtypeStruct((8, 3328), F32),
            SMALL,
        ),
        in_specs=[VM, ANY, ANY, VM, VM, ANY, VM, ANY, ANY, ANY, ANY, VM, VM],
        out_specs=(VM,) * 5,
        scratch_shapes=[pltpu.VMEM((128, D), BF)] * 3
        + xrs_scratch()
        + xrs_scratch()
        + rs_scratch()
        + wgrad_scratch()
        + small_scratch()
        + [pltpu.VMEM((2, 8, 640), F32), pltpu.VMEM((8, 8, 640), F32)]
        + [pltpu.SemaphoreType.DMA((3,))]
        + sems(61 + 20 * NSUB),
        compiler_params=params(4),
    )(part0, tok, eall, ng, part1, xall, stat1, *wsrc, small0, small1)


def nt(a, b):
    return lax.dot_general(a, b, (((1,), (1,)), ((), ())), preferred_element_type=F32)


def tn(a, b):
    return lax.dot_general(a, b, (((0,), (0,)), ((), ())), preferred_element_type=F32)


def iotas():
    i = lax.broadcasted_iota(jnp.int32, (128, 128), 0)
    j = lax.broadcasted_iota(jnp.int32, (128, 128), 1)
    return i, j


def seg_of(st, chunk, places):
    seg = jnp.full(places.shape, -1, jnp.int32)
    for k in range(4):
        seg = seg + (st[chunk, k] <= places).astype(jnp.int32)
    return seg


def masks(st, chunk):
    i, j = iotas()
    seg = seg_of(st, chunk, i)
    keep = jnp.logical_and(seg == seg_of(st, chunk, j), i >= j)
    valid = [None] + [
        (seg_of(st, chunk, i - k) == seg).astype(F32) for k in range(1, 4)
    ]
    return keep, valid


def conv_tile(xt, cv, t, valid):
    lanes = slice(128 * t, 128 * t + 128)
    pre = cv[4:5, lanes] + cv[3:4, lanes] * xt
    moved = [xt]
    for k in range(1, 4):
        m = pltpu.roll(xt, k, axis=0) * valid[k]
        moved.append(m)
        pre = pre + cv[3 - k : 4 - k, lanes] * m
    return pre, moved


def rates(rt, cv):
    i, j = iotas()
    head = j < NH
    v = rt + cv[7:8, 0:128]
    dt = jnp.where(head, jnp.maximum(v, 0.0) + jnp.log1p(jnp.exp(-jnp.abs(v))), 0.0)
    lower = (i >= j).astype(F32)
    cum = jnp.dot(
        lower, -dt * cv[8:9, 0:128], precision=HIGH, preferred_element_type=F32
    )
    return v, dt, cum


def half_masks():
    _, j = iotas()
    return j < 64


def split_pair(v, low):
    zero = jnp.zeros_like(v)
    return jnp.concatenate([jnp.where(low, v, zero), jnp.where(low, zero, v)], axis=0)


def decay_of(keep, cum, cum_t, h):
    spread = jnp.where(keep, cum[:, h : h + 1] - cum_t[h : h + 1, :], -1e30)
    return jnp.exp(spread)


def load_const(cv):
    return cv[...]


def rows_spec(cols):
    return pl.BlockSpec((256, cols), lambda i: (i, 0))


def whole(*shape):
    return pl.BlockSpec(shape, lambda i: (0,) * len(shape))


class Gather:
    def __init__(self, net, blk, out, lsem):
        s, z, h, x, c = place()
        self.local = pltpu.make_async_copy(blk, out.at[z, :, x], lsem)
        every = slice(None)
        self.parts = []
        for lanes, i, axis_i, j, axis_j, pick in (
            (pl.ds(0, HALF), x, "x", z, "z", lambda i, j, p: (j, p, i)),
            (pl.ds(HALF, HALF), z, "z", x, "x", lambda i, j, p: (i, p, j)),
        ):
            ir, il, _ = ring(i)
            jr, jl, _ = ring(j)

            def at(i, j, p, pick=pick, lanes=lanes):
                return out.at[pick(i, j, p) + (every, lanes)]

            def make(i, j, p, dev, src=None):
                ref = at(i, j, p)
                return net.make(ref if src is None else src, ref, dev)

            own = blk.at[:, :, lanes]
            first, second = ({axis_i: ir}, {axis_i: il}), ({axis_j: jr}, {axis_j: jl})
            self.parts.append(
                [
                    (make(i, j, every, first[0], own), make(i, j, every, first[1], own)),
                    (make(il, j, 0, first[0]), make(ir, j, 1, first[1])),
                    (make(every, j, every, second[0]), make(every, j, every, second[1])),
                    (make(every, jl, 0, second[0]), make(every, jr, 1, second[1])),
                ]
            )

    def step(self, k):
        if k == 0:
            self.local.start()
        if k == 2:
            self.local.wait()
        for part in self.parts:
            for n in range(2):
                if k > 0:
                    part[k - 1][n].wait_recv()
                if k < 4 and k != 2:
                    part[k][n].start()
            if k == 2:
                part[2][0].start()
                part[2][1].start()


class RingSum:
    def __init__(self, net, part, bufs):
        self.part = part
        self.cb, self.sb, self.b1, self.b2 = bufs
        s, z, h, x, c = place()
        self.c = c
        sib = {"c": 1 - c}
        outer, inner = {"h": 1 - h, "s": 1 - s}, {"s": 1 - s}
        self.units = [(1 - h, s), (1 - h, 1 - s), (h, 1 - s), (h, s)]
        self.core = [
            net.make(part.at[hh, 1 - c, mm], self.cb.at[k], sib)
            for k, (hh, mm) in enumerate(self.units)
        ]
        sb, b1, b2 = self.sb, self.b1, self.b2
        lo, hi = pl.ds(0, 64), pl.ds(64, 64)
        self.far = [
            net.make(sb.at[0, lo], b1.at[0], outer),
            net.make(sb.at[0, hi], b1.at[1], inner),
        ]
        self.direct = [
            net.make(sb.at[1, lo], b2.at[0, lo], outer),
            net.make(sb.at[2, hi], b2.at[1, hi], inner),
        ]
        self.summed = [
            net.make(sb.at[1, hi], b2.at[0, hi], outer),
            net.make(sb.at[2, lo], b2.at[1, lo], inner),
        ]

    def core_send(self, ks):
        for k in ks:
            self.core[k].start()

    def add(self, k):
        self.core[k].wait_recv()
        hh, mm = self.units[k]
        self.sb[k] = (self.part[hh, self.c, mm].astype(F32) + self.cb[k].astype(F32)).astype(BF)

    def early(self):
        self.add(0)
        self.far[0].start()
        self.far[1].start()
        self.add(1)
        self.direct[0].start()

    def late(self):
        self.add(2)
        self.direct[1].start()
        lo, hi = slice(0, 64), slice(64, 128)
        self.far[1].wait_recv()
        self.sb[1, hi] = (self.sb[1, hi].astype(F32) + self.b1[1].astype(F32)).astype(BF)
        self.summed[0].start()
        self.far[0].wait_recv()
        self.sb[2, lo] = (self.sb[2, lo].astype(F32) + self.b1[0].astype(F32)).astype(BF)
        self.summed[1].start()

    def total(self):
        self.core[3].wait_recv()
        for copy in self.direct + self.summed:
            copy.wait_recv()
        hh, mm = self.units[3]
        total = self.part[hh, self.c, mm].astype(F32) + self.cb[3].astype(F32)
        return total + self.b2[0].astype(F32) + self.b2[1].astype(F32)


def ring_scratch():
    return [
        pltpu.VMEM((4, 128, D), BF),
        pltpu.VMEM((3, 128, D), BF),
        pltpu.VMEM((2, 64, D), BF),
        pltpu.VMEM((2, 128, D), BF),
    ]


class Spread:
    def __init__(self, net, out):
        s, z, h, x, c = place()
        sib = {"c": 1 - c}
        outer, inner = {"h": 1 - h, "s": 1 - s}, {"s": 1 - s}
        lo, hi = pl.ds(0, 64), pl.ds(64, 64)
        own, far = out.at[h, c, s], out.at[1 - h, c, s]
        from_outer, from_inner = out.at[1 - h, c, 1 - s], out.at[h, c, 1 - s]
        self.mine = own
        self.ring = [net.make(own, own, outer), net.make(own, own, inner)]
        self.hand = [
            net.make(from_inner.at[lo], from_inner.at[lo], outer),
            net.make(from_outer.at[hi], from_outer.at[hi], inner),
        ]
        self.sib = [net.make(r, r, sib) for r in (own, from_inner, from_outer, far)]

    def start(self):
        self.ring[0].start()
        self.ring[1].start()
        self.sib[0].start()

    def hand_on(self):
        self.ring[1].wait_recv()
        self.hand[0].start()
        self.ring[0].wait_recv()
        self.hand[1].start()
        self.sib[1].start()
        self.sib[2].start()

    def wait_same(self):
        self.sib[0].wait_recv()
        self.sib[1].wait_recv()

    def wait_far(self):
        self.hand[0].wait_recv()
        self.hand[1].wait_recv()
        self.sib[3].start()

    def wait_other(self):
        self.sib[2].wait_recv()
        self.sib[3].wait_recv()


def block_at(i, h, c, other_first):
    first = 1 if other_first else 0
    hi = lax.rem(h + first + i // 2, 2)
    ci = lax.rem(c + (i + first if other_first else i), 2)
    return hi, ci


def forward_block(b, chunk_rows, x, w, ng, cv, st, refs, e=None):
    part, stat, proj, yout, uout, doo, og = refs
    with_do = e is not None
    xf = x[...].reshape(256, D).astype(F32)
    r = lax.rsqrt(jnp.mean(xf * xf, axis=-1, keepdims=True) + EPS)
    u = (xf * r * ng).astype(BF)
    uout[...] = u
    proj[...] = jnp.dot(u, w[:, :, :, :, 0:CIN].reshape(D, CIN), preferred_element_type=F32)
    if with_do:
        doo[...] = jnp.dot(
            e[...].reshape(256, D),
            w[:, :, :, :, CIN:D].reshape(D, HC),
            preferred_element_type=F32,
        )
    low = half_masks()
    for m in range(2):
        rows = slice(128 * m, 128 * m + 128)
        chunk = b * 2 + m
        keep, valid = masks(st, chunk)
        act = []
        for t in range(5):
            pre, _ = conv_tile(proj[rows, HC + 128 * t : HC + 128 * t + 128], cv, t, valid)
            act.append((pre * jax.nn.sigmoid(pre)).astype(BF))
        _, dt, cum = rates(proj[rows, RT:CIN], cv)
        cum_t, dt_t = jnp.transpose(cum), jnp.transpose(dt)
        gram = nt(act[4], act[3])
        gsum = jnp.zeros((128, 1), F32)
        tsum = jnp.zeros((128, 1), F32)
        for t in range(3):
            lanes = slice(128 * t, 128 * t + 128)
            mixes = []
            for h in (2 * t, 2 * t + 1):
                dec = decay_of(keep, cum, cum_t, h)
                mixes.append((gram * dec * dt_t[h : h + 1, :]).astype(BF))
            y = jnp.dot(
                jnp.concatenate(mixes, axis=1),
                split_pair(act[t], low),
                preferred_element_type=F32,
            )
            y = y + cv[6:7, lanes] * act[t].astype(F32)
            yout[rows, lanes] = y
            zt = proj[rows, lanes]
            g = y * (zt * jax.nn.sigmoid(zt))
            gsum = gsum + jnp.sum(g * g, axis=1, keepdims=True)
            gain = cv[5:6, lanes]
            og[rows, lanes] = (g * gain).astype(BF)
            if with_do:
                tsum = tsum + jnp.sum(g * gain * doo[rows, lanes], axis=1, keepdims=True)
        stat[pl.ds(chunk, 1), :] = col_to_row(gsum)
        if with_do:
            stat[pl.ds(chunk + 8, 1), :] = col_to_row(tsum)
    out = nt(og[...], w[:, :, :, :, CIN:D].reshape(D, HC))
    part[...] = out.astype(BF).reshape(2, 128, D)


def two_forward(st, x0, w0, ng, cv, call, blk):
    def kernel(
        st, x0h, w0h, ng, cv, callh, blk,
        w1o, x1o, s0o, s1o, p1o, proj0o, proj1o, y0o, y1o, u0o, u1o, doo,
        w0, w1, x0, x1, e1, part, part1, proj, yv, uv, dov, og, stat0, stat1, stb0, stb1,
        cb, sb, b1, b2, isem, osem, lsem, ssem, rsem,
    ):
        s, z, h, x, c = place()
        loads = [pltpu.make_async_copy(w0h, w0, isem.at[0]), pltpu.make_async_copy(callh, e1, isem.at[1])]
        loads[0].start()
        xl = [pltpu.make_async_copy(x0h.at[k // 2, k % 2], x0.at[k // 2, k % 2], isem.at[2 + k]) for k in range(4)]
        for copy in xl:
            copy.start()
        greet(zx_devs() + group_devs())
        net = Net(ssem, rsem)
        gather = Gather(net, blk, w1, lsem.at[0])
        ring = RingSum(net, part, (cb, sb, b1, b2))
        spread = Spread(net, x1)
        devs = group_devs()
        stats0 = [net.make(stat0, stb0.at[k], dev) for k, dev in enumerate(devs)]
        stats1 = [net.make(stat1, stb1.at[k], dev) for k, dev in enumerate(devs)]
        gather.step(0)
        loads[0].wait()
        loads[1].start()
        for copy in xl:
            copy.wait()

        def saves(b, layer, proj_o, y_o, u_o):
            return [
                pltpu.make_async_copy(v.at[b], o.at[b], osem.at[layer, n, b])
                for n, (v, o) in enumerate(((proj, proj_o), (yv, y_o), (uv, u_o)))
            ]

        def first(i, carry):
            hi, ci = block_at(i, h, c, True)
            b = 2 * hi + ci
            forward_block(
                b, None, x0.at[hi, ci], w0, ng[0], cv.at[0], st,
                (part.at[hi, ci], stat0, proj.at[b], yv.at[b], uv.at[b], None, og),
            )
            for copy in saves(b, 0, proj0o, y0o, u0o):
                copy.start()

            @pl.when(i == 0)
            def _():
                ring.core_send((0, 1))

            @pl.when(i == 1)
            def _():
                ring.early()
                gather.step(1)

            @pl.when(i == 2)
            def _():
                ring.core_send((2, 3))
                gather.step(2)

            return carry

        lax.fori_loop(0, 4, first, 0)
        for copy in stats0:
            copy.start()
        ring.late()
        acc = stat0[...]
        for k, copy in enumerate(stats0):
            copy.wait_recv()
            acc = acc + stb0[k]
        s0o[...] = acc
        for b in range(4):
            for copy in saves(b, 0, proj0o, y0o, u0o):
                copy.wait()
        loads[1].wait()
        gather.step(3)
        total = ring.total()
        x1[h, c, s] = (x0[h, c, s].astype(F32) + own_scale(s0o) * total).astype(BF)
        spread.start()
        gather.step(4)
        keep_w = pltpu.make_async_copy(w1, w1o, isem.at[0])
        keep_w.start()
        spread.hand_on()

        def second(i, carry):
            @pl.when(i == 1)
            def _():
                spread.wait_same()

            @pl.when(i == 2)
            def _():
                spread.wait_far()

            @pl.when(i == 3)
            def _():
                spread.wait_other()

            hi, ci = block_at(i, h, c, False)
            b = 2 * hi + ci
            forward_block(
                b, None, x1.at[hi, ci], w1, ng[1], cv.at[1], st,
                (part1.at[hi, ci], stat1, proj.at[b], yv.at[b], uv.at[b], dov.at[b], og),
                e1.at[hi, ci],
            )
            for copy in saves(b, 1, proj1o, y1o, u1o):
                copy.start()
            for n, (v, o) in enumerate(((dov.at[b], doo.at[b]), (x1.at[hi, ci], x1o.at[hi, ci]), (part1.at[hi, ci], p1o.at[hi, ci]))):
                pltpu.make_async_copy(v, o, osem.at[2, n, b]).start()
            return carry

        lax.fori_loop(0, 4, second, 0)
        for copy in stats1:
            copy.start()
        acc = stat1[...]
        for k, copy in enumerate(stats1):
            copy.wait_recv()
            acc = acc + stb1[k]
        s1o[...] = acc
        keep_w.wait()
        for b in range(4):
            for copy in saves(b, 1, proj1o, y1o, u1o):
                copy.wait()
            p = (b // 2, b % 2)
            for n, (v, o) in enumerate(((dov.at[b], doo.at[b]), (x1.at[p], x1o.at[p]), (part1.at[p], p1o.at[p]))):
                pltpu.make_async_copy(v, o, osem.at[2, n, b]).wait()
        net.finish()

    blocks = lambda cols, t: jax.ShapeDtypeStruct((4, 256, cols), t)
    return pl.pallas_call(
        kernel,
        name="two_forward",
        out_shape=(
            GATHERED,
            CHUNKS,
            jax.ShapeDtypeStruct((8, 128), F32),
            jax.ShapeDtypeStruct((16, 128), F32),
            CHUNKS,
            blocks(CIN, F32),
            blocks(CIN, F32),
            blocks(HC, F32),
            blocks(HC, F32),
            blocks(D, BF),
            blocks(D, BF),
            blocks(HC, F32),
        ),
        in_specs=[SM, ANY, ANY, VM, VM, ANY, VM],
        out_specs=(ANY, ANY, VM, VM) + (ANY,) * 8,
        scratch_shapes=[
            pltpu.VMEM((4, 2, 4, 48, D), BF),
            pltpu.VMEM((4, 2, 4, 48, D), BF),
            pltpu.VMEM((2, 2, 2, 128, D), BF),
            pltpu.VMEM((2, 2, 2, 128, D), BF),
            pltpu.VMEM((2, 2, 2, 128, D), BF),
            pltpu.VMEM((2, 2, 2, 128, D), BF),
            pltpu.VMEM((2, 2, 2, 128, D), BF),
            pltpu.VMEM((4, 256, CIN), F32),
            pltpu.VMEM((4, 256, HC), F32),
            pltpu.VMEM((4, 256, D), BF),
            pltpu.VMEM((4, 256, HC), F32),
            pltpu.VMEM((256, HC), BF),
            pltpu.VMEM((8, 128), F32),
            pltpu.VMEM((16, 128), F32),
            pltpu.VMEM((7, 8, 128), F32),
            pltpu.VMEM((7, 16, 128), F32),
        ]
        + ring_scratch()
        + [
            pltpu.SemaphoreType.DMA((6,)),
            pltpu.SemaphoreType.DMA((3, 3, 4)),
            pltpu.SemaphoreType.DMA((1,)),
        ]
        + sems(56),
        compiler_params=params(1),
    )(st, x0, w0, ng, cv, call, blk)


def make_backward(first):
    def kernel(st, e, w, cv, proj, yin, stat, *rest):
        if first:
            x, x1, dproj, oo, part, sm, do = rest
        else:
            do, dproj, oo, part, sm = rest
        step = pl.program_id(0)

        @pl.when(step == 0)
        def _():
            sm[...] = jnp.zeros_like(sm)

        if first:
            do[...] = jnp.dot(e[...], w[:, CIN:D], preferred_element_type=F32)
        low = half_masks()
        i, j = iotas()
        upper = (j >= i).astype(F32)

        def add(row, lanes, v):
            sm[row : row + 1, lanes] += jnp.sum(v, axis=0, keepdims=True)

        for m in range(2):
            rows = slice(128 * m, 128 * m + 128)
            chunk = step * 2 + m
            keep, valid = masks(st, chunk)
            pres, moves, act = [], [], []
            for t in range(5):
                pre, moved = conv_tile(
                    proj[rows, HC + 128 * t : HC + 128 * t + 128], cv, t, valid
                )
                pres.append(pre)
                moves.append(moved)
                act.append((pre * jax.nn.sigmoid(pre)).astype(BF))
            v, dt, cum = rates(proj[rows, RT:CIN], cv)
            cum_t, dt_t = jnp.transpose(cum), jnp.transpose(dt)
            gram = nt(act[4], act[3])
            r = lax.rsqrt(row_to_col(stat[pl.ds(chunk, 1), :]) * (1.0 / 3072) + EPS)
            if first:
                dots = jnp.sum(
                    e[rows, :].astype(F32) * (x1[rows, :].astype(F32) - x[rows, :].astype(F32)),
                    axis=1,
                    keepdims=True,
                )
                k = r * r * dots * (1.0 / 3072)
            else:
                k = r * r * r * row_to_col(stat[pl.ds(chunk + 8, 1), :]) * (1.0 / 3072)
            dact = []
            dgram = jnp.zeros((128, 128), F32)
            dcum = jnp.zeros((128, 128), F32)
            col_rows = []
            for t in range(3):
                lanes = slice(128 * t, 128 * t + 128)
                zt, y, dot_ = proj[rows, lanes], yin[rows, lanes], do[rows, lanes]
                gain = cv[5:6, lanes]
                sig = jax.nn.sigmoid(zt)
                sz = zt * sig
                g = y * sz
                oo[rows, lanes] = (g * r * gain).astype(BF)
                add(5, lanes, dot_ * g * r)
                dg = r * (dot_ * gain) - g * k
                dproj[rows, lanes] = (dg * y * (sig + sz * (1.0 - sig))).astype(BF)
                dy = (dg * sz).astype(BF)
                dyf = dy.astype(F32)
                xs = act[t]
                add(6, lanes, dyf * xs.astype(F32))
                dy2 = split_pair(dy, low)
                dmix2 = nt(dy2, xs)
                mixes = []
                for q in range(2):
                    h = 2 * t + q
                    dec = decay_of(keep, cum, cum_t, h)
                    dt_row = dt_t[h : h + 1, :]
                    pm = gram * dec
                    mixes.append((pm * dt_row).astype(BF))
                    dmix = dmix2[128 * q : 128 * q + 128]
                    dgram = dgram + dmix * (dec * dt_row)
                    vm = dmix * pm
                    col_rows.append(jnp.sum(vm, axis=0, keepdims=True))
                    rsum = jnp.sum(vm * dt_row, axis=1, keepdims=True)
                    dcum = dcum + jnp.where(j == h, rsum, 0.0)
                dxs = tn(jnp.concatenate(mixes, axis=0), dy2)
                dact.append(dxs + cv[6:7, lanes] * dyf)
            dgl = dgram.astype(BF)
            dact.append(tn(dgl, act[4]))
            dact.append(jnp.dot(dgl, act[3], preferred_element_type=F32))
            ddt = jnp.transpose(
                jnp.concatenate(col_rows + [jnp.zeros((128 - NH, 128), F32)], axis=0)
            )
            dcum = dcum - ddt * dt
            dla = jnp.dot(upper, dcum, precision=HIGH, preferred_element_type=F32)
            nexp = -cv[8:9, 0:128]
            drate = (ddt + dla * nexp) * jax.nn.sigmoid(v)
            drate = jnp.where(j < NH, drate, 0.0)
            add(5, slice(HC, HC + 128), drate)
            add(5, slice(HC + 128, 640), dla * dt * nexp)
            dproj[rows, RT:CIN] = drate.astype(BF)
            for t in range(5):
                lanes = slice(128 * t, 128 * t + 128)
                pre = pres[t]
                sp = jax.nn.sigmoid(pre)
                dpre = dact[t] * (sp + pre * sp * (1.0 - sp))
                add(4, lanes, dpre)
                add(3, lanes, dpre * moves[t][0])
                dx = cv[3:4, lanes] * dpre
                for n in range(1, 4):
                    add(3 - n, lanes, dpre * moves[t][n])
                    dx = dx + cv[3 - n : 4 - n, lanes] * pltpu.roll(
                        dpre * valid[n], 128 - n, axis=0
                    )
                dproj[rows, HC + 128 * t : HC + 128 * t + 128] = dx.astype(BF)
        part[...] = nt(dproj[...], w[:, 0:CIN]).astype(BF)

    return kernel


def layer_backward(st, e, w, cv, proj, y, stat, do=None, x=None, x1=None):
    first = do is None
    extra = [x, x1] if first else [do]
    ins = [st, e, w, cv, proj, y, stat] + extra
    in_specs = [
        SM,
        rows_spec(D),
        whole(D, D),
        whole(16, 640),
        rows_spec(CIN),
        rows_spec(HC),
        whole(*stat.shape),
    ] + ([rows_spec(D), rows_spec(D)] if first else [rows_spec(HC)])
    outs = [
        jax.ShapeDtypeStruct((1024, CIN), BF),
        jax.ShapeDtypeStruct((1024, HC), BF),
        jax.ShapeDtypeStruct((1024, D), BF),
        SMALL,
    ]
    return pl.pallas_call(
        make_backward(first),
        name="layer_backward",
        grid=(4,),
        in_specs=in_specs,
        out_specs=[rows_spec(CIN), rows_spec(HC), rows_spec(D), whole(8, 640)],
        out_shape=outs,
        scratch_shapes=[pltpu.VMEM((256, HC), F32)] if first else [],
        compiler_params=pltpu.CompilerParams(vmem_limit_bytes=VLIM),
    )(*ins)


def pack_shards(starts, norm_gain, w_in, conv_weight, conv_bias, gate_gain, w_out):
    small = jnp.concatenate(
        [
            conv_weight.reshape(-1),
            conv_bias,
            gate_gain,
            starts.reshape(-1).astype(BF),
            jnp.zeros((20,), BF),
        ]
    ).reshape(24, PKN)
    wide = jnp.concatenate([norm_gain[:, None], small], axis=1)

    def each(v):
        return jnp.broadcast_to(v[:, None], (24, 8, v.shape[-1]))

    rate = jnp.concatenate(
        [w_in[:, 6400:].reshape(24, 8, NH), each(wide), jnp.zeros((24, 8, 107), BF)], axis=-1
    )
    pieces = jnp.concatenate(
        [
            w_in[:, :3072].reshape(24, 8, HC),
            w_in[:, 3072:6144].reshape(24, 8, HC),
            each(w_in[:, 6144:6400]),
            rate,
            jnp.transpose(w_out).reshape(24, 8, HC),
        ],
        axis=-1,
    )
    return jnp.transpose(pieces, (1, 0, 2))


def constants(w, q, dt_bias, a_log, skip_d):
    tile = w[:, RT : RT + 128].astype(F32)
    pairs = jnp.transpose(tile[:, NH : NH + 2 * (PKN + 1)].reshape(D, 2, PKN + 1), (1, 0, 2))
    ng = pairs[:, None, :, 0]
    small = pairs[:, :, 1:].reshape(2, 64, 24 * PKN)
    taps = jnp.transpose(small[:, :, :208].reshape(2, 64, 4, 52), (0, 2, 1, 3)).reshape(2, 4, 3328)
    conv = jnp.concatenate([taps, small[:, :, 208:260].reshape(2, 1, 3328)], axis=1)
    gate = small[:, :, 260:308].reshape(2, 1, 3072)
    conv = jnp.concatenate(
        [lax.dynamic_slice_in_dim(conv, q * HC, HC, 2), conv[:, :, 3072:]], axis=2
    )
    gate = lax.dynamic_slice_in_dim(gate, q * HC, HC, 2)

    def heads(v):
        return lax.dynamic_slice_in_dim(v, q * NH, NH, 1)

    skip = jnp.repeat(heads(skip_d), 64, axis=1)[:, None]
    pad = lambda v: jnp.pad(v, ((0, 0), (0, 0), (0, 640 - v.shape[2])))
    rows = [
        conv,
        pad(gate),
        pad(skip),
        pad(heads(dt_bias)[:, None]),
        pad(heads(jnp.exp(a_log))[:, None]),
        jnp.zeros((2, 7, 640), F32),
    ]
    return jnp.concatenate(rows, axis=1), ng


def unpack_grads(rec, vec, heads, w_in, norm_gain, place_dp):
    rec = rec.astype(F32)
    flat = lambda v: jnp.transpose(v, (1, 0, 2)).reshape(24, -1)
    w_in_grad = jnp.concatenate(
        [
            flat(rec[:, :, 0:HC]),
            flat(rec[:, :, HC : 2 * HC]),
            jnp.sum(rec[:, :, 2 * HC : RT], axis=0),
            flat(rec[:, :, RT : RT + NH]),
        ],
        axis=1,
    )
    w_out_grad = jnp.transpose(flat(rec[:, :, CIN:D]))
    conv = lax.dynamic_slice_in_dim(vec[0:5], 52 * place_dp, 52, 1)
    gate = lax.dynamic_slice_in_dim(vec[5], 48 * place_dp, 48, 0)
    norm_grad = jnp.sum(w_in.astype(F32) * w_in_grad, axis=1) / norm_gain.astype(F32)
    return (
        norm_grad,
        w_in_grad,
        conv[0:4],
        conv[4],
        heads[:, 0:NH].reshape(48),
        heads[:, 128 : 128 + NH].reshape(48),
        jnp.sum(heads[:, 256:640].reshape(48, 64), axis=1),
        gate,
        w_out_grad,
    )


GROUP = ("s", "h", "c")


def body(
    tokens,
    cotangent,
    starts,
    norm_gain,
    w_in,
    conv_weight,
    conv_bias,
    dt_bias,
    a_log,
    skip_d,
    gate_gain,
    w_out,
):
    s, z, h, x, c = place()
    q = (s * 2 + h) * 2 + c
    mine = pack_shards(
        starts[:, 0], norm_gain[0], w_in[0], conv_weight[0], conv_bias[0], gate_gain[0], w_out[0]
    )
    rec = lax.all_to_all(mine, GROUP, 0, 0, tiled=True)
    blocks = rec.reshape(2, 2, 48, D)
    st = (
        rec[0:4, :, RT + PK0 : RT + PK0 + PKN]
        .reshape(4, 24 * PKN)[:, 308:316]
        .reshape(8, 4)
        .astype(jnp.int32)
    )
    gap = lambda v, n: jnp.pad(v, ((0, 0), (0, 0), (n, D - n - v.shape[2])))
    blk0 = blocks[0] + gap(blocks[1, :, :, RT + NH : RT + PK0 + PKN], RT + PK0 + PKN)
    heads = jnp.stack([dt_bias[0], a_log[0], skip_d[0]])
    other = lax.ppermute(heads, "s", [(0, 1), (1, 0)])
    heads = jnp.where(s == 0, jnp.stack([heads, other]), jnp.stack([other, heads]))

    w0g, tall, call = first_gathers(blk0, tokens, cotangent)
    w0 = w0g.reshape(D, D)
    x0 = tall.reshape(1024, D)
    e1 = call.reshape(1024, D)
    cv, ng = constants(w0, q, heads[:, 0], heads[:, 1], heads[:, 2])
    w1, xall, stat0, stat1, part1, proj0, proj1, y0, y1, u0, u1, do1 = two_forward(
        st, tall, w0g, ng, cv, call, blocks[1]
    )
    flat = lambda v: v.reshape(1024, v.shape[-1])
    proj0, proj1, y0, y1, u0, u1, do1 = map(flat, (proj0, proj1, y0, y1, u0, u1, do1))
    w1 = w1.reshape(D, D)
    x1 = xall.reshape(1024, D)
    dproj1, o1, dpart1, sm1 = layer_backward(st, e1, w1, cv[1], proj1, y1, stat1, do=do1)
    eall, gs1, sm1 = backward_sum(
        dpart1.reshape(2, 2, 2, 128, D), xall, cotangent, ng[1], (u1, e1, dproj1, o1), sm1
    )
    e0 = eall.reshape(1024, D)
    dproj0, o0, dpart0, sm0 = layer_backward(st, e0, w0, cv[0], proj0, y0, stat0, x=x0, x1=x1)
    ig0, so1, gs0, vec, hd = last_sums(
        dpart0.reshape(2, 2, 2, 128, D),
        tokens,
        eall,
        ng[0],
        part1,
        xall,
        stat1[0:8],
        (u0, e0, dproj0, o0),
        sm0,
        sm1,
    )
    back = lax.all_to_all(jnp.stack([gs0, gs1]).reshape(8, 24, D), GROUP, 0, 0, tiled=True)
    place_dp = ((z * 2 + h) * 4 + x) * 2 + c
    outs = unpack_grads(back, vec, hd, w_in[0], norm_gain[0], place_dp)

    got = lax.ppermute(jnp.where(s == 0, so1, ig0), "s", [(0, 1), (1, 0)])
    ig = jnp.where(s == 0, jnp.stack([ig0, got]), eall[h, c])
    so = jnp.where(s == 0, xall[h, c], jnp.stack([got, so1]))
    return (so[None], ig.astype(F32)[None]) + tuple(o[None] for o in outs)


def solution(mesh):
    inner = Mesh(mesh.devices.reshape(2, 4, 2, 4, 2), ("s", "z", "h", "x", "c"))
    dp = ("z", "h", "x", "c")
    in_specs = (
        P(None, dp, None),
        P(None, dp, None),
        P(None, dp, None),
        P("s", dp),
        P("s", dp, None),
        P("s", None, dp),
        P("s", dp),
        P("s", None),
        P("s", None),
        P("s", None),
        P("s", dp),
        P("s", None, dp),
    )
    out_specs = (
        P("s", None, dp, None),
        P("s", None, dp, None),
        P("s", dp),
        P("s", dp, None),
        P("s", None, dp),
        P("s", dp),
        P("s", None),
        P("s", None),
        P("s", None),
        P("s", dp),
        P("s", None, dp),
    )
    return jax.shard_map(body, mesh=inner, in_specs=in_specs, out_specs=out_specs, check_vma=False)
```

```python
import jax
import jax.numpy as jnp
from jax import lax
from jax.experimental import pallas as pl
from jax.experimental.pallas import tpu as pltpu
from jax.sharding import Mesh, PartitionSpec as P

EPS = 1e-05
BF = jnp.bfloat16
F32 = jnp.float32
HIGH = lax.Precision.HIGHEST
D = 1536
CIN = 1152
HC = 384
NH = 6
RT = 1024
PK0 = 7
PKN = 14
HEAD0 = RT + 32
HALF = 768
ANY = pl.BlockSpec(memory_space=pl.ANY)
VM = pl.BlockSpec(memory_space=pltpu.VMEM)
SM = pl.BlockSpec(memory_space=pltpu.SMEM)
VLIM = 56 * 1024 * 1024


class Net:
    def __init__(self, ssem, rsem):
        self.ssem, self.rsem, self.n, self.all = ssem, rsem, 0, []

    def make(self, src, dst, dev):
        i = self.n
        self.n += 1
        assert i < self.ssem.shape[0]
        copy = pltpu.make_async_remote_copy(
            src_ref=src,
            dst_ref=dst,
            send_sem=self.ssem.at[i],
            recv_sem=self.rsem.at[i],
            device_id=dev,
            device_id_type=pl.DeviceIdType.MESH,
        )
        self.all.append(copy)
        return copy

    def send(self, src, dst, dev):
        copy = self.make(src, dst, dev)
        copy.start()
        return copy

    def finish(self):
        for copy in self.all:
            copy.wait_send()


def place():
    s, z, h, x, c = (lax.axis_index(a) for a in ("s", "z", "h", "x", "c"))
    return s, z, h, x, c


def ring(i):
    return lax.rem(i + 1, 4), lax.rem(i + 3, 4), lax.rem(i + 2, 4)


def greet(devs):
    barrier = pltpu.get_barrier_semaphore()
    for dev in devs:
        pl.semaphore_signal(barrier, inc=1, device_id=dev, device_id_type=pl.DeviceIdType.MESH)
    pl.semaphore_wait(barrier, len(devs))


def zx_devs():
    s, z, h, x, c = place()
    zr, zl, _ = ring(z)
    xr, xl, _ = ring(x)
    return [{"z": zr}, {"z": zl}, {"x": xr}, {"x": xl}]


def ydev(y):
    return {"h": y // 2, "s": lax.rem(y, 2)}


def y_devs():
    s, z, h, x, c = place()
    yr, yl, _ = ring(2 * h + s)
    return [ydev(yr), ydev(yl), {"c": 1 - c}]


def group_devs():
    s, z, h, x, c = place()
    out = []
    for k in range(1, 8):
        out.append(
            {
                "s": 1 - s if k & 4 else s,
                "h": 1 - h if k & 2 else h,
                "c": 1 - c if k & 1 else c,
            }
        )
    return out


LAT = 1.7


def inter(gens):
    gens = [[0.0, g] for g in gens]
    while gens:
        item = min(gens, key=lambda v: v[0])
        if item[0] > 0:
            yield item[0]
        try:
            item[0] = next(item[1])
        except StopIteration:
            gens.remove(item)


def run(gens):
    for _ in inter(gens):
        pass


def g_pairs(net, own, out, lsem, t0):
    s, z, h, x, c = place()
    outer, inner, sib = {"h": 1 - h, "s": 1 - s}, {"s": 1 - s}, {"c": 1 - c}
    first = []
    for k in range(2):
        rows = pl.ds(64 * k, 64)
        first.append(net.send(own.at[s, rows], out.at[h, c, s, rows], outer))
    local = pltpu.make_async_copy(own, out.at[h, c], lsem)
    local.start()
    c0 = net.send(own, out.at[h, c], sib)
    yield t0 + 4.6 + LAT
    second = []
    for k in range(2):
        first[k].wait_recv()
        r = out.at[1 - h, c, 1 - s, pl.ds(64 * k, 64)]
        second.append(net.send(r, r, inner))
        if k == 0:
            yield t0 + 9.2 + LAT
    r = out.at[1 - h, c, 1 - s]
    c1 = net.send(r, r, sib)
    yield t0 + 14 + LAT
    for copy in second:
        copy.wait_recv()
    r = out.at[1 - h, c, s]
    c2 = net.send(r, r, sib)
    yield t0 + 16 + LAT
    for copy in (c0, c1, c2):
        copy.wait_recv()
    local.wait()


def g_small(net, mine, bz, bx, total, t0=0.0):
    s, z, h, x, c = place()
    sends = [net.send(mine, bz.at[z], {"z": lax.rem(z + k, 4)}) for k in range(1, 4)]
    bz[z] = mine[...]
    yield t0 + 4.0
    for copy in sends:
        copy.wait_recv()
    bx[x] = bz[0] + bz[1] + bz[2] + bz[3]
    r = bx.at[x]
    sends = [net.send(r, r, {"x": lax.rem(x + k, 4)}) for k in range(1, 4)]
    yield t0 + 10.0
    for copy in sends:
        copy.wait_recv()
    total[...] = bx[0] + bx[1] + bx[2] + bx[3]


def small_scratch():
    return [pltpu.VMEM((4, 2, 8, 640), F32), pltpu.VMEM((4, 2, 8, 640), F32)]


def small_devs():
    s, z, h, x, c = place()
    return [{"z": lax.rem(z + k, 4)} for k in range(1, 4)] + [
        {"x": lax.rem(x + k, 4)} for k in range(1, 4)
    ]


def g_share(net, sums, got, vec, heads):
    s, z, h, x, c = place()
    me = (2 * s + h) * 2 + c
    sends = []
    for dev in group_devs():
        sends.append(net.send(sums.at[dev["s"]], got.at[me], dev))
    got[me] = sums[s]
    yield 20.0
    for copy in sends:
        copy.wait_recv()
    vec[...] = jnp.zeros_like(vec)
    tail = jnp.zeros((5, 256), F32)
    for q in range(8):
        lanes = slice(q * HC, q * HC + HC)
        vec[0:5, lanes] = got[q, 0:5, 0:HC]
        vec[5:6, lanes] = got[q, 5:6, 0:HC]
        tail = tail + got[q, 0:5, HC:640]
        heads[q : q + 1, 0:256] = got[q, 5:6, HC:640]
        heads[q : q + 1, 256:640] = got[q, 6:7, 0:HC]
    vec[0:5, 3072:3328] = tail


def params(cid):
    return pltpu.CompilerParams(
        collective_id=cid, has_side_effects=True, vmem_limit_bytes=VLIM
    )


def sems(n):
    return [pltpu.SemaphoreType.DMA((n,)), pltpu.SemaphoreType.DMA((n,))]


GATHERED = jax.ShapeDtypeStruct((4, 2, 4, 48, D), BF)
CHUNKS = jax.ShapeDtypeStruct((2, 2, 2, 128, D), BF)
SMALL = jax.ShapeDtypeStruct((8, 640), F32)
CHUNK = jax.ShapeDtypeStruct((128, D), BF)


def g_gather(gather):
    for k, t in enumerate((5.0, 7.0, 21.0, 29.0, 0.0)):
        gather.step(k)
        yield t


def first_gathers(blk, tok, cot):
    def kernel(blk, tok, cot, w, tall, call, lsem, ssem, rsem):
        greet(zx_devs() + y_devs())
        net = Net(ssem, rsem)
        run(
            [
                g_gather(Gather(net, blk, w, lsem.at[0])),
                g_pairs(net, tok, tall, lsem.at[1], 0.0),
                g_pairs(net, cot, call, lsem.at[2], 9.2),
            ]
        )
        net.finish()

    return pl.pallas_call(
        kernel,
        name="first_gathers",
        out_shape=(GATHERED, CHUNKS, CHUNKS),
        in_specs=[VM] * 3,
        out_specs=(ANY,) * 3,
        scratch_shapes=[pltpu.SemaphoreType.DMA((3,))] + sems(48),
        compiler_params=params(0),
    )(blk, tok, cot)


def row_to_col(row):
    i = lax.broadcasted_iota(jnp.int32, (128, 128), 0)
    j = lax.broadcasted_iota(jnp.int32, (128, 128), 1)
    return jnp.sum(jnp.where(i == j, row, 0.0), axis=1, keepdims=True)


def col_to_row(col):
    i = lax.broadcasted_iota(jnp.int32, (128, 128), 0)
    j = lax.broadcasted_iota(jnp.int32, (128, 128), 1)
    return jnp.sum(jnp.where(i == j, col, 0.0), axis=0, keepdims=True)


def own_scale(total):
    s, z, h, x, c = place()
    row = total[pl.ds((2 * h + c) * 2 + s, 1), :]
    return lax.rsqrt(row_to_col(row) * (1.0 / 3072) + EPS)


def norm_back(v, x, e, ng):
    xf = x.astype(F32)
    vg = v * ng[...]
    r = lax.rsqrt(jnp.mean(xf * xf, axis=-1, keepdims=True) + EPS)
    dot = jnp.mean(xf * vg, axis=-1, keepdims=True)
    return e.astype(F32) + r * vg - xf * (r * r * r * dot)


def nt(a, b):
    return lax.dot_general(a, b, (((1,), (1,)), ((), ())), preferred_element_type=F32)


def tn(a, b):
    return lax.dot_general(a, b, (((0,), (0,)), ((), ())), preferred_element_type=F32)


def iotas():
    i = lax.broadcasted_iota(jnp.int32, (128, 128), 0)
    j = lax.broadcasted_iota(jnp.int32, (128, 128), 1)
    return i, j


def seg_of(st, chunk, places):
    seg = jnp.full(places.shape, -1, jnp.int32)
    for k in range(4):
        seg = seg + (st[chunk, k] <= places).astype(jnp.int32)
    return seg


def masks(st, chunk):
    i, j = iotas()
    seg = seg_of(st, chunk, i)
    keep = jnp.logical_and(seg == seg_of(st, chunk, j), i >= j)
    valid = [None] + [
        (seg_of(st, chunk, i - k) == seg).astype(F32) for k in range(1, 4)
    ]
    return keep, valid


def conv_tile(xt, cv, t, valid):
    lanes = slice(128 * t, 128 * t + 128)
    pre = cv[4:5, lanes] + cv[3:4, lanes] * xt
    moved = [xt]
    for k in range(1, 4):
        m = pltpu.roll(xt, k, axis=0) * valid[k]
        moved.append(m)
        pre = pre + cv[3 - k : 4 - k, lanes] * m
    return pre, moved


def rates(rt, cv):
    i, j = iotas()
    head = j < NH
    v = rt + cv[7:8, 0:128]
    dt = jnp.where(head, jnp.maximum(v, 0.0) + jnp.log1p(jnp.exp(-jnp.abs(v))), 0.0)
    lower = (i >= j).astype(F32)
    cum = jnp.dot(
        lower, -dt * cv[8:9, 0:128], precision=HIGH, preferred_element_type=F32
    )
    return v, dt, cum


def half_masks():
    _, j = iotas()
    return j < 64


def split_pair(v, low):
    zero = jnp.zeros_like(v)
    return jnp.concatenate([jnp.where(low, v, zero), jnp.where(low, zero, v)], axis=0)


def decay_of(keep, cum, cum_t, h):
    spread = jnp.where(keep, cum[:, h : h + 1] - cum_t[h : h + 1, :], -1e30)
    return jnp.exp(spread)


class Gather:
    def __init__(self, net, blk, out, lsem):
        s, z, h, x, c = place()
        self.local = pltpu.make_async_copy(blk, out.at[z, :, x], lsem)
        every = slice(None)
        self.parts = []
        for lanes, i, axis_i, j, axis_j, pick in (
            (pl.ds(0, HALF), x, "x", z, "z", lambda i, j, p: (j, p, i)),
            (pl.ds(HALF, HALF), z, "z", x, "x", lambda i, j, p: (i, p, j)),
        ):
            ir, il, _ = ring(i)
            jr, jl, _ = ring(j)

            def at(i, j, p, pick=pick, lanes=lanes):
                return out.at[pick(i, j, p) + (every, lanes)]

            def make(i, j, p, dev, src=None):
                ref = at(i, j, p)
                return net.make(ref if src is None else src, ref, dev)

            own = blk.at[:, :, lanes]
            first, second = ({axis_i: ir}, {axis_i: il}), ({axis_j: jr}, {axis_j: jl})
            self.parts.append(
                [
                    (make(i, j, every, first[0], own), make(i, j, every, first[1], own)),
                    (make(il, j, 0, first[0]), make(ir, j, 1, first[1])),
                    (make(every, j, every, second[0]), make(every, j, every, second[1])),
                    (make(every, jl, 0, second[0]), make(every, jr, 1, second[1])),
                ]
            )

    def step(self, k):
        if k == 0:
            self.local.start()
        if k == 2:
            self.local.wait()
        for part in self.parts:
            for n in range(2):
                if k > 0:
                    part[k - 1][n].wait_recv()
                if k < 4 and k != 2:
                    part[k][n].start()
            if k == 2:
                part[2][0].start()
                part[2][1].start()


class RingSum:
    def __init__(self, net, part, bufs):
        self.part = part
        self.cb, self.sb, self.b1, self.b2 = bufs
        s, z, h, x, c = place()
        self.c = c
        sib = {"c": 1 - c}
        outer, inner = {"h": 1 - h, "s": 1 - s}, {"s": 1 - s}
        self.units = [(1 - h, s), (1 - h, 1 - s), (h, 1 - s), (h, s)]
        self.core = [
            net.make(part.at[hh, 1 - c, mm], self.cb.at[k], sib)
            for k, (hh, mm) in enumerate(self.units)
        ]
        sb, b1, b2 = self.sb, self.b1, self.b2
        lo, hi = pl.ds(0, 64), pl.ds(64, 64)
        self.far = [
            net.make(sb.at[0, lo], b1.at[0], outer),
            net.make(sb.at[0, hi], b1.at[1], inner),
        ]
        self.direct = [
            net.make(sb.at[1, lo], b2.at[0, lo], outer),
            net.make(sb.at[2, hi], b2.at[1, hi], inner),
        ]
        self.summed = [
            net.make(sb.at[1, hi], b2.at[0, hi], outer),
            net.make(sb.at[2, lo], b2.at[1, lo], inner),
        ]

    def core_send(self, ks):
        for k in ks:
            self.core[k].start()

    def add(self, k):
        self.core[k].wait_recv()
        hh, mm = self.units[k]
        self.sb[k] = (self.part[hh, self.c, mm].astype(F32) + self.cb[k].astype(F32)).astype(BF)

    def early(self):
        self.add(0)
        self.far[0].start()
        self.far[1].start()
        self.add(1)
        self.direct[0].start()

    def late(self):
        self.add(2)
        self.direct[1].start()
        lo, hi = slice(0, 64), slice(64, 128)
        self.far[1].wait_recv()
        self.sb[1, hi] = (self.sb[1, hi].astype(F32) + self.b1[1].astype(F32)).astype(BF)
        self.summed[0].start()
        self.far[0].wait_recv()
        self.sb[2, lo] = (self.sb[2, lo].astype(F32) + self.b1[0].astype(F32)).astype(BF)
        self.summed[1].start()

    def total(self):
        self.core[3].wait_recv()
        for copy in self.direct + self.summed:
            copy.wait_recv()
        hh, mm = self.units[3]
        total = self.part[hh, self.c, mm].astype(F32) + self.cb[3].astype(F32)
        return total + self.b2[0].astype(F32) + self.b2[1].astype(F32)


def ring_scratch():
    return [
        pltpu.VMEM((4, 128, D), BF),
        pltpu.VMEM((3, 128, D), BF),
        pltpu.VMEM((2, 64, D), BF),
        pltpu.VMEM((2, 128, D), BF),
    ]


class Spread:
    def __init__(self, net, out):
        s, z, h, x, c = place()
        sib = {"c": 1 - c}
        outer, inner = {"h": 1 - h, "s": 1 - s}, {"s": 1 - s}
        lo, hi = pl.ds(0, 64), pl.ds(64, 64)
        own, far = out.at[h, c, s], out.at[1 - h, c, s]
        from_outer, from_inner = out.at[1 - h, c, 1 - s], out.at[h, c, 1 - s]
        self.mine = own
        self.ring = [net.make(own, own, outer), net.make(own, own, inner)]
        self.hand = [
            net.make(from_inner.at[lo], from_inner.at[lo], outer),
            net.make(from_outer.at[hi], from_outer.at[hi], inner),
        ]
        self.sib = [net.make(r, r, sib) for r in (own, from_inner, from_outer, far)]

    def start(self):
        self.ring[0].start()
        self.ring[1].start()
        self.sib[0].start()

    def hand_on(self):
        self.ring[1].wait_recv()
        self.hand[0].start()
        self.ring[0].wait_recv()
        self.hand[1].start()
        self.sib[1].start()
        self.sib[2].start()

    def wait_same(self):
        self.sib[0].wait_recv()
        self.sib[1].wait_recv()

    def wait_far(self):
        self.hand[0].wait_recv()
        self.hand[1].wait_recv()
        self.sib[3].start()

    def wait_other(self):
        self.sib[2].wait_recv()
        self.sib[3].wait_recv()


def block_at(i, h, c, other_first):
    first = 1 if other_first else 0
    hi = lax.rem(h + first + i // 2, 2)
    ci = lax.rem(c + (i + first if other_first else i), 2)
    return hi, ci


def forward_block(b, chunk_rows, x, w, ng, cv, st, refs, e=None):
    part, stat, proj, yout, uout, doo, og = refs
    with_do = e is not None
    xf = x[...].reshape(256, D).astype(F32)
    r = lax.rsqrt(jnp.mean(xf * xf, axis=-1, keepdims=True) + EPS)
    u = (xf * r * ng).astype(BF)
    uout[...] = u
    proj[...] = jnp.dot(u, w[:, :, :, :, 0:CIN].reshape(D, CIN), preferred_element_type=F32)
    if with_do:
        doo[...] = jnp.dot(
            e[...].reshape(256, D),
            w[:, :, :, :, CIN:D].reshape(D, HC),
            preferred_element_type=F32,
        )
    low = half_masks()
    for m in range(2):
        rows = slice(128 * m, 128 * m + 128)
        chunk = b * 2 + m
        keep, valid = masks(st, chunk)
        act = []
        for t in range(5):
            pre, _ = conv_tile(proj[rows, HC + 128 * t : HC + 128 * t + 128], cv, t, valid)
            act.append((pre * jax.nn.sigmoid(pre)).astype(BF))
        _, dt, cum = rates(proj[rows, RT:CIN], cv)
        cum_t, dt_t = jnp.transpose(cum), jnp.transpose(dt)
        gram = nt(act[4], act[3])
        gsum = jnp.zeros((128, 1), F32)
        tsum = jnp.zeros((128, 1), F32)
        for t in range(3):
            lanes = slice(128 * t, 128 * t + 128)
            mixes = []
            for h in (2 * t, 2 * t + 1):
                dec = decay_of(keep, cum, cum_t, h)
                mixes.append((gram * dec * dt_t[h : h + 1, :]).astype(BF))
            y = jnp.dot(
                jnp.concatenate(mixes, axis=1),
                split_pair(act[t], low),
                preferred_element_type=F32,
            )
            y = y + cv[6:7, lanes] * act[t].astype(F32)
            yout[rows, lanes] = y
            zt = proj[rows, lanes]
            g = y * (zt * jax.nn.sigmoid(zt))
            gsum = gsum + jnp.sum(g * g, axis=1, keepdims=True)
            gain = cv[5:6, lanes]
            og[rows, lanes] = (g * gain).astype(BF)
            if with_do:
                tsum = tsum + jnp.sum(g * gain * doo[rows, lanes], axis=1, keepdims=True)
        stat[pl.ds(chunk, 1), :] = col_to_row(gsum)
        if with_do:
            stat[pl.ds(chunk + 8, 1), :] = col_to_row(tsum)
    out = nt(og[...], w[:, :, :, :, CIN:D].reshape(D, HC))
    part[...] = out.astype(BF).reshape(2, 128, D)


def two_forward(st, x0, w0, ng, cv, call, blk):
    def kernel(
        st, x0h, w0h, ng, cv, callh, blk,
        w1o, x1o, s0o, s1o, p1o, proj0o, proj1o, y0o, y1o, u0o, u1o, doo,
        w0, w1, x0, x1, e1, part, part1, proj, yv, uv, dov, og, stat0, stat1, stb0, stb1,
        cb, sb, b1, b2, isem, osem, lsem, ssem, rsem,
    ):
        s, z, h, x, c = place()
        loads = [pltpu.make_async_copy(w0h, w0, isem.at[0]), pltpu.make_async_copy(callh, e1, isem.at[1])]
        loads[0].start()
        xl = [pltpu.make_async_copy(x0h.at[k // 2, k % 2], x0.at[k // 2, k % 2], isem.at[2 + k]) for k in range(4)]
        for copy in xl:
            copy.start()
        greet(zx_devs() + group_devs())
        net = Net(ssem, rsem)
        gather = Gather(net, blk, w1, lsem.at[0])
        ring = RingSum(net, part, (cb, sb, b1, b2))
        spread = Spread(net, x1)
        devs = group_devs()
        stats0 = [net.make(stat0, stb0.at[k], dev) for k, dev in enumerate(devs)]
        stats1 = [net.make(stat1, stb1.at[k], dev) for k, dev in enumerate(devs)]
        gather.step(0)
        loads[0].wait()
        loads[1].start()
        for copy in xl:
            copy.wait()

        def saves(b, layer, proj_o, y_o, u_o):
            return [
                pltpu.make_async_copy(v.at[b], o.at[b], osem.at[layer, n, b])
                for n, (v, o) in enumerate(((proj, proj_o), (yv, y_o), (uv, u_o)))
            ]

        def first(i, carry):
            hi, ci = block_at(i, h, c, True)
            b = 2 * hi + ci
            forward_block(
                b, None, x0.at[hi, ci], w0, ng[0], cv.at[0], st,
                (part.at[hi, ci], stat0, proj.at[b], yv.at[b], uv.at[b], None, og),
            )
            for copy in saves(b, 0, proj0o, y0o, u0o):
                copy.start()

            @pl.when(i == 0)
            def _():
                ring.core_send((0, 1))

            @pl.when(i == 1)
            def _():
                ring.early()
                gather.step(1)

            @pl.when(i == 2)
            def _():
                ring.core_send((2, 3))
                gather.step(2)

            return carry

        lax.fori_loop(0, 4, first, 0)
        for copy in stats0:
            copy.start()
        ring.late()
        acc = stat0[...]
        for k, copy in enumerate(stats0):
            copy.wait_recv()
            acc = acc + stb0[k]
        s0o[...] = acc
        for b in range(4):
            for copy in saves(b, 0, proj0o, y0o, u0o):
                copy.wait()
        loads[1].wait()
        gather.step(3)
        total = ring.total()
        x1[h, c, s] = (x0[h, c, s].astype(F32) + own_scale(s0o) * total).astype(BF)
        spread.start()
        gather.step(4)
        keep_w = pltpu.make_async_copy(w1, w1o, isem.at[0])
        keep_w.start()
        spread.hand_on()

        def second(i, carry):
            @pl.when(i == 1)
            def _():
                spread.wait_same()

            @pl.when(i == 2)
            def _():
                spread.wait_far()

            @pl.when(i == 3)
            def _():
                spread.wait_other()

            hi, ci = block_at(i, h, c, False)
            b = 2 * hi + ci
            forward_block(
                b, None, x1.at[hi, ci], w1, ng[1], cv.at[1], st,
                (part1.at[hi, ci], stat1, proj.at[b], yv.at[b], uv.at[b], dov.at[b], og),
                e1.at[hi, ci],
            )
            for copy in saves(b, 1, proj1o, y1o, u1o):
                copy.start()
            for n, (v, o) in enumerate(((dov.at[b], doo.at[b]), (x1.at[hi, ci], x1o.at[hi, ci]), (part1.at[hi, ci], p1o.at[hi, ci]))):
                pltpu.make_async_copy(v, o, osem.at[2, n, b]).start()
            return carry

        lax.fori_loop(0, 4, second, 0)
        for copy in stats1:
            copy.start()
        acc = stat1[...]
        for k, copy in enumerate(stats1):
            copy.wait_recv()
            acc = acc + stb1[k]
        s1o[...] = acc
        keep_w.wait()
        for b in range(4):
            for copy in saves(b, 1, proj1o, y1o, u1o):
                copy.wait()
            p = (b // 2, b % 2)
            for n, (v, o) in enumerate(((dov.at[b], doo.at[b]), (x1.at[p], x1o.at[p]), (part1.at[p], p1o.at[p]))):
                pltpu.make_async_copy(v, o, osem.at[2, n, b]).wait()
        net.finish()

    blocks = lambda cols, t: jax.ShapeDtypeStruct((4, 256, cols), t)
    return pl.pallas_call(
        kernel,
        name="two_forward",
        out_shape=(
            GATHERED,
            CHUNKS,
            jax.ShapeDtypeStruct((8, 128), F32),
            jax.ShapeDtypeStruct((16, 128), F32),
            CHUNKS,
            blocks(CIN, F32),
            blocks(CIN, F32),
            blocks(HC, F32),
            blocks(HC, F32),
            blocks(D, BF),
            blocks(D, BF),
            blocks(HC, F32),
        ),
        in_specs=[SM, ANY, ANY, VM, VM, ANY, VM],
        out_specs=(ANY, ANY, VM, VM) + (ANY,) * 8,
        scratch_shapes=[
            pltpu.VMEM((4, 2, 4, 48, D), BF),
            pltpu.VMEM((4, 2, 4, 48, D), BF),
            pltpu.VMEM((2, 2, 2, 128, D), BF),
            pltpu.VMEM((2, 2, 2, 128, D), BF),
            pltpu.VMEM((2, 2, 2, 128, D), BF),
            pltpu.VMEM((2, 2, 2, 128, D), BF),
            pltpu.VMEM((2, 2, 2, 128, D), BF),
            pltpu.VMEM((4, 256, CIN), F32),
            pltpu.VMEM((4, 256, HC), F32),
            pltpu.VMEM((4, 256, D), BF),
            pltpu.VMEM((4, 256, HC), F32),
            pltpu.VMEM((256, HC), BF),
            pltpu.VMEM((8, 128), F32),
            pltpu.VMEM((16, 128), F32),
            pltpu.VMEM((7, 8, 128), F32),
            pltpu.VMEM((7, 16, 128), F32),
        ]
        + ring_scratch()
        + [
            pltpu.SemaphoreType.DMA((6,)),
            pltpu.SemaphoreType.DMA((3, 3, 4)),
            pltpu.SemaphoreType.DMA((1,)),
        ]
        + sems(56),
        compiler_params=params(1),
    )(st, x0, w0, ng, cv, call, blk)


class Scatter:
    def __init__(self, net, grads, bufs, out):
        s, z, h, x, c = place()
        self.out = out
        self.parts = []
        for k, (i, axis_i, j, axis_j) in enumerate(((z, "z", x, "x"), (x, "x", z, "z"))):
            lanes = pl.ds(k * HALF, HALF)
            b1, b2, t, sums, b3, b4, t2 = [b.at[k] for b in bufs]
            ir, il, io = ring(i)
            jr, jl, jo = ring(j)
            if k == 0:
                unit = lambda i, p, lanes=lanes: grads.at[i, p, :, :, lanes]
            else:
                unit = lambda i, p, lanes=lanes: grads.at[:, p, i, :, lanes]
            right, left = {axis_i: ir}, {axis_i: il}
            part = dict(unit=unit, bufs=(b1, b2, t, sums, b3, b4, t2), i=i, j=j)
            part.update(ir=ir, il=il, jr=jr, jl=jl, jo=jo, k=k)
            part["far"] = [
                net.make(unit(io, 0), b1.at[0], right),
                net.make(unit(io, 1), b1.at[1], left),
            ]
            part["near"] = [
                net.make(unit(ir, 1), b2.at[0, 1], right),
                net.make(unit(il, 0), b2.at[1, 0], left),
                net.make(t.at[0], b2.at[0, 0], right),
                net.make(t.at[1], b2.at[1, 1], left),
            ]
            right, left = {axis_j: jr}, {axis_j: jl}
            part["far2"] = [
                net.make(sums.at[0, jo], b3.at[0], right),
                net.make(sums.at[1, jo], b3.at[1], left),
            ]
            part["near2"] = [
                net.make(sums.at[1, jr], b4.at[0, 1], right),
                net.make(sums.at[0, jl], b4.at[1, 0], left),
                net.make(t2.at[0], b4.at[0, 0], right),
                net.make(t2.at[1], b4.at[1, 1], left),
            ]
            self.parts.append(part)

    def start(self, k):
        for copy in self.parts[k]["far"]:
            copy.start()

    def direct(self, k):
        self.parts[k]["near"][0].start()
        self.parts[k]["near"][1].start()

    def summed(self, k):
        v = self.parts[k]
        b1, b2, t, sums, b3, b4, t2 = v["bufs"]
        for p, near in ((0, v["ir"]), (1, v["il"])):
            v["far"][p].wait_recv()
            for n in range(4):
                t[p, n] = (v["unit"](near, p)[n].astype(F32) + b1[p, n].astype(F32)).astype(BF)
            v["near"][2 + p].start()

    def total(self, v, p, n):
        b2 = v["bufs"][1]
        return (
            v["unit"](v["i"], p)[n].astype(F32)
            + b2[0, p, n].astype(F32)
            + b2[1, p, n].astype(F32)
        )

    def second(self, k):
        v = self.parts[k]
        sums = v["bufs"][3]
        for copy in v["near"]:
            copy.wait_recv()
        for copy, p, n in (
            (v["far2"][0], 0, v["jo"]),
            (v["far2"][1], 1, v["jo"]),
            (v["near2"][0], 1, v["jr"]),
            (v["near2"][1], 0, v["jl"]),
        ):
            sums[p, n] = self.total(v, p, n).astype(BF)
            copy.start()

    def second_summed(self, k):
        v = self.parts[k]
        b1, b2, t, sums, b3, b4, t2 = v["bufs"]
        for p, near in ((0, v["jr"]), (1, v["jl"])):
            v["far2"][p].wait_recv()
            t2[p] = (self.total(v, p, near) + b3[p].astype(F32)).astype(BF)
            v["near2"][2 + p].start()

    def finish(self, k):
        v = self.parts[k]
        b4 = v["bufs"][5]
        for copy in v["near2"]:
            copy.wait_recv()
        for p in range(2):
            total = self.total(v, p, v["j"]) + b4[0, p].astype(F32) + b4[1, p].astype(F32)
            self.out[p, :, k * HALF : (k + 1) * HALF] = total.astype(BF)


def scatter_scratch():
    return [
        pltpu.VMEM((2, 2, 4, 48, HALF), BF),
        pltpu.VMEM((2, 2, 2, 4, 48, HALF), BF),
        pltpu.VMEM((2, 2, 4, 48, HALF), BF),
        pltpu.VMEM((2, 2, 4, 48, HALF), BF),
        pltpu.VMEM((2, 2, 48, HALF), BF),
        pltpu.VMEM((2, 2, 2, 48, HALF), BF),
        pltpu.VMEM((2, 2, 48, HALF), BF),
    ]


def weight_tile(k, u, e, dproj, o, grads):
    cols = pl.ds(pl.multiple_of(k * 384, 128), 384)
    rows = 1024
    a = tn(u[:, :, cols].reshape(rows, 384), dproj[...].reshape(rows, CIN))
    grads[k, :, :, :, 0:CIN] = a.astype(BF).reshape(2, 4, 48, CIN)
    a = tn(e[:, :, :, :, cols].reshape(rows, 384), o[...].reshape(rows, HC))
    grads[k, :, :, :, CIN:D] = a.astype(BF).reshape(2, 4, 48, HC)


def backward_block(b, e, w, cv, st, stat, dots, refs):
    proj, yin, do, dproj, oo, part, sm = refs
    if dots is not None:
        do[...] = jnp.dot(
            e[...].reshape(256, D),
            w[:, :, :, :, CIN:D].reshape(D, HC),
            preferred_element_type=F32,
        )
    low = half_masks()
    i, j = iotas()
    upper = (j >= i).astype(F32)

    def add(row, lanes, v):
        sm[row : row + 1, lanes] += jnp.sum(v, axis=0, keepdims=True)

    for m in range(2):
        rows = slice(128 * m, 128 * m + 128)
        chunk = b * 2 + m
        keep, valid = masks(st, chunk)
        pres, moves, act = [], [], []
        for t in range(5):
            pre, moved = conv_tile(proj[rows, HC + 128 * t : HC + 128 * t + 128], cv, t, valid)
            pres.append(pre)
            moves.append(moved)
            act.append((pre * jax.nn.sigmoid(pre)).astype(BF))
        v, dt, cum = rates(proj[rows, RT:CIN], cv)
        cum_t, dt_t = jnp.transpose(cum), jnp.transpose(dt)
        gram = nt(act[4], act[3])
        r = lax.rsqrt(row_to_col(stat[pl.ds(chunk, 1), :]) * (1.0 / 3072) + EPS)
        if dots is not None:
            k = r * r * row_to_col(dots[chunk, 0:1, :]) * (1.0 / 3072)
        else:
            k = r * r * r * row_to_col(stat[pl.ds(chunk + 8, 1), :]) * (1.0 / 3072)
        dact = []
        dgram = jnp.zeros((128, 128), F32)
        dcum = jnp.zeros((128, 128), F32)
        col_rows = []
        for t in range(3):
            lanes = slice(128 * t, 128 * t + 128)
            zt, y, dot_ = proj[rows, lanes], yin[rows, lanes], do[rows, lanes]
            gain = cv[5:6, lanes]
            sig = jax.nn.sigmoid(zt)
            sz = zt * sig
            g = y * sz
            oo[rows, lanes] = (g * r * gain).astype(BF)
            add(5, lanes, dot_ * g * r)
            dg = r * (dot_ * gain) - g * k
            dproj[rows, lanes] = (dg * y * (sig + sz * (1.0 - sig))).astype(BF)
            dy = (dg * sz).astype(BF)
            dyf = dy.astype(F32)
            xs = act[t]
            add(6, lanes, dyf * xs.astype(F32))
            dy2 = split_pair(dy, low)
            dmix2 = nt(dy2, xs)
            mixes = []
            for q in range(2):
                h = 2 * t + q
                dec = decay_of(keep, cum, cum_t, h)
                dt_row = dt_t[h : h + 1, :]
                pm = gram * dec
                mixes.append((pm * dt_row).astype(BF))
                dmix = dmix2[128 * q : 128 * q + 128]
                dgram = dgram + dmix * (dec * dt_row)
                vm = dmix * pm
                col_rows.append(jnp.sum(vm, axis=0, keepdims=True))
                rsum = jnp.sum(vm * dt_row, axis=1, keepdims=True)
                dcum = dcum + jnp.where(j == h, rsum, 0.0)
            dxs = tn(jnp.concatenate(mixes, axis=0), dy2)
            dact.append(dxs + cv[6:7, lanes] * dyf)
        dgl = dgram.astype(BF)
        dact.append(tn(dgl, act[4]))
        dact.append(jnp.dot(dgl, act[3], preferred_element_type=F32))
        ddt = jnp.transpose(
            jnp.concatenate(col_rows + [jnp.zeros((128 - NH, 128), F32)], axis=0)
        )
        dcum = dcum - ddt * dt
        dla = jnp.dot(upper, dcum, precision=HIGH, preferred_element_type=F32)
        nexp = -cv[8:9, 0:128]
        drate = (ddt + dla * nexp) * jax.nn.sigmoid(v)
        drate = jnp.where(j < NH, drate, 0.0)
        add(5, slice(HC, HC + 128), drate)
        add(5, slice(HC + 128, 640), dla * dt * nexp)
        dproj[rows, RT:CIN] = drate.astype(BF)
        for t in range(5):
            lanes = slice(128 * t, 128 * t + 128)
            pre = pres[t]
            sp = jax.nn.sigmoid(pre)
            dpre = dact[t] * (sp + pre * sp * (1.0 - sp))
            add(4, lanes, dpre)
            add(3, lanes, dpre * moves[t][0])
            dx = cv[3:4, lanes] * dpre
            for n in range(1, 4):
                add(3 - n, lanes, dpre * moves[t][n])
                dx = dx + cv[3 - n : 4 - n, lanes] * pltpu.roll(
                    dpre * valid[n], 128 - n, axis=0
                )
            dproj[rows, HC + 128 * t : HC + 128 * t + 128] = dx.astype(BF)
    out = nt(dproj[...], w[:, :, :, :, 0:CIN].reshape(D, CIN))
    part[...] = out.astype(BF).reshape(2, 128, D)


def two_backward(st, w1, w0, ng, cv, call, xall, tall, proj1, proj0, y1, y0, do1, u1, stat1, stat0):
    def kernel(
        st, w1h, w0h, ng, cv, callh, xallh, tallh, proj1h, proj0h, y1h, y0h, do1h, u1h, stat1, stat0,
        e0o, dproj0o, o0o, part0o, sm1, sm0, gs1,
        w, e1, e0, proj, yv, do, dproj, oo, u, part, part0, x1own, x0own, dtile, db, grads, *rest,
    ):
        rbufs, sbufs, (isem, bsem, osem, ssem, rsem) = rest[:4], rest[4:11], rest[11:]
        s, z, h, x, c = place()

        def block_loads(i, other_first, proj_h, y_h, do_h, layer):
            hi, ci = block_at(i, h, c, other_first)
            b = 2 * hi + ci
            pairs = [(proj_h, proj), (y_h, yv)] + ([(do_h, do)] if do_h is not None else [])
            return [
                pltpu.make_async_copy(src.at[b], dst.at[b], bsem.at[layer, n, i])
                for n, (src, dst) in enumerate(pairs)
            ]

        loads1 = lambda i: block_loads(i, True, proj1h, y1h, do1h, 1)
        loads0 = lambda i: block_loads(i, False, proj0h, y0h, None, 0)
        for copy in loads1(0):
            copy.start()
        lw1 = pltpu.make_async_copy(w1h, w, isem.at[0])
        lw1.start()
        for i in range(1, 4):
            for copy in loads1(i):
                copy.start()
        later = [
            pltpu.make_async_copy(callh, e1, isem.at[1]),
            pltpu.make_async_copy(u1h, u, isem.at[2]),
            pltpu.make_async_copy(xallh.at[h, c, s], x1own, isem.at[3]),
            pltpu.make_async_copy(tallh.at[h, c, s], x0own, isem.at[4]),
        ]
        for copy in later:
            copy.start()
        greet(zx_devs() + group_devs())
        net = Net(ssem, rsem)
        ring_sum = RingSum(net, part, rbufs)
        spread = Spread(net, e0)
        scatter = Scatter(net, grads, sbufs, gs1)
        me = (2 * h + c) * 2 + s
        dsends = [net.make(dtile, db.at[me], dev) for dev in group_devs()]
        sm1[...] = jnp.zeros_like(sm1)
        sm0[...] = jnp.zeros_like(sm0)
        lw1.wait()

        def first(i, carry):
            hi, ci = block_at(i, h, c, True)
            b = 2 * hi + ci
            for copy in loads1(i):
                copy.wait()
            backward_block(
                b, None, w, cv.at[1], st, stat1, None,
                (proj.at[b], yv.at[b], do.at[b], dproj.at[b], oo.at[b], part.at[hi, ci], sm1),
            )

            @pl.when(i == 0)
            def _():
                ring_sum.core_send((0, 1))

            @pl.when(i == 1)
            def _():
                ring_sum.early()

            @pl.when(i == 2)
            def _():
                ring_sum.core_send((2, 3))

            return carry

        lax.fori_loop(0, 4, first, 0)
        lw0 = pltpu.make_async_copy(w0h, w, isem.at[5])
        lw0.start()
        for i in range(4):
            for copy in loads0(i):
                copy.start()
        ring_sum.late()
        for copy in later:
            copy.wait()
        _, _, zo = ring(z)
        weight_tile(zo, u, e1, dproj, oo, grads)
        scatter.start(0)
        zr, zl, _ = ring(z)
        weight_tile(zr, u, e1, dproj, oo, grads)
        weight_tile(zl, u, e1, dproj, oo, grads)
        weight_tile(z, u, e1, dproj, oo, grads)
        scatter.start(1)
        total = ring_sum.total()
        e0f = norm_back(total, x1own[...], e1[h, c, s], ng.at[1])
        e0l = e0f.astype(BF)
        e0[h, c, s] = e0l
        spread.start()
        diff = x1own[...].astype(F32) - x0own[...].astype(F32)
        dots = jnp.sum(e0l.astype(F32) * diff, axis=1, keepdims=True)
        dtile[...] = jnp.broadcast_to(col_to_row(dots), (8, 128))
        db[me] = dtile[...]
        for copy in dsends:
            copy.start()
        for k in range(2):
            scatter.direct(k)
            scatter.summed(k)
        spread.hand_on()
        for copy in dsends:
            copy.wait_recv()
        lw0.wait()

        def saves(i):
            hi, ci = block_at(i, h, c, False)
            b = 2 * hi + ci
            return [
                pltpu.make_async_copy(src, dst, osem.at[n, i])
                for n, (src, dst) in enumerate(
                    (
                        (dproj.at[b], dproj0o.at[b]),
                        (oo.at[b], o0o.at[b]),
                        (part0.at[hi, ci], part0o.at[hi, ci]),
                        (e0.at[hi, ci], e0o.at[hi, ci]),
                    )
                )
            ]

        def second(i, carry):
            @pl.when(i == 1)
            def _():
                spread.wait_same()

            @pl.when(i == 2)
            def _():
                spread.wait_far()

            @pl.when(i == 3)
            def _():
                spread.wait_other()

            hi, ci = block_at(i, h, c, False)
            b = 2 * hi + ci
            for copy in loads0(i):
                copy.wait()
            backward_block(
                b, e0.at[hi, ci], w, cv.at[0], st, stat0, db,
                (proj.at[b], yv.at[b], do.at[b], dproj.at[b], oo.at[b], part0.at[hi, ci], sm0),
            )
            for copy in saves(i):
                copy.start()

            @pl.when(i == 1)
            def _():
                scatter.second(0)
                scatter.second(1)

            @pl.when(i == 2)
            def _():
                scatter.second_summed(0)
                scatter.second_summed(1)

            return carry

        lax.fori_loop(0, 4, second, 0)
        scatter.finish(0)
        scatter.finish(1)
        for i in range(4):
            for copy in saves(i):
                copy.wait()
        net.finish()

    blocks = lambda cols, t: jax.ShapeDtypeStruct((4, 256, cols), t)
    big = pltpu.VMEM((4, 2, 4, 48, D), BF)
    rows = pltpu.VMEM((2, 2, 2, 128, D), BF)
    return pl.pallas_call(
        kernel,
        name="two_backward",
        out_shape=(
            CHUNKS,
            blocks(CIN, BF),
            blocks(HC, BF),
            CHUNKS,
            SMALL,
            SMALL,
            jax.ShapeDtypeStruct((2, 48, D), BF),
        ),
        in_specs=[SM, ANY, ANY, VM, VM] + [ANY] * 9 + [VM, VM],
        out_specs=(ANY, ANY, ANY, ANY, VM, VM, VM),
        scratch_shapes=[
            big,
            rows,
            rows,
            pltpu.VMEM((4, 256, CIN), F32),
            pltpu.VMEM((4, 256, HC), F32),
            pltpu.VMEM((4, 256, HC), F32),
            pltpu.VMEM((4, 256, CIN), BF),
            pltpu.VMEM((4, 256, HC), BF),
            pltpu.VMEM((4, 256, D), BF),
            rows,
            rows,
            pltpu.VMEM((128, D), BF),
            pltpu.VMEM((128, D), BF),
            pltpu.VMEM((8, 128), F32),
            pltpu.VMEM((8, 8, 128), F32),
            big,
        ]
        + ring_scratch()
        + scatter_scratch()
        + [
            pltpu.SemaphoreType.DMA((6,)),
            pltpu.SemaphoreType.DMA((2, 3, 4)),
            pltpu.SemaphoreType.DMA((4, 4)),
        ]
        + sems(60),
        compiler_params=params(3),
    )(st, w1, w0, ng, cv, call, xall, tall, proj1, proj0, y1, y0, do1, u1, stat1, stat0)


def last_sums(part0, tall, eall, ng, part1, xall, stat1, wsrc, small):
    def kernel(
        p0h, tall, eall, ng, p1h, xall, st, uh, dprojh, oh, small, ig, so, out, vec, heads,
        p0, p1, xo, x1, u, e, dproj, o, grads, *rest,
    ):
        ba, bb, sbufs = rest[:4], rest[4:8], rest[8:15]
        bz, bx, sums, got, lsem, ssem, rsem = rest[15:]
        s, z, h, x, c = place()
        loads = [
            pltpu.make_async_copy(src, dst, lsem.at[n])
            for n, (src, dst) in enumerate(
                (
                    (uh, u),
                    (dprojh, dproj),
                    (eall, e),
                    (oh, o),
                    (p0h, p0),
                    (p1h, p1),
                    (tall.at[h, c, s], xo),
                    (xall.at[h, c, s], x1),
                )
            )
        ]
        for copy in loads:
            copy.start()
        greet(small_devs() + group_devs())
        net = Net(ssem, rsem)
        scatter = Scatter(net, grads, sbufs, out)
        ring0, ring1 = RingSum(net, p0, ba), RingSum(net, p1, bb)
        zr, zl, zo = ring(z)

        def smalls():
            yield from g_small(net, small, bz, bx, sums)
            yield from g_share(net, sums, got, vec, heads)

        sm = smalls()
        next(sm)
        for n in range(4):
            loads[n].wait()
        weight_tile(zo, u, e, dproj, o, grads)
        scatter.start(0)
        loads[4].wait()
        ring0.core_send((0, 1, 2, 3))
        weight_tile(zr, u, e, dproj, o, grads)
        loads[5].wait()
        ring1.core_send((0, 1, 2, 3))
        ring0.early()
        weight_tile(zl, u, e, dproj, o, grads)
        scatter.direct(0)
        weight_tile(z, u, e, dproj, o, grads)
        scatter.start(1)
        next(sm)
        scatter.summed(0)
        ring0.late()
        ring1.early()
        scatter.direct(1)
        scatter.summed(1)
        ring1.late()
        loads[6].wait()
        loads[7].wait()
        ig[...] = norm_back(ring0.total(), xo[...], e[h, c, s], ng).astype(BF)
        next(sm)
        scatter.second(0)
        so[...] = (x1[...].astype(F32) + own_scale(st) * ring1.total()).astype(BF)
        scatter.second(1)
        scatter.second_summed(0)
        scatter.second_summed(1)
        for _ in sm:
            pass
        scatter.finish(0)
        scatter.finish(1)
        net.finish()

    rows = pltpu.VMEM((2, 2, 2, 128, D), BF)
    return pl.pallas_call(
        kernel,
        name="last_sums",
        out_shape=(
            CHUNK,
            CHUNK,
            jax.ShapeDtypeStruct((2, 48, D), BF),
            jax.ShapeDtypeStruct((8, 3328), F32),
            SMALL,
        ),
        in_specs=[ANY, ANY, ANY, VM, ANY, ANY, VM, ANY, ANY, ANY, VM],
        out_specs=(VM,) * 5,
        scratch_shapes=[
            rows,
            rows,
            pltpu.VMEM((128, D), BF),
            pltpu.VMEM((128, D), BF),
            pltpu.VMEM((4, 256, D), BF),
            rows,
            pltpu.VMEM((4, 256, CIN), BF),
            pltpu.VMEM((4, 256, HC), BF),
            pltpu.VMEM((4, 2, 4, 48, D), BF),
        ]
        + ring_scratch()
        + ring_scratch()
        + scatter_scratch()
        + small_scratch()
        + [pltpu.VMEM((2, 8, 640), F32), pltpu.VMEM((8, 8, 640), F32)]
        + [pltpu.SemaphoreType.DMA((8,))]
        + sems(64),
        compiler_params=params(4),
    )(part0, tall, eall, ng, part1, xall, stat1, *wsrc, small)


def pack_shards(starts, norm_gain, w_in, conv_weight, conv_bias, gate_gain, w_out):
    small = jnp.concatenate(
        [
            conv_weight.reshape(-1),
            conv_bias,
            gate_gain,
            starts.reshape(-1).astype(BF),
            jnp.zeros((20,), BF),
        ]
    ).reshape(24, PKN)
    wide = jnp.concatenate([norm_gain[:, None], small], axis=1)

    def each(v):
        return jnp.broadcast_to(v[:, None], (24, 8, v.shape[-1]))

    rate = jnp.concatenate(
        [w_in[:, 6400:].reshape(24, 8, NH), each(wide), jnp.zeros((24, 8, 107), BF)], axis=-1
    )
    pieces = jnp.concatenate(
        [
            w_in[:, :3072].reshape(24, 8, HC),
            w_in[:, 3072:6144].reshape(24, 8, HC),
            each(w_in[:, 6144:6400]),
            rate,
            jnp.transpose(w_out).reshape(24, 8, HC),
        ],
        axis=-1,
    )
    return jnp.transpose(pieces, (1, 0, 2))


def constants(w, q, dt_bias, a_log, skip_d):
    tile = w[:, RT : RT + 128].astype(F32)
    pairs = jnp.transpose(tile[:, NH : NH + 2 * (PKN + 1)].reshape(D, 2, PKN + 1), (1, 0, 2))
    ng = pairs[:, None, :, 0]
    small = pairs[:, :, 1:].reshape(2, 64, 24 * PKN)
    taps = jnp.transpose(small[:, :, :208].reshape(2, 64, 4, 52), (0, 2, 1, 3)).reshape(2, 4, 3328)
    conv = jnp.concatenate([taps, small[:, :, 208:260].reshape(2, 1, 3328)], axis=1)
    gate = small[:, :, 260:308].reshape(2, 1, 3072)
    conv = jnp.concatenate(
        [lax.dynamic_slice_in_dim(conv, q * HC, HC, 2), conv[:, :, 3072:]], axis=2
    )
    gate = lax.dynamic_slice_in_dim(gate, q * HC, HC, 2)

    def heads(v):
        return lax.dynamic_slice_in_dim(v, q * NH, NH, 1)

    skip = jnp.repeat(heads(skip_d), 64, axis=1)[:, None]
    pad = lambda v: jnp.pad(v, ((0, 0), (0, 0), (0, 640 - v.shape[2])))
    rows = [
        conv,
        pad(gate),
        pad(skip),
        pad(heads(dt_bias)[:, None]),
        pad(heads(jnp.exp(a_log))[:, None]),
        jnp.zeros((2, 7, 640), F32),
    ]
    return jnp.concatenate(rows, axis=1), ng


def unpack_grads(rec, vec, heads, w_in, norm_gain, place_dp):
    rec = rec.astype(F32)
    flat = lambda v: jnp.transpose(v, (1, 0, 2)).reshape(24, -1)
    w_in_grad = jnp.concatenate(
        [
            flat(rec[:, :, 0:HC]),
            flat(rec[:, :, HC : 2 * HC]),
            jnp.sum(rec[:, :, 2 * HC : RT], axis=0),
            flat(rec[:, :, RT : RT + NH]),
        ],
        axis=1,
    )
    w_out_grad = jnp.transpose(flat(rec[:, :, CIN:D]))
    conv = lax.dynamic_slice_in_dim(vec[0:5], 52 * place_dp, 52, 1)
    gate = lax.dynamic_slice_in_dim(vec[5], 48 * place_dp, 48, 0)
    norm_grad = jnp.sum(w_in.astype(F32) * w_in_grad, axis=1) / norm_gain.astype(F32)
    return (
        norm_grad,
        w_in_grad,
        conv[0:4],
        conv[4],
        heads[:, 0:NH].reshape(48),
        heads[:, 128 : 128 + NH].reshape(48),
        jnp.sum(heads[:, 256:640].reshape(48, 64), axis=1),
        gate,
        w_out_grad,
    )


GROUP = ("s", "h", "c")


def body(
    tokens,
    cotangent,
    starts,
    norm_gain,
    w_in,
    conv_weight,
    conv_bias,
    dt_bias,
    a_log,
    skip_d,
    gate_gain,
    w_out,
):
    s, z, h, x, c = place()
    q = (s * 2 + h) * 2 + c
    mine = pack_shards(
        starts[:, 0], norm_gain[0], w_in[0], conv_weight[0], conv_bias[0], gate_gain[0], w_out[0]
    )
    rec = lax.all_to_all(mine, GROUP, 0, 0, tiled=True)
    blocks = rec.reshape(2, 2, 48, D)
    st = (
        rec[0:4, :, RT + PK0 : RT + PK0 + PKN]
        .reshape(4, 24 * PKN)[:, 308:316]
        .reshape(8, 4)
        .astype(jnp.int32)
    )
    gap = lambda v, n: jnp.pad(v, ((0, 0), (0, 0), (n, D - n - v.shape[2])))
    blk0 = blocks[0] + gap(blocks[1, :, :, RT + NH : RT + PK0 + PKN], RT + PK0 + PKN)
    heads = jnp.stack([dt_bias[0], a_log[0], skip_d[0]])
    other = lax.ppermute(heads, "s", [(0, 1), (1, 0)])
    heads = jnp.where(s == 0, jnp.stack([heads, other]), jnp.stack([other, heads]))

    w0g, tall, call = first_gathers(blk0, tokens, cotangent)
    cv, ng = constants(w0g.reshape(D, D), q, heads[:, 0], heads[:, 1], heads[:, 2])
    w1, xall, stat0, stat1, part1, proj0, proj1, y0, y1, u0, u1, do1 = two_forward(
        st, tall, w0g, ng, cv, call, blocks[1]
    )
    eall, dproj0, o0, part0, sm1, sm0, gs1 = two_backward(
        st, w1, w0g, ng, cv, call, xall, tall, proj1, proj0, y1, y0, do1, u1, stat1, stat0
    )
    ig0, so1, gs0, vec, hd = last_sums(
        part0,
        tall,
        eall,
        ng[0],
        part1,
        xall,
        stat1[0:8],
        (u0, dproj0, o0),
        jnp.stack([sm0, sm1]),
    )
    back = lax.all_to_all(jnp.stack([gs0, gs1]).reshape(8, 24, D), GROUP, 0, 0, tiled=True)
    place_dp = ((z * 2 + h) * 4 + x) * 2 + c
    outs = unpack_grads(back, vec, hd, w_in[0], norm_gain[0], place_dp)

    got = lax.ppermute(jnp.where(s == 0, so1, ig0), "s", [(0, 1), (1, 0)])
    ig = jnp.where(s == 0, jnp.stack([ig0, got]), eall[h, c])
    so = jnp.where(s == 0, xall[h, c], jnp.stack([got, so1]))
    return (so[None], ig.astype(F32)[None]) + tuple(o[None] for o in outs)


def solution(mesh):
    inner = Mesh(mesh.devices.reshape(2, 4, 2, 4, 2), ("s", "z", "h", "x", "c"))
    dp = ("z", "h", "x", "c")
    in_specs = (
        P(None, dp, None),
        P(None, dp, None),
        P(None, dp, None),
        P("s", dp),
        P("s", dp, None),
        P("s", None, dp),
        P("s", dp),
        P("s", None),
        P("s", None),
        P("s", None),
        P("s", dp),
        P("s", None, dp),
    )
    out_specs = (
        P("s", None, dp, None),
        P("s", None, dp, None),
        P("s", dp),
        P("s", dp, None),
        P("s", None, dp),
        P("s", dp),
        P("s", None),
        P("s", None),
        P("s", None),
        P("s", dp),
        P("s", None, dp),
    )
    return jax.shard_map(body, mesh=inner, in_specs=in_specs, out_specs=out_specs, check_vma=False)
```

```python
import jax
import jax.numpy as jnp
from jax import lax
from jax.experimental import pallas as pl
from jax.experimental.pallas import tpu as pltpu
from jax.sharding import Mesh, PartitionSpec as P

EPS = 1e-05
BF = jnp.bfloat16
F32 = jnp.float32
HIGH = lax.Precision.HIGHEST
D = 1536
CIN = 1152
HC = 384
NH = 6
RT = 1024
HALF = 768
ANY = pl.BlockSpec(memory_space=pl.ANY)
VM = pl.BlockSpec(memory_space=pltpu.VMEM)
SM = pl.BlockSpec(memory_space=pltpu.SMEM)
VLIM = 59 * 1024 * 1024


class Net:
    def __init__(self, ssem, rsem):
        self.ssem, self.rsem, self.n, self.all = ssem, rsem, 0, []

    def make(self, src, dst, dev):
        i = self.n
        self.n += 1
        assert i < self.ssem.shape[0]
        copy = pltpu.make_async_remote_copy(
            src_ref=src,
            dst_ref=dst,
            send_sem=self.ssem.at[i],
            recv_sem=self.rsem.at[i],
            device_id=dev,
            device_id_type=pl.DeviceIdType.MESH,
        )
        self.all.append(copy)
        return copy

    def send(self, src, dst, dev):
        copy = self.make(src, dst, dev)
        copy.start()
        return copy

    def sent(self, copy):
        copy.wait_send()
        self.all = [v for v in self.all if v is not copy]

    def finish(self):
        for copy in self.all:
            copy.wait_send()


def place():
    s, z, h, x, c = (lax.axis_index(a) for a in ("s", "z", "h", "x", "c"))
    return s, z, h, x, c


def ring(i):
    return lax.rem(i + 1, 4), lax.rem(i + 3, 4), lax.rem(i + 2, 4)


def greet(devs):
    barrier = pltpu.get_barrier_semaphore()
    for dev in devs:
        pl.semaphore_signal(barrier, inc=1, device_id=dev, device_id_type=pl.DeviceIdType.MESH)
    pl.semaphore_wait(barrier, len(devs))


def zx_devs():
    s, z, h, x, c = place()
    zr, zl, _ = ring(z)
    xr, xl, _ = ring(x)
    return [{"z": zr}, {"z": zl}, {"x": xr}, {"x": xl}]


def ydev(y):
    return {"h": y // 2, "s": lax.rem(y, 2)}


def y_devs():
    s, z, h, x, c = place()
    yr, yl, _ = ring(2 * h + s)
    return [ydev(yr), ydev(yl), {"c": 1 - c}]


def group_devs():
    s, z, h, x, c = place()
    out = []
    for k in range(1, 8):
        out.append(
            {
                "s": 1 - s if k & 4 else s,
                "h": 1 - h if k & 2 else h,
                "c": 1 - c if k & 1 else c,
            }
        )
    return out


LAT = 1.7


def inter(gens):
    gens = [[0.0, g] for g in gens]
    while gens:
        item = min(gens, key=lambda v: v[0])
        if item[0] > 0:
            yield item[0]
        try:
            item[0] = next(item[1])
        except StopIteration:
            gens.remove(item)


def run(gens):
    for _ in inter(gens):
        pass


def g_pairs(net, own, out, lsem, t0):
    s, z, h, x, c = place()
    outer, inner, sib = {"h": 1 - h, "s": 1 - s}, {"s": 1 - s}, {"c": 1 - c}
    first = []
    for k in range(2):
        rows = pl.ds(64 * k, 64)
        first.append(net.send(own.at[s, rows], out.at[h, s, c, rows], outer))
    local = pltpu.make_async_copy(own, out.at[h, :, c], lsem)
    local.start()
    c0 = net.send(own, out.at[h, :, c], sib)
    yield t0 + 4.6 + LAT
    second = []
    for k in range(2):
        first[k].wait_recv()
        r = out.at[1 - h, 1 - s, c, pl.ds(64 * k, 64)]
        second.append(net.send(r, r, inner))
        if k == 0:
            yield t0 + 9.2 + LAT
    r = out.at[1 - h, 1 - s, c]
    c1 = net.send(r, r, sib)
    yield t0 + 14 + LAT
    for copy in second:
        copy.wait_recv()
    r = out.at[1 - h, s, c]
    c2 = net.send(r, r, sib)
    yield t0 + 16 + LAT
    for copy in (c0, c1, c2):
        copy.wait_recv()
    local.wait()


def g_small(net, mine, bz, bx, total, t0=0.0):
    s, z, h, x, c = place()
    sends = [net.send(mine, bz.at[z], {"z": lax.rem(z + k, 4)}) for k in range(1, 4)]
    bz[z] = mine[...]
    yield t0 + 4.0
    for copy in sends:
        copy.wait_recv()
    bx[x] = bz[0] + bz[1] + bz[2] + bz[3]
    r = bx.at[x]
    sends = [net.send(r, r, {"x": lax.rem(x + k, 4)}) for k in range(1, 4)]
    yield t0 + 10.0
    for copy in sends:
        copy.wait_recv()
    total[...] = bx[0] + bx[1] + bx[2] + bx[3]


def small_scratch():
    return [pltpu.VMEM((4, 2, 8, 640), F32), pltpu.VMEM((4, 2, 8, 640), F32)]


def small_devs():
    s, z, h, x, c = place()
    return [{"z": lax.rem(z + k, 4)} for k in range(1, 4)] + [
        {"x": lax.rem(x + k, 4)} for k in range(1, 4)
    ]


def g_share(net, sums, got, vec, heads):
    s, z, h, x, c = place()
    me = (2 * s + h) * 2 + c
    sends = []
    for dev in group_devs():
        sends.append(net.send(sums.at[dev["s"]], got.at[me], dev))
    got[me] = sums[s]
    yield 20.0
    for copy in sends:
        copy.wait_recv()
    vec[...] = jnp.zeros_like(vec)
    tail = jnp.zeros((5, 256), F32)
    for q in range(8):
        lanes = slice(q * HC, q * HC + HC)
        vec[0:5, lanes] = got[q, 0:5, 0:HC]
        vec[5:6, lanes] = got[q, 5:6, 0:HC]
        tail = tail + got[q, 0:5, HC:640]
        heads[q : q + 1, 0:256] = got[q, 5:6, HC:640]
        heads[q : q + 1, 256:640] = got[q, 6:7, 0:HC]
    vec[0:5, 3072:3328] = tail


def params(cid):
    return pltpu.CompilerParams(
        collective_id=cid, has_side_effects=True, vmem_limit_bytes=VLIM
    )


def sems(n):
    return [pltpu.SemaphoreType.DMA((n,)), pltpu.SemaphoreType.DMA((n,))]


GATHERED = jax.ShapeDtypeStruct((4, 2, 4, 48, D), BF)
CHUNKS = jax.ShapeDtypeStruct((2, 2, 2, 128, D), BF)
SMALL = jax.ShapeDtypeStruct((8, 640), F32)
CHUNK = jax.ShapeDtypeStruct((128, D), BF)


def row_to_col(row):
    i = lax.broadcasted_iota(jnp.int32, (128, 128), 0)
    j = lax.broadcasted_iota(jnp.int32, (128, 128), 1)
    return jnp.sum(jnp.where(i == j, row, 0.0), axis=1, keepdims=True)


def col_to_row(col):
    i = lax.broadcasted_iota(jnp.int32, (128, 128), 0)
    j = lax.broadcasted_iota(jnp.int32, (128, 128), 1)
    return jnp.sum(jnp.where(i == j, col, 0.0), axis=0, keepdims=True)


def own_scale(total):
    s, z, h, x, c = place()
    row = total[pl.ds((2 * h + s) * 2 + c, 1), :]
    return lax.rsqrt(row_to_col(row) * (1.0 / 3072) + EPS)


def norm_back(v, x, e, ng):
    xf = x.astype(F32)
    vg = v * ng[...]
    r = lax.rsqrt(jnp.mean(xf * xf, axis=-1, keepdims=True) + EPS)
    dot = jnp.mean(xf * vg, axis=-1, keepdims=True)
    return e.astype(F32) + r * vg - xf * (r * r * r * dot)


def nt(a, b):
    return lax.dot_general(a, b, (((1,), (1,)), ((), ())), preferred_element_type=F32)


def tn(a, b):
    return lax.dot_general(a, b, (((0,), (0,)), ((), ())), preferred_element_type=F32)


def iotas():
    i = lax.broadcasted_iota(jnp.int32, (128, 128), 0)
    j = lax.broadcasted_iota(jnp.int32, (128, 128), 1)
    return i, j


def seg_of(firsts, places):
    seg = jnp.full(places.shape, -1, jnp.int32)
    for k in range(4):
        seg = seg + (firsts[k] <= places).astype(jnp.int32)
    return seg


def masks(st, chunk):
    i, j = iotas()
    firsts = [st[chunk, k] for k in range(4)]
    seg = seg_of(firsts, i)
    keep = jnp.logical_and(seg == seg_of(firsts, j), i >= j)
    valid = [None] + [(seg_of(firsts, i - k) == seg).astype(F32) for k in range(1, 4)]
    return keep, valid


def conv_tile(xt, cv, t, valid):
    lanes = slice(128 * t, 128 * t + 128)
    pre = cv[4:5, lanes] + cv[3:4, lanes] * xt
    moved = [xt]
    for k in range(1, 4):
        m = pltpu.roll(xt, k, axis=0) * valid[k]
        moved.append(m)
        pre = pre + cv[3 - k : 4 - k, lanes] * m
    return pre, moved


def rates(rt, cv):
    i, j = iotas()
    head = j < NH
    v = rt + cv[7:8, 0:128]
    dt = jnp.where(head, jnp.maximum(v, 0.0) + jnp.log1p(jnp.exp(-jnp.abs(v))), 0.0)
    lower = (i >= j).astype(F32)
    cum = jnp.dot(
        lower, -dt * cv[8:9, 0:128], precision=HIGH, preferred_element_type=F32
    )
    return v, dt, cum


def half_masks():
    _, j = iotas()
    return j < 64


def split_pair(v, low):
    zero = jnp.zeros_like(v)
    return jnp.concatenate([jnp.where(low, v, zero), jnp.where(low, zero, v)], axis=0)


def decay_of(keep, cum, cum_t, h):
    spread = jnp.where(keep, cum[:, h : h + 1] - cum_t[h : h + 1, :], -1e30)
    return jnp.exp(spread)


class Gather:
    def __init__(self, net, blk, out, lsem):
        s, z, h, x, c = place()
        self.local = pltpu.make_async_copy(blk, out.at[z, :, x], lsem)
        every = slice(None)
        self.parts = []
        for lanes, i, axis_i, j, axis_j, pick in (
            (pl.ds(0, HALF), x, "x", z, "z", lambda i, j, p: (j, p, i)),
            (pl.ds(HALF, HALF), z, "z", x, "x", lambda i, j, p: (i, p, j)),
        ):
            ir, il, _ = ring(i)
            jr, jl, _ = ring(j)

            def at(i, j, p, pick=pick, lanes=lanes):
                return out.at[pick(i, j, p) + (every, lanes)]

            def make(i, j, p, dev, src=None):
                ref = at(i, j, p)
                return net.make(ref if src is None else src, ref, dev)

            own = blk.at[:, :, lanes]
            first, second = ({axis_i: ir}, {axis_i: il}), ({axis_j: jr}, {axis_j: jl})
            self.parts.append(
                [
                    (make(i, j, every, first[0], own), make(i, j, every, first[1], own)),
                    (make(il, j, 0, first[0]), make(ir, j, 1, first[1])),
                    (make(every, j, every, second[0]), make(every, j, every, second[1])),
                    (make(every, jl, 0, second[0]), make(every, jr, 1, second[1])),
                ]
            )

    def step(self, k):
        if k == 0:
            self.local.start()
        if k == 2:
            self.local.wait()
        for part in self.parts:
            for n in range(2):
                if k > 0:
                    part[k - 1][n].wait_recv()
                if k < 4 and k != 2:
                    part[k][n].start()
            if k == 2:
                part[2][0].start()
                part[2][1].start()


class RingSum:
    def __init__(self, net, part, bufs):
        self.part = part
        self.cb, self.sb, self.b1, self.b2 = bufs
        s, z, h, x, c = place()
        self.c = c
        sib = {"c": 1 - c}
        outer, inner = {"h": 1 - h, "s": 1 - s}, {"s": 1 - s}
        self.units = [(1 - h, s), (1 - h, 1 - s), (h, 1 - s), (h, s)]
        self.core = [
            net.make(part.at[hh, mm, 1 - c], self.cb.at[k], sib)
            for k, (hh, mm) in enumerate(self.units)
        ]
        sb, b1, b2 = self.sb, self.b1, self.b2
        lo, hi = pl.ds(0, 64), pl.ds(64, 64)
        self.far = [
            net.make(sb.at[0, lo], b1.at[0], outer),
            net.make(sb.at[0, hi], b1.at[1], inner),
        ]
        self.direct = [
            net.make(sb.at[1, lo], b2.at[0, lo], outer),
            net.make(sb.at[2, hi], b2.at[1, hi], inner),
        ]
        self.summed = [
            net.make(sb.at[1, hi], b2.at[0, hi], outer),
            net.make(sb.at[2, lo], b2.at[1, lo], inner),
        ]

    def add(self, k):
        self.core[k].wait_recv()
        hh, mm = self.units[k]
        self.sb[k] = (self.part[hh, mm, self.c].astype(F32) + self.cb[k].astype(F32)).astype(BF)

    def step(self, k):
        self.core[k].start()
        if k > 0:
            self.add(k - 1)
        if k == 1:
            self.far[0].start()
            self.far[1].start()
        if k > 1:
            self.direct[k - 2].start()

    def late(self):
        lo, hi = slice(0, 64), slice(64, 128)
        self.far[1].wait_recv()
        self.sb[1, hi] = (self.sb[1, hi].astype(F32) + self.b1[1].astype(F32)).astype(BF)
        self.summed[0].start()
        self.far[0].wait_recv()
        self.sb[2, lo] = (self.sb[2, lo].astype(F32) + self.b1[0].astype(F32)).astype(BF)
        self.summed[1].start()

    def total(self):
        self.core[3].wait_recv()
        for copy in self.direct + self.summed:
            copy.wait_recv()
        hh, mm = self.units[3]
        total = self.part[hh, mm, self.c].astype(F32) + self.cb[3].astype(F32)
        return total + self.b2[0].astype(F32) + self.b2[1].astype(F32)


def ring_scratch():
    return [
        pltpu.VMEM((4, 128, D), BF),
        pltpu.VMEM((3, 128, D), BF),
        pltpu.VMEM((2, 64, D), BF),
        pltpu.VMEM((2, 128, D), BF),
    ]


class Spread:
    def __init__(self, net, out):
        s, z, h, x, c = place()
        sib = {"c": 1 - c}
        outer, inner = {"h": 1 - h, "s": 1 - s}, {"s": 1 - s}
        lo, hi = pl.ds(0, 64), pl.ds(64, 64)
        own, far = out.at[h, s, c], out.at[1 - h, s, c]
        from_outer, from_inner = out.at[1 - h, 1 - s, c], out.at[h, 1 - s, c]
        self.mine = own
        self.ring = [net.make(own, own, outer), net.make(own, own, inner)]
        self.hand = [
            net.make(from_inner.at[lo], from_inner.at[lo], outer),
            net.make(from_outer.at[hi], from_outer.at[hi], inner),
        ]
        self.sib = [net.make(r, r, sib) for r in (own, from_inner, from_outer, far)]

    def start(self):
        self.ring[0].start()
        self.ring[1].start()
        self.sib[0].start()

    def ready(self, k):
        if k == 1:
            self.ring[1].wait_recv()
            self.hand[0].start()
            self.sib[1].start()
            self.ring[0].wait_recv()
            self.hand[1].start()
            self.sib[2].start()
        if k == 3:
            self.hand[0].wait_recv()
            self.hand[1].wait_recv()
            self.sib[3].start()
        self.sib[k].wait_recv()


def when_each(i, n, step):
    for k in range(n):
        pl.when(i == k)(lambda k=k: step(k))


def block_at(i, h, s, far_first):
    k = i if far_first else 3 - i
    return lax.rem(h + 1 + k // 2, 2), lax.rem(s + (k + 1) // 2, 2)


def forward_block(b, chunk_rows, x, w, ng, cv, st, refs, e=None):
    part, stat, proj, yout, uout, doo, og = refs
    with_do = e is not None
    xf = x[...].reshape(256, D).astype(F32)
    r = lax.rsqrt(jnp.mean(xf * xf, axis=-1, keepdims=True) + EPS)
    u = (xf * r * ng).astype(BF)
    uout[...] = u
    proj[...] = jnp.dot(u, w[:, :, :, :, 0:CIN].reshape(D, CIN), preferred_element_type=F32)
    if with_do:
        doo[...] = jnp.dot(
            e[...].reshape(256, D),
            w[:, :, :, :, CIN:D].reshape(D, HC),
            preferred_element_type=F32,
        )
    low = half_masks()
    for m in range(2):
        rows = slice(128 * m, 128 * m + 128)
        chunk = b * 2 + m
        keep, valid = masks(st, chunk)
        act = []
        for t in range(5):
            pre, _ = conv_tile(proj[rows, HC + 128 * t : HC + 128 * t + 128], cv, t, valid)
            act.append((pre * jax.nn.sigmoid(pre)).astype(BF))
        _, dt, cum = rates(proj[rows, RT:CIN], cv)
        cum_t, dt_t = jnp.transpose(cum), jnp.transpose(dt)
        gram = nt(act[4], act[3])
        gsum = jnp.zeros((128, 1), F32)
        tsum = jnp.zeros((128, 1), F32)
        for t in range(3):
            lanes = slice(128 * t, 128 * t + 128)
            mixes = []
            for h in (2 * t, 2 * t + 1):
                dec = decay_of(keep, cum, cum_t, h)
                mixes.append((gram * dec * dt_t[h : h + 1, :]).astype(BF))
            y = jnp.dot(
                jnp.concatenate(mixes, axis=1),
                split_pair(act[t], low),
                preferred_element_type=F32,
            )
            y = y + cv[6:7, lanes] * act[t].astype(F32)
            yout[rows, lanes] = y
            zt = proj[rows, lanes]
            g = y * (zt * jax.nn.sigmoid(zt))
            gsum = gsum + jnp.sum(g * g, axis=1, keepdims=True)
            gain = cv[5:6, lanes]
            og[rows, lanes] = (g * gain).astype(BF)
            if with_do:
                tsum = tsum + jnp.sum(g * gain * doo[rows, lanes], axis=1, keepdims=True)
        stat[pl.ds(chunk, 1), :] = col_to_row(gsum)
        if with_do:
            stat[pl.ds(chunk + 8, 1), :] = col_to_row(tsum)
    out = nt(og[...], w[:, :, :, :, CIN:D].reshape(D, HC))
    part[...] = out.astype(BF).reshape(2, 128, D)


def two_forward(st, x0, w0, ng, cv, call, blk):
    def kernel(
        st, x0h, w0h, ng, cv, callh, blk,
        w1o, x1o, s0o, s1o, p1o, proj0o, proj1o, y0o, y1o, u0o, u1o, doo,
        w0, w1, x0, x1, e1, part, part1, proj, yv, uv, dov, og, stat0, stat1, stb0, stb1,
        cb, sb, b1, b2, isem, osem, lsem, ssem, rsem,
    ):
        s, z, h, x, c = place()
        loads = [pltpu.make_async_copy(w0h, w0, isem.at[0]), pltpu.make_async_copy(callh, e1, isem.at[1])]
        loads[0].start()
        xl = [pltpu.make_async_copy(x0h.at[k // 2, k % 2], x0.at[k // 2, k % 2], isem.at[2 + k]) for k in range(4)]
        for copy in xl:
            copy.start()
        greet(zx_devs() + group_devs())
        net = Net(ssem, rsem)
        gather = Gather(net, blk, w1, lsem.at[0])
        ring = RingSum(net, part, (cb, sb, b1, b2))
        spread = Spread(net, x1)
        devs = group_devs()
        stats0 = [net.make(stat0, stb0.at[k], dev) for k, dev in enumerate(devs)]
        stats1 = [net.make(stat1, stb1.at[k], dev) for k, dev in enumerate(devs)]
        gather.step(0)
        loads[0].wait()
        loads[1].start()
        for copy in xl:
            copy.wait()

        def saves(b, layer, proj_o, y_o, u_o):
            return [
                pltpu.make_async_copy(v.at[b], o.at[b], osem.at[layer, n, b])
                for n, (v, o) in enumerate(((proj, proj_o), (yv, y_o), (uv, u_o)))
            ]

        def first(i, carry):
            hi, ci = block_at(i, h, s, True)
            b = 2 * hi + ci
            forward_block(
                b, None, x0.at[hi, ci], w0, ng[0], cv.at[0], st,
                (part.at[hi, ci], stat0, proj.at[b], yv.at[b], uv.at[b], None, og),
            )
            for copy in saves(b, 0, proj0o, y0o, u0o):
                copy.start()

            when_each(i, 4, ring.step)

            @pl.when(i == 1)
            def _():
                gather.step(1)

            @pl.when(i == 2)
            def _():
                gather.step(2)

            return carry

        lax.fori_loop(0, 4, first, 0)
        for copy in stats0:
            copy.start()
        ring.late()
        acc = stat0[...]
        for k, copy in enumerate(stats0):
            copy.wait_recv()
            acc = acc + stb0[k]
        s0o[...] = acc
        for b in range(4):
            for copy in saves(b, 0, proj0o, y0o, u0o):
                copy.wait()
        loads[1].wait()
        gather.step(3)
        total = ring.total()
        x1[h, s, c] = (x0[h, s, c].astype(F32) + own_scale(s0o) * total).astype(BF)
        spread.start()
        gather.step(4)
        keep_w = pltpu.make_async_copy(w1, w1o, isem.at[0])
        keep_w.start()

        def second(i, carry):
            when_each(i, 4, spread.ready)
            hi, ci = block_at(i, h, s, False)
            b = 2 * hi + ci
            forward_block(
                b, None, x1.at[hi, ci], w1, ng[1], cv.at[1], st,
                (part1.at[hi, ci], stat1, proj.at[b], yv.at[b], uv.at[b], dov.at[b], og),
                e1.at[hi, ci],
            )
            for copy in saves(b, 1, proj1o, y1o, u1o):
                copy.start()
            for n, (v, o) in enumerate(((dov.at[b], doo.at[b]), (x1.at[hi, ci], x1o.at[hi, ci]), (part1.at[hi, ci], p1o.at[hi, ci]))):
                pltpu.make_async_copy(v, o, osem.at[2, n, b]).start()
            return carry

        lax.fori_loop(0, 4, second, 0)
        for copy in stats1:
            copy.start()
        acc = stat1[...]
        for k, copy in enumerate(stats1):
            copy.wait_recv()
            acc = acc + stb1[k]
        s1o[...] = acc
        keep_w.wait()
        for b in range(4):
            for copy in saves(b, 1, proj1o, y1o, u1o):
                copy.wait()
            p = (b // 2, b % 2)
            for n, (v, o) in enumerate(((dov.at[b], doo.at[b]), (x1.at[p], x1o.at[p]), (part1.at[p], p1o.at[p]))):
                pltpu.make_async_copy(v, o, osem.at[2, n, b]).wait()
        net.finish()

    blocks = lambda cols, t: jax.ShapeDtypeStruct((4, 256, cols), t)
    return pl.pallas_call(
        kernel,
        name="two_forward",
        out_shape=(
            GATHERED,
            CHUNKS,
            jax.ShapeDtypeStruct((8, 128), F32),
            jax.ShapeDtypeStruct((16, 128), F32),
            CHUNKS,
            blocks(CIN, F32),
            blocks(CIN, F32),
            blocks(HC, F32),
            blocks(HC, F32),
            blocks(D, BF),
            blocks(D, BF),
            blocks(HC, F32),
        ),
        in_specs=[SM, ANY, ANY, VM, VM, ANY, VM],
        out_specs=(ANY, ANY, VM, VM) + (ANY,) * 8,
        scratch_shapes=[
            pltpu.VMEM((4, 2, 4, 48, D), BF),
            pltpu.VMEM((4, 2, 4, 48, D), BF),
            pltpu.VMEM((2, 2, 2, 128, D), BF),
            pltpu.VMEM((2, 2, 2, 128, D), BF),
            pltpu.VMEM((2, 2, 2, 128, D), BF),
            pltpu.VMEM((2, 2, 2, 128, D), BF),
            pltpu.VMEM((2, 2, 2, 128, D), BF),
            pltpu.VMEM((4, 256, CIN), F32),
            pltpu.VMEM((4, 256, HC), F32),
            pltpu.VMEM((4, 256, D), BF),
            pltpu.VMEM((4, 256, HC), F32),
            pltpu.VMEM((256, HC), BF),
            pltpu.VMEM((8, 128), F32),
            pltpu.VMEM((16, 128), F32),
            pltpu.VMEM((7, 8, 128), F32),
            pltpu.VMEM((7, 16, 128), F32),
        ]
        + ring_scratch()
        + [
            pltpu.SemaphoreType.DMA((6,)),
            pltpu.SemaphoreType.DMA((3, 3, 4)),
            pltpu.SemaphoreType.DMA((1,)),
        ]
        + sems(56),
        compiler_params=params(1),
    )(st, x0, w0, ng, cv, call, blk)


class Scatter:
    def __init__(self, net, grads, bufs, out):
        s, z, h, x, c = place()
        self.out = out
        self.parts = []
        for k, (i, axis_i, j, axis_j) in enumerate(((z, "z", x, "x"), (x, "x", z, "z"))):
            lanes = pl.ds(k * HALF, HALF)
            b1, b2, t, sums, b3, b4, t2 = [b.at[k] for b in bufs]
            ir, il, io = ring(i)
            jr, jl, jo = ring(j)
            if k == 0:
                unit = lambda i, p, lanes=lanes: grads.at[i, p, :, :, lanes]
            else:
                unit = lambda i, p, lanes=lanes: grads.at[:, p, i, :, lanes]
            right, left = {axis_i: ir}, {axis_i: il}
            part = dict(unit=unit, bufs=(b1, b2, t, sums, b3, b4, t2), i=i, j=j)
            part.update(ir=ir, il=il, jr=jr, jl=jl, jo=jo, k=k)
            part["far"] = [
                net.make(unit(io, 0), b1.at[0], right),
                net.make(unit(io, 1), b1.at[1], left),
            ]
            part["near"] = [
                net.make(unit(ir, 1), b2.at[0, 1], right),
                net.make(unit(il, 0), b2.at[1, 0], left),
                net.make(t.at[0], b2.at[0, 0], right),
                net.make(t.at[1], b2.at[1, 1], left),
            ]
            right, left = {axis_j: jr}, {axis_j: jl}
            part["far2"] = [
                net.make(sums.at[0, jo], b3.at[0], right),
                net.make(sums.at[1, jo], b3.at[1], left),
            ]
            part["near2"] = [
                net.make(sums.at[1, jr], b4.at[0, 1], right),
                net.make(sums.at[0, jl], b4.at[1, 0], left),
                net.make(t2.at[0], b4.at[0, 0], right),
                net.make(t2.at[1], b4.at[1, 1], left),
            ]
            self.parts.append(part)

    def start(self, k):
        for copy in self.parts[k]["far"]:
            copy.start()

    def direct(self, k):
        self.parts[k]["near"][0].start()
        self.parts[k]["near"][1].start()

    def summed(self, k):
        v = self.parts[k]
        b1, b2, t, sums, b3, b4, t2 = v["bufs"]
        for p, near in ((0, v["ir"]), (1, v["il"])):
            v["far"][p].wait_recv()
            for n in range(4):
                t[p, n] = (v["unit"](near, p)[n].astype(F32) + b1[p, n].astype(F32)).astype(BF)
            v["near"][2 + p].start()

    def total(self, v, p, n):
        b2 = v["bufs"][1]
        return (
            v["unit"](v["i"], p)[n].astype(F32)
            + b2[0, p, n].astype(F32)
            + b2[1, p, n].astype(F32)
        )

    def second(self, k):
        v = self.parts[k]
        sums = v["bufs"][3]
        for copy in v["near"]:
            copy.wait_recv()
        for copy, p, n in (
            (v["far2"][0], 0, v["jo"]),
            (v["far2"][1], 1, v["jo"]),
            (v["near2"][0], 1, v["jr"]),
            (v["near2"][1], 0, v["jl"]),
        ):
            sums[p, n] = self.total(v, p, n).astype(BF)
            copy.start()
        for p, n in ((0, v["jr"]), (1, v["jl"]), (0, v["j"]), (1, v["j"])):
            sums[p, n] = self.total(v, p, n).astype(BF)

    def second_summed(self, k):
        v = self.parts[k]
        b1, b2, t, sums, b3, b4, t2 = v["bufs"]
        for p, near in ((0, v["jr"]), (1, v["jl"])):
            v["far2"][p].wait_recv()
            t2[p] = (sums[p, near].astype(F32) + b3[p].astype(F32)).astype(BF)
            v["near2"][2 + p].start()

    def finish(self, k):
        v = self.parts[k]
        sums, b4 = v["bufs"][3], v["bufs"][5]
        for copy in v["near2"]:
            copy.wait_recv()
        for p in range(2):
            total = sums[p, v["j"]].astype(F32) + b4[0, p].astype(F32) + b4[1, p].astype(F32)
            self.out[p, :, k * HALF : (k + 1) * HALF] = total.astype(BF)


def scatter_scratch():
    return [
        pltpu.VMEM((2, 2, 4, 48, HALF), BF),
        pltpu.VMEM((2, 2, 2, 4, 48, HALF), BF),
        pltpu.VMEM((2, 2, 4, 48, HALF), BF),
        pltpu.VMEM((2, 2, 4, 48, HALF), BF),
        pltpu.VMEM((2, 2, 48, HALF), BF),
        pltpu.VMEM((2, 2, 2, 48, HALF), BF),
        pltpu.VMEM((2, 2, 48, HALF), BF),
    ]


def weight_tile(k, u, e, dproj, o, grads):
    cols = pl.ds(pl.multiple_of(k * 384, 128), 384)
    rows = 1024
    a = tn(u[:, :, cols].reshape(rows, 384), dproj[...].reshape(rows, CIN))
    grads[k, :, :, :, 0:CIN] = a.astype(BF).reshape(2, 4, 48, CIN)
    a = tn(e[:, :, :, :, cols].reshape(rows, 384), o[...].reshape(rows, HC))
    grads[k, :, :, :, CIN:D] = a.astype(BF).reshape(2, 4, 48, HC)


def backward_block(b, e, w, cv, st, stat, dots, refs):
    proj, yin, do, dproj, oo, part, sm = refs
    if dots is not None:
        do[...] = jnp.dot(
            e[...].reshape(256, D),
            w[:, :, :, :, CIN:D].reshape(D, HC),
            preferred_element_type=F32,
        )
    low = half_masks()
    i, j = iotas()
    upper = (j >= i).astype(F32)

    def add(row, lanes, v):
        sm[row : row + 1, lanes] += jnp.sum(v, axis=0, keepdims=True)

    for m in range(2):
        rows = slice(128 * m, 128 * m + 128)
        chunk = b * 2 + m
        keep, valid = masks(st, chunk)
        pres, moves, act = [], [], []
        for t in range(5):
            pre, moved = conv_tile(proj[rows, HC + 128 * t : HC + 128 * t + 128], cv, t, valid)
            pres.append(pre)
            moves.append(moved)
            act.append((pre * jax.nn.sigmoid(pre)).astype(BF))
        v, dt, cum = rates(proj[rows, RT:CIN], cv)
        cum_t, dt_t = jnp.transpose(cum), jnp.transpose(dt)
        gram = nt(act[4], act[3])
        r = lax.rsqrt(row_to_col(stat[pl.ds(chunk, 1), :]) * (1.0 / 3072) + EPS)
        if dots is not None:
            k = r * r * row_to_col(dots[chunk, 0:1, :]) * (1.0 / 3072)
        else:
            k = r * r * r * row_to_col(stat[pl.ds(chunk + 8, 1), :]) * (1.0 / 3072)
        dact = []
        dgram = jnp.zeros((128, 128), F32)
        dcum = jnp.zeros((128, 128), F32)
        col_rows = []
        for t in range(3):
            lanes = slice(128 * t, 128 * t + 128)
            zt, y, dot_ = proj[rows, lanes], yin[rows, lanes], do[rows, lanes]
            gain = cv[5:6, lanes]
            sig = jax.nn.sigmoid(zt)
            sz = zt * sig
            g = y * sz
            oo[rows, lanes] = (g * r * gain).astype(BF)
            add(5, lanes, dot_ * g * r)
            dg = r * (dot_ * gain) - g * k
            dproj[rows, lanes] = (dg * y * (sig + sz * (1.0 - sig))).astype(BF)
            dy = (dg * sz).astype(BF)
            dyf = dy.astype(F32)
            xs = act[t]
            add(6, lanes, dyf * xs.astype(F32))
            dy2 = split_pair(dy, low)
            dmix2 = nt(dy2, xs)
            mixes = []
            for q in range(2):
                h = 2 * t + q
                dec = decay_of(keep, cum, cum_t, h)
                dt_row = dt_t[h : h + 1, :]
                pm = gram * dec
                mixes.append((pm * dt_row).astype(BF))
                dmix = dmix2[128 * q : 128 * q + 128]
                dgram = dgram + dmix * (dec * dt_row)
                vm = dmix * pm
                col_rows.append(jnp.sum(vm, axis=0, keepdims=True))
                rsum = jnp.sum(vm * dt_row, axis=1, keepdims=True)
                dcum = dcum + jnp.where(j == h, rsum, 0.0)
            dxs = tn(jnp.concatenate(mixes, axis=0), dy2)
            dact.append(dxs + cv[6:7, lanes] * dyf)
        dgl = dgram.astype(BF)
        dact.append(tn(dgl, act[4]))
        dact.append(jnp.dot(dgl, act[3], preferred_element_type=F32))
        ddt = jnp.transpose(
            jnp.concatenate(col_rows + [jnp.zeros((128 - NH, 128), F32)], axis=0)
        )
        dcum = dcum - ddt * dt
        dla = jnp.dot(upper, dcum, precision=HIGH, preferred_element_type=F32)
        nexp = -cv[8:9, 0:128]
        drate = (ddt + dla * nexp) * jax.nn.sigmoid(v)
        drate = jnp.where(j < NH, drate, 0.0)
        add(5, slice(HC, HC + 128), drate)
        add(5, slice(HC + 128, 640), dla * dt * nexp)
        dproj[rows, RT:CIN] = drate.astype(BF)
        for t in range(5):
            lanes = slice(128 * t, 128 * t + 128)
            pre = pres[t]
            sp = jax.nn.sigmoid(pre)
            dpre = dact[t] * (sp + pre * sp * (1.0 - sp))
            add(4, lanes, dpre)
            add(3, lanes, dpre * moves[t][0])
            dx = cv[3:4, lanes] * dpre
            for n in range(1, 4):
                add(3 - n, lanes, dpre * moves[t][n])
                dx = dx + cv[3 - n : 4 - n, lanes] * pltpu.roll(
                    dpre * valid[n], 128 - n, axis=0
                )
            dproj[rows, HC + 128 * t : HC + 128 * t + 128] = dx.astype(BF)
    out = nt(dproj[...], w[:, :, :, :, 0:CIN].reshape(D, CIN))
    part[...] = out.astype(BF).reshape(2, 128, D)


def two_backward(
    st, w1, w0, ng, cv, call, xall, tall, proj1, proj0, y1, y0, do1, u1, u0, part1, stat1, stat0
):
    def kernel(
        st, w1h, w0h, ng, cv, callh, xallh, tallh, proj1h, proj0h, y1h, y0h, do1h, u1h, u0h, part1h, stat1, stat0,
        e0o, sm, rp, vec, heads, ig, so, got,
        w, e1, e0, proj, yv, do, dproj, oo, u, part, x1own, x0own, dtile, db, grads, gp, gs, swap, *rest,
    ):
        rbufs, ra, sa = rest[:4], rest[4:8], rest[8:15]
        sb = (rest[15], rest[16], sa[2], sa[3], rest[17], rest[18], sa[6])
        bz, bx, sums, ghead, isem, bsem, osem, ssem, rsem = rest[19:]
        s, z, h, x, c = place()

        def block_loads(i, far_first, proj_h, y_h, do_h, layer):
            hi, ci = block_at(i, h, s, far_first)
            b = 2 * hi + ci
            pairs = [(proj_h, proj), (y_h, yv)] + ([(do_h, do)] if do_h is not None else [])
            return [
                pltpu.make_async_copy(src.at[b], dst.at[lax.rem(i, 2)], bsem.at[layer, n, i])
                for n, (src, dst) in enumerate(pairs)
            ]

        loads1 = lambda i: block_loads(i, True, proj1h, y1h, do1h, 1)
        loads0 = lambda i: block_loads(i, False, proj0h, y0h, None, 0)
        for copy in loads1(0):
            copy.start()
        lw1 = pltpu.make_async_copy(w1h, w, isem.at[0])
        lw1.start()
        for copy in loads1(1):
            copy.start()
        later = [
            pltpu.make_async_copy(callh, e1, isem.at[1]),
            pltpu.make_async_copy(u1h, u, isem.at[2]),
            pltpu.make_async_copy(xallh.at[h, s, c], x1own, isem.at[3]),
            pltpu.make_async_copy(tallh.at[h, s, c], x0own, isem.at[4]),
        ]
        for copy in later:
            copy.start()
        greet(small_devs() + group_devs())
        net = Net(ssem, rsem)
        devs = group_devs()
        ring_sum = RingSum(net, part, rbufs)
        spread = Spread(net, e0)
        scatter1 = Scatter(net, grads, sa, gs.at[1])
        scatter0 = Scatter(net, w, sb, gs.at[0])
        ring0, ring1 = RingSum(net, part, rbufs), RingSum(net, e1, ra)
        me = (2 * h + s) * 2 + c
        q = 4 * s + 2 * h + c
        dsends = [net.make(dtile, db.at[me], dev) for dev in devs]
        gsends = [
            net.make(gp.at[dev["s"], 2 * dev["h"] + dev["c"]], rp.at[q], dev) for dev in devs
        ]
        swap_send = net.make(swap, got, {"s": 1 - s})
        sm[...] = jnp.zeros_like(sm)
        zr, zl, zo = ring(z)
        lw1.wait()

        def first(i, carry):
            hi, ci = block_at(i, h, s, True)
            b = 2 * hi + ci
            slot = lax.rem(i, 2)
            for copy in loads1(i):
                copy.wait()
            backward_block(
                b, None, w, cv.at[1], st, stat1, None,
                (proj.at[slot], yv.at[slot], do.at[slot], dproj.at[b], oo.at[b], part.at[hi, ci], sm.at[1]),
            )
            when_each(i, 4, ring_sum.step)

            @pl.when(i < 2)
            def _():
                for copy in loads1(i + 2):
                    copy.start()

            return carry

        lax.fori_loop(0, 4, first, 0)
        lw0 = pltpu.make_async_copy(w0h, w, isem.at[5])
        lw0.start()
        for i in range(2):
            for copy in loads0(i):
                copy.start()
        ring_sum.late()
        for copy in later:
            copy.wait()
        for n, k in enumerate((zo, zr, zl, z)):
            weight_tile(k, u, e1, dproj, oo, grads)
            if n == 0:
                scatter1.start(0)
            if n == 2:
                scatter1.direct(0)
        scatter1.start(1)
        scatter1.direct(1)
        total = ring_sum.total()
        e0f = norm_back(total, x1own[...], e1[h, s, c], ng.at[1])
        e0l = e0f.astype(BF)
        e0[h, s, c] = e0l
        spread.start()
        diff = x1own[...].astype(F32) - x0own[...].astype(F32)
        dots = jnp.sum(e0l.astype(F32) * diff, axis=1, keepdims=True)
        dtile[...] = jnp.broadcast_to(col_to_row(dots), (8, 128))
        db[me] = dtile[...]
        for copy in dsends:
            copy.start()
        for copy in ring_sum.core + ring_sum.far + ring_sum.direct + ring_sum.summed:
            net.sent(copy)
        lu0 = pltpu.make_async_copy(u0h, u, isem.at[2])
        lu0.start()
        lp1 = pltpu.make_async_copy(part1h, e1, isem.at[1])
        lp1.start()
        for copy in dsends:
            copy.wait_recv()
        lw0.wait()

        def save(i):
            hi, ci = block_at(i, h, s, False)
            return pltpu.make_async_copy(e0.at[hi, ci], e0o.at[hi, ci], osem.at[i])

        def second(i, carry):
            when_each(i, 4, spread.ready)
            hi, ci = block_at(i, h, s, False)
            b = 2 * hi + ci
            slot = lax.rem(i, 2)
            for copy in loads0(i):
                copy.wait()
            save(i).start()
            backward_block(
                b, e0.at[hi, ci], w, cv.at[0], st, stat0, db,
                (proj.at[slot], yv.at[slot], do.at[slot], dproj.at[b], oo.at[b], part.at[hi, ci], sm.at[0]),
            )
            when_each(i, 4, lambda k: ring0.core[3 - k].start())

            @pl.when(i < 2)
            def _():
                for copy in loads0(i + 2):
                    copy.start()

            @pl.when(i == 1)
            def _():
                scatter1.summed(0)
                scatter1.summed(1)

            return carry

        lax.fori_loop(0, 4, second, 0)

        def smalls():
            yield from g_small(net, sm, bz, bx, sums)
            yield from g_share(net, sums, ghead, vec, heads)

        def pieces(layer):
            for k in range(4):
                gp[layer, k, 0:24] = gs[layer, k // 2, 24 * (k % 2) : 24 * (k % 2) + 24]
                gp[layer, k, 24:32] = jnp.zeros((8, D), BF)

            @pl.when(s == layer)
            def _():
                rp[q] = gp[layer, 2 * h + c]
                for copy in gsends[0:3]:
                    copy.start()

            @pl.when(s != layer)
            def _():
                for copy in gsends[3:7]:
                    copy.start()

        sg = smalls()
        next(sg)
        lu0.wait()
        weight_tile(zo, u, e0, dproj, oo, w)
        scatter0.start(0)
        ring0.add(0)
        ring0.far[0].start()
        ring0.far[1].start()
        ring0.add(1)
        ring0.direct[0].start()
        ring0.add(2)
        ring0.direct[1].start()
        scatter1.second(0)
        scatter1.second(1)
        weight_tile(zr, u, e0, dproj, oo, w)
        weight_tile(zl, u, e0, dproj, oo, w)
        scatter0.direct(0)
        scatter1.second_summed(0)
        scatter1.second_summed(1)
        weight_tile(z, u, e0, dproj, oo, w)
        scatter0.start(1)
        scatter0.direct(1)
        next(sg)
        ring0.late()
        scatter1.finish(0)
        scatter1.finish(1)
        lp1.wait()
        for k in range(4):
            ring1.step(k)
        for half in scatter1.parts:
            for copy in half["near"][2:] + half["far2"] + half["near2"]:
                net.sent(copy)
        scatter0.summed(0)
        scatter0.summed(1)
        ring1.late()
        ig[...] = norm_back(ring0.total(), x0own[...], e0[h, s, c], ng.at[0]).astype(BF)
        next(sg)
        scatter0.second(0)
        scatter0.second(1)
        so[...] = (x1own[...].astype(F32) + own_scale(stat1) * ring1.total()).astype(BF)
        scatter0.second_summed(0)
        scatter0.second_summed(1)
        swap[...] = jnp.where(s == 0, so[...], ig[...])
        swap_send.start()
        pieces(1)
        for _ in sg:
            pass
        scatter0.finish(0)
        scatter0.finish(1)
        pieces(0)
        for i in range(4):
            save(i).wait()
        for copy in gsends:
            copy.wait_recv()
        swap_send.wait_recv()
        net.finish()

    big = pltpu.VMEM((4, 2, 4, 48, D), BF)
    rows = pltpu.VMEM((2, 2, 2, 128, D), BF)
    chunk = pltpu.VMEM((128, D), BF)
    return pl.pallas_call(
        kernel,
        name="two_backward",
        out_shape=(
            CHUNKS,
            jax.ShapeDtypeStruct((2, 8, 640), F32),
            jax.ShapeDtypeStruct((8, 32, D), BF),
            jax.ShapeDtypeStruct((8, 3328), F32),
            SMALL,
            CHUNK,
            CHUNK,
            CHUNK,
        ),
        in_specs=[SM, ANY, ANY, VM, VM] + [ANY] * 11 + [VM, VM],
        out_specs=(ANY,) + (VM,) * 7,
        scratch_shapes=[
            big,
            rows,
            rows,
            pltpu.VMEM((2, 256, CIN), F32),
            pltpu.VMEM((2, 256, HC), F32),
            pltpu.VMEM((2, 256, HC), F32),
            pltpu.VMEM((4, 256, CIN), BF),
            pltpu.VMEM((4, 256, HC), BF),
            pltpu.VMEM((4, 256, D), BF),
            rows,
            chunk,
            chunk,
            pltpu.VMEM((8, 128), F32),
            pltpu.VMEM((8, 8, 128), F32),
            big,
            pltpu.VMEM((2, 4, 32, D), BF),
            pltpu.VMEM((2, 2, 48, D), BF),
            chunk,
        ]
        + ring_scratch()
        + ring_scratch()
        + scatter_scratch()
        + [scatter_scratch()[k] for k in (0, 1, 4, 5)]
        + small_scratch()
        + [pltpu.VMEM((2, 8, 640), F32), pltpu.VMEM((8, 8, 640), F32)]
        + [
            pltpu.SemaphoreType.DMA((6,)),
            pltpu.SemaphoreType.DMA((2, 3, 4)),
            pltpu.SemaphoreType.DMA((4,)),
        ]
        + sems(120),
        compiler_params=params(3),
    )(
        st, w1, w0, ng, cv, call, xall, tall, proj1, proj0, y1, y0, do1, u1, u0, part1, stat1, stat0
    )


def shift_div(v, m):
    return (v * {52: 20165, 48: 21846, 24: 43691}[m]) >> 20


def place_rows(x, rows, m, chan):
    n = chan.shape[1]
    row = lax.broadcasted_iota(jnp.int32, (512, n), 0)
    zz, xx, hh, cc = row >> 7, (row >> 5) & 3, (row >> 4) & 1, (row >> 3) & 1
    owner = shift_div(chan, m)
    same = ((zz * 2 + hh) * 4 + xx) * 2 + cc == owner
    col = lax.broadcasted_iota(jnp.int32, (128, n), 0) == chan - m * owner
    out = []
    for r in rows:
        pick = jnp.where(jnp.logical_and(same, (row & 7) == r), 1.0, 0.0).astype(BF)
        vals = tn(x, pick)
        out.append(jnp.sum(jnp.where(col, vals, 0.0), axis=0, keepdims=True))
    return out


def first_gathers(starts, ngain, w_in, cw, cb, dtb, alog, skip, gate, w_out, tok, cot):
    def kernel(
        starts, ngain, w_in, cw, cb, dtb, alog, skip, gate, w_out, tok, cot,
        w, tall, call, blk1, cv, ng, stt,
        tile, tg, tb, ta, pieces, pb, blk0, wt, lsem, ssem, rsem,
    ):
        s, z, h, x, c = place()
        hc = 2 * h + c
        q = 4 * s + hc
        greet(small_devs() + group_devs())
        net = Net(ssem, rsem)
        devs = group_devs()
        tile[...] = jnp.zeros_like(tile)
        tile[0:4, 0:52] = cw[0].astype(F32)
        tile[4:5, 0:52] = cb[...].astype(F32)
        tile[5:6, 0:48] = gate[...].astype(F32)
        tile[6:7, 0:24] = ngain[...].astype(F32)
        tile[7:8, 0:4] = starts[0].astype(F32)
        tile[7:8, 4:8] = starts[1].astype(F32)
        tile[8:9, 0:48] = dtb[...]
        tile[9:10, 0:48] = jnp.exp(alog[...])
        tile[10:11, 0:48] = skip[...]
        tsend = [net.send(tile, tg.at[q], dev) for dev in devs]
        tg[q] = tile[...]
        eye = (
            lax.broadcasted_iota(jnp.int32, (32, 24), 0) == lax.broadcasted_iota(jnp.int32, (32, 24), 1)
        ).astype(BF)
        wt[...] = nt(eye, w_out[0]).astype(BF)
        low6 = lax.broadcasted_iota(jnp.int32, (24, 128), 1) < NH
        rate = jnp.concatenate(
            [w_in[0, :, 6400:6448].astype(F32), jnp.zeros((24, 80), F32)], axis=1
        )
        for k in range(8):
            lanes = slice(k * HC, k * HC + HC)
            pieces[k, 0:24, 0:HC] = w_in[0, :, k * HC : k * HC + HC]
            pieces[k, 0:24, HC : 2 * HC] = w_in[0, :, 3072 + k * HC : 3072 + k * HC + HC]
            pieces[k, 0:24, 2 * HC : RT] = w_in[0, :, 6144:6400]
            moved = rate if k == 0 else pltpu.roll(rate, 128 - NH * k, axis=1)
            pieces[k, 0:24, RT:CIN] = jnp.where(low6, moved, 0.0).astype(BF)
            pieces[k, :, CIN:D] = wt[:, lanes]
            pieces[k, 24:32, 0:CIN] = jnp.zeros((8, CIN), BF)
        ids = [4 * d["s"] + 2 * d["h"] + d["c"] for d in devs]
        psend = [
            net.make(pieces.at[k], pb.at[s, hc], dev) for k, dev in zip(ids, devs)
        ]
        pb[s, hc] = pieces[q]

        def p_send():
            for copy in psend:
                copy.start()

        def p_wait(layer):
            @pl.when(s == layer)
            def _():
                for copy in psend[0:3]:
                    copy.wait_recv()

            @pl.when(s != layer)
            def _():
                for copy in psend[3:7]:
                    copy.wait_recv()

        def block(layer, out):
            for hh in range(2):
                out[hh, 0:24] = pb[layer, 2 * hh, 0:24]
                out[hh, 24:48] = pb[layer, 2 * hh + 1, 0:24]

        pl.when(s == 0)(p_send)
        gather = Gather(net, blk0, w, lsem.at[0])

        def weights():
            yield 9.0
            p_wait(0)
            block(0, blk0)
            gather.step(0)
            pl.when(s == 1)(p_send)
            for k, t in enumerate((5.0, 7.0, 21.0, 29.0)):
                yield 10.0 + t
                gather.step(k + 1)

        def second():
            yield 30.0
            p_wait(1)
            block(1, blk1)

        def vectors():
            yield 10.0
            for copy in tsend:
                copy.wait_recv()
            for k in range(8):
                tb[z, k // 4, 8 * (k % 4) : 8 * (k % 4) + 8] = tg[k, 0:8].astype(BF)
            for n in range(4):
                v = tg[n, 7:8, :]
                first = 4 * (n // 2) + n % 2
                stt[first : first + 1] = v.astype(jnp.int32)
                stt[first + 2 : first + 3] = pltpu.roll(v, 124, axis=1).astype(jnp.int32)
            r = tb.at[z]
            sends = [net.send(r, r, {"z": lax.rem(z + k, 4)}) for k in range(1, 4)]
            yield 14.0
            for copy in sends:
                copy.wait_recv()
            ta[x] = tb[...]
            r = ta.at[x]
            sends = [net.send(r, r, {"x": lax.rem(x + k, 4)}) for k in range(1, 4)]
            yield 20.0
            for copy in sends:
                copy.wait_recv()
            n = lax.broadcasted_iota(jnp.int32, (1, 640), 1)
            chan = jnp.where(n < HC, q * HC + n, 3072 - HC + n)
            gchan = q * HC + lax.broadcasted_iota(jnp.int32, (1, HC), 1)
            nchan = lax.broadcasted_iota(jnp.int32, (1, D), 1)
            head = lax.broadcasted_iota(jnp.int32, (1, HC), 1) >> 6
            cv[...] = jnp.zeros_like(cv)
            for layer in range(2):
                vals = jnp.concatenate(
                    [ta[k % 4, k // 4, layer] for k in range(16)], axis=0
                )
                for r, v in enumerate(place_rows(vals, range(5), 52, chan)):
                    cv[layer, r : r + 1, :] = v
                cv[layer, 5:6, 0:HC] = place_rows(vals, [5], 48, gchan)[0]
                ng[layer] = place_rows(vals, [6], 24, nchan)[0]
                back = lax.rem(128 - NH * q, 128)
                heads = pltpu.roll(tg[4 * layer, 8:16, :], back, axis=1)
                cv[layer, 7:8, 0:128] = heads[0:1]
                cv[layer, 8:9, 0:128] = heads[1:2]
                lanes = jnp.zeros((1, HC), F32)
                for k in range(NH):
                    lanes = jnp.where(head == k, heads[2:3, k : k + 1], lanes)
                cv[layer, 6:7, 0:HC] = lanes
                yield 21.0

        run(
            [
                weights(),
                vectors(),
                g_pairs(net, tok, tall, lsem.at[1], 10.0),
                g_pairs(net, cot, call, lsem.at[2], 19.2),
                second(),
            ]
        )
        net.finish()

    return pl.pallas_call(
        kernel,
        name="first_gathers",
        out_shape=(
            GATHERED,
            CHUNKS,
            CHUNKS,
            jax.ShapeDtypeStruct((2, 48, D), BF),
            jax.ShapeDtypeStruct((2, 16, 640), F32),
            jax.ShapeDtypeStruct((2, 1, D), F32),
            jax.ShapeDtypeStruct((8, 128), jnp.int32),
        ),
        in_specs=[VM] * 12,
        out_specs=(ANY,) * 3 + (VM,) * 4,
        scratch_shapes=[
            pltpu.VMEM((16, 128), F32),
            pltpu.VMEM((8, 16, 128), F32),
            pltpu.VMEM((4, 2, 32, 128), BF),
            pltpu.VMEM((4, 4, 2, 32, 128), BF),
            pltpu.VMEM((8, 32, D), BF),
            pltpu.VMEM((2, 4, 32, D), BF),
            pltpu.VMEM((2, 48, D), BF),
            pltpu.VMEM((32, 3072), BF),
            pltpu.SemaphoreType.DMA((3,)),
        ]
        + sems(56),
        compiler_params=params(0),
    )(starts, ngain, w_in, cw, cb, dtb, alog, skip, gate, w_out, tok, cot)


def unpack_grads(rec, vec, heads, w_in, norm_gain, place_dp):
    rec = rec.astype(F32)
    flat = lambda v: jnp.transpose(v, (1, 0, 2)).reshape(24, -1)
    w_in_grad = jnp.concatenate(
        [
            flat(rec[:, :, 0:HC]),
            flat(rec[:, :, HC : 2 * HC]),
            jnp.sum(rec[:, :, 2 * HC : RT], axis=0),
            flat(rec[:, :, RT : RT + NH]),
        ],
        axis=1,
    )
    w_out_grad = jnp.transpose(flat(rec[:, :, CIN:D]))
    conv = lax.dynamic_slice_in_dim(vec[0:5], 52 * place_dp, 52, 1)
    gate = lax.dynamic_slice_in_dim(vec[5], 48 * place_dp, 48, 0)
    norm_grad = jnp.sum(w_in.astype(F32) * w_in_grad, axis=1) / norm_gain.astype(F32)
    return (
        norm_grad,
        w_in_grad,
        conv[0:4],
        conv[4],
        heads[:, 0:NH].reshape(48),
        heads[:, 128 : 128 + NH].reshape(48),
        jnp.sum(heads[:, 256:640].reshape(48, 64), axis=1),
        gate,
        w_out_grad,
    )


def body(
    tokens,
    cotangent,
    starts,
    norm_gain,
    w_in,
    conv_weight,
    conv_bias,
    dt_bias,
    a_log,
    skip_d,
    gate_gain,
    w_out,
):
    s, z, h, x, c = place()
    w0g, tall, call, blk1, cv, ng, st = first_gathers(
        starts,
        norm_gain,
        w_in,
        conv_weight,
        conv_bias,
        dt_bias,
        a_log,
        skip_d,
        gate_gain,
        w_out,
        tokens,
        cotangent,
    )
    w1, xall, stat0, stat1, part1, proj0, proj1, y0, y1, u0, u1, do1 = two_forward(
        st, tall, w0g, ng, cv, call, blk1
    )
    eall, _, rec, vec, hd, ig0, so1, got = two_backward(
        st, w1, w0g, ng, cv, call, xall, tall, proj1, proj0, y1, y0, do1, u1, u0, part1, stat1, stat0
    )
    place_dp = ((z * 2 + h) * 4 + x) * 2 + c
    outs = unpack_grads(rec[:, :24], vec, hd, w_in[0], norm_gain[0], place_dp)

    own = lambda v: lax.dynamic_slice(v, (h, 0, c, 0, 0), (1, 2, 1, 128, D)).reshape(2, 128, D)
    ig = jnp.where(s == 0, jnp.stack([ig0, got]), own(eall))
    so = jnp.where(s == 0, own(xall), jnp.stack([got, so1]))
    return (so[None], ig.astype(F32)[None]) + tuple(o[None] for o in outs)


def solution(mesh):
    inner = Mesh(mesh.devices.reshape(2, 4, 2, 4, 2), ("s", "z", "h", "x", "c"))
    dp = ("z", "h", "x", "c")
    in_specs = (
        P(None, dp, None),
        P(None, dp, None),
        P(None, dp, None),
        P("s", dp),
        P("s", dp, None),
        P("s", None, dp),
        P("s", dp),
        P("s", None),
        P("s", None),
        P("s", None),
        P("s", dp),
        P("s", None, dp),
    )
    out_specs = (
        P("s", None, dp, None),
        P("s", None, dp, None),
        P("s", dp),
        P("s", dp, None),
        P("s", None, dp),
        P("s", dp),
        P("s", None),
        P("s", None),
        P("s", None),
        P("s", dp),
        P("s", None, dp),
    )
    return jax.shard_map(body, mesh=inner, in_specs=in_specs, out_specs=out_specs, check_vma=False)
```

```python
import jax
import jax.numpy as jnp
from jax import lax
from jax.experimental import pallas as pl
from jax.experimental.pallas import tpu as pltpu
from jax.sharding import Mesh, PartitionSpec as P

EPS = 1e-05
BF = jnp.bfloat16
F32 = jnp.float32
HIGH = lax.Precision.HIGHEST
D = 1536
CIN = 1152
HC = 384
NH = 6
RT = 1024
HALF = 768
ANY = pl.BlockSpec(memory_space=pl.ANY)
VM = pl.BlockSpec(memory_space=pltpu.VMEM)
SM = pl.BlockSpec(memory_space=pltpu.SMEM)
VLIM = 59 * 1024 * 1024


class Net:
    def __init__(self, ssem, rsem):
        self.ssem, self.rsem, self.n, self.all = ssem, rsem, 0, []

    def make(self, src, dst, dev):
        i = self.n
        self.n += 1
        assert i < self.ssem.shape[0]
        copy = pltpu.make_async_remote_copy(
            src_ref=src,
            dst_ref=dst,
            send_sem=self.ssem.at[i],
            recv_sem=self.rsem.at[i],
            device_id=dev,
            device_id_type=pl.DeviceIdType.MESH,
        )
        self.all.append(copy)
        return copy

    def send(self, src, dst, dev):
        copy = self.make(src, dst, dev)
        copy.start()
        return copy

    def sent(self, copy):
        copy.wait_send()
        self.all = [v for v in self.all if v is not copy]

    def finish(self):
        for copy in self.all:
            copy.wait_send()


def place():
    s, z, h, x, c = (lax.axis_index(a) for a in ("s", "z", "h", "x", "c"))
    return s, z, h, x, c


def ring(i):
    return lax.rem(i + 1, 4), lax.rem(i + 3, 4), lax.rem(i + 2, 4)


def greet(devs):
    barrier = pltpu.get_barrier_semaphore()
    for dev in devs:
        pl.semaphore_signal(barrier, inc=1, device_id=dev, device_id_type=pl.DeviceIdType.MESH)
    pl.semaphore_wait(barrier, len(devs))


def zx_devs():
    s, z, h, x, c = place()
    zr, zl, _ = ring(z)
    xr, xl, _ = ring(x)
    return [{"z": zr}, {"z": zl}, {"x": xr}, {"x": xl}]


def ydev(y):
    return {"h": y // 2, "s": lax.rem(y, 2)}


def y_devs():
    s, z, h, x, c = place()
    yr, yl, _ = ring(2 * h + s)
    return [ydev(yr), ydev(yl), {"c": 1 - c}]


def group_devs():
    s, z, h, x, c = place()
    out = []
    for k in range(1, 8):
        out.append(
            {
                "s": 1 - s if k & 4 else s,
                "h": 1 - h if k & 2 else h,
                "c": 1 - c if k & 1 else c,
            }
        )
    return out


LAT = 1.7


def inter(gens):
    gens = [[0.0, g] for g in gens]
    while gens:
        item = min(gens, key=lambda v: v[0])
        if item[0] > 0:
            yield item[0]
        try:
            item[0] = next(item[1])
        except StopIteration:
            gens.remove(item)


def run(gens):
    for _ in inter(gens):
        pass


def g_pairs(net, own, out, lsem, t0):
    s, z, h, x, c = place()
    outer, inner, sib = {"h": 1 - h, "s": 1 - s}, {"s": 1 - s}, {"c": 1 - c}
    first = []
    for k in range(2):
        rows = pl.ds(64 * k, 64)
        first.append(net.send(own.at[s, rows], out.at[h, s, c, rows], outer))
    local = pltpu.make_async_copy(own, out.at[h, :, c], lsem)
    local.start()
    c0 = net.send(own, out.at[h, :, c], sib)
    yield t0 + 4.6 + LAT
    second = []
    for k in range(2):
        first[k].wait_recv()
        r = out.at[1 - h, 1 - s, c, pl.ds(64 * k, 64)]
        second.append(net.send(r, r, inner))
        if k == 0:
            yield t0 + 9.2 + LAT
    r = out.at[1 - h, 1 - s, c]
    c1 = net.send(r, r, sib)
    yield t0 + 14 + LAT
    for copy in second:
        copy.wait_recv()
    r = out.at[1 - h, s, c]
    c2 = net.send(r, r, sib)
    yield t0 + 16 + LAT
    for copy in (c0, c1, c2):
        copy.wait_recv()
    local.wait()


def g_small(net, mine, bz, bx, total, t0=0.0):
    s, z, h, x, c = place()
    sends = [net.send(mine, bz.at[z], {"z": lax.rem(z + k, 4)}) for k in range(1, 4)]
    bz[z] = mine[...]
    yield t0 + 4.0
    for copy in sends:
        copy.wait_recv()
    bx[x] = bz[0] + bz[1] + bz[2] + bz[3]
    r = bx.at[x]
    sends = [net.send(r, r, {"x": lax.rem(x + k, 4)}) for k in range(1, 4)]
    yield t0 + 10.0
    for copy in sends:
        copy.wait_recv()
    total[...] = bx[0] + bx[1] + bx[2] + bx[3]


def small_scratch():
    return [pltpu.VMEM((4, 2, 8, 640), F32), pltpu.VMEM((4, 2, 8, 640), F32)]


def small_devs():
    s, z, h, x, c = place()
    return [{"z": lax.rem(z + k, 4)} for k in range(1, 4)] + [
        {"x": lax.rem(x + k, 4)} for k in range(1, 4)
    ]


def g_share(net, sums, got, vec, heads):
    s, z, h, x, c = place()
    me = (2 * s + h) * 2 + c
    sends = []
    for dev in group_devs():
        sends.append(net.send(sums.at[dev["s"]], got.at[me], dev))
    got[me] = sums[s]
    yield 20.0
    for copy in sends:
        copy.wait_recv()
    vec[...] = jnp.zeros_like(vec)
    tail = jnp.zeros((5, 256), F32)
    for q in range(8):
        lanes = slice(q * HC, q * HC + HC)
        vec[0:5, lanes] = got[q, 0:5, 0:HC]
        vec[5:6, lanes] = got[q, 5:6, 0:HC]
        tail = tail + got[q, 0:5, HC:640]
        heads[q : q + 1, 0:256] = got[q, 5:6, HC:640]
        heads[q : q + 1, 256:640] = got[q, 6:7, 0:HC]
    vec[0:5, 3072:3328] = tail


def params(cid):
    return pltpu.CompilerParams(
        collective_id=cid, has_side_effects=True, vmem_limit_bytes=VLIM
    )


def sems(n):
    return [pltpu.SemaphoreType.DMA((n,)), pltpu.SemaphoreType.DMA((n,))]


GATHERED = jax.ShapeDtypeStruct((4, 2, 4, 48, D), BF)
CHUNKS = jax.ShapeDtypeStruct((2, 2, 2, 128, D), BF)
SMALL = jax.ShapeDtypeStruct((8, 640), F32)
CHUNK = jax.ShapeDtypeStruct((128, D), BF)


def row_to_col(row):
    i = lax.broadcasted_iota(jnp.int32, (128, 128), 0)
    j = lax.broadcasted_iota(jnp.int32, (128, 128), 1)
    return jnp.sum(jnp.where(i == j, row, 0.0), axis=1, keepdims=True)


def col_to_row(col):
    i = lax.broadcasted_iota(jnp.int32, (128, 128), 0)
    j = lax.broadcasted_iota(jnp.int32, (128, 128), 1)
    return jnp.sum(jnp.where(i == j, col, 0.0), axis=0, keepdims=True)


def own_scale(total):
    s, z, h, x, c = place()
    row = total[pl.ds((2 * h + s) * 2 + c, 1), :]
    return lax.rsqrt(row_to_col(row) * (1.0 / 3072) + EPS)


def norm_back(v, x, e, ng):
    xf = x.astype(F32)
    vg = v * ng[...]
    r = lax.rsqrt(jnp.mean(xf * xf, axis=-1, keepdims=True) + EPS)
    dot = jnp.mean(xf * vg, axis=-1, keepdims=True)
    return e.astype(F32) + r * vg - xf * (r * r * r * dot)


def nt(a, b):
    return lax.dot_general(a, b, (((1,), (1,)), ((), ())), preferred_element_type=F32)


def tn(a, b):
    return lax.dot_general(a, b, (((0,), (0,)), ((), ())), preferred_element_type=F32)


def iotas():
    i = lax.broadcasted_iota(jnp.int32, (128, 128), 0)
    j = lax.broadcasted_iota(jnp.int32, (128, 128), 1)
    return i, j


def seg_of(firsts, places):
    seg = jnp.full(places.shape, -1, jnp.int32)
    for k in range(4):
        seg = seg + (firsts[k] <= places).astype(jnp.int32)
    return seg


def masks(st, chunk):
    i, j = iotas()
    firsts = [st[chunk, k] for k in range(4)]
    seg = seg_of(firsts, i)
    keep = jnp.logical_and(seg == seg_of(firsts, j), i >= j)
    valid = [None] + [(seg_of(firsts, i - k) == seg).astype(F32) for k in range(1, 4)]
    return keep, valid


def conv_tile(xt, cv, t, valid):
    lanes = slice(128 * t, 128 * t + 128)
    pre = cv[4:5, lanes] + cv[3:4, lanes] * xt
    moved = [xt]
    for k in range(1, 4):
        m = pltpu.roll(xt, k, axis=0) * valid[k]
        moved.append(m)
        pre = pre + cv[3 - k : 4 - k, lanes] * m
    return pre, moved


def rates(rt, cv):
    i, j = iotas()
    head = j < NH
    v = rt + cv[7:8, 0:128]
    dt = jnp.where(head, jnp.maximum(v, 0.0) + jnp.log1p(jnp.exp(-jnp.abs(v))), 0.0)
    lower = (i >= j).astype(F32)
    cum = jnp.dot(
        lower, -dt * cv[8:9, 0:128], precision=HIGH, preferred_element_type=F32
    )
    return v, dt, cum


def half_masks():
    _, j = iotas()
    return j < 64


def split_pair(v, low):
    zero = jnp.zeros_like(v)
    return jnp.concatenate([jnp.where(low, v, zero), jnp.where(low, zero, v)], axis=0)


def decay_of(keep, cum, cum_t, h):
    spread = jnp.where(keep, cum[:, h : h + 1] - cum_t[h : h + 1, :], -1e30)
    return jnp.exp(spread)


class Gather:
    def __init__(self, net, blk, out, lsem):
        s, z, h, x, c = place()
        self.local = pltpu.make_async_copy(blk, out.at[z, :, x], lsem)
        every = slice(None)
        self.parts = []
        for lanes, i, axis_i, j, axis_j, pick in (
            (pl.ds(0, HALF), x, "x", z, "z", lambda i, j, p: (j, p, i)),
            (pl.ds(HALF, HALF), z, "z", x, "x", lambda i, j, p: (i, p, j)),
        ):
            ir, il, _ = ring(i)
            jr, jl, _ = ring(j)

            def at(i, j, p, pick=pick, lanes=lanes):
                return out.at[pick(i, j, p) + (every, lanes)]

            def make(i, j, p, dev, src=None):
                ref = at(i, j, p)
                return net.make(ref if src is None else src, ref, dev)

            own = blk.at[:, :, lanes]
            first, second = ({axis_i: ir}, {axis_i: il}), ({axis_j: jr}, {axis_j: jl})
            self.parts.append(
                [
                    (make(i, j, every, first[0], own), make(i, j, every, first[1], own)),
                    (make(il, j, 0, first[0]), make(ir, j, 1, first[1])),
                    (make(every, j, every, second[0]), make(every, j, every, second[1])),
                    (make(every, jl, 0, second[0]), make(every, jr, 1, second[1])),
                ]
            )

    def step(self, k):
        if k == 0:
            self.local.start()
        if k == 2:
            self.local.wait()
        for part in self.parts:
            for n in range(2):
                if k > 0:
                    part[k - 1][n].wait_recv()
                if k < 4 and k != 2:
                    part[k][n].start()
            if k == 2:
                part[2][0].start()
                part[2][1].start()


class RingSum:
    def __init__(self, net, part, bufs):
        self.part = part
        self.cb, self.sb, self.b1, self.b2 = bufs
        s, z, h, x, c = place()
        self.c = c
        sib = {"c": 1 - c}
        outer, inner = {"h": 1 - h, "s": 1 - s}, {"s": 1 - s}
        self.units = [(1 - h, s), (1 - h, 1 - s), (h, 1 - s), (h, s)]
        self.core = [
            net.make(part.at[hh, mm, 1 - c], self.cb.at[k], sib)
            for k, (hh, mm) in enumerate(self.units)
        ]
        sb, b1, b2 = self.sb, self.b1, self.b2
        lo, hi = pl.ds(0, 64), pl.ds(64, 64)
        self.far = [
            net.make(sb.at[0, lo], b1.at[0], outer),
            net.make(sb.at[0, hi], b1.at[1], inner),
        ]
        self.direct = [
            net.make(sb.at[1, lo], b2.at[0, lo], outer),
            net.make(sb.at[2, hi], b2.at[1, hi], inner),
        ]
        self.summed = [
            net.make(sb.at[1, hi], b2.at[0, hi], outer),
            net.make(sb.at[2, lo], b2.at[1, lo], inner),
        ]

    def add(self, k):
        self.core[k].wait_recv()
        hh, mm = self.units[k]
        self.sb[k] = (self.part[hh, mm, self.c].astype(F32) + self.cb[k].astype(F32)).astype(BF)

    def step(self, k):
        self.core[k].start()
        if k > 0:
            self.add(k - 1)
        if k == 1:
            self.far[0].start()
            self.far[1].start()
        if k > 1:
            self.direct[k - 2].start()

    def all_adds(self):
        self.add(0)
        self.far[0].start()
        self.far[1].start()
        self.add(1)
        self.direct[0].start()
        self.add(2)
        self.direct[1].start()

    def late(self):
        lo, hi = slice(0, 64), slice(64, 128)
        self.far[1].wait_recv()
        self.sb[1, hi] = (self.sb[1, hi].astype(F32) + self.b1[1].astype(F32)).astype(BF)
        self.summed[0].start()
        self.far[0].wait_recv()
        self.sb[2, lo] = (self.sb[2, lo].astype(F32) + self.b1[0].astype(F32)).astype(BF)
        self.summed[1].start()

    def total(self):
        self.core[3].wait_recv()
        for copy in self.direct + self.summed:
            copy.wait_recv()
        hh, mm = self.units[3]
        total = self.part[hh, mm, self.c].astype(F32) + self.cb[3].astype(F32)
        return total + self.b2[0].astype(F32) + self.b2[1].astype(F32)


def ring_scratch():
    return [
        pltpu.VMEM((4, 128, D), BF),
        pltpu.VMEM((3, 128, D), BF),
        pltpu.VMEM((2, 64, D), BF),
        pltpu.VMEM((2, 128, D), BF),
    ]


class Spread:
    def __init__(self, net, out):
        s, z, h, x, c = place()
        sib = {"c": 1 - c}
        outer, inner = {"h": 1 - h, "s": 1 - s}, {"s": 1 - s}
        lo, hi = pl.ds(0, 64), pl.ds(64, 64)
        own, far = out.at[h, s, c], out.at[1 - h, s, c]
        from_outer, from_inner = out.at[1 - h, 1 - s, c], out.at[h, 1 - s, c]
        self.mine = own
        self.ring = [net.make(own, own, outer), net.make(own, own, inner)]
        self.hand = [
            net.make(from_inner.at[lo], from_inner.at[lo], outer),
            net.make(from_outer.at[hi], from_outer.at[hi], inner),
        ]
        self.sib = [net.make(r, r, sib) for r in (own, from_inner, from_outer, far)]

    def start(self):
        self.ring[0].start()
        self.ring[1].start()
        self.sib[0].start()

    def ready(self, k):
        if k == 1:
            self.ring[1].wait_recv()
            self.hand[0].start()
            self.sib[1].start()
            self.ring[0].wait_recv()
            self.hand[1].start()
            self.sib[2].start()
        if k == 3:
            self.hand[0].wait_recv()
            self.hand[1].wait_recv()
            self.sib[3].start()
        self.sib[k].wait_recv()


def when_each(i, n, step):
    for k in range(n):
        pl.when(i == k)(lambda k=k: step(k))


def block_at(i, h, s, far_first):
    k = i if far_first else 3 - i
    return lax.rem(h + 1 + k // 2, 2), lax.rem(s + (k + 1) // 2, 2)


def forward_block(b, x, w, ng, cv, st, refs, e=None):
    part, stat, proj, yout, uout, doo, og = refs
    with_do = e is not None
    xf = x[...].reshape(256, D).astype(F32)
    r = lax.rsqrt(jnp.mean(xf * xf, axis=-1, keepdims=True) + EPS)
    u = (xf * r * ng).astype(BF)
    uout[...] = u
    proj[...] = jnp.dot(u, w[:, :, :, :, 0:CIN].reshape(D, CIN), preferred_element_type=F32)
    if with_do:
        doo[...] = jnp.dot(
            e[...].reshape(256, D),
            w[:, :, :, :, CIN:D].reshape(D, HC),
            preferred_element_type=F32,
        )
    low = half_masks()
    for m in range(2):
        rows = slice(128 * m, 128 * m + 128)
        chunk = b * 2 + m
        keep, valid = masks(st, chunk)
        act = []
        for t in range(5):
            pre, _ = conv_tile(proj[rows, HC + 128 * t : HC + 128 * t + 128], cv, t, valid)
            act.append((pre * jax.nn.sigmoid(pre)).astype(BF))
        _, dt, cum = rates(proj[rows, RT:CIN], cv)
        cum_t, dt_t = jnp.transpose(cum), jnp.transpose(dt)
        gram = nt(act[4], act[3])
        gsum = jnp.zeros((128, 1), F32)
        tsum = jnp.zeros((128, 1), F32)
        for t in range(3):
            lanes = slice(128 * t, 128 * t + 128)
            mixes = []
            for h in (2 * t, 2 * t + 1):
                dec = decay_of(keep, cum, cum_t, h)
                mixes.append((gram * dec * dt_t[h : h + 1, :]).astype(BF))
            y = jnp.dot(
                jnp.concatenate(mixes, axis=1),
                split_pair(act[t], low),
                preferred_element_type=F32,
            )
            y = y + cv[6:7, lanes] * act[t].astype(F32)
            yout[rows, lanes] = y
            zt = proj[rows, lanes]
            g = y * (zt * jax.nn.sigmoid(zt))
            gsum = gsum + jnp.sum(g * g, axis=1, keepdims=True)
            gain = cv[5:6, lanes]
            og[rows, lanes] = (g * gain).astype(BF)
            if with_do:
                tsum = tsum + jnp.sum(g * gain * doo[rows, lanes], axis=1, keepdims=True)
        stat[pl.ds(chunk, 1), :] = col_to_row(gsum)
        if with_do:
            stat[pl.ds(chunk + 8, 1), :] = col_to_row(tsum)
    out = nt(og[...], w[:, :, :, :, CIN:D].reshape(D, HC))
    part[...] = out.astype(BF).reshape(2, 128, D)


class Scatter:
    def __init__(self, net, grads, bufs, out):
        s, z, h, x, c = place()
        self.out = out
        self.parts = []
        for k, (i, axis_i, j, axis_j) in enumerate(((z, "z", x, "x"), (x, "x", z, "z"))):
            lanes = pl.ds(k * HALF, HALF)
            b1, b2, t, sums, b3, b4, t2 = [b.at[k] for b in bufs]
            ir, il, io = ring(i)
            jr, jl, jo = ring(j)
            if k == 0:
                unit = lambda i, p, lanes=lanes: grads.at[i, p, :, :, lanes]
            else:
                unit = lambda i, p, lanes=lanes: grads.at[:, p, i, :, lanes]
            right, left = {axis_i: ir}, {axis_i: il}
            part = dict(unit=unit, bufs=(b1, b2, t, sums, b3, b4, t2), i=i, j=j)
            part.update(ir=ir, il=il, jr=jr, jl=jl, jo=jo, k=k)
            part["far"] = [
                net.make(unit(io, 0), b1.at[0], right),
                net.make(unit(io, 1), b1.at[1], left),
            ]
            part["near"] = [
                net.make(unit(ir, 1), b2.at[0, 1], right),
                net.make(unit(il, 0), b2.at[1, 0], left),
                net.make(t.at[0], b2.at[0, 0], right),
                net.make(t.at[1], b2.at[1, 1], left),
            ]
            right, left = {axis_j: jr}, {axis_j: jl}
            part["far2"] = [
                net.make(sums.at[0, jo], b3.at[0], right),
                net.make(sums.at[1, jo], b3.at[1], left),
            ]
            part["near2"] = [
                net.make(sums.at[1, jr], b4.at[0, 1], right),
                net.make(sums.at[0, jl], b4.at[1, 0], left),
                net.make(t2.at[0], b4.at[0, 0], right),
                net.make(t2.at[1], b4.at[1, 1], left),
            ]
            self.parts.append(part)

    def start(self, k):
        for copy in self.parts[k]["far"]:
            copy.start()

    def direct(self, k):
        self.parts[k]["near"][0].start()
        self.parts[k]["near"][1].start()

    def summed(self, k):
        v = self.parts[k]
        b1, b2, t, sums, b3, b4, t2 = v["bufs"]
        for p, near in ((0, v["ir"]), (1, v["il"])):
            v["far"][p].wait_recv()
            for n in range(4):
                t[p, n] = (v["unit"](near, p)[n].astype(F32) + b1[p, n].astype(F32)).astype(BF)
            v["near"][2 + p].start()

    def total(self, v, p, n):
        b2 = v["bufs"][1]
        return (
            v["unit"](v["i"], p)[n].astype(F32)
            + b2[0, p, n].astype(F32)
            + b2[1, p, n].astype(F32)
        )

    def second(self, k):
        v = self.parts[k]
        sums = v["bufs"][3]
        for copy in v["near"]:
            copy.wait_recv()
        for copy, p, n in (
            (v["far2"][0], 0, v["jo"]),
            (v["far2"][1], 1, v["jo"]),
            (v["near2"][0], 1, v["jr"]),
            (v["near2"][1], 0, v["jl"]),
        ):
            sums[p, n] = self.total(v, p, n).astype(BF)
            copy.start()
        for p, n in ((0, v["jr"]), (1, v["jl"]), (0, v["j"]), (1, v["j"])):
            sums[p, n] = self.total(v, p, n).astype(BF)

    def second_summed(self, k):
        v = self.parts[k]
        b1, b2, t, sums, b3, b4, t2 = v["bufs"]
        for p, near in ((0, v["jr"]), (1, v["jl"])):
            v["far2"][p].wait_recv()
            t2[p] = (sums[p, near].astype(F32) + b3[p].astype(F32)).astype(BF)
            v["near2"][2 + p].start()

    def finish(self, k):
        v = self.parts[k]
        sums, b4 = v["bufs"][3], v["bufs"][5]
        for copy in v["near2"]:
            copy.wait_recv()
        for p in range(2):
            total = sums[p, v["j"]].astype(F32) + b4[0, p].astype(F32) + b4[1, p].astype(F32)
            self.out[p, :, k * HALF : (k + 1) * HALF] = total.astype(BF)


def scatter_scratch():
    return [
        pltpu.VMEM((2, 2, 4, 48, HALF), BF),
        pltpu.VMEM((2, 2, 2, 4, 48, HALF), BF),
        pltpu.VMEM((2, 2, 4, 48, HALF), BF),
        pltpu.VMEM((2, 2, 4, 48, HALF), BF),
        pltpu.VMEM((2, 2, 48, HALF), BF),
        pltpu.VMEM((2, 2, 2, 48, HALF), BF),
        pltpu.VMEM((2, 2, 48, HALF), BF),
    ]


def weight_tile(k, half, u, e, dproj, o, grads):
    cols = pl.ds(pl.multiple_of(k * 384, 128), 384)
    rows = 1024
    ut = u[:, :, cols].reshape(rows, 384)
    if half == 0:
        a = tn(ut, dproj[:, :, 0:HALF].reshape(rows, HALF))
        grads[k, :, :, :, 0:HALF] = a.astype(BF).reshape(2, 4, 48, HALF)
        return
    a = tn(ut, dproj[:, :, HALF:CIN].reshape(rows, CIN - HALF))
    grads[k, :, :, :, HALF:CIN] = a.astype(BF).reshape(2, 4, 48, CIN - HALF)
    a = tn(e[:, :, :, :, cols].reshape(rows, 384), o[...].reshape(rows, HC))
    grads[k, :, :, :, CIN:D] = a.astype(BF).reshape(2, 4, 48, HC)


def backward_block(b, e, w, cv, st, stat, dots, refs):
    proj, yin, do, dproj, oo, part, sm = refs
    if dots is not None:
        do[...] = jnp.dot(
            e[...].reshape(256, D),
            w[:, :, :, :, CIN:D].reshape(D, HC),
            preferred_element_type=F32,
        )
    low = half_masks()
    i, j = iotas()
    upper = (j >= i).astype(F32)

    def add(row, lanes, v):
        sm[row : row + 1, lanes] += jnp.sum(v, axis=0, keepdims=True)

    for m in range(2):
        rows = slice(128 * m, 128 * m + 128)
        chunk = b * 2 + m
        keep, valid = masks(st, chunk)
        pres, moves, act = [], [], []
        for t in range(5):
            pre, moved = conv_tile(proj[rows, HC + 128 * t : HC + 128 * t + 128], cv, t, valid)
            pres.append(pre)
            moves.append(moved)
            act.append((pre * jax.nn.sigmoid(pre)).astype(BF))
        v, dt, cum = rates(proj[rows, RT:CIN], cv)
        cum_t, dt_t = jnp.transpose(cum), jnp.transpose(dt)
        gram = nt(act[4], act[3])
        r = lax.rsqrt(row_to_col(stat[pl.ds(chunk, 1), :]) * (1.0 / 3072) + EPS)
        if dots is not None:
            k = r * r * row_to_col(dots[chunk, 0:1, :]) * (1.0 / 3072)
        else:
            k = r * r * r * row_to_col(stat[pl.ds(chunk + 8, 1), :]) * (1.0 / 3072)
        dact = []
        dgram = jnp.zeros((128, 128), F32)
        dcum = jnp.zeros((128, 128), F32)
        col_rows = []
        for t in range(3):
            lanes = slice(128 * t, 128 * t + 128)
            zt, y, dot_ = proj[rows, lanes], yin[rows, lanes], do[rows, lanes]
            gain = cv[5:6, lanes]
            sig = jax.nn.sigmoid(zt)
            sz = zt * sig
            g = y * sz
            oo[rows, lanes] = (g * r * gain).astype(BF)
            add(5, lanes, dot_ * g * r)
            dg = r * (dot_ * gain) - g * k
            dproj[rows, lanes] = (dg * y * (sig + sz * (1.0 - sig))).astype(BF)
            dy = (dg * sz).astype(BF)
            dyf = dy.astype(F32)
            xs = act[t]
            add(6, lanes, dyf * xs.astype(F32))
            dy2 = split_pair(dy, low)
            dmix2 = nt(dy2, xs)
            mixes = []
            for q in range(2):
                h = 2 * t + q
                dec = decay_of(keep, cum, cum_t, h)
                dt_row = dt_t[h : h + 1, :]
                pm = gram * dec
                mixes.append((pm * dt_row).astype(BF))
                dmix = dmix2[128 * q : 128 * q + 128]
                dgram = dgram + dmix * (dec * dt_row)
                vm = dmix * pm
                col_rows.append(jnp.sum(vm, axis=0, keepdims=True))
                rsum = jnp.sum(vm * dt_row, axis=1, keepdims=True)
                dcum = dcum + jnp.where(j == h, rsum, 0.0)
            dxs = tn(jnp.concatenate(mixes, axis=0), dy2)
            dact.append(dxs + cv[6:7, lanes] * dyf)
        dgl = dgram.astype(BF)
        dact.append(tn(dgl, act[4]))
        dact.append(jnp.dot(dgl, act[3], preferred_element_type=F32))
        ddt = jnp.transpose(
            jnp.concatenate(col_rows + [jnp.zeros((128 - NH, 128), F32)], axis=0)
        )
        dcum = dcum - ddt * dt
        dla = jnp.dot(upper, dcum, precision=HIGH, preferred_element_type=F32)
        nexp = -cv[8:9, 0:128]
        drate = (ddt + dla * nexp) * jax.nn.sigmoid(v)
        drate = jnp.where(j < NH, drate, 0.0)
        add(5, slice(HC, HC + 128), drate)
        add(5, slice(HC + 128, 640), dla * dt * nexp)
        dproj[rows, RT:CIN] = drate.astype(BF)
        for t in range(5):
            lanes = slice(128 * t, 128 * t + 128)
            pre = pres[t]
            sp = jax.nn.sigmoid(pre)
            dpre = dact[t] * (sp + pre * sp * (1.0 - sp))
            add(4, lanes, dpre)
            add(3, lanes, dpre * moves[t][0])
            dx = cv[3:4, lanes] * dpre
            for n in range(1, 4):
                add(3 - n, lanes, dpre * moves[t][n])
                dx = dx + cv[3 - n : 4 - n, lanes] * pltpu.roll(
                    dpre * valid[n], 128 - n, axis=0
                )
            dproj[rows, HC + 128 * t : HC + 128 * t + 128] = dx.astype(BF)
    out = nt(dproj[...], w[:, :, :, :, 0:CIN].reshape(D, CIN))
    part[...] = out.astype(BF).reshape(2, 128, D)


def two_backward(
    st, w1, w0, ng, cv, call, xall, x0own, proj1, proj0, y1, y0, do1, u1, u0, part1, stat1, stat0
):
    def kernel(
        st, w1h, w0h, ng, cv, callh, xallh, x0h, proj1h, proj0h, y1h, y0h, do1h, u1h, u0h, part1h, stat1p, stat0,
        e0o, sm, rp, vec, heads, ig, so, got,
        w, e1, e0, proj, yv, do, dproj, oo, u, part, x1own, x0own, dtile, db, grads, gp, gs, swap, stat1, stb, *rest,
    ):
        rbufs, ra, sa = rest[:4], rest[4:8], rest[8:15]
        sb = (rest[15], rest[16], sa[2], sa[3], rest[17], rest[18], sa[6])
        bz, bx, sums, ghead, isem, bsem, osem, ssem, rsem = rest[19:]
        s, z, h, x, c = place()

        def block_loads(i, far_first, proj_h, y_h, do_h, layer):
            hi, ci = block_at(i, h, s, far_first)
            b = 2 * hi + ci
            pairs = [(proj_h, proj), (y_h, yv)] + ([(do_h, do)] if do_h is not None else [])
            return [
                pltpu.make_async_copy(src.at[b], dst.at[lax.rem(i, 2)], bsem.at[layer, n, i])
                for n, (src, dst) in enumerate(pairs)
            ]

        loads1 = lambda i: block_loads(i, True, proj1h, y1h, do1h, 1)
        loads0 = lambda i: block_loads(i, False, proj0h, y0h, None, 0)
        for copy in loads1(0):
            copy.start()
        lw1 = pltpu.make_async_copy(w1h, w, isem.at[0])
        lw1.start()
        for copy in loads1(1):
            copy.start()
        later = [
            pltpu.make_async_copy(callh, e1, isem.at[1]),
            pltpu.make_async_copy(u1h, u, isem.at[2]),
            pltpu.make_async_copy(xallh.at[h, s, c], x1own, isem.at[3]),
            pltpu.make_async_copy(x0h, x0own, isem.at[4]),
        ]
        for copy in later:
            copy.start()
        greet(small_devs() + group_devs())
        net = Net(ssem, rsem)
        devs = group_devs()
        ring_sum = RingSum(net, part, rbufs)
        spread = Spread(net, e0)
        scatter1 = Scatter(net, grads, sa, gs.at[1])
        scatter0 = Scatter(net, w, sb, gs.at[0])
        ring0, ring1 = RingSum(net, part, rbufs), RingSum(net, e1, ra)
        me = (2 * h + s) * 2 + c
        q = 4 * s + 2 * h + c
        dsends = [net.make(dtile, db.at[me], dev) for dev in devs]
        gsends = [
            net.make(gp.at[dev["s"], 2 * dev["h"] + dev["c"]], rp.at[q], dev) for dev in devs
        ]
        swap_send = net.make(swap, got, {"s": 1 - s})
        stats = [net.send(stat1p, stb.at[k], dev) for k, dev in enumerate(devs)]
        sm[...] = jnp.zeros_like(sm)
        zr, zl, zo = ring(z)
        acc = stat1p[...]
        for k, copy in enumerate(stats):
            copy.wait_recv()
            acc = acc + stb[k]
        stat1[...] = acc
        lw1.wait()

        def first(i, carry):
            hi, ci = block_at(i, h, s, True)
            b = 2 * hi + ci
            slot = lax.rem(i, 2)
            for copy in loads1(i):
                copy.wait()
            backward_block(
                b, None, w, cv.at[1], st, stat1, None,
                (proj.at[slot], yv.at[slot], do.at[slot], dproj.at[b], oo.at[b], part.at[hi, ci], sm.at[1]),
            )
            when_each(i, 4, ring_sum.step)

            @pl.when(i < 2)
            def _():
                for copy in loads1(i + 2):
                    copy.start()

            return carry

        lax.fori_loop(0, 4, first, 0)
        lw0 = pltpu.make_async_copy(w0h, w, isem.at[5])
        lw0.start()
        for i in range(2):
            for copy in loads0(i):
                copy.start()
        ring_sum.late()
        for copy in later:
            copy.wait()
        for k in range(4):
            weight_tile(k, 1, u, e1, dproj, oo, grads)
        scatter1.start(1)
        scatter1.direct(1)
        for n, k in enumerate((zo, zr, zl, z)):
            weight_tile(k, 0, u, e1, dproj, oo, grads)
            if n == 0:
                scatter1.start(0)
            if n == 2:
                scatter1.direct(0)
        total = ring_sum.total()
        e0f = norm_back(total, x1own[...], e1[h, s, c], ng.at[1])
        e0l = e0f.astype(BF)
        e0[h, s, c] = e0l
        spread.start()
        diff = x1own[...].astype(F32) - x0own[...].astype(F32)
        dots = jnp.sum(e0l.astype(F32) * diff, axis=1, keepdims=True)
        dtile[...] = jnp.broadcast_to(col_to_row(dots), (8, 128))
        db[me] = dtile[...]
        for copy in dsends:
            copy.start()
        for copy in ring_sum.core + ring_sum.far + ring_sum.direct + ring_sum.summed:
            net.sent(copy)
        lu0 = pltpu.make_async_copy(u0h, u, isem.at[2])
        lu0.start()
        lp1 = pltpu.make_async_copy(part1h, e1, isem.at[1])
        lp1.start()
        for copy in dsends:
            copy.wait_recv()
        lw0.wait()
        lp1.wait()

        def save(i):
            hi, ci = block_at(i, h, s, False)
            return pltpu.make_async_copy(e0.at[hi, ci], e0o.at[hi, ci], osem.at[i])

        def second(i, carry):
            when_each(i, 4, spread.ready)
            hi, ci = block_at(i, h, s, False)
            b = 2 * hi + ci
            slot = lax.rem(i, 2)
            for copy in loads0(i):
                copy.wait()
            save(i).start()
            backward_block(
                b, e0.at[hi, ci], w, cv.at[0], st, stat0, db,
                (proj.at[slot], yv.at[slot], do.at[slot], dproj.at[b], oo.at[b], part.at[hi, ci], sm.at[0]),
            )
            when_each(i, 4, lambda k: ring0.core[3 - k].start())

            @pl.when(i < 2)
            def _():
                for copy in loads0(i + 2):
                    copy.start()

            @pl.when(i == 0)
            def _():
                for copy in ring1.core:
                    copy.start()

            @pl.when(i == 1)
            def _():
                scatter1.summed(1)
                scatter1.summed(0)
                ring1.all_adds()

            @pl.when(i == 3)
            def _():
                ring1.late()
                scatter1.second(1)
                scatter1.second(0)

            return carry

        lax.fori_loop(0, 4, second, 0)

        def smalls():
            yield from g_small(net, sm, bz, bx, sums)
            yield from g_share(net, sums, ghead, vec, heads)

        def pieces(layer):
            for k in range(4):
                rows = slice(24 * (k % 2), 24 * (k % 2) + 24)
                gp[layer, k, 0:24] = gs[layer, k // 2, rows, 0:HALF]
                gp[layer, k, 24:48] = gs[layer, k // 2, rows, HALF:D]

            @pl.when(s == layer)
            def _():
                rp[q] = gp[layer, 2 * h + c]
                for copy in gsends[0:3]:
                    copy.start()

            @pl.when(s != layer)
            def _():
                for copy in gsends[3:7]:
                    copy.start()

        sg = smalls()
        next(sg)
        lu0.wait()
        ring0.all_adds()
        for k in range(4):
            weight_tile(k, 1, u, e0, dproj, oo, w)
        scatter0.start(1)
        scatter0.direct(1)
        weight_tile(zo, 0, u, e0, dproj, oo, w)
        scatter0.start(0)
        scatter1.second_summed(1)
        scatter1.second_summed(0)
        weight_tile(zr, 0, u, e0, dproj, oo, w)
        weight_tile(zl, 0, u, e0, dproj, oo, w)
        scatter0.direct(0)
        weight_tile(z, 0, u, e0, dproj, oo, w)
        next(sg)
        ring0.late()
        so[...] = (x1own[...].astype(F32) + own_scale(stat1) * ring1.total()).astype(BF)
        scatter1.finish(1)
        scatter1.finish(0)
        for half in scatter1.parts:
            for copy in half["near"][2:] + half["far2"] + half["near2"]:
                net.sent(copy)
        pieces(1)
        scatter0.summed(1)
        scatter0.summed(0)
        ig[...] = norm_back(ring0.total(), x0own[...], e0[h, s, c], ng.at[0]).astype(BF)
        swap[...] = jnp.where(s == 0, so[...], ig[...])
        swap_send.start()
        next(sg)
        scatter0.second(1)
        scatter0.second(0)
        for _ in sg:
            pass
        scatter0.second_summed(1)
        scatter0.second_summed(0)
        scatter0.finish(0)
        scatter0.finish(1)
        pieces(0)
        for i in range(4):
            save(i).wait()
        for copy in gsends:
            copy.wait_recv()
        swap_send.wait_recv()
        net.finish()

    big = pltpu.VMEM((4, 2, 4, 48, D), BF)
    rows = pltpu.VMEM((2, 2, 2, 128, D), BF)
    chunk = pltpu.VMEM((128, D), BF)
    return pl.pallas_call(
        kernel,
        name="two_backward",
        out_shape=(
            CHUNKS,
            jax.ShapeDtypeStruct((2, 8, 640), F32),
            jax.ShapeDtypeStruct((8, 48, HALF), BF),
            jax.ShapeDtypeStruct((8, 3328), F32),
            SMALL,
            CHUNK,
            CHUNK,
            CHUNK,
        ),
        in_specs=[SM, ANY, ANY, VM, VM] + [ANY] * 11 + [VM, VM],
        out_specs=(ANY,) + (VM,) * 7,
        scratch_shapes=[
            big,
            rows,
            rows,
            pltpu.VMEM((2, 256, CIN), F32),
            pltpu.VMEM((2, 256, HC), F32),
            pltpu.VMEM((2, 256, HC), F32),
            pltpu.VMEM((4, 256, CIN), BF),
            pltpu.VMEM((4, 256, HC), BF),
            pltpu.VMEM((4, 256, D), BF),
            rows,
            chunk,
            chunk,
            pltpu.VMEM((8, 128), F32),
            pltpu.VMEM((8, 8, 128), F32),
            big,
            pltpu.VMEM((2, 4, 48, HALF), BF),
            pltpu.VMEM((2, 2, 48, D), BF),
            chunk,
            pltpu.VMEM((16, 128), F32),
            pltpu.VMEM((7, 16, 128), F32),
        ]
        + ring_scratch()
        + ring_scratch()
        + scatter_scratch()
        + [scatter_scratch()[k] for k in (0, 1, 4, 5)]
        + small_scratch()
        + [pltpu.VMEM((2, 8, 640), F32), pltpu.VMEM((8, 8, 640), F32)]
        + [
            pltpu.SemaphoreType.DMA((6,)),
            pltpu.SemaphoreType.DMA((2, 3, 4)),
            pltpu.SemaphoreType.DMA((4,)),
        ]
        + sems(128),
        compiler_params=params(3),
    )(
        st, w1, w0, ng, cv, call, xall, x0own, proj1, proj0, y1, y0, do1, u1, u0, part1, stat1, stat0
    )


def shift_div(v, m):
    return (v * {52: 20165, 48: 21846, 24: 43691}[m]) >> 20


def place_rows(x, rows, m, chan):
    n = chan.shape[1]
    row = lax.broadcasted_iota(jnp.int32, (512, n), 0)
    zz, xx, hh, cc = row >> 7, (row >> 5) & 3, (row >> 4) & 1, (row >> 3) & 1
    owner = shift_div(chan, m)
    same = ((zz * 2 + hh) * 4 + xx) * 2 + cc == owner
    col = lax.broadcasted_iota(jnp.int32, (128, n), 0) == chan - m * owner
    out = []
    for r in rows:
        pick = jnp.where(jnp.logical_and(same, (row & 7) == r), 1.0, 0.0).astype(BF)
        vals = tn(x, pick)
        out.append(jnp.sum(jnp.where(col, vals, 0.0), axis=0, keepdims=True))
    return out


def forward(starts, ngain, w_in, cw, cb, dtb, alog, skip, gate, w_out, tok, cot):
    def kernel(
        starts, ngain, w_in, cw, cb, dtb, alog, skip, gate, w_out, tok, cot,
        cv, ng, stt, x0o, s0o, s1o, w0o, w1o, e1o, x1o, p1o, proj0o, proj1o, y0o, y1o, u0o, u1o, doo,
        tile, tg, tb, ta, pieces, pb, blk0, blk1, st,
        w0, w1, x0, x1, e1, part, part1, proj, yv, uv, dov, og, stat0, stat1, stb0,
        rb0, rb1, rb2, rb3, ksem, osem, lsem, ssem, rsem,
    ):
        s, z, h, x, c = place()
        hc = 2 * h + c
        q = 4 * s + hc
        greet(small_devs() + group_devs())
        net = Net(ssem, rsem)
        devs = group_devs()
        low6 = lax.broadcasted_iota(jnp.int32, (24, 128), 1) < NH
        rate = jnp.concatenate(
            [w_in[0, :, 6400:6448].astype(F32), jnp.zeros((24, 80), F32)], axis=1
        )
        for k in range(8):
            lanes = slice(k * HC, k * HC + HC)
            moved = rate if k == 0 else pltpu.roll(rate, 128 - NH * k, axis=1)
            left = [w_in[0, :, lanes], w_in[0, :, 3072 + k * HC : 3072 + k * HC + HC]]
            right = [
                w_in[0, :, 6144:6400],
                jnp.where(low6, moved, 0.0).astype(BF),
                w_out[:, lanes],
            ]
            pieces[k, 0:24, :] = jnp.concatenate(left, axis=1)
            pieces[k, 24:48, :] = jnp.concatenate(right, axis=1)
        ids = [4 * d["s"] + 2 * d["h"] + d["c"] for d in devs]
        psend = [net.make(pieces.at[k], pb.at[s, hc], dev) for k, dev in zip(ids, devs)]

        def p_send():
            for copy in psend:
                copy.start()

        def p_wait(layer):
            @pl.when(s == layer)
            def _():
                for copy in psend[0:3]:
                    copy.wait_recv()

            @pl.when(s != layer)
            def _():
                for copy in psend[3:7]:
                    copy.wait_recv()

        def block(layer, out):
            for hh in range(2):
                for cc in range(2):
                    rows = slice(24 * cc, 24 * cc + 24)
                    out[hh, rows, 0:HALF] = pb[layer, 2 * hh + cc, 0:24]
                    out[hh, rows, HALF:D] = pb[layer, 2 * hh + cc, 24:48]

        pl.when(s == 0)(p_send)
        pb[s, hc] = pieces[q]
        tile[...] = jnp.zeros_like(tile)
        tile[0:4, 0:52] = cw[0].astype(F32)
        tile[4:5, 0:52] = cb[...].astype(F32)
        tile[5:6, 0:48] = gate[...].astype(F32)
        tile[6:7, 0:24] = ngain[...].astype(F32)
        tile[7:8, 0:4] = starts[0].astype(F32)
        tile[7:8, 4:8] = starts[1].astype(F32)
        tile[8:9, 0:48] = dtb[...]
        tile[9:10, 0:48] = jnp.exp(alog[...])
        tile[10:11, 0:48] = skip[...]
        tsend = [net.send(tile, tg.at[q], dev) for dev in devs]
        tg[q] = tile[...]
        gather0 = Gather(net, blk0, w0, lsem.at[0])
        gather1 = Gather(net, blk1, w1, lsem.at[3])
        ring = RingSum(net, part, (rb0, rb1, rb2, rb3))
        spread = Spread(net, x1)
        stats0 = [net.make(stat0, stb0.at[k], dev) for k, dev in enumerate(devs)]

        def weights():
            yield 9.0
            p_wait(0)
            block(0, blk0)
            gather0.step(0)
            pl.when(s == 1)(p_send)
            for k, n in enumerate((5.0, 7.0, 21.0)):
                yield 10.0 + n
                gather0.step(k + 1)
            p_wait(1)
            block(1, blk1)
            gather1.step(0)
            yield 39.0
            gather0.step(4)
            gather1.step(1)

        def vectors():
            yield 10.0
            for copy in tsend:
                copy.wait_recv()
            for k in range(8):
                tb[z, k // 4, 8 * (k % 4) : 8 * (k % 4) + 8] = tg[k, 0:8].astype(BF)
            for n in range(4):
                v = tg[n, 7:8, :]
                first = 4 * (n // 2) + n % 2
                stt[first : first + 1] = v.astype(jnp.int32)
                stt[first + 2 : first + 3] = pltpu.roll(v, 124, axis=1).astype(jnp.int32)
            to_smem = pltpu.make_async_copy(stt, st, ksem.at[0])
            to_smem.start()
            r = tb.at[z]
            sends = [net.send(r, r, {"z": lax.rem(z + k, 4)}) for k in range(1, 4)]
            yield 14.0
            to_smem.wait()
            for copy in sends:
                copy.wait_recv()
            ta[x] = tb[...]
            r = ta.at[x]
            sends = [net.send(r, r, {"x": lax.rem(x + k, 4)}) for k in range(1, 4)]
            yield 20.0
            for copy in sends:
                copy.wait_recv()
            n = lax.broadcasted_iota(jnp.int32, (1, 640), 1)
            chan = jnp.where(n < HC, q * HC + n, 3072 - HC + n)
            gchan = q * HC + lax.broadcasted_iota(jnp.int32, (1, HC), 1)
            nchan = lax.broadcasted_iota(jnp.int32, (1, D), 1)
            head = lax.broadcasted_iota(jnp.int32, (1, HC), 1) >> 6
            cv[...] = jnp.zeros_like(cv)
            for layer in range(2):
                vals = jnp.concatenate([ta[k % 4, k // 4, layer] for k in range(16)], axis=0)
                for r, v in enumerate(place_rows(vals, range(5), 52, chan)):
                    cv[layer, r : r + 1, :] = v
                cv[layer, 5:6, 0:HC] = place_rows(vals, [5], 48, gchan)[0]
                ng[layer] = place_rows(vals, [6], 24, nchan)[0]
                back = lax.rem(128 - NH * q, 128)
                heads = pltpu.roll(tg[4 * layer, 8:16, :], back, axis=1)
                cv[layer, 7:8, 0:128] = heads[0:1]
                cv[layer, 8:9, 0:128] = heads[1:2]
                lanes = jnp.zeros((1, HC), F32)
                for k in range(NH):
                    lanes = jnp.where(head == k, heads[2:3, k : k + 1], lanes)
                cv[layer, 6:7, 0:HC] = lanes
                yield 21.0

        run(
            [
                weights(),
                vectors(),
                g_pairs(net, tok, x0, lsem.at[1], 10.0),
                g_pairs(net, cot, e1, lsem.at[2], 19.2),
            ]
        )
        x0o[...] = x0[h, s, c]
        keep = [
            pltpu.make_async_copy(src, dst, ksem.at[n])
            for n, (src, dst) in enumerate(((w0, w0o), (e1, e1o), (w1, w1o)))
        ]
        keep[0].start()
        keep[1].start()

        def saves(b, layer, proj_o, y_o, u_o):
            return [
                pltpu.make_async_copy(v.at[b], o.at[b], osem.at[layer, n, b])
                for n, (v, o) in enumerate(((proj, proj_o), (yv, y_o), (uv, u_o)))
            ]

        def more(b, p):
            return [
                pltpu.make_async_copy(v, o, osem.at[2, n, b])
                for n, (v, o) in enumerate(
                    (
                        (dov.at[b], doo.at[b]),
                        (x1.at[p], x1o.at[p]),
                        (part1.at[p], p1o.at[p]),
                    )
                )
            ]

        def first(i, carry):
            hi, mi = block_at(i, h, s, True)
            b = 2 * hi + mi
            forward_block(
                b, x0.at[hi, mi], w0, ng[0], cv.at[0], st,
                (part.at[hi, mi], stat0, proj.at[b], yv.at[b], uv.at[b], None, og),
            )
            for copy in saves(b, 0, proj0o, y0o, u0o):
                copy.start()
            when_each(i, 4, ring.step)

            @pl.when(i == 0)
            def _():
                gather1.step(2)

            return carry

        lax.fori_loop(0, 4, first, 0)
        for copy in stats0:
            copy.start()
        ring.late()
        gather1.step(3)
        acc = stat0[...]
        for k, copy in enumerate(stats0):
            copy.wait_recv()
            acc = acc + stb0[k]
        s0o[...] = acc
        for b in range(4):
            for copy in saves(b, 0, proj0o, y0o, u0o):
                copy.wait()
        x1[h, s, c] = (x0[h, s, c].astype(F32) + own_scale(s0o) * ring.total()).astype(BF)
        spread.start()
        gather1.step(4)
        keep[2].start()

        def second(i, carry):
            when_each(i, 4, spread.ready)
            hi, mi = block_at(i, h, s, False)
            b = 2 * hi + mi
            forward_block(
                b, x1.at[hi, mi], w1, ng[1], cv.at[1], st,
                (part1.at[hi, mi], stat1, proj.at[b], yv.at[b], uv.at[b], dov.at[b], og),
                e1.at[hi, mi],
            )
            for copy in saves(b, 1, proj1o, y1o, u1o) + more(b, (hi, mi)):
                copy.start()
            return carry

        lax.fori_loop(0, 4, second, 0)
        s1o[...] = stat1[...]
        for copy in keep:
            copy.wait()
        for b in range(4):
            for copy in saves(b, 1, proj1o, y1o, u1o) + more(b, (b // 2, b % 2)):
                copy.wait()
        net.finish()

    blocks = lambda cols, t: jax.ShapeDtypeStruct((4, 256, cols), t)
    big = pltpu.VMEM((4, 2, 4, 48, D), BF)
    rows = pltpu.VMEM((2, 2, 2, 128, D), BF)
    return pl.pallas_call(
        kernel,
        name="forward",
        out_shape=(
            jax.ShapeDtypeStruct((2, 16, 640), F32),
            jax.ShapeDtypeStruct((2, 1, D), F32),
            jax.ShapeDtypeStruct((8, 128), jnp.int32),
            CHUNK,
            jax.ShapeDtypeStruct((8, 128), F32),
            jax.ShapeDtypeStruct((16, 128), F32),
            GATHERED,
            GATHERED,
            CHUNKS,
            CHUNKS,
            CHUNKS,
            blocks(CIN, F32),
            blocks(CIN, F32),
            blocks(HC, F32),
            blocks(HC, F32),
            blocks(D, BF),
            blocks(D, BF),
            blocks(HC, F32),
        ),
        in_specs=[VM] * 12,
        out_specs=(VM,) * 6 + (ANY,) * 12,
        scratch_shapes=[
            pltpu.VMEM((16, 128), F32),
            pltpu.VMEM((8, 16, 128), F32),
            pltpu.VMEM((4, 2, 32, 128), BF),
            pltpu.VMEM((4, 4, 2, 32, 128), BF),
            pltpu.VMEM((8, 48, HALF), BF),
            pltpu.VMEM((2, 4, 48, HALF), BF),
            pltpu.VMEM((2, 48, D), BF),
            pltpu.VMEM((2, 48, D), BF),
            pltpu.SMEM((8, 128), jnp.int32),
            big,
            big,
            rows,
            rows,
            rows,
            rows,
            rows,
            pltpu.VMEM((4, 256, CIN), F32),
            pltpu.VMEM((4, 256, HC), F32),
            pltpu.VMEM((4, 256, D), BF),
            pltpu.VMEM((4, 256, HC), F32),
            pltpu.VMEM((256, HC), BF),
            pltpu.VMEM((8, 128), F32),
            pltpu.VMEM((16, 128), F32),
            pltpu.VMEM((7, 8, 128), F32),
        ]
        + ring_scratch()
        + [
            pltpu.SemaphoreType.DMA((3,)),
            pltpu.SemaphoreType.DMA((3, 3, 4)),
            pltpu.SemaphoreType.DMA((4,)),
        ]
        + sems(100),
        compiler_params=params(1),
    )(starts, ngain, w_in, cw, cb, dtb, alog, skip, gate, w_out, tok, cot)


def results(rec, vec, heads, ig0, so1, got, eall, xall, w_in, ngain):
    def kernel(rec, vec, heads, ig0, so1, got, eall, xall, w_in, ngain, so, ig, gng, gwi, gcw, gcb, gdt, gal, gsk, ggg, gwo, buf, sem):
        s, z, h, x, c = place()
        dp = ((z * 2 + h) * 4 + x) * 2 + c
        copies = [
            pltpu.make_async_copy(src.at[h, :, c], buf.at[n], sem.at[n])
            for n, src in enumerate((eall, xall))
        ]
        for copy in copies:
            copy.start()
        tail = jnp.zeros((24, 256), F32)
        rate = jnp.zeros((24, 128), F32)
        lane = lax.broadcasted_iota(jnp.int32, (24, 128), 1)
        dots = jnp.zeros((24, 1), F32)

        def put(lanes, v):
            gwi[0, :, lanes] = v
            return jnp.sum(w_in[0, :, lanes].astype(F32) * v, axis=1, keepdims=True)

        for k in range(8):
            lanes = slice(k * HC, k * HC + HC)
            dots = dots + put(lanes, rec[k, 0:24, 0:HC].astype(F32))
            lanes = slice(3072 + k * HC, 3072 + k * HC + HC)
            dots = dots + put(lanes, rec[k, 0:24, HC:HALF].astype(F32))
            tail = tail + rec[k, 24:48, 0:256].astype(F32)
            part = jnp.where(lane < NH, rec[k, 24:48, 256:384].astype(F32), 0.0)
            rate = rate + (part if k == 0 else pltpu.roll(part, NH * k, axis=1))
            gwo[:, k * HC : k * HC + HC] = rec[k, 24:48, HC:HALF].astype(F32)
        dots = dots + put(slice(6144, 6400), tail)
        dots = dots + put(slice(6400, 6448), rate[:, 0:48])
        i = lax.broadcasted_iota(jnp.int32, (24, 24), 0)
        j = lax.broadcasted_iota(jnp.int32, (24, 24), 1)
        gng[...] = jnp.sum(jnp.where(i == j, dots, 0.0), axis=0, keepdims=True) / ngain[...].astype(F32)

        def exact(a, b):
            return jnp.dot(a, b, precision=HIGH, preferred_element_type=F32)

        def window(m):
            ch = lax.broadcasted_iota(jnp.int32, (3328, 128), 0)
            j = lax.broadcasted_iota(jnp.int32, (3328, 128), 1)
            return exact(vec[...], (ch == m * dp + j).astype(F32))

        conv = window(52)
        gcw[0] = conv[0:4, 0:52]
        gcb[...] = conv[4:5, 0:52]
        ggg[...] = window(48)[5:6, 0:48]
        ch = lax.broadcasted_iota(jnp.int32, (HC, 128), 0) >> 6
        j = lax.broadcasted_iota(jnp.int32, (HC, 128), 1)
        skip = exact(heads[:, 256:640], (ch == j).astype(F32))
        row = lax.broadcasted_iota(jnp.int32, (1, 128), 1)
        for out, v in ((gdt, heads[:, 0:128]), (gal, heads[:, 128:256]), (gsk, skip)):
            acc = jnp.zeros((1, 128), F32)
            for k in range(8):
                part = jnp.where(row < NH, v[k : k + 1], 0.0)
                acc = acc + (part if k == 0 else pltpu.roll(part, NH * k, axis=1))
            out[...] = acc[:, 0:48]
        for copy in copies:
            copy.wait()

        @pl.when(s == 0)
        def _():
            ig[0, 0] = ig0[...].astype(F32)
            ig[0, 1] = got[...].astype(F32)
            so[0] = buf[1]

        @pl.when(s == 1)
        def _():
            ig[0] = buf[0].astype(F32)
            so[0, 0] = got[...]
            so[0, 1] = so1[...]

    f = lambda *shape: jax.ShapeDtypeStruct(shape, F32)
    return pl.pallas_call(
        kernel,
        name="results",
        out_shape=(
            jax.ShapeDtypeStruct((1, 2, 128, D), BF),
            f(1, 2, 128, D),
            f(1, 24),
            f(1, 24, 6448),
            f(1, 4, 52),
            f(1, 52),
            f(1, 48),
            f(1, 48),
            f(1, 48),
            f(1, 48),
            f(24, 3072),
        ),
        in_specs=[VM] * 6 + [ANY] * 2 + [VM] * 2,
        out_specs=(VM,) * 11,
        scratch_shapes=[pltpu.VMEM((2, 2, 128, D), BF), pltpu.SemaphoreType.DMA((2,))],
        compiler_params=pltpu.CompilerParams(vmem_limit_bytes=VLIM),
    )(rec, vec, heads, ig0, so1, got, eall, xall, w_in, ngain)


def body(
    tokens,
    cotangent,
    starts,
    norm_gain,
    w_in,
    conv_weight,
    conv_bias,
    dt_bias,
    a_log,
    skip_d,
    gate_gain,
    w_out,
):
    cv, ng, st, x0own, stat0, stat1, w0, w1, call, xall, part1, proj0, proj1, y0, y1, u0, u1, do1 = forward(
        starts,
        norm_gain,
        w_in,
        conv_weight,
        conv_bias,
        dt_bias,
        a_log,
        skip_d,
        gate_gain,
        jnp.transpose(w_out[0]),
        tokens,
        cotangent,
    )
    eall, _, rec, vec, hd, ig0, so1, got = two_backward(
        st, w1, w0, ng, cv, call, xall, x0own, proj1, proj0, y1, y0, do1, u1, u0, part1, stat1, stat0
    )
    outs = results(rec, vec, hd, ig0, so1, got, eall, xall, w_in, norm_gain)
    return outs[:10] + (jnp.transpose(outs[10])[None],)


def solution(mesh):
    inner = Mesh(mesh.devices.reshape(2, 4, 2, 4, 2), ("s", "z", "h", "x", "c"))
    dp = ("z", "h", "x", "c")
    in_specs = (
        P(None, dp, None),
        P(None, dp, None),
        P(None, dp, None),
        P("s", dp),
        P("s", dp, None),
        P("s", None, dp),
        P("s", dp),
        P("s", None),
        P("s", None),
        P("s", None),
        P("s", dp),
        P("s", None, dp),
    )
    out_specs = (
        P("s", None, dp, None),
        P("s", None, dp, None),
        P("s", dp),
        P("s", dp, None),
        P("s", None, dp),
        P("s", dp),
        P("s", None),
        P("s", None),
        P("s", None),
        P("s", dp),
        P("s", None, dp),
    )
    return jax.shard_map(body, mesh=inner, in_specs=in_specs, out_specs=out_specs, check_vma=False)
```

```python
import jax
import jax.numpy as jnp
from jax import lax
from jax.experimental import pallas as pl
from jax.experimental.pallas import tpu as pltpu
from jax.sharding import Mesh, PartitionSpec as P

EPS = 1e-05
BF = jnp.bfloat16
F32 = jnp.float32
HIGH = lax.Precision.HIGHEST
D = 1536
CIN = 1152
HC = 384
NH = 6
RT = 1024
HALF = 768
ANY = pl.BlockSpec(memory_space=pl.ANY)
VM = pl.BlockSpec(memory_space=pltpu.VMEM)
SM = pl.BlockSpec(memory_space=pltpu.SMEM)
VLIM = 59 * 1024 * 1024


class Net:
    def __init__(self, ssem, rsem):
        self.ssem, self.rsem, self.n, self.all = ssem, rsem, 0, []

    def make(self, src, dst, dev):
        i = self.n
        self.n += 1
        assert i < self.ssem.shape[0]
        copy = pltpu.make_async_remote_copy(
            src_ref=src,
            dst_ref=dst,
            send_sem=self.ssem.at[i],
            recv_sem=self.rsem.at[i],
            device_id=dev,
            device_id_type=pl.DeviceIdType.MESH,
        )
        self.all.append(copy)
        return copy

    def send(self, src, dst, dev):
        copy = self.make(src, dst, dev)
        copy.start()
        return copy

    def sent(self, copy):
        copy.wait_send()
        self.all = [v for v in self.all if v is not copy]

    def finish(self):
        for copy in self.all:
            copy.wait_send()


def place():
    s, z, h, x, c = (lax.axis_index(a) for a in ("s", "z", "h", "x", "c"))
    return s, z, h, x, c


def ring(i):
    return lax.rem(i + 1, 4), lax.rem(i + 3, 4), lax.rem(i + 2, 4)


def greet(devs):
    barrier = pltpu.get_barrier_semaphore()
    for dev in devs:
        pl.semaphore_signal(barrier, inc=1, device_id=dev, device_id_type=pl.DeviceIdType.MESH)
    pl.semaphore_wait(barrier, len(devs))


def zx_devs():
    s, z, h, x, c = place()
    zr, zl, _ = ring(z)
    xr, xl, _ = ring(x)
    return [{"z": zr}, {"z": zl}, {"x": xr}, {"x": xl}]


def ydev(y):
    return {"h": y // 2, "s": lax.rem(y, 2)}


def y_devs():
    s, z, h, x, c = place()
    yr, yl, _ = ring(2 * h + s)
    return [ydev(yr), ydev(yl), {"c": 1 - c}]


def group_devs():
    s, z, h, x, c = place()
    out = []
    for k in range(1, 8):
        out.append(
            {
                "s": 1 - s if k & 4 else s,
                "h": 1 - h if k & 2 else h,
                "c": 1 - c if k & 1 else c,
            }
        )
    return out


LAT = 1.7


def inter(gens):
    gens = [[0.0, g] for g in gens]
    while gens:
        item = min(gens, key=lambda v: v[0])
        if item[0] > 0:
            yield item[0]
        try:
            item[0] = next(item[1])
        except StopIteration:
            gens.remove(item)


def run(gens):
    for _ in inter(gens):
        pass


def g_pairs(net, own, out, lsem, t0):
    s, z, h, x, c = place()
    outer, inner, sib = {"h": 1 - h, "s": 1 - s}, {"s": 1 - s}, {"c": 1 - c}
    first = []
    for k in range(2):
        rows = pl.ds(64 * k, 64)
        first.append(net.send(own.at[s, rows], out.at[h, s, c, rows], outer))
    local = pltpu.make_async_copy(own, out.at[h, :, c], lsem)
    local.start()
    c0 = net.send(own, out.at[h, :, c], sib)
    yield t0 + 4.6 + LAT
    second = []
    for k in range(2):
        first[k].wait_recv()
        r = out.at[1 - h, 1 - s, c, pl.ds(64 * k, 64)]
        second.append(net.send(r, r, inner))
        if k == 0:
            yield t0 + 9.2 + LAT
    r = out.at[1 - h, 1 - s, c]
    c1 = net.send(r, r, sib)
    yield t0 + 14 + LAT
    for copy in second:
        copy.wait_recv()
    r = out.at[1 - h, s, c]
    c2 = net.send(r, r, sib)
    yield t0 + 16 + LAT
    for copy in (c0, c1, c2):
        copy.wait_recv()
    local.wait()


def g_small(net, mine, bz, bx, total, t0=0.0):
    s, z, h, x, c = place()
    sends = [net.send(mine, bz.at[z], {"z": lax.rem(z + k, 4)}) for k in range(1, 4)]
    bz[z] = mine[...]
    yield t0 + 4.0
    for copy in sends:
        copy.wait_recv()
    bx[x] = bz[0] + bz[1] + bz[2] + bz[3]
    r = bx.at[x]
    sends = [net.send(r, r, {"x": lax.rem(x + k, 4)}) for k in range(1, 4)]
    yield t0 + 10.0
    for copy in sends:
        copy.wait_recv()
    total[...] = bx[0] + bx[1] + bx[2] + bx[3]


def small_scratch():
    return [pltpu.VMEM((4, 2, 8, 640), F32), pltpu.VMEM((4, 2, 8, 640), F32)]


def small_devs():
    s, z, h, x, c = place()
    return [{"z": lax.rem(z + k, 4)} for k in range(1, 4)] + [
        {"x": lax.rem(x + k, 4)} for k in range(1, 4)
    ]


def g_share(net, sums, got, vec, heads):
    s, z, h, x, c = place()
    me = (2 * s + h) * 2 + c
    sends = []
    for dev in group_devs():
        sends.append(net.send(sums.at[dev["s"]], got.at[me], dev))
    got[me] = sums[s]
    yield 20.0
    for copy in sends:
        copy.wait_recv()
    vec[...] = jnp.zeros_like(vec)
    tail = jnp.zeros((5, 256), F32)
    for q in range(8):
        lanes = slice(q * HC, q * HC + HC)
        vec[0:5, lanes] = got[q, 0:5, 0:HC]
        vec[5:6, lanes] = got[q, 5:6, 0:HC]
        tail = tail + got[q, 0:5, HC:640]
        heads[q : q + 1, 0:256] = got[q, 5:6, HC:640]
        heads[q : q + 1, 256:640] = got[q, 6:7, 0:HC]
    vec[0:5, 3072:3328] = tail


def params(cid):
    return pltpu.CompilerParams(
        collective_id=cid, has_side_effects=True, vmem_limit_bytes=VLIM
    )


def sems(n):
    return [pltpu.SemaphoreType.DMA((n,)), pltpu.SemaphoreType.DMA((n,))]


GATHERED = jax.ShapeDtypeStruct((4, 2, 4, 48, D), BF)
CHUNKS = jax.ShapeDtypeStruct((2, 2, 2, 128, D), BF)
SMALL = jax.ShapeDtypeStruct((8, 640), F32)
CHUNK = jax.ShapeDtypeStruct((128, D), BF)


def row_to_col(row):
    i = lax.broadcasted_iota(jnp.int32, (128, 128), 0)
    j = lax.broadcasted_iota(jnp.int32, (128, 128), 1)
    return jnp.sum(jnp.where(i == j, row, 0.0), axis=1, keepdims=True)


def col_to_row(col):
    i = lax.broadcasted_iota(jnp.int32, (128, 128), 0)
    j = lax.broadcasted_iota(jnp.int32, (128, 128), 1)
    return jnp.sum(jnp.where(i == j, col, 0.0), axis=0, keepdims=True)


def own_scale(total):
    s, z, h, x, c = place()
    row = total[pl.ds((2 * h + s) * 2 + c, 1), :]
    return lax.rsqrt(row_to_col(row) * (1.0 / 3072) + EPS)


def norm_back(v, x, e, ng):
    xf = x.astype(F32)
    vg = v * ng[...]
    r = lax.rsqrt(jnp.mean(xf * xf, axis=-1, keepdims=True) + EPS)
    dot = jnp.mean(xf * vg, axis=-1, keepdims=True)
    return e.astype(F32) + r * vg - xf * (r * r * r * dot)


def nt(a, b):
    return lax.dot_general(a, b, (((1,), (1,)), ((), ())), preferred_element_type=F32)


def tn(a, b):
    return lax.dot_general(a, b, (((0,), (0,)), ((), ())), preferred_element_type=F32)


def iotas():
    i = lax.broadcasted_iota(jnp.int32, (128, 128), 0)
    j = lax.broadcasted_iota(jnp.int32, (128, 128), 1)
    return i, j


def seg_of(firsts, places):
    seg = jnp.full(places.shape, -1, jnp.int32)
    for k in range(4):
        seg = seg + (firsts[k] <= places).astype(jnp.int32)
    return seg


def masks(st, chunk):
    i, j = iotas()
    firsts = [st[chunk, k] for k in range(4)]
    seg = seg_of(firsts, i)
    keep = jnp.logical_and(seg == seg_of(firsts, j), i >= j)
    valid = [None] + [(seg_of(firsts, i - k) == seg).astype(F32) for k in range(1, 4)]
    return keep, valid


def conv_tile(xt, cv, t, valid):
    lanes = slice(128 * t, 128 * t + 128)
    pre = cv[4:5, lanes] + cv[3:4, lanes] * xt
    moved = [xt]
    for k in range(1, 4):
        m = pltpu.roll(xt, k, axis=0) * valid[k]
        moved.append(m)
        pre = pre + cv[3 - k : 4 - k, lanes] * m
    return pre, moved


def rates(rt, cv):
    i, j = iotas()
    head = j < NH
    v = rt + cv[7:8, 0:128]
    dt = jnp.where(head, jnp.maximum(v, 0.0) + jnp.log1p(jnp.exp(-jnp.abs(v))), 0.0)
    lower = (i >= j).astype(F32)
    cum = jnp.dot(
        lower, -dt * cv[8:9, 0:128], precision=HIGH, preferred_element_type=F32
    )
    return v, dt, cum


def half_masks():
    _, j = iotas()
    return j < 64


def split_pair(v, low):
    zero = jnp.zeros_like(v)
    return jnp.concatenate([jnp.where(low, v, zero), jnp.where(low, zero, v)], axis=0)


def decay_of(keep, cum, cum_t, h):
    spread = jnp.where(keep, cum[:, h : h + 1] - cum_t[h : h + 1, :], -1e30)
    return jnp.exp(spread)


class Gather:
    def __init__(self, net, blk, out, lsem):
        s, z, h, x, c = place()
        self.local = pltpu.make_async_copy(blk, out.at[z, :, x], lsem)
        every = slice(None)
        self.parts = []
        for lanes, i, axis_i, j, axis_j, pick in (
            (pl.ds(0, HALF), x, "x", z, "z", lambda i, j, p: (j, p, i)),
            (pl.ds(HALF, HALF), z, "z", x, "x", lambda i, j, p: (i, p, j)),
        ):
            ir, il, _ = ring(i)
            jr, jl, _ = ring(j)

            def at(i, j, p, pick=pick, lanes=lanes):
                return out.at[pick(i, j, p) + (every, lanes)]

            def make(i, j, p, dev, src=None):
                ref = at(i, j, p)
                return net.make(ref if src is None else src, ref, dev)

            own = blk.at[:, :, lanes]
            first, second = ({axis_i: ir}, {axis_i: il}), ({axis_j: jr}, {axis_j: jl})
            self.parts.append(
                [
                    (make(i, j, every, first[0], own), make(i, j, every, first[1], own)),
                    (make(il, j, 0, first[0]), make(ir, j, 1, first[1])),
                    (make(every, j, every, second[0]), make(every, j, every, second[1])),
                    (make(every, jl, 0, second[0]), make(every, jr, 1, second[1])),
                ]
            )

    def step(self, k):
        if k == 0:
            self.local.start()
        if k == 2:
            self.local.wait()
        for part in self.parts:
            for n in range(2):
                if k > 0:
                    part[k - 1][n].wait_recv()
                if k < 4 and k != 2:
                    part[k][n].start()
            if k == 2:
                part[2][0].start()
                part[2][1].start()


class RingSum:
    def __init__(self, net, part, bufs):
        self.part = part
        self.cb, self.sb, self.b1, self.b2 = bufs
        s, z, h, x, c = place()
        self.c = c
        sib = {"c": 1 - c}
        outer, inner = {"h": 1 - h, "s": 1 - s}, {"s": 1 - s}
        self.units = [(1 - h, s), (1 - h, 1 - s), (h, 1 - s), (h, s)]
        self.core = [
            net.make(part.at[hh, mm, 1 - c], self.cb.at[k], sib)
            for k, (hh, mm) in enumerate(self.units)
        ]
        sb, b1, b2 = self.sb, self.b1, self.b2
        lo, hi = pl.ds(0, 64), pl.ds(64, 64)
        self.far = [
            net.make(sb.at[0, lo], b1.at[0], outer),
            net.make(sb.at[0, hi], b1.at[1], inner),
        ]
        self.direct = [
            net.make(sb.at[1, lo], b2.at[0, lo], outer),
            net.make(sb.at[2, hi], b2.at[1, hi], inner),
        ]
        self.summed = [
            net.make(sb.at[1, hi], b2.at[0, hi], outer),
            net.make(sb.at[2, lo], b2.at[1, lo], inner),
        ]

    def add(self, k):
        self.core[k].wait_recv()
        hh, mm = self.units[k]
        self.sb[k] = (self.part[hh, mm, self.c].astype(F32) + self.cb[k].astype(F32)).astype(BF)

    def step(self, k):
        self.core[k].start()
        if k == 1:
            self.add(0)
            self.far[0].start()
            self.far[1].start()
        if k == 2:
            self.add(1)
            self.direct[0].start()
            self.add(2)
            self.direct[1].start()

    def all_adds(self):
        self.add(0)
        self.far[0].start()
        self.far[1].start()
        self.add(1)
        self.direct[0].start()
        self.add(2)
        self.direct[1].start()

    def late(self):
        lo, hi = slice(0, 64), slice(64, 128)
        self.far[1].wait_recv()
        self.sb[1, hi] = (self.sb[1, hi].astype(F32) + self.b1[1].astype(F32)).astype(BF)
        self.summed[0].start()
        self.far[0].wait_recv()
        self.sb[2, lo] = (self.sb[2, lo].astype(F32) + self.b1[0].astype(F32)).astype(BF)
        self.summed[1].start()

    def total(self):
        self.core[3].wait_recv()
        for copy in self.direct + self.summed:
            copy.wait_recv()
        hh, mm = self.units[3]
        total = self.part[hh, mm, self.c].astype(F32) + self.cb[3].astype(F32)
        return total + self.b2[0].astype(F32) + self.b2[1].astype(F32)


def ring_scratch():
    return [
        pltpu.VMEM((4, 128, D), BF),
        pltpu.VMEM((3, 128, D), BF),
        pltpu.VMEM((2, 64, D), BF),
        pltpu.VMEM((2, 128, D), BF),
    ]


class Spread:
    def __init__(self, net, out):
        s, z, h, x, c = place()
        sib = {"c": 1 - c}
        outer, inner = {"h": 1 - h, "s": 1 - s}, {"s": 1 - s}
        lo, hi = pl.ds(0, 64), pl.ds(64, 64)
        own, far = out.at[h, s, c], out.at[1 - h, s, c]
        from_outer, from_inner = out.at[1 - h, 1 - s, c], out.at[h, 1 - s, c]
        self.mine = own
        self.ring = [net.make(own, own, outer), net.make(own, own, inner)]
        self.hand = [
            net.make(from_inner.at[lo], from_inner.at[lo], outer),
            net.make(from_outer.at[hi], from_outer.at[hi], inner),
        ]
        self.sib = [net.make(r, r, sib) for r in (own, from_inner, from_outer, far)]

    def start(self):
        self.ring[0].start()
        self.ring[1].start()
        self.sib[0].start()

    def ready(self, k):
        if k == 1:
            self.ring[1].wait_recv()
            self.hand[0].start()
            self.sib[1].start()
            self.ring[0].wait_recv()
            self.hand[1].start()
            self.sib[2].start()
        if k == 3:
            self.hand[0].wait_recv()
            self.hand[1].wait_recv()
            self.sib[3].start()
        self.sib[k].wait_recv()


def when_each(i, n, step):
    for k in range(n):
        pl.when(i == k)(lambda k=k: step(k))


def block_at(i, h, s, far_first):
    k = i if far_first else 3 - i
    return lax.rem(h + 1 + k // 2, 2), lax.rem(s + (k + 1) // 2, 2)


def forward_block(b, x, w, ng, cv, st, refs, e=None):
    part, stat, proj, yout, uout, doo, og = refs
    with_do = e is not None
    xf = x[...].reshape(256, D).astype(F32)
    r = lax.rsqrt(jnp.mean(xf * xf, axis=-1, keepdims=True) + EPS)
    u = (xf * r * ng).astype(BF)
    uout[...] = u
    proj[...] = jnp.dot(u, w[:, :, :, :, 0:CIN].reshape(D, CIN), preferred_element_type=F32)
    if with_do:
        doo[...] = jnp.dot(
            e[...].reshape(256, D),
            w[:, :, :, :, CIN:D].reshape(D, HC),
            preferred_element_type=F32,
        )
    low = half_masks()
    for m in range(2):
        rows = slice(128 * m, 128 * m + 128)
        chunk = b * 2 + m
        keep, valid = masks(st, chunk)
        act = []
        for t in range(5):
            pre, _ = conv_tile(proj[rows, HC + 128 * t : HC + 128 * t + 128], cv, t, valid)
            act.append((pre * jax.nn.sigmoid(pre)).astype(BF))
        _, dt, cum = rates(proj[rows, RT:CIN], cv)
        cum_t, dt_t = jnp.transpose(cum), jnp.transpose(dt)
        gram = nt(act[4], act[3])
        gsum = jnp.zeros((128, 1), F32)
        tsum = jnp.zeros((128, 1), F32)
        for t in range(3):
            lanes = slice(128 * t, 128 * t + 128)
            mixes = []
            for h in (2 * t, 2 * t + 1):
                dec = decay_of(keep, cum, cum_t, h)
                mixes.append((gram * dec * dt_t[h : h + 1, :]).astype(BF))
            y = jnp.dot(
                jnp.concatenate(mixes, axis=1),
                split_pair(act[t], low),
                preferred_element_type=F32,
            )
            y = y + cv[6:7, lanes] * act[t].astype(F32)
            yout[rows, lanes] = y
            zt = proj[rows, lanes]
            g = y * (zt * jax.nn.sigmoid(zt))
            gsum = gsum + jnp.sum(g * g, axis=1, keepdims=True)
            gain = cv[5:6, lanes]
            og[rows, lanes] = (g * gain).astype(BF)
            if with_do:
                tsum = tsum + jnp.sum(g * gain * doo[rows, lanes], axis=1, keepdims=True)
        stat[pl.ds(chunk, 1), :] = col_to_row(gsum)
        if with_do:
            stat[pl.ds(chunk + 8, 1), :] = col_to_row(tsum)
    out = nt(og[...], w[:, :, :, :, CIN:D].reshape(D, HC))
    part[...] = out.astype(BF).reshape(2, 128, D)


class Scatter:
    def __init__(self, net, grads, bufs, out):
        s, z, h, x, c = place()
        self.out = out
        self.parts = []
        for k, (i, axis_i, j, axis_j) in enumerate(((z, "z", x, "x"), (x, "x", z, "z"))):
            lanes = pl.ds(k * HALF, HALF)
            b1, b2, t, sums, b3, b4, t2 = [b.at[k] for b in bufs]
            ir, il, io = ring(i)
            jr, jl, jo = ring(j)
            if k == 0:
                unit = lambda i, p, lanes=lanes: grads.at[i, p, :, :, lanes]
            else:
                unit = lambda i, p, lanes=lanes: grads.at[:, p, i, :, lanes]
            right, left = {axis_i: ir}, {axis_i: il}
            part = dict(unit=unit, bufs=(b1, b2, t, sums, b3, b4, t2), i=i, j=j)
            part.update(ir=ir, il=il, jr=jr, jl=jl, jo=jo, k=k)
            part["far"] = [
                net.make(unit(io, 0), b1.at[0], right),
                net.make(unit(io, 1), b1.at[1], left),
            ]
            part["near"] = [
                net.make(unit(ir, 1), b2.at[0, 1], right),
                net.make(unit(il, 0), b2.at[1, 0], left),
                net.make(t.at[0], b2.at[0, 0], right),
                net.make(t.at[1], b2.at[1, 1], left),
            ]
            right, left = {axis_j: jr}, {axis_j: jl}
            part["far2"] = [
                net.make(sums.at[0, jo], b3.at[0], right),
                net.make(sums.at[1, jo], b3.at[1], left),
            ]
            part["near2"] = [
                net.make(sums.at[1, jr], b4.at[0, 1], right),
                net.make(sums.at[0, jl], b4.at[1, 0], left),
                net.make(t2.at[0], b4.at[0, 0], right),
                net.make(t2.at[1], b4.at[1, 1], left),
            ]
            self.parts.append(part)

    def start(self, k):
        for copy in self.parts[k]["far"]:
            copy.start()

    def direct(self, k):
        self.parts[k]["near"][0].start()
        self.parts[k]["near"][1].start()

    def summed(self, k):
        v = self.parts[k]
        b1, b2, t, sums, b3, b4, t2 = v["bufs"]
        for p, near in ((0, v["ir"]), (1, v["il"])):
            v["far"][p].wait_recv()
            for n in range(4):
                t[p, n] = (v["unit"](near, p)[n].astype(F32) + b1[p, n].astype(F32)).astype(BF)
            v["near"][2 + p].start()

    def total(self, v, p, n):
        b2 = v["bufs"][1]
        return (
            v["unit"](v["i"], p)[n].astype(F32)
            + b2[0, p, n].astype(F32)
            + b2[1, p, n].astype(F32)
        )

    def second(self, k):
        v = self.parts[k]
        sums = v["bufs"][3]
        for copy in v["near"]:
            copy.wait_recv()
        for copy, p, n in (
            (v["far2"][0], 0, v["jo"]),
            (v["far2"][1], 1, v["jo"]),
            (v["near2"][0], 1, v["jr"]),
            (v["near2"][1], 0, v["jl"]),
        ):
            sums[p, n] = self.total(v, p, n).astype(BF)
            copy.start()
        for p, n in ((0, v["jr"]), (1, v["jl"]), (0, v["j"]), (1, v["j"])):
            sums[p, n] = self.total(v, p, n).astype(BF)

    def second_summed(self, k):
        v = self.parts[k]
        b1, b2, t, sums, b3, b4, t2 = v["bufs"]
        for p, near in ((0, v["jr"]), (1, v["jl"])):
            v["far2"][p].wait_recv()
            t2[p] = (sums[p, near].astype(F32) + b3[p].astype(F32)).astype(BF)
            v["near2"][2 + p].start()

    def finish(self, k):
        v = self.parts[k]
        sums, b4 = v["bufs"][3], v["bufs"][5]
        for copy in v["near2"]:
            copy.wait_recv()
        for p in range(2):
            total = sums[p, v["j"]].astype(F32) + b4[0, p].astype(F32) + b4[1, p].astype(F32)
            self.out[p, :, k * HALF : (k + 1) * HALF] = total.astype(BF)


def scatter_scratch():
    return [
        pltpu.VMEM((2, 2, 4, 48, HALF), BF),
        pltpu.VMEM((2, 2, 2, 4, 48, HALF), BF),
        pltpu.VMEM((2, 2, 4, 48, HALF), BF),
        pltpu.VMEM((2, 2, 4, 48, HALF), BF),
        pltpu.VMEM((2, 2, 48, HALF), BF),
        pltpu.VMEM((2, 2, 2, 48, HALF), BF),
        pltpu.VMEM((2, 2, 48, HALF), BF),
    ]


def weight_tile(k, half, u, e, dproj, o, grads):
    cols = pl.ds(pl.multiple_of(k * 384, 128), 384)
    rows = 1024
    ut = u[:, :, cols].reshape(rows, 384)
    if half == 0:
        a = tn(ut, dproj[:, :, 0:HALF].reshape(rows, HALF))
        grads[k, :, :, :, 0:HALF] = a.astype(BF).reshape(2, 4, 48, HALF)
        return
    a = tn(ut, dproj[:, :, HALF:CIN].reshape(rows, CIN - HALF))
    grads[k, :, :, :, HALF:CIN] = a.astype(BF).reshape(2, 4, 48, CIN - HALF)
    a = tn(e[:, :, :, :, cols].reshape(rows, 384), o[...].reshape(rows, HC))
    grads[k, :, :, :, CIN:D] = a.astype(BF).reshape(2, 4, 48, HC)


def backward_block(b, e, w, cv, st, stat, dots, refs):
    proj, yin, do, dproj, oo, part, sm = refs
    if dots is not None:
        do[...] = jnp.dot(
            e[...].reshape(256, D),
            w[:, :, :, :, CIN:D].reshape(D, HC),
            preferred_element_type=F32,
        )
    low = half_masks()
    i, j = iotas()
    upper = (j >= i).astype(F32)

    def add(row, lanes, v):
        sm[row : row + 1, lanes] += jnp.sum(v, axis=0, keepdims=True)

    for m in range(2):
        rows = slice(128 * m, 128 * m + 128)
        chunk = b * 2 + m
        keep, valid = masks(st, chunk)
        pres, moves, act = [], [], []
        for t in range(5):
            pre, moved = conv_tile(proj[rows, HC + 128 * t : HC + 128 * t + 128], cv, t, valid)
            pres.append(pre)
            moves.append(moved)
            act.append((pre * jax.nn.sigmoid(pre)).astype(BF))
        v, dt, cum = rates(proj[rows, RT:CIN], cv)
        cum_t, dt_t = jnp.transpose(cum), jnp.transpose(dt)
        gram = nt(act[4], act[3])
        r = lax.rsqrt(row_to_col(stat[pl.ds(chunk, 1), :]) * (1.0 / 3072) + EPS)
        if dots is not None:
            k = r * r * row_to_col(dots[chunk, 0:1, :]) * (1.0 / 3072)
        else:
            k = r * r * r * row_to_col(stat[pl.ds(chunk + 8, 1), :]) * (1.0 / 3072)
        dact = []
        dgram = jnp.zeros((128, 128), F32)
        dcum = jnp.zeros((128, 128), F32)
        col_rows = []
        for t in range(3):
            lanes = slice(128 * t, 128 * t + 128)
            zt, y, dot_ = proj[rows, lanes], yin[rows, lanes], do[rows, lanes]
            gain = cv[5:6, lanes]
            sig = jax.nn.sigmoid(zt)
            sz = zt * sig
            g = y * sz
            oo[rows, lanes] = (g * r * gain).astype(BF)
            add(5, lanes, dot_ * g * r)
            dg = r * (dot_ * gain) - g * k
            dproj[rows, lanes] = (dg * y * (sig + sz * (1.0 - sig))).astype(BF)
            dy = (dg * sz).astype(BF)
            dyf = dy.astype(F32)
            xs = act[t]
            add(6, lanes, dyf * xs.astype(F32))
            dy2 = split_pair(dy, low)
            dmix2 = nt(dy2, xs)
            mixes = []
            for q in range(2):
                h = 2 * t + q
                dec = decay_of(keep, cum, cum_t, h)
                dt_row = dt_t[h : h + 1, :]
                pm = gram * dec
                mixes.append((pm * dt_row).astype(BF))
                dmix = dmix2[128 * q : 128 * q + 128]
                dgram = dgram + dmix * (dec * dt_row)
                vm = dmix * pm
                col_rows.append(jnp.sum(vm, axis=0, keepdims=True))
                rsum = jnp.sum(vm * dt_row, axis=1, keepdims=True)
                dcum = dcum + jnp.where(j == h, rsum, 0.0)
            dxs = tn(jnp.concatenate(mixes, axis=0), dy2)
            dact.append(dxs + cv[6:7, lanes] * dyf)
        dgl = dgram.astype(BF)
        dact.append(tn(dgl, act[4]))
        dact.append(jnp.dot(dgl, act[3], preferred_element_type=F32))
        ddt = jnp.transpose(
            jnp.concatenate(col_rows + [jnp.zeros((128 - NH, 128), F32)], axis=0)
        )
        dcum = dcum - ddt * dt
        dla = jnp.dot(upper, dcum, precision=HIGH, preferred_element_type=F32)
        nexp = -cv[8:9, 0:128]
        drate = (ddt + dla * nexp) * jax.nn.sigmoid(v)
        drate = jnp.where(j < NH, drate, 0.0)
        add(5, slice(HC, HC + 128), drate)
        add(5, slice(HC + 128, 640), dla * dt * nexp)
        dproj[rows, RT:CIN] = drate.astype(BF)
        for t in range(5):
            lanes = slice(128 * t, 128 * t + 128)
            pre = pres[t]
            sp = jax.nn.sigmoid(pre)
            dpre = dact[t] * (sp + pre * sp * (1.0 - sp))
            add(4, lanes, dpre)
            add(3, lanes, dpre * moves[t][0])
            dx = cv[3:4, lanes] * dpre
            for n in range(1, 4):
                add(3 - n, lanes, dpre * moves[t][n])
                dx = dx + cv[3 - n : 4 - n, lanes] * pltpu.roll(
                    dpre * valid[n], 128 - n, axis=0
                )
            dproj[rows, HC + 128 * t : HC + 128 * t + 128] = dx.astype(BF)
    out = nt(dproj[...], w[:, :, :, :, 0:CIN].reshape(D, CIN))
    part[...] = out.astype(BF).reshape(2, 128, D)


def two_backward(
    st, w1, w0, ng, cv, call, xall, x0own, proj1, proj0, y1, y0, do1, u1, u0, part1, stat1, stat0
):
    def kernel(
        st, w1h, w0h, ng, cv, callh, xallh, x0h, proj1h, proj0h, y1h, y0h, do1h, u1h, u0h, part1h, stat1p, stat0,
        e0o, sm, rp, vec, heads, ig, so, got,
        w, e1, e0, proj, yv, do, dproj, oo, u, part, x1own, x0own, dtile, db, grads, gp, gs, swap, stat1, stb, *rest,
    ):
        rbufs, ra, sa = rest[:4], rest[4:8], rest[8:15]
        sb = (rest[15], rest[16], sa[2], sa[3], rest[17], rest[18], sa[6])
        bz, bx, sums, ghead, isem, bsem, osem, ssem, rsem = rest[19:]
        s, z, h, x, c = place()

        def block_loads(i, far_first, proj_h, y_h, do_h, layer):
            hi, ci = block_at(i, h, s, far_first)
            b = 2 * hi + ci
            pairs = [(proj_h, proj), (y_h, yv)] + ([(do_h, do)] if do_h is not None else [])
            return [
                pltpu.make_async_copy(src.at[b], dst.at[lax.rem(i, 2)], bsem.at[layer, n, i])
                for n, (src, dst) in enumerate(pairs)
            ]

        loads1 = lambda i: block_loads(i, True, proj1h, y1h, do1h, 1)
        loads0 = lambda i: block_loads(i, False, proj0h, y0h, None, 0)
        for copy in loads1(0):
            copy.start()
        lw1 = pltpu.make_async_copy(w1h, w, isem.at[0])
        lw1.start()
        for copy in loads1(1):
            copy.start()
        later = [
            pltpu.make_async_copy(callh, e1, isem.at[1]),
            pltpu.make_async_copy(u1h, u, isem.at[2]),
            pltpu.make_async_copy(xallh.at[h, s, c], x1own, isem.at[3]),
            pltpu.make_async_copy(x0h, x0own, isem.at[4]),
        ]
        for copy in later:
            copy.start()
        greet(small_devs() + group_devs())
        net = Net(ssem, rsem)
        devs = group_devs()
        ring_sum = RingSum(net, part, rbufs)
        spread = Spread(net, e0)
        scatter1 = Scatter(net, grads, sa, gs.at[1])
        scatter0 = Scatter(net, w, sb, gs.at[0])
        ring0, ring1 = RingSum(net, part, rbufs), RingSum(net, e1, ra)
        me = (2 * h + s) * 2 + c
        q = 4 * s + 2 * h + c
        dsends = [net.make(dtile, db.at[me], dev) for dev in devs]
        gsends = [
            net.make(gp.at[dev["s"], 2 * dev["h"] + dev["c"]], rp.at[q], dev) for dev in devs
        ]
        swap_send = net.make(swap, got, {"s": 1 - s})
        stats = [net.send(stat1p, stb.at[k], dev) for k, dev in enumerate(devs)]
        sm[...] = jnp.zeros_like(sm)
        zr, zl, zo = ring(z)
        acc = stat1p[...]
        for k, copy in enumerate(stats):
            copy.wait_recv()
            acc = acc + stb[k]
        stat1[...] = acc
        lw1.wait()

        def first(i, carry):
            hi, ci = block_at(i, h, s, True)
            b = 2 * hi + ci
            slot = lax.rem(i, 2)
            for copy in loads1(i):
                copy.wait()
            backward_block(
                b, None, w, cv.at[1], st, stat1, None,
                (proj.at[slot], yv.at[slot], do.at[slot], dproj.at[b], oo.at[b], part.at[hi, ci], sm.at[1]),
            )
            when_each(i, 4, ring_sum.step)

            @pl.when(i < 2)
            def _():
                for copy in loads1(i + 2):
                    copy.start()

            return carry

        lax.fori_loop(0, 4, first, 0)
        lw0 = pltpu.make_async_copy(w0h, w, isem.at[5])
        lw0.start()
        for i in range(2):
            for copy in loads0(i):
                copy.start()
        ring_sum.late()
        for copy in later:
            copy.wait()
        for k in range(4):
            weight_tile(k, 1, u, e1, dproj, oo, grads)
        scatter1.start(1)
        scatter1.direct(1)
        for n, k in enumerate((zo, zr, zl, z)):
            weight_tile(k, 0, u, e1, dproj, oo, grads)
            if n == 0:
                scatter1.start(0)
            if n == 2:
                scatter1.direct(0)
        total = ring_sum.total()
        e0f = norm_back(total, x1own[...], e1[h, s, c], ng.at[1])
        e0l = e0f.astype(BF)
        e0[h, s, c] = e0l
        spread.start()
        diff = x1own[...].astype(F32) - x0own[...].astype(F32)
        dots = jnp.sum(e0l.astype(F32) * diff, axis=1, keepdims=True)
        dtile[...] = jnp.broadcast_to(col_to_row(dots), (8, 128))
        db[me] = dtile[...]
        for copy in dsends:
            copy.start()
        for copy in ring_sum.core + ring_sum.far + ring_sum.direct + ring_sum.summed:
            net.sent(copy)
        lu0 = pltpu.make_async_copy(u0h, u, isem.at[2])
        lu0.start()
        lp1 = pltpu.make_async_copy(part1h, e1, isem.at[1])
        lp1.start()
        for copy in dsends:
            copy.wait_recv()
        lw0.wait()
        lp1.wait()

        def save(i):
            hi, ci = block_at(i, h, s, False)
            return pltpu.make_async_copy(e0.at[hi, ci], e0o.at[hi, ci], osem.at[i])

        def second(i, carry):
            when_each(i, 4, spread.ready)
            hi, ci = block_at(i, h, s, False)
            b = 2 * hi + ci
            slot = lax.rem(i, 2)
            for copy in loads0(i):
                copy.wait()
            save(i).start()
            backward_block(
                b, e0.at[hi, ci], w, cv.at[0], st, stat0, db,
                (proj.at[slot], yv.at[slot], do.at[slot], dproj.at[b], oo.at[b], part.at[hi, ci], sm.at[0]),
            )
            when_each(i, 4, lambda k: ring0.core[3 - k].start())

            @pl.when(i < 2)
            def _():
                for copy in loads0(i + 2):
                    copy.start()

            @pl.when(i == 0)
            def _():
                for copy in ring1.core:
                    copy.start()

            @pl.when(i == 1)
            def _():
                scatter1.summed(1)
                scatter1.summed(0)
                ring1.all_adds()

            @pl.when(i == 3)
            def _():
                ring1.late()
                scatter1.second(1)
                scatter1.second(0)

            return carry

        lax.fori_loop(0, 4, second, 0)

        def smalls():
            yield from g_small(net, sm, bz, bx, sums)
            yield from g_share(net, sums, ghead, vec, heads)

        def pieces(layer):
            for k in range(4):
                rows = slice(24 * (k % 2), 24 * (k % 2) + 24)
                gp[layer, k, 0:24] = gs[layer, k // 2, rows, 0:HALF]
                gp[layer, k, 24:48] = gs[layer, k // 2, rows, HALF:D]

            @pl.when(s == layer)
            def _():
                rp[q] = gp[layer, 2 * h + c]
                for copy in gsends[0:3]:
                    copy.start()

            @pl.when(s != layer)
            def _():
                for copy in gsends[3:7]:
                    copy.start()

        sg = smalls()
        next(sg)
        lu0.wait()
        for k in range(4):
            weight_tile(k, 1, u, e0, dproj, oo, w)
        scatter0.start(1)
        weight_tile(zo, 0, u, e0, dproj, oo, w)
        scatter0.start(0)
        ring0.all_adds()
        scatter1.second_summed(1)
        scatter1.second_summed(0)
        weight_tile(zr, 0, u, e0, dproj, oo, w)
        weight_tile(zl, 0, u, e0, dproj, oo, w)
        scatter0.direct(1)
        scatter0.direct(0)
        weight_tile(z, 0, u, e0, dproj, oo, w)
        next(sg)
        for half in scatter1.parts:
            for copy in half["near"][2:] + half["far2"] + half["near2"]:
                net.sent(copy)
        scatter0.summed(1)
        scatter0.summed(0)
        ring0.late()
        scatter1.finish(1)
        scatter1.finish(0)
        pieces(1)
        so[...] = (x1own[...].astype(F32) + own_scale(stat1) * ring1.total()).astype(BF)
        ig[...] = norm_back(ring0.total(), x0own[...], e0[h, s, c], ng.at[0]).astype(BF)
        swap[...] = jnp.where(s == 0, so[...], ig[...])
        swap_send.start()
        next(sg)
        scatter0.second(1)
        scatter0.second(0)
        for _ in sg:
            pass
        scatter0.second_summed(1)
        scatter0.second_summed(0)
        scatter0.finish(0)
        scatter0.finish(1)
        pieces(0)
        for i in range(4):
            save(i).wait()
        for copy in gsends:
            copy.wait_recv()
        swap_send.wait_recv()
        net.finish()

    big = pltpu.VMEM((4, 2, 4, 48, D), BF)
    rows = pltpu.VMEM((2, 2, 2, 128, D), BF)
    chunk = pltpu.VMEM((128, D), BF)
    return pl.pallas_call(
        kernel,
        name="two_backward",
        out_shape=(
            CHUNKS,
            jax.ShapeDtypeStruct((2, 8, 640), F32),
            jax.ShapeDtypeStruct((8, 48, HALF), BF),
            jax.ShapeDtypeStruct((8, 3328), F32),
            SMALL,
            CHUNK,
            CHUNK,
            CHUNK,
        ),
        in_specs=[SM, ANY, ANY, VM, VM] + [ANY] * 11 + [VM, VM],
        out_specs=(ANY,) + (VM,) * 7,
        scratch_shapes=[
            big,
            rows,
            rows,
            pltpu.VMEM((2, 256, CIN), F32),
            pltpu.VMEM((2, 256, HC), F32),
            pltpu.VMEM((2, 256, HC), F32),
            pltpu.VMEM((4, 256, CIN), BF),
            pltpu.VMEM((4, 256, HC), BF),
            pltpu.VMEM((4, 256, D), BF),
            rows,
            chunk,
            chunk,
            pltpu.VMEM((8, 128), F32),
            pltpu.VMEM((8, 8, 128), F32),
            big,
            pltpu.VMEM((2, 4, 48, HALF), BF),
            pltpu.VMEM((2, 2, 48, D), BF),
            chunk,
            pltpu.VMEM((16, 128), F32),
            pltpu.VMEM((7, 16, 128), F32),
        ]
        + ring_scratch()
        + ring_scratch()
        + scatter_scratch()
        + [scatter_scratch()[k] for k in (0, 1, 4, 5)]
        + small_scratch()
        + [pltpu.VMEM((2, 8, 640), F32), pltpu.VMEM((8, 8, 640), F32)]
        + [
            pltpu.SemaphoreType.DMA((6,)),
            pltpu.SemaphoreType.DMA((2, 3, 4)),
            pltpu.SemaphoreType.DMA((4,)),
        ]
        + sems(128),
        compiler_params=params(3),
    )(
        st, w1, w0, ng, cv, call, xall, x0own, proj1, proj0, y1, y0, do1, u1, u0, part1, stat1, stat0
    )


def shift_div(v, m):
    return (v * {52: 20165, 48: 21846, 24: 43691}[m]) >> 20


def place_rows(x, rows, m, chan):
    n = chan.shape[1]
    row = lax.broadcasted_iota(jnp.int32, (512, n), 0)
    zz, xx, hh, cc = row >> 7, (row >> 5) & 3, (row >> 4) & 1, (row >> 3) & 1
    owner = shift_div(chan, m)
    same = ((zz * 2 + hh) * 4 + xx) * 2 + cc == owner
    col = lax.broadcasted_iota(jnp.int32, (128, n), 0) == chan - m * owner
    out = []
    for r in rows:
        pick = jnp.where(jnp.logical_and(same, (row & 7) == r), 1.0, 0.0).astype(BF)
        vals = tn(x, pick)
        out.append(jnp.sum(jnp.where(col, vals, 0.0), axis=0, keepdims=True))
    return out


def forward(starts, ngain, w_in, cw, cb, dtb, alog, skip, gate, w_out, tok, cot):
    def kernel(
        starts, ngain, w_in, cw, cb, dtb, alog, skip, gate, w_out, tok, cot,
        cv, ng, stt, x0o, s0o, s1o, w0o, w1o, e1o, x1o, p1o, proj0o, proj1o, y0o, y1o, u0o, u1o, doo,
        tile, tg, tb, ta, pieces, pb, blk0, blk1, st,
        w0, w1, x0, x1, e1, part, part1, proj, yv, uv, dov, og, stat0, stat1, stb0,
        rb0, rb1, rb2, rb3, ksem, osem, lsem, ssem, rsem,
    ):
        s, z, h, x, c = place()
        hc = 2 * h + c
        q = 4 * s + hc
        greet(small_devs() + group_devs())
        net = Net(ssem, rsem)
        devs = group_devs()
        low6 = lax.broadcasted_iota(jnp.int32, (24, 128), 1) < NH
        rate = jnp.concatenate(
            [w_in[0, :, 6400:6448].astype(F32), jnp.zeros((24, 80), F32)], axis=1
        )
        for k in range(8):
            lanes = slice(k * HC, k * HC + HC)
            moved = rate if k == 0 else pltpu.roll(rate, 128 - NH * k, axis=1)
            left = [w_in[0, :, lanes], w_in[0, :, 3072 + k * HC : 3072 + k * HC + HC]]
            right = [
                w_in[0, :, 6144:6400],
                jnp.where(low6, moved, 0.0).astype(BF),
                w_out[:, lanes],
            ]
            pieces[k, 0:24, :] = jnp.concatenate(left, axis=1)
            pieces[k, 24:48, :] = jnp.concatenate(right, axis=1)
        ids = [4 * d["s"] + 2 * d["h"] + d["c"] for d in devs]
        psend = [net.make(pieces.at[k], pb.at[s, hc], dev) for k, dev in zip(ids, devs)]

        def p_send():
            for copy in psend:
                copy.start()

        def p_wait(layer):
            @pl.when(s == layer)
            def _():
                for copy in psend[0:3]:
                    copy.wait_recv()

            @pl.when(s != layer)
            def _():
                for copy in psend[3:7]:
                    copy.wait_recv()

        def block(layer, out):
            for hh in range(2):
                for cc in range(2):
                    rows = slice(24 * cc, 24 * cc + 24)
                    out[hh, rows, 0:HALF] = pb[layer, 2 * hh + cc, 0:24]
                    out[hh, rows, HALF:D] = pb[layer, 2 * hh + cc, 24:48]

        pl.when(s == 0)(p_send)
        pb[s, hc] = pieces[q]
        tile[...] = jnp.zeros_like(tile)
        tile[0:4, 0:52] = cw[0].astype(F32)
        tile[4:5, 0:52] = cb[...].astype(F32)
        tile[5:6, 0:48] = gate[...].astype(F32)
        tile[6:7, 0:24] = ngain[...].astype(F32)
        tile[7:8, 0:4] = starts[0].astype(F32)
        tile[7:8, 4:8] = starts[1].astype(F32)
        tile[8:9, 0:48] = dtb[...]
        tile[9:10, 0:48] = jnp.exp(alog[...])
        tile[10:11, 0:48] = skip[...]
        tsend = [net.send(tile, tg.at[q], dev) for dev in devs]
        tg[q] = tile[...]
        gather0 = Gather(net, blk0, w0, lsem.at[0])
        gather1 = Gather(net, blk1, w1, lsem.at[3])
        ring = RingSum(net, part, (rb0, rb1, rb2, rb3))
        spread = Spread(net, x1)
        stats0 = [net.make(stat0, stb0.at[k], dev) for k, dev in enumerate(devs)]

        def weights():
            yield 9.0
            p_wait(0)
            block(0, blk0)
            gather0.step(0)
            pl.when(s == 1)(p_send)
            for k, n in enumerate((5.0, 7.0, 21.0)):
                yield 10.0 + n
                gather0.step(k + 1)
            p_wait(1)
            block(1, blk1)
            gather1.step(0)
            yield 39.0
            gather0.step(4)
            gather1.step(1)

        def vectors():
            yield 10.0
            for copy in tsend:
                copy.wait_recv()
            for k in range(8):
                tb[z, k // 4, 8 * (k % 4) : 8 * (k % 4) + 8] = tg[k, 0:8].astype(BF)
            for n in range(4):
                v = tg[n, 7:8, :]
                first = 4 * (n // 2) + n % 2
                stt[first : first + 1] = v.astype(jnp.int32)
                stt[first + 2 : first + 3] = pltpu.roll(v, 124, axis=1).astype(jnp.int32)
            to_smem = pltpu.make_async_copy(stt, st, ksem.at[0])
            to_smem.start()
            r = tb.at[z]
            sends = [net.send(r, r, {"z": lax.rem(z + k, 4)}) for k in range(1, 4)]
            yield 14.0
            to_smem.wait()
            for copy in sends:
                copy.wait_recv()
            ta[x] = tb[...]
            r = ta.at[x]
            sends = [net.send(r, r, {"x": lax.rem(x + k, 4)}) for k in range(1, 4)]
            yield 20.0
            for copy in sends:
                copy.wait_recv()
            n = lax.broadcasted_iota(jnp.int32, (1, 640), 1)
            chan = jnp.where(n < HC, q * HC + n, 3072 - HC + n)
            gchan = q * HC + lax.broadcasted_iota(jnp.int32, (1, HC), 1)
            nchan = lax.broadcasted_iota(jnp.int32, (1, D), 1)
            head = lax.broadcasted_iota(jnp.int32, (1, HC), 1) >> 6
            cv[...] = jnp.zeros_like(cv)
            for layer in range(2):
                vals = jnp.concatenate([ta[k % 4, k // 4, layer] for k in range(16)], axis=0)
                for r, v in enumerate(place_rows(vals, range(5), 52, chan)):
                    cv[layer, r : r + 1, :] = v
                cv[layer, 5:6, 0:HC] = place_rows(vals, [5], 48, gchan)[0]
                ng[layer] = place_rows(vals, [6], 24, nchan)[0]
                back = lax.rem(128 - NH * q, 128)
                heads = pltpu.roll(tg[4 * layer, 8:16, :], back, axis=1)
                cv[layer, 7:8, 0:128] = heads[0:1]
                cv[layer, 8:9, 0:128] = heads[1:2]
                lanes = jnp.zeros((1, HC), F32)
                for k in range(NH):
                    lanes = jnp.where(head == k, heads[2:3, k : k + 1], lanes)
                cv[layer, 6:7, 0:HC] = lanes
                yield 21.0

        run(
            [
                weights(),
                vectors(),
                g_pairs(net, tok, x0, lsem.at[1], 10.0),
                g_pairs(net, cot, e1, lsem.at[2], 19.2),
            ]
        )
        x0o[...] = x0[h, s, c]
        keep = [
            pltpu.make_async_copy(src, dst, ksem.at[n])
            for n, (src, dst) in enumerate(((w0, w0o), (e1, e1o), (w1, w1o)))
        ]
        keep[0].start()
        keep[1].start()

        def saves(b, layer, proj_o, y_o, u_o):
            return [
                pltpu.make_async_copy(v.at[b], o.at[b], osem.at[layer, n, b])
                for n, (v, o) in enumerate(((proj, proj_o), (yv, y_o), (uv, u_o)))
            ]

        def more(b, p):
            return [
                pltpu.make_async_copy(v, o, osem.at[2, n, b])
                for n, (v, o) in enumerate(
                    (
                        (dov.at[b], doo.at[b]),
                        (x1.at[p], x1o.at[p]),
                        (part1.at[p], p1o.at[p]),
                    )
                )
            ]

        def first(i, carry):
            hi, mi = block_at(i, h, s, True)
            b = 2 * hi + mi
            forward_block(
                b, x0.at[hi, mi], w0, ng[0], cv.at[0], st,
                (part.at[hi, mi], stat0, proj.at[b], yv.at[b], uv.at[b], None, og),
            )
            for copy in saves(b, 0, proj0o, y0o, u0o):
                copy.start()
            when_each(i, 4, ring.step)

            @pl.when(i == 0)
            def _():
                gather1.step(2)

            return carry

        lax.fori_loop(0, 4, first, 0)
        for copy in stats0:
            copy.start()
        ring.late()
        gather1.step(3)
        acc = stat0[...]
        for k, copy in enumerate(stats0):
            copy.wait_recv()
            acc = acc + stb0[k]
        s0o[...] = acc
        for b in range(4):
            for copy in saves(b, 0, proj0o, y0o, u0o):
                copy.wait()
        x1[h, s, c] = (x0[h, s, c].astype(F32) + own_scale(s0o) * ring.total()).astype(BF)
        spread.start()
        gather1.step(4)
        keep[2].start()

        def second(i, carry):
            when_each(i, 4, spread.ready)
            hi, mi = block_at(i, h, s, False)
            b = 2 * hi + mi
            forward_block(
                b, x1.at[hi, mi], w1, ng[1], cv.at[1], st,
                (part1.at[hi, mi], stat1, proj.at[b], yv.at[b], uv.at[b], dov.at[b], og),
                e1.at[hi, mi],
            )
            for copy in saves(b, 1, proj1o, y1o, u1o) + more(b, (hi, mi)):
                copy.start()
            return carry

        lax.fori_loop(0, 4, second, 0)
        s1o[...] = stat1[...]
        for copy in keep:
            copy.wait()
        for b in range(4):
            for copy in saves(b, 1, proj1o, y1o, u1o) + more(b, (b // 2, b % 2)):
                copy.wait()
        net.finish()

    blocks = lambda cols, t: jax.ShapeDtypeStruct((4, 256, cols), t)
    big = pltpu.VMEM((4, 2, 4, 48, D), BF)
    rows = pltpu.VMEM((2, 2, 2, 128, D), BF)
    return pl.pallas_call(
        kernel,
        name="forward",
        out_shape=(
            jax.ShapeDtypeStruct((2, 16, 640), F32),
            jax.ShapeDtypeStruct((2, 1, D), F32),
            jax.ShapeDtypeStruct((8, 128), jnp.int32),
            CHUNK,
            jax.ShapeDtypeStruct((8, 128), F32),
            jax.ShapeDtypeStruct((16, 128), F32),
            GATHERED,
            GATHERED,
            CHUNKS,
            CHUNKS,
            CHUNKS,
            blocks(CIN, F32),
            blocks(CIN, F32),
            blocks(HC, F32),
            blocks(HC, F32),
            blocks(D, BF),
            blocks(D, BF),
            blocks(HC, F32),
        ),
        in_specs=[VM] * 12,
        out_specs=(VM,) * 6 + (ANY,) * 12,
        scratch_shapes=[
            pltpu.VMEM((16, 128), F32),
            pltpu.VMEM((8, 16, 128), F32),
            pltpu.VMEM((4, 2, 32, 128), BF),
            pltpu.VMEM((4, 4, 2, 32, 128), BF),
            pltpu.VMEM((8, 48, HALF), BF),
            pltpu.VMEM((2, 4, 48, HALF), BF),
            pltpu.VMEM((2, 48, D), BF),
            pltpu.VMEM((2, 48, D), BF),
            pltpu.SMEM((8, 128), jnp.int32),
            big,
            big,
            rows,
            rows,
            rows,
            rows,
            rows,
            pltpu.VMEM((4, 256, CIN), F32),
            pltpu.VMEM((4, 256, HC), F32),
            pltpu.VMEM((4, 256, D), BF),
            pltpu.VMEM((4, 256, HC), F32),
            pltpu.VMEM((256, HC), BF),
            pltpu.VMEM((8, 128), F32),
            pltpu.VMEM((16, 128), F32),
            pltpu.VMEM((7, 8, 128), F32),
        ]
        + ring_scratch()
        + [
            pltpu.SemaphoreType.DMA((3,)),
            pltpu.SemaphoreType.DMA((3, 3, 4)),
            pltpu.SemaphoreType.DMA((4,)),
        ]
        + sems(100),
        compiler_params=params(1),
    )(starts, ngain, w_in, cw, cb, dtb, alog, skip, gate, w_out, tok, cot)


def results(rec, vec, heads, ig0, so1, got, eall, xall, w_in, ngain):
    def kernel(rec, vec, heads, ig0, so1, got, eall, xall, w_in, ngain, so, ig, gng, gwi, gcw, gcb, gdt, gal, gsk, ggg, gwo, buf, sem):
        s, z, h, x, c = place()
        dp = ((z * 2 + h) * 4 + x) * 2 + c
        copies = [
            pltpu.make_async_copy(src.at[h, :, c], buf.at[n], sem.at[n])
            for n, src in enumerate((eall, xall))
        ]
        for copy in copies:
            copy.start()
        tail = jnp.zeros((24, 256), F32)
        rate = jnp.zeros((24, 128), F32)
        lane = lax.broadcasted_iota(jnp.int32, (24, 128), 1)
        dots = jnp.zeros((24, 1), F32)

        def put(lanes, v):
            gwi[0, :, lanes] = v
            return jnp.sum(w_in[0, :, lanes].astype(F32) * v, axis=1, keepdims=True)

        for k in range(8):
            lanes = slice(k * HC, k * HC + HC)
            dots = dots + put(lanes, rec[k, 0:24, 0:HC].astype(F32))
            lanes = slice(3072 + k * HC, 3072 + k * HC + HC)
            dots = dots + put(lanes, rec[k, 0:24, HC:HALF].astype(F32))
            tail = tail + rec[k, 24:48, 0:256].astype(F32)
            part = jnp.where(lane < NH, rec[k, 24:48, 256:384].astype(F32), 0.0)
            rate = rate + (part if k == 0 else pltpu.roll(part, NH * k, axis=1))
            gwo[:, k * HC : k * HC + HC] = rec[k, 24:48, HC:HALF].astype(F32)
        dots = dots + put(slice(6144, 6400), tail)
        dots = dots + put(slice(6400, 6448), rate[:, 0:48])
        i = lax.broadcasted_iota(jnp.int32, (24, 24), 0)
        j = lax.broadcasted_iota(jnp.int32, (24, 24), 1)
        gng[...] = jnp.sum(jnp.where(i == j, dots, 0.0), axis=0, keepdims=True) / ngain[...].astype(F32)

        def exact(a, b):
            return jnp.dot(a, b, precision=HIGH, preferred_element_type=F32)

        def window(m):
            ch = lax.broadcasted_iota(jnp.int32, (3328, 128), 0)
            j = lax.broadcasted_iota(jnp.int32, (3328, 128), 1)
            return exact(vec[...], (ch == m * dp + j).astype(F32))

        conv = window(52)
        gcw[0] = conv[0:4, 0:52]
        gcb[...] = conv[4:5, 0:52]
        ggg[...] = window(48)[5:6, 0:48]
        ch = lax.broadcasted_iota(jnp.int32, (HC, 128), 0) >> 6
        j = lax.broadcasted_iota(jnp.int32, (HC, 128), 1)
        skip = exact(heads[:, 256:640], (ch == j).astype(F32))
        row = lax.broadcasted_iota(jnp.int32, (1, 128), 1)
        for out, v in ((gdt, heads[:, 0:128]), (gal, heads[:, 128:256]), (gsk, skip)):
            acc = jnp.zeros((1, 128), F32)
            for k in range(8):
                part = jnp.where(row < NH, v[k : k + 1], 0.0)
                acc = acc + (part if k == 0 else pltpu.roll(part, NH * k, axis=1))
            out[...] = acc[:, 0:48]
        for copy in copies:
            copy.wait()

        @pl.when(s == 0)
        def _():
            ig[0, 0] = ig0[...].astype(F32)
            ig[0, 1] = got[...].astype(F32)
            so[0] = buf[1]

        @pl.when(s == 1)
        def _():
            ig[0] = buf[0].astype(F32)
            so[0, 0] = got[...]
            so[0, 1] = so1[...]

    f = lambda *shape: jax.ShapeDtypeStruct(shape, F32)
    return pl.pallas_call(
        kernel,
        name="results",
        out_shape=(
            jax.ShapeDtypeStruct((1, 2, 128, D), BF),
            f(1, 2, 128, D),
            f(1, 24),
            f(1, 24, 6448),
            f(1, 4, 52),
            f(1, 52),
            f(1, 48),
            f(1, 48),
            f(1, 48),
            f(1, 48),
            f(24, 3072),
        ),
        in_specs=[VM] * 6 + [ANY] * 2 + [VM] * 2,
        out_specs=(VM,) * 11,
        scratch_shapes=[pltpu.VMEM((2, 2, 128, D), BF), pltpu.SemaphoreType.DMA((2,))],
        compiler_params=pltpu.CompilerParams(vmem_limit_bytes=VLIM),
    )(rec, vec, heads, ig0, so1, got, eall, xall, w_in, ngain)


def body(
    tokens,
    cotangent,
    starts,
    norm_gain,
    w_in,
    conv_weight,
    conv_bias,
    dt_bias,
    a_log,
    skip_d,
    gate_gain,
    w_out,
):
    cv, ng, st, x0own, stat0, stat1, w0, w1, call, xall, part1, proj0, proj1, y0, y1, u0, u1, do1 = forward(
        starts,
        norm_gain,
        w_in,
        conv_weight,
        conv_bias,
        dt_bias,
        a_log,
        skip_d,
        gate_gain,
        jnp.transpose(w_out[0]),
        tokens,
        cotangent,
    )
    eall, _, rec, vec, hd, ig0, so1, got = two_backward(
        st, w1, w0, ng, cv, call, xall, x0own, proj1, proj0, y1, y0, do1, u1, u0, part1, stat1, stat0
    )
    outs = results(rec, vec, hd, ig0, so1, got, eall, xall, w_in, norm_gain)
    return outs[:10] + (jnp.transpose(outs[10])[None],)


def solution(mesh):
    inner = Mesh(mesh.devices.reshape(2, 4, 2, 4, 2), ("s", "z", "h", "x", "c"))
    dp = ("z", "h", "x", "c")
    in_specs = (
        P(None, dp, None),
        P(None, dp, None),
        P(None, dp, None),
        P("s", dp),
        P("s", dp, None),
        P("s", None, dp),
        P("s", dp),
        P("s", None),
        P("s", None),
        P("s", None),
        P("s", dp),
        P("s", None, dp),
    )
    out_specs = (
        P("s", None, dp, None),
        P("s", None, dp, None),
        P("s", dp),
        P("s", dp, None),
        P("s", None, dp),
        P("s", dp),
        P("s", None),
        P("s", None),
        P("s", None),
        P("s", dp),
        P("s", None, dp),
    )
    return jax.shard_map(body, mesh=inner, in_specs=in_specs, out_specs=out_specs, check_vma=False)
```

```python
import jax
import jax.numpy as jnp
from jax import lax
from jax.experimental import pallas as pl
from jax.experimental.pallas import tpu as pltpu
from jax.sharding import Mesh, PartitionSpec as P

EPS = 1e-05
BF = jnp.bfloat16
F32 = jnp.float32
HIGH = lax.Precision.HIGHEST
D = 1536
CIN = 1152
HC = 384
NH = 6
RT = 1024
HALF = 768
ANY = pl.BlockSpec(memory_space=pl.ANY)
VM = pl.BlockSpec(memory_space=pltpu.VMEM)
SM = pl.BlockSpec(memory_space=pltpu.SMEM)
VLIM = 59 * 1024 * 1024


class Net:
    def __init__(self, ssem, rsem):
        self.ssem, self.rsem, self.n, self.all = ssem, rsem, 0, []

    def make(self, src, dst, dev):
        i = self.n
        self.n += 1
        assert i < self.ssem.shape[0]
        copy = pltpu.make_async_remote_copy(
            src_ref=src,
            dst_ref=dst,
            send_sem=self.ssem.at[i],
            recv_sem=self.rsem.at[i],
            device_id=dev,
            device_id_type=pl.DeviceIdType.MESH,
        )
        self.all.append(copy)
        return copy

    def send(self, src, dst, dev):
        copy = self.make(src, dst, dev)
        copy.start()
        return copy

    def sent(self, copy):
        copy.wait_send()
        self.all = [v for v in self.all if v is not copy]

    def finish(self):
        for copy in self.all:
            copy.wait_send()


def place():
    s, z, h, x, c = (lax.axis_index(a) for a in ("s", "z", "h", "x", "c"))
    return s, z, h, x, c


def ring(i):
    return lax.rem(i + 1, 4), lax.rem(i + 3, 4), lax.rem(i + 2, 4)


def greet(devs):
    barrier = pltpu.get_barrier_semaphore()
    for dev in devs:
        pl.semaphore_signal(barrier, inc=1, device_id=dev, device_id_type=pl.DeviceIdType.MESH)
    pl.semaphore_wait(barrier, len(devs))


def zx_devs():
    s, z, h, x, c = place()
    zr, zl, _ = ring(z)
    xr, xl, _ = ring(x)
    return [{"z": zr}, {"z": zl}, {"x": xr}, {"x": xl}]


def ydev(y):
    return {"h": y // 2, "s": lax.rem(y, 2)}


def y_devs():
    s, z, h, x, c = place()
    yr, yl, _ = ring(2 * h + s)
    return [ydev(yr), ydev(yl), {"c": 1 - c}]


def group_devs():
    s, z, h, x, c = place()
    out = []
    for k in range(1, 8):
        out.append(
            {
                "s": 1 - s if k & 4 else s,
                "h": 1 - h if k & 2 else h,
                "c": 1 - c if k & 1 else c,
            }
        )
    return out


LAT = 1.7


def inter(gens):
    gens = [[0.0, g] for g in gens]
    while gens:
        item = min(gens, key=lambda v: v[0])
        if item[0] > 0:
            yield item[0]
        try:
            item[0] = next(item[1])
        except StopIteration:
            gens.remove(item)


def run(gens):
    for _ in inter(gens):
        pass


def g_pairs(net, own, out, lsem, t0):
    s, z, h, x, c = place()
    outer, inner, sib = {"h": 1 - h, "s": 1 - s}, {"s": 1 - s}, {"c": 1 - c}
    first = []
    for k in range(2):
        rows = pl.ds(64 * k, 64)
        first.append(net.send(own.at[s, rows], out.at[h, s, c, rows], outer))
    local = pltpu.make_async_copy(own, out.at[h, :, c], lsem)
    local.start()
    c0 = net.send(own, out.at[h, :, c], sib)
    yield t0 + 4.6 + LAT
    second = []
    for k in range(2):
        first[k].wait_recv()
        r = out.at[1 - h, 1 - s, c, pl.ds(64 * k, 64)]
        second.append(net.send(r, r, inner))
        if k == 0:
            yield t0 + 9.2 + LAT
    r = out.at[1 - h, 1 - s, c]
    c1 = net.send(r, r, sib)
    yield t0 + 14 + LAT
    for copy in second:
        copy.wait_recv()
    r = out.at[1 - h, s, c]
    c2 = net.send(r, r, sib)
    yield t0 + 16 + LAT
    for copy in (c0, c1, c2):
        copy.wait_recv()
    local.wait()


def g_small(net, mine, bz, bx, total, t0=0.0):
    s, z, h, x, c = place()
    sends = [net.send(mine, bz.at[z], {"z": lax.rem(z + k, 4)}) for k in range(1, 4)]
    bz[z] = mine[...]
    yield t0 + 4.0
    for copy in sends:
        copy.wait_recv()
    bx[x] = bz[0] + bz[1] + bz[2] + bz[3]
    r = bx.at[x]
    sends = [net.send(r, r, {"x": lax.rem(x + k, 4)}) for k in range(1, 4)]
    yield t0 + 10.0
    for copy in sends:
        copy.wait_recv()
    total[...] = bx[0] + bx[1] + bx[2] + bx[3]


def small_scratch():
    return [pltpu.VMEM((4, 2, 8, 640), F32), pltpu.VMEM((4, 2, 8, 640), F32)]


def small_devs():
    s, z, h, x, c = place()
    return [{"z": lax.rem(z + k, 4)} for k in range(1, 4)] + [
        {"x": lax.rem(x + k, 4)} for k in range(1, 4)
    ]


def g_share(net, sums, got, vec, heads):
    s, z, h, x, c = place()
    me = (2 * s + h) * 2 + c
    sends = []
    for dev in group_devs():
        sends.append(net.send(sums.at[dev["s"]], got.at[me], dev))
    got[me] = sums[s]
    yield 20.0
    for copy in sends:
        copy.wait_recv()
    vec[...] = jnp.zeros_like(vec)
    tail = jnp.zeros((5, 256), F32)
    for q in range(8):
        lanes = slice(q * HC, q * HC + HC)
        vec[0:5, lanes] = got[q, 0:5, 0:HC]
        vec[5:6, lanes] = got[q, 5:6, 0:HC]
        tail = tail + got[q, 0:5, HC:640]
        heads[q : q + 1, 0:256] = got[q, 5:6, HC:640]
        heads[q : q + 1, 256:640] = got[q, 6:7, 0:HC]
    vec[0:5, 3072:3328] = tail


def params(cid):
    return pltpu.CompilerParams(
        collective_id=cid, has_side_effects=True, vmem_limit_bytes=VLIM
    )


def sems(n):
    return [pltpu.SemaphoreType.DMA((n,)), pltpu.SemaphoreType.DMA((n,))]


GATHERED = jax.ShapeDtypeStruct((4, 2, 4, 48, D), BF)
CHUNKS = jax.ShapeDtypeStruct((2, 2, 2, 128, D), BF)
SMALL = jax.ShapeDtypeStruct((8, 640), F32)
CHUNK = jax.ShapeDtypeStruct((128, D), BF)


def row_to_col(row):
    i = lax.broadcasted_iota(jnp.int32, (128, 128), 0)
    j = lax.broadcasted_iota(jnp.int32, (128, 128), 1)
    return jnp.sum(jnp.where(i == j, row, 0.0), axis=1, keepdims=True)


def col_to_row(col):
    i = lax.broadcasted_iota(jnp.int32, (128, 128), 0)
    j = lax.broadcasted_iota(jnp.int32, (128, 128), 1)
    return jnp.sum(jnp.where(i == j, col, 0.0), axis=0, keepdims=True)


def own_scale(total):
    s, z, h, x, c = place()
    row = total[pl.ds((2 * h + s) * 2 + c, 1), :]
    return lax.rsqrt(row_to_col(row) * (1.0 / 3072) + EPS)


def norm_back(v, x, e, ng):
    xf = x.astype(F32)
    vg = v * ng[...]
    r = lax.rsqrt(jnp.mean(xf * xf, axis=-1, keepdims=True) + EPS)
    dot = jnp.mean(xf * vg, axis=-1, keepdims=True)
    return e.astype(F32) + r * vg - xf * (r * r * r * dot)


def nt(a, b):
    return lax.dot_general(a, b, (((1,), (1,)), ((), ())), preferred_element_type=F32)


def tn(a, b):
    return lax.dot_general(a, b, (((0,), (0,)), ((), ())), preferred_element_type=F32)


def iotas():
    i = lax.broadcasted_iota(jnp.int32, (128, 128), 0)
    j = lax.broadcasted_iota(jnp.int32, (128, 128), 1)
    return i, j


def seg_of(firsts, places):
    seg = jnp.full(places.shape, -1, jnp.int32)
    for k in range(4):
        seg = seg + (firsts[k] <= places).astype(jnp.int32)
    return seg


def masks(st, chunk):
    i, j = iotas()
    firsts = [st[chunk, k] for k in range(4)]
    seg = seg_of(firsts, i)
    keep = jnp.logical_and(seg == seg_of(firsts, j), i >= j)
    valid = [None] + [(seg_of(firsts, i - k) == seg).astype(F32) for k in range(1, 4)]
    return keep, valid


def conv_tile(xt, cv, t, valid):
    lanes = slice(128 * t, 128 * t + 128)
    pre = cv[4:5, lanes] + cv[3:4, lanes] * xt
    moved = [xt]
    for k in range(1, 4):
        m = pltpu.roll(xt, k, axis=0) * valid[k]
        moved.append(m)
        pre = pre + cv[3 - k : 4 - k, lanes] * m
    return pre, moved


def rates(rt, cv):
    i, j = iotas()
    head = j < NH
    v = rt + cv[7:8, 0:128]
    dt = jnp.where(head, jnp.maximum(v, 0.0) + jnp.log1p(jnp.exp(-jnp.abs(v))), 0.0)
    lower = (i >= j).astype(F32)
    cum = jnp.dot(
        lower, -dt * cv[8:9, 0:128], precision=HIGH, preferred_element_type=F32
    )
    return v, dt, cum


def half_masks():
    _, j = iotas()
    return j < 64


def split_pair(v, low):
    zero = jnp.zeros_like(v)
    return jnp.concatenate([jnp.where(low, v, zero), jnp.where(low, zero, v)], axis=0)


def decay_of(keep, cum, cum_t, h):
    spread = jnp.where(keep, cum[:, h : h + 1] - cum_t[h : h + 1, :], -1e30)
    return jnp.exp(spread)


class Gather:
    def __init__(self, net, blk, out, lsem):
        s, z, h, x, c = place()
        self.local = pltpu.make_async_copy(blk, out.at[z, :, x], lsem)
        every = slice(None)
        self.parts = []
        for lanes, i, axis_i, j, axis_j, pick in (
            (pl.ds(0, HALF), x, "x", z, "z", lambda i, j, p: (j, p, i)),
            (pl.ds(HALF, HALF), z, "z", x, "x", lambda i, j, p: (i, p, j)),
        ):
            ir, il, _ = ring(i)
            jr, jl, _ = ring(j)

            def at(i, j, p, pick=pick, lanes=lanes):
                return out.at[pick(i, j, p) + (every, lanes)]

            def make(i, j, p, dev, src=None):
                ref = at(i, j, p)
                return net.make(ref if src is None else src, ref, dev)

            own = blk.at[:, :, lanes]
            first, second = ({axis_i: ir}, {axis_i: il}), ({axis_j: jr}, {axis_j: jl})
            self.parts.append(
                [
                    (make(i, j, every, first[0], own), make(i, j, every, first[1], own)),
                    (make(il, j, 0, first[0]), make(ir, j, 1, first[1])),
                    (make(every, j, every, second[0]), make(every, j, every, second[1])),
                    (make(every, jl, 0, second[0]), make(every, jr, 1, second[1])),
                ]
            )

    def step(self, k):
        if k == 0:
            self.local.start()
        if k == 2:
            self.local.wait()
        for part in self.parts:
            for n in range(2):
                if k > 0:
                    part[k - 1][n].wait_recv()
                if k < 4 and k != 2:
                    part[k][n].start()
            if k == 2:
                part[2][0].start()
                part[2][1].start()


class RingSum:
    def __init__(self, net, part, bufs):
        self.part = part
        self.cb, self.sb, self.b1, self.b2 = bufs
        s, z, h, x, c = place()
        self.c = c
        sib = {"c": 1 - c}
        outer, inner = {"h": 1 - h, "s": 1 - s}, {"s": 1 - s}
        self.units = [(1 - h, s), (1 - h, 1 - s), (h, 1 - s), (h, s)]
        self.core = [
            net.make(part.at[hh, mm, 1 - c], self.cb.at[k], sib)
            for k, (hh, mm) in enumerate(self.units)
        ]
        sb, b1, b2 = self.sb, self.b1, self.b2
        lo, hi = pl.ds(0, 64), pl.ds(64, 64)
        self.far = [
            net.make(sb.at[0, lo], b1.at[0], outer),
            net.make(sb.at[0, hi], b1.at[1], inner),
        ]
        self.direct = [
            net.make(sb.at[1, lo], b2.at[0, lo], outer),
            net.make(sb.at[2, hi], b2.at[1, hi], inner),
        ]
        self.summed = [
            net.make(sb.at[1, hi], b2.at[0, hi], outer),
            net.make(sb.at[2, lo], b2.at[1, lo], inner),
        ]

    def add(self, k):
        self.core[k].wait_recv()
        hh, mm = self.units[k]
        self.sb[k] = (self.part[hh, mm, self.c].astype(F32) + self.cb[k].astype(F32)).astype(BF)

    def step(self, k):
        self.core[k].start()
        if k == 1:
            self.add(0)
            self.far[0].start()
            self.far[1].start()
        if k == 2:
            self.add(1)
            self.direct[0].start()
            self.add(2)
            self.direct[1].start()

    def all_adds(self):
        self.add(0)
        self.far[0].start()
        self.far[1].start()
        self.add(1)
        self.direct[0].start()
        self.add(2)
        self.direct[1].start()

    def late(self):
        lo, hi = slice(0, 64), slice(64, 128)
        self.far[1].wait_recv()
        self.sb[1, hi] = (self.sb[1, hi].astype(F32) + self.b1[1].astype(F32)).astype(BF)
        self.summed[0].start()
        self.far[0].wait_recv()
        self.sb[2, lo] = (self.sb[2, lo].astype(F32) + self.b1[0].astype(F32)).astype(BF)
        self.summed[1].start()

    def total(self):
        self.core[3].wait_recv()
        for copy in self.direct + self.summed:
            copy.wait_recv()
        hh, mm = self.units[3]
        total = self.part[hh, mm, self.c].astype(F32) + self.cb[3].astype(F32)
        return total + self.b2[0].astype(F32) + self.b2[1].astype(F32)


def ring_scratch():
    return [
        pltpu.VMEM((4, 128, D), BF),
        pltpu.VMEM((3, 128, D), BF),
        pltpu.VMEM((2, 64, D), BF),
        pltpu.VMEM((2, 128, D), BF),
    ]


class Spread:
    def __init__(self, net, out):
        s, z, h, x, c = place()
        sib = {"c": 1 - c}
        outer, inner = {"h": 1 - h, "s": 1 - s}, {"s": 1 - s}
        lo, hi = pl.ds(0, 64), pl.ds(64, 64)
        own, far = out.at[h, s, c], out.at[1 - h, s, c]
        from_outer, from_inner = out.at[1 - h, 1 - s, c], out.at[h, 1 - s, c]
        self.mine = own
        self.ring = [net.make(own, own, outer), net.make(own, own, inner)]
        self.hand = [
            net.make(from_inner.at[lo], from_inner.at[lo], outer),
            net.make(from_outer.at[hi], from_outer.at[hi], inner),
        ]
        self.sib = [net.make(r, r, sib) for r in (own, from_inner, from_outer, far)]

    def start(self):
        self.ring[0].start()
        self.ring[1].start()
        self.sib[0].start()

    def ready(self, k):
        if k == 1:
            self.ring[1].wait_recv()
            self.hand[0].start()
            self.sib[1].start()
            self.ring[0].wait_recv()
            self.hand[1].start()
            self.sib[2].start()
        if k == 3:
            self.hand[0].wait_recv()
            self.hand[1].wait_recv()
            self.sib[3].start()
        self.sib[k].wait_recv()


def when_each(i, n, step):
    for k in range(n):
        pl.when(i == k)(lambda k=k: step(k))


def block_at(i, h, s, far_first):
    k = i if far_first else 3 - i
    return lax.rem(h + 1 + k // 2, 2), lax.rem(s + (k + 1) // 2, 2)


def forward_block(b, x, w, ng, cv, st, refs, e=None):
    part, stat, proj, yout, uout, doo, og = refs
    with_do = e is not None
    xf = x[...].reshape(256, D).astype(F32)
    r = lax.rsqrt(jnp.mean(xf * xf, axis=-1, keepdims=True) + EPS)
    u = (xf * r * ng).astype(BF)
    uout[...] = u
    proj[...] = jnp.dot(u, w[:, :, :, :, 0:CIN].reshape(D, CIN), preferred_element_type=F32)
    if with_do:
        doo[...] = jnp.dot(
            e[...].reshape(256, D),
            w[:, :, :, :, CIN:D].reshape(D, HC),
            preferred_element_type=F32,
        )
    low = half_masks()
    for m in range(2):
        rows = slice(128 * m, 128 * m + 128)
        chunk = b * 2 + m
        keep, valid = masks(st, chunk)
        act = []
        for t in range(5):
            pre, _ = conv_tile(proj[rows, HC + 128 * t : HC + 128 * t + 128], cv, t, valid)
            act.append((pre * jax.nn.sigmoid(pre)).astype(BF))
        _, dt, cum = rates(proj[rows, RT:CIN], cv)
        cum_t, dt_t = jnp.transpose(cum), jnp.transpose(dt)
        gram = nt(act[4], act[3])
        gsum = jnp.zeros((128, 1), F32)
        tsum = jnp.zeros((128, 1), F32)
        for t in range(3):
            lanes = slice(128 * t, 128 * t + 128)
            mixes = []
            for h in (2 * t, 2 * t + 1):
                dec = decay_of(keep, cum, cum_t, h)
                mixes.append((gram * dec * dt_t[h : h + 1, :]).astype(BF))
            y = jnp.dot(
                jnp.concatenate(mixes, axis=1),
                split_pair(act[t], low),
                preferred_element_type=F32,
            )
            y = y + cv[6:7, lanes] * act[t].astype(F32)
            yout[rows, lanes] = y
            zt = proj[rows, lanes]
            g = y * (zt * jax.nn.sigmoid(zt))
            gsum = gsum + jnp.sum(g * g, axis=1, keepdims=True)
            gain = cv[5:6, lanes]
            og[rows, lanes] = (g * gain).astype(BF)
            if with_do:
                tsum = tsum + jnp.sum(g * gain * doo[rows, lanes], axis=1, keepdims=True)
        stat[pl.ds(chunk, 1), :] = col_to_row(gsum)
        if with_do:
            stat[pl.ds(chunk + 8, 1), :] = col_to_row(tsum)
    out = nt(og[...], w[:, :, :, :, CIN:D].reshape(D, HC))
    part[...] = out.astype(BF).reshape(2, 128, D)


class Scatter:
    def __init__(self, net, grads, bufs, out):
        s, z, h, x, c = place()
        self.out = out
        self.parts = []
        for k, (i, axis_i, j, axis_j) in enumerate(((z, "z", x, "x"), (x, "x", z, "z"))):
            lanes = pl.ds(k * HALF, HALF)
            b1, b2, t, sums, b3, b4, t2 = [b.at[k] for b in bufs]
            ir, il, io = ring(i)
            jr, jl, jo = ring(j)
            if k == 0:
                unit = lambda i, p, lanes=lanes: grads.at[i, p, :, :, lanes]
            else:
                unit = lambda i, p, lanes=lanes: grads.at[:, p, i, :, lanes]
            right, left = {axis_i: ir}, {axis_i: il}
            part = dict(unit=unit, bufs=(b1, b2, t, sums, b3, b4, t2), i=i, j=j)
            part.update(ir=ir, il=il, jr=jr, jl=jl, jo=jo, k=k)
            part["far"] = [
                net.make(unit(io, 0), b1.at[0], right),
                net.make(unit(io, 1), b1.at[1], left),
            ]
            part["near"] = [
                net.make(unit(ir, 1), b2.at[0, 1], right),
                net.make(unit(il, 0), b2.at[1, 0], left),
                net.make(t.at[0], b2.at[0, 0], right),
                net.make(t.at[1], b2.at[1, 1], left),
            ]
            right, left = {axis_j: jr}, {axis_j: jl}
            part["far2"] = [
                net.make(sums.at[0, jo], b3.at[0], right),
                net.make(sums.at[1, jo], b3.at[1], left),
            ]
            part["near2"] = [
                net.make(sums.at[1, jr], b4.at[0, 1], right),
                net.make(sums.at[0, jl], b4.at[1, 0], left),
                net.make(t2.at[0], b4.at[0, 0], right),
                net.make(t2.at[1], b4.at[1, 1], left),
            ]
            self.parts.append(part)

    def start(self, k):
        for copy in self.parts[k]["far"]:
            copy.start()

    def direct(self, k):
        self.parts[k]["near"][0].start()
        self.parts[k]["near"][1].start()

    def summed(self, k):
        v = self.parts[k]
        b1, b2, t, sums, b3, b4, t2 = v["bufs"]
        for p, near in ((0, v["ir"]), (1, v["il"])):
            v["far"][p].wait_recv()
            for n in range(4):
                t[p, n] = (v["unit"](near, p)[n].astype(F32) + b1[p, n].astype(F32)).astype(BF)
            v["near"][2 + p].start()

    def total(self, v, p, n):
        b2 = v["bufs"][1]
        return (
            v["unit"](v["i"], p)[n].astype(F32)
            + b2[0, p, n].astype(F32)
            + b2[1, p, n].astype(F32)
        )

    def second(self, k):
        v = self.parts[k]
        sums = v["bufs"][3]
        for copy in v["near"]:
            copy.wait_recv()
        for copy, p, n in (
            (v["far2"][0], 0, v["jo"]),
            (v["far2"][1], 1, v["jo"]),
            (v["near2"][0], 1, v["jr"]),
            (v["near2"][1], 0, v["jl"]),
        ):
            sums[p, n] = self.total(v, p, n).astype(BF)
            copy.start()
        for p, n in ((0, v["jr"]), (1, v["jl"]), (0, v["j"]), (1, v["j"])):
            sums[p, n] = self.total(v, p, n).astype(BF)

    def second_summed(self, k):
        v = self.parts[k]
        b1, b2, t, sums, b3, b4, t2 = v["bufs"]
        for p, near in ((0, v["jr"]), (1, v["jl"])):
            v["far2"][p].wait_recv()
            t2[p] = (sums[p, near].astype(F32) + b3[p].astype(F32)).astype(BF)
            v["near2"][2 + p].start()

    def finish(self, k):
        v = self.parts[k]
        sums, b4 = v["bufs"][3], v["bufs"][5]
        for copy in v["near2"]:
            copy.wait_recv()
        for p in range(2):
            total = sums[p, v["j"]].astype(F32) + b4[0, p].astype(F32) + b4[1, p].astype(F32)
            self.out[p, :, k * HALF : (k + 1) * HALF] = total.astype(BF)


def scatter_scratch():
    return [
        pltpu.VMEM((2, 2, 4, 48, HALF), BF),
        pltpu.VMEM((2, 2, 2, 4, 48, HALF), BF),
        pltpu.VMEM((2, 2, 4, 48, HALF), BF),
        pltpu.VMEM((2, 2, 4, 48, HALF), BF),
        pltpu.VMEM((2, 2, 48, HALF), BF),
        pltpu.VMEM((2, 2, 2, 48, HALF), BF),
        pltpu.VMEM((2, 2, 48, HALF), BF),
    ]


def weight_tile(k, half, u, e, dproj, o, grads):
    cols = pl.ds(pl.multiple_of(k * 384, 128), 384)
    rows = 1024
    ut = u[:, :, cols].reshape(rows, 384)
    if half == 0:
        a = tn(ut, dproj[:, :, 0:HALF].reshape(rows, HALF))
        grads[k, :, :, :, 0:HALF] = a.astype(BF).reshape(2, 4, 48, HALF)
        return
    a = tn(ut, dproj[:, :, HALF:CIN].reshape(rows, CIN - HALF))
    grads[k, :, :, :, HALF:CIN] = a.astype(BF).reshape(2, 4, 48, CIN - HALF)
    a = tn(e[:, :, :, :, cols].reshape(rows, 384), o[...].reshape(rows, HC))
    grads[k, :, :, :, CIN:D] = a.astype(BF).reshape(2, 4, 48, HC)


def backward_block(b, e, w, cv, st, stat, dots, refs):
    proj, yin, do, dproj, oo, part, sm = refs
    if dots is not None:
        do[...] = jnp.dot(
            e[...].reshape(256, D),
            w[:, :, :, :, CIN:D].reshape(D, HC),
            preferred_element_type=F32,
        )
    low = half_masks()
    i, j = iotas()
    upper = (j >= i).astype(F32)

    def add(row, lanes, v):
        sm[row : row + 1, lanes] += jnp.sum(v, axis=0, keepdims=True)

    for m in range(2):
        rows = slice(128 * m, 128 * m + 128)
        chunk = b * 2 + m
        keep, valid = masks(st, chunk)
        pres, moves, act = [], [], []
        for t in range(5):
            pre, moved = conv_tile(proj[rows, HC + 128 * t : HC + 128 * t + 128], cv, t, valid)
            pres.append(pre)
            moves.append(moved)
            act.append((pre * jax.nn.sigmoid(pre)).astype(BF))
        v, dt, cum = rates(proj[rows, RT:CIN], cv)
        cum_t, dt_t = jnp.transpose(cum), jnp.transpose(dt)
        gram = nt(act[4], act[3])
        r = lax.rsqrt(row_to_col(stat[pl.ds(chunk, 1), :]) * (1.0 / 3072) + EPS)
        if dots is not None:
            k = r * r * row_to_col(dots[chunk, 0:1, :]) * (1.0 / 3072)
        else:
            k = r * r * r * row_to_col(stat[pl.ds(chunk + 8, 1), :]) * (1.0 / 3072)
        dact = []
        dgram = jnp.zeros((128, 128), F32)
        dcum = jnp.zeros((128, 128), F32)
        col_rows = []
        for t in range(3):
            lanes = slice(128 * t, 128 * t + 128)
            zt, y, dot_ = proj[rows, lanes], yin[rows, lanes], do[rows, lanes]
            gain = cv[5:6, lanes]
            sig = jax.nn.sigmoid(zt)
            sz = zt * sig
            g = y * sz
            oo[rows, lanes] = (g * r * gain).astype(BF)
            add(5, lanes, dot_ * g * r)
            dg = r * (dot_ * gain) - g * k
            dproj[rows, lanes] = (dg * y * (sig + sz * (1.0 - sig))).astype(BF)
            dy = (dg * sz).astype(BF)
            dyf = dy.astype(F32)
            xs = act[t]
            add(6, lanes, dyf * xs.astype(F32))
            dy2 = split_pair(dy, low)
            dmix2 = nt(dy2, xs)
            mixes = []
            for q in range(2):
                h = 2 * t + q
                dec = decay_of(keep, cum, cum_t, h)
                dt_row = dt_t[h : h + 1, :]
                pm = gram * dec
                mixes.append((pm * dt_row).astype(BF))
                dmix = dmix2[128 * q : 128 * q + 128]
                dgram = dgram + dmix * (dec * dt_row)
                vm = dmix * pm
                col_rows.append(jnp.sum(vm, axis=0, keepdims=True))
                rsum = jnp.sum(vm * dt_row, axis=1, keepdims=True)
                dcum = dcum + jnp.where(j == h, rsum, 0.0)
            dxs = tn(jnp.concatenate(mixes, axis=0), dy2)
            dact.append(dxs + cv[6:7, lanes] * dyf)
        dgl = dgram.astype(BF)
        dact.append(tn(dgl, act[4]))
        dact.append(jnp.dot(dgl, act[3], preferred_element_type=F32))
        ddt = jnp.transpose(
            jnp.concatenate(col_rows + [jnp.zeros((128 - NH, 128), F32)], axis=0)
        )
        dcum = dcum - ddt * dt
        dla = jnp.dot(upper, dcum, precision=HIGH, preferred_element_type=F32)
        nexp = -cv[8:9, 0:128]
        drate = (ddt + dla * nexp) * jax.nn.sigmoid(v)
        drate = jnp.where(j < NH, drate, 0.0)
        add(5, slice(HC, HC + 128), drate)
        add(5, slice(HC + 128, 640), dla * dt * nexp)
        dproj[rows, RT:CIN] = drate.astype(BF)
        for t in range(5):
            lanes = slice(128 * t, 128 * t + 128)
            pre = pres[t]
            sp = jax.nn.sigmoid(pre)
            dpre = dact[t] * (sp + pre * sp * (1.0 - sp))
            add(4, lanes, dpre)
            add(3, lanes, dpre * moves[t][0])
            dx = cv[3:4, lanes] * dpre
            for n in range(1, 4):
                add(3 - n, lanes, dpre * moves[t][n])
                dx = dx + cv[3 - n : 4 - n, lanes] * pltpu.roll(
                    dpre * valid[n], 128 - n, axis=0
                )
            dproj[rows, HC + 128 * t : HC + 128 * t + 128] = dx.astype(BF)
    out = nt(dproj[...], w[:, :, :, :, 0:CIN].reshape(D, CIN))
    part[...] = out.astype(BF).reshape(2, 128, D)


def two_backward(
    st, w1, w0, ng, cv, call, xall, x0own, proj1, proj0, y1, y0, do1, u1, u0, part1, stat1, stat0
):
    def kernel(
        st, w1h, w0h, ng, cv, callh, xallh, x0h, proj1h, proj0h, y1h, y0h, do1h, u1h, u0h, part1h, stat1p, stat0,
        e0o, sm, rp, vec, heads, ig, so, got,
        w, e1, e0, proj, yv, do, dproj, oo, u, part, x1own, x0own, dtile, db, grads, gp, gs, swap, stat1, stb, *rest,
    ):
        rbufs, ra, sa = rest[:4], rest[4:8], rest[8:15]
        sb = (rest[15], rest[16], sa[2], sa[3], rest[17], rest[18], sa[6])
        bz, bx, sums, ghead, isem, bsem, osem, ssem, rsem = rest[19:]
        s, z, h, x, c = place()

        def block_loads(i, far_first, proj_h, y_h, do_h, layer):
            hi, ci = block_at(i, h, s, far_first)
            b = 2 * hi + ci
            pairs = [(proj_h, proj), (y_h, yv)] + ([(do_h, do)] if do_h is not None else [])
            return [
                pltpu.make_async_copy(src.at[b], dst.at[lax.rem(i, 2)], bsem.at[layer, n, i])
                for n, (src, dst) in enumerate(pairs)
            ]

        loads1 = lambda i: block_loads(i, True, proj1h, y1h, do1h, 1)
        loads0 = lambda i: block_loads(i, False, proj0h, y0h, None, 0)
        for copy in loads1(0):
            copy.start()
        lw1 = pltpu.make_async_copy(w1h, w, isem.at[0])
        lw1.start()
        for copy in loads1(1):
            copy.start()
        later = [
            pltpu.make_async_copy(callh, e1, isem.at[1]),
            pltpu.make_async_copy(u1h, u, isem.at[2]),
            pltpu.make_async_copy(xallh.at[h, s, c], x1own, isem.at[3]),
            pltpu.make_async_copy(x0h, x0own, isem.at[4]),
        ]
        for copy in later:
            copy.start()
        greet(small_devs() + group_devs())
        net = Net(ssem, rsem)
        devs = group_devs()
        ring_sum = RingSum(net, part, rbufs)
        spread = Spread(net, e0)
        scatter1 = Scatter(net, grads, sa, gs.at[1])
        scatter0 = Scatter(net, w, sb, gs.at[0])
        ring0, ring1 = RingSum(net, part, rbufs), RingSum(net, e1, ra)
        me = (2 * h + s) * 2 + c
        q = 4 * s + 2 * h + c
        dsends = [net.make(dtile, db.at[me], dev) for dev in devs]
        gsends = [
            net.make(gp.at[dev["s"], 2 * dev["h"] + dev["c"]], rp.at[q], dev) for dev in devs
        ]
        swap_send = net.make(swap, got, {"s": 1 - s})
        stats = [net.send(stat1p, stb.at[k], dev) for k, dev in enumerate(devs)]
        sm[...] = jnp.zeros_like(sm)
        zr, zl, zo = ring(z)
        acc = stat1p[...]
        for k, copy in enumerate(stats):
            copy.wait_recv()
            acc = acc + stb[k]
        stat1[...] = acc
        lw1.wait()

        def first(i, carry):
            hi, ci = block_at(i, h, s, True)
            b = 2 * hi + ci
            slot = lax.rem(i, 2)
            for copy in loads1(i):
                copy.wait()
            backward_block(
                b, None, w, cv.at[1], st, stat1, None,
                (proj.at[slot], yv.at[slot], do.at[slot], dproj.at[b], oo.at[b], part.at[hi, ci], sm.at[1]),
            )
            when_each(i, 4, ring_sum.step)

            @pl.when(i < 2)
            def _():
                for copy in loads1(i + 2):
                    copy.start()

            return carry

        lax.fori_loop(0, 4, first, 0)
        lw0 = pltpu.make_async_copy(w0h, w, isem.at[5])
        lw0.start()
        for i in range(2):
            for copy in loads0(i):
                copy.start()
        ring_sum.late()
        for copy in later:
            copy.wait()
        for k in range(4):
            weight_tile(k, 1, u, e1, dproj, oo, grads)
        scatter1.start(1)
        for n, k in enumerate((zo, zr, zl, z)):
            weight_tile(k, 0, u, e1, dproj, oo, grads)
            if n == 0:
                scatter1.start(0)
        scatter1.direct(1)
        scatter1.direct(0)
        total = ring_sum.total()
        e0f = norm_back(total, x1own[...], e1[h, s, c], ng.at[1])
        e0l = e0f.astype(BF)
        e0[h, s, c] = e0l
        spread.start()
        diff = x1own[...].astype(F32) - x0own[...].astype(F32)
        dots = jnp.sum(e0l.astype(F32) * diff, axis=1, keepdims=True)
        dtile[...] = jnp.broadcast_to(col_to_row(dots), (8, 128))
        db[me] = dtile[...]
        for copy in dsends:
            copy.start()
        for copy in ring_sum.core + ring_sum.far + ring_sum.direct + ring_sum.summed:
            net.sent(copy)
        lu0 = pltpu.make_async_copy(u0h, u, isem.at[2])
        lu0.start()
        lp1 = pltpu.make_async_copy(part1h, e1, isem.at[1])
        lp1.start()
        for copy in dsends:
            copy.wait_recv()
        lw0.wait()
        lp1.wait()

        def save(i):
            hi, ci = block_at(i, h, s, False)
            return pltpu.make_async_copy(e0.at[hi, ci], e0o.at[hi, ci], osem.at[i])

        def second(i, carry):
            when_each(i, 4, spread.ready)
            hi, ci = block_at(i, h, s, False)
            b = 2 * hi + ci
            slot = lax.rem(i, 2)
            for copy in loads0(i):
                copy.wait()
            save(i).start()
            backward_block(
                b, e0.at[hi, ci], w, cv.at[0], st, stat0, db,
                (proj.at[slot], yv.at[slot], do.at[slot], dproj.at[b], oo.at[b], part.at[hi, ci], sm.at[0]),
            )
            when_each(i, 4, lambda k: ring0.core[3 - k].start())

            @pl.when(i < 2)
            def _():
                for copy in loads0(i + 2):
                    copy.start()

            @pl.when(i == 0)
            def _():
                for copy in ring1.core:
                    copy.start()

            @pl.when(i == 1)
            def _():
                scatter1.summed(1)
                scatter1.summed(0)
                ring1.all_adds()

            @pl.when(i == 3)
            def _():
                ring1.late()
                scatter1.second(1)
                scatter1.second(0)

            return carry

        lax.fori_loop(0, 4, second, 0)

        def smalls():
            yield from g_small(net, sm, bz, bx, sums)
            yield from g_share(net, sums, ghead, vec, heads)

        def pieces(layer):
            for k in range(4):
                rows = slice(24 * (k % 2), 24 * (k % 2) + 24)
                gp[layer, k, 0:24] = gs[layer, k // 2, rows, 0:HALF]
                gp[layer, k, 24:48] = gs[layer, k // 2, rows, HALF:D]

            @pl.when(s == layer)
            def _():
                rp[q] = gp[layer, 2 * h + c]
                for copy in gsends[0:3]:
                    copy.start()

            @pl.when(s != layer)
            def _():
                for copy in gsends[3:7]:
                    copy.start()

        sg = smalls()
        next(sg)
        lu0.wait()
        for k in range(4):
            weight_tile(k, 1, u, e0, dproj, oo, w)
        scatter0.start(1)
        weight_tile(zo, 0, u, e0, dproj, oo, w)
        scatter0.start(0)
        ring0.all_adds()
        scatter1.second_summed(1)
        scatter1.second_summed(0)
        weight_tile(zr, 0, u, e0, dproj, oo, w)
        weight_tile(zl, 0, u, e0, dproj, oo, w)
        scatter0.direct(1)
        scatter0.direct(0)
        weight_tile(z, 0, u, e0, dproj, oo, w)
        next(sg)
        for half in scatter1.parts:
            for copy in half["near"][2:] + half["far2"] + half["near2"]:
                net.sent(copy)
        ring0.late()
        scatter0.summed(1)
        scatter0.summed(0)
        scatter1.finish(1)
        scatter1.finish(0)
        pieces(1)
        so[...] = (x1own[...].astype(F32) + own_scale(stat1) * ring1.total()).astype(BF)
        ig[...] = norm_back(ring0.total(), x0own[...], e0[h, s, c], ng.at[0]).astype(BF)
        swap[...] = jnp.where(s == 0, so[...], ig[...])
        swap_send.start()
        next(sg)
        scatter0.second(1)
        scatter0.second(0)
        for _ in sg:
            pass
        scatter0.second_summed(1)
        scatter0.second_summed(0)
        scatter0.finish(0)
        scatter0.finish(1)
        pieces(0)
        for i in range(4):
            save(i).wait()
        for copy in gsends:
            copy.wait_recv()
        swap_send.wait_recv()
        net.finish()

    big = pltpu.VMEM((4, 2, 4, 48, D), BF)
    rows = pltpu.VMEM((2, 2, 2, 128, D), BF)
    chunk = pltpu.VMEM((128, D), BF)
    return pl.pallas_call(
        kernel,
        name="two_backward",
        out_shape=(
            CHUNKS,
            jax.ShapeDtypeStruct((2, 8, 640), F32),
            jax.ShapeDtypeStruct((8, 48, HALF), BF),
            jax.ShapeDtypeStruct((8, 3328), F32),
            SMALL,
            CHUNK,
            CHUNK,
            CHUNK,
        ),
        in_specs=[SM, ANY, ANY, VM, VM] + [ANY] * 11 + [VM, VM],
        out_specs=(ANY,) + (VM,) * 7,
        scratch_shapes=[
            big,
            rows,
            rows,
            pltpu.VMEM((2, 256, CIN), F32),
            pltpu.VMEM((2, 256, HC), F32),
            pltpu.VMEM((2, 256, HC), F32),
            pltpu.VMEM((4, 256, CIN), BF),
            pltpu.VMEM((4, 256, HC), BF),
            pltpu.VMEM((4, 256, D), BF),
            rows,
            chunk,
            chunk,
            pltpu.VMEM((8, 128), F32),
            pltpu.VMEM((8, 8, 128), F32),
            big,
            pltpu.VMEM((2, 4, 48, HALF), BF),
            pltpu.VMEM((2, 2, 48, D), BF),
            chunk,
            pltpu.VMEM((16, 128), F32),
            pltpu.VMEM((7, 16, 128), F32),
        ]
        + ring_scratch()
        + ring_scratch()
        + scatter_scratch()
        + [scatter_scratch()[k] for k in (0, 1, 4, 5)]
        + small_scratch()
        + [pltpu.VMEM((2, 8, 640), F32), pltpu.VMEM((8, 8, 640), F32)]
        + [
            pltpu.SemaphoreType.DMA((6,)),
            pltpu.SemaphoreType.DMA((2, 3, 4)),
            pltpu.SemaphoreType.DMA((4,)),
        ]
        + sems(128),
        compiler_params=params(3),
    )(
        st, w1, w0, ng, cv, call, xall, x0own, proj1, proj0, y1, y0, do1, u1, u0, part1, stat1, stat0
    )


def shift_div(v, m):
    return (v * {52: 20165, 48: 21846, 24: 43691}[m]) >> 20


def place_rows(x, rows, m, chan):
    n = chan.shape[1]
    row = lax.broadcasted_iota(jnp.int32, (512, n), 0)
    zz, xx, hh, cc = row >> 7, (row >> 5) & 3, (row >> 4) & 1, (row >> 3) & 1
    owner = shift_div(chan, m)
    same = ((zz * 2 + hh) * 4 + xx) * 2 + cc == owner
    col = lax.broadcasted_iota(jnp.int32, (128, n), 0) == chan - m * owner
    out = []
    for r in rows:
        pick = jnp.where(jnp.logical_and(same, (row & 7) == r), 1.0, 0.0).astype(BF)
        vals = tn(x, pick)
        out.append(jnp.sum(jnp.where(col, vals, 0.0), axis=0, keepdims=True))
    return out


def forward(starts, ngain, w_in, cw, cb, dtb, alog, skip, gate, w_out, tok, cot):
    def kernel(
        starts, ngain, w_in, cw, cb, dtb, alog, skip, gate, w_out, tok, cot,
        cv, ng, stt, x0o, s0o, s1o, w0o, w1o, e1o, x1o, p1o, proj0o, proj1o, y0o, y1o, u0o, u1o, doo,
        tile, tg, tb, ta, pieces, pb, blk0, blk1, st,
        w0, w1, x0, x1, e1, part, part1, proj, yv, uv, dov, og, stat0, stat1, stb0,
        rb0, rb1, rb2, rb3, ksem, osem, lsem, ssem, rsem,
    ):
        s, z, h, x, c = place()
        hc = 2 * h + c
        q = 4 * s + hc
        greet(small_devs() + group_devs())
        net = Net(ssem, rsem)
        devs = group_devs()
        low6 = lax.broadcasted_iota(jnp.int32, (24, 128), 1) < NH
        rate = jnp.concatenate(
            [w_in[0, :, 6400:6448].astype(F32), jnp.zeros((24, 80), F32)], axis=1
        )
        for k in range(8):
            lanes = slice(k * HC, k * HC + HC)
            moved = rate if k == 0 else pltpu.roll(rate, 128 - NH * k, axis=1)
            left = [w_in[0, :, lanes], w_in[0, :, 3072 + k * HC : 3072 + k * HC + HC]]
            right = [
                w_in[0, :, 6144:6400],
                jnp.where(low6, moved, 0.0).astype(BF),
                w_out[:, lanes],
            ]
            pieces[k, 0:24, :] = jnp.concatenate(left, axis=1)
            pieces[k, 24:48, :] = jnp.concatenate(right, axis=1)
        ids = [4 * d["s"] + 2 * d["h"] + d["c"] for d in devs]
        psend = [net.make(pieces.at[k], pb.at[s, hc], dev) for k, dev in zip(ids, devs)]

        def p_send():
            for copy in psend:
                copy.start()

        def p_wait(layer):
            @pl.when(s == layer)
            def _():
                for copy in psend[0:3]:
                    copy.wait_recv()

            @pl.when(s != layer)
            def _():
                for copy in psend[3:7]:
                    copy.wait_recv()

        def block(layer, out):
            for hh in range(2):
                for cc in range(2):
                    rows = slice(24 * cc, 24 * cc + 24)
                    out[hh, rows, 0:HALF] = pb[layer, 2 * hh + cc, 0:24]
                    out[hh, rows, HALF:D] = pb[layer, 2 * hh + cc, 24:48]

        pl.when(s == 0)(p_send)
        pb[s, hc] = pieces[q]
        tile[...] = jnp.zeros_like(tile)
        tile[0:4, 0:52] = cw[0].astype(F32)
        tile[4:5, 0:52] = cb[...].astype(F32)
        tile[5:6, 0:48] = gate[...].astype(F32)
        tile[6:7, 0:24] = ngain[...].astype(F32)
        tile[7:8, 0:4] = starts[0].astype(F32)
        tile[7:8, 4:8] = starts[1].astype(F32)
        tile[8:9, 0:48] = dtb[...]
        tile[9:10, 0:48] = jnp.exp(alog[...])
        tile[10:11, 0:48] = skip[...]
        tsend = [net.send(tile, tg.at[q], dev) for dev in devs]
        tg[q] = tile[...]
        gather0 = Gather(net, blk0, w0, lsem.at[0])
        gather1 = Gather(net, blk1, w1, lsem.at[3])
        ring = RingSum(net, part, (rb0, rb1, rb2, rb3))
        spread = Spread(net, x1)
        stats0 = [net.make(stat0, stb0.at[k], dev) for k, dev in enumerate(devs)]

        def weights():
            yield 9.0
            p_wait(0)
            block(0, blk0)
            gather0.step(0)
            pl.when(s == 1)(p_send)
            for k, n in enumerate((5.0, 7.0, 21.0)):
                yield 10.0 + n
                gather0.step(k + 1)
            p_wait(1)
            block(1, blk1)
            gather1.step(0)
            yield 39.0
            gather0.step(4)
            gather1.step(1)

        def vectors():
            yield 10.0
            for copy in tsend:
                copy.wait_recv()
            for k in range(8):
                tb[z, k // 4, 8 * (k % 4) : 8 * (k % 4) + 8] = tg[k, 0:8].astype(BF)
            for n in range(4):
                v = tg[n, 7:8, :]
                first = 4 * (n // 2) + n % 2
                stt[first : first + 1] = v.astype(jnp.int32)
                stt[first + 2 : first + 3] = pltpu.roll(v, 124, axis=1).astype(jnp.int32)
            to_smem = pltpu.make_async_copy(stt, st, ksem.at[0])
            to_smem.start()
            r = tb.at[z]
            sends = [net.send(r, r, {"z": lax.rem(z + k, 4)}) for k in range(1, 4)]
            yield 14.0
            to_smem.wait()
            for copy in sends:
                copy.wait_recv()
            ta[x] = tb[...]
            r = ta.at[x]
            sends = [net.send(r, r, {"x": lax.rem(x + k, 4)}) for k in range(1, 4)]
            yield 20.0
            for copy in sends:
                copy.wait_recv()
            n = lax.broadcasted_iota(jnp.int32, (1, 640), 1)
            chan = jnp.where(n < HC, q * HC + n, 3072 - HC + n)
            gchan = q * HC + lax.broadcasted_iota(jnp.int32, (1, HC), 1)
            nchan = lax.broadcasted_iota(jnp.int32, (1, D), 1)
            head = lax.broadcasted_iota(jnp.int32, (1, HC), 1) >> 6
            cv[...] = jnp.zeros_like(cv)
            for layer in range(2):
                vals = jnp.concatenate([ta[k % 4, k // 4, layer] for k in range(16)], axis=0)
                for r, v in enumerate(place_rows(vals, range(5), 52, chan)):
                    cv[layer, r : r + 1, :] = v
                cv[layer, 5:6, 0:HC] = place_rows(vals, [5], 48, gchan)[0]
                ng[layer] = place_rows(vals, [6], 24, nchan)[0]
                back = lax.rem(128 - NH * q, 128)
                heads = pltpu.roll(tg[4 * layer, 8:16, :], back, axis=1)
                cv[layer, 7:8, 0:128] = heads[0:1]
                cv[layer, 8:9, 0:128] = heads[1:2]
                lanes = jnp.zeros((1, HC), F32)
                for k in range(NH):
                    lanes = jnp.where(head == k, heads[2:3, k : k + 1], lanes)
                cv[layer, 6:7, 0:HC] = lanes
                yield 21.0

        run(
            [
                weights(),
                vectors(),
                g_pairs(net, tok, x0, lsem.at[1], 10.0),
                g_pairs(net, cot, e1, lsem.at[2], 19.2),
            ]
        )
        x0o[...] = x0[h, s, c]
        keep = [
            pltpu.make_async_copy(src, dst, ksem.at[n])
            for n, (src, dst) in enumerate(((w0, w0o), (e1, e1o), (w1, w1o)))
        ]
        keep[0].start()
        keep[1].start()

        def saves(b, layer, proj_o, y_o, u_o):
            return [
                pltpu.make_async_copy(v.at[b], o.at[b], osem.at[layer, n, b])
                for n, (v, o) in enumerate(((proj, proj_o), (yv, y_o), (uv, u_o)))
            ]

        def more(b, p):
            return [
                pltpu.make_async_copy(v, o, osem.at[2, n, b])
                for n, (v, o) in enumerate(
                    (
                        (dov.at[b], doo.at[b]),
                        (x1.at[p], x1o.at[p]),
                        (part1.at[p], p1o.at[p]),
                    )
                )
            ]

        def first(i, carry):
            hi, mi = block_at(i, h, s, True)
            b = 2 * hi + mi
            forward_block(
                b, x0.at[hi, mi], w0, ng[0], cv.at[0], st,
                (part.at[hi, mi], stat0, proj.at[b], yv.at[b], uv.at[b], None, og),
            )
            for copy in saves(b, 0, proj0o, y0o, u0o):
                copy.start()
            when_each(i, 4, ring.step)

            @pl.when(i == 0)
            def _():
                gather1.step(2)

            return carry

        lax.fori_loop(0, 4, first, 0)
        for copy in stats0:
            copy.start()
        ring.late()
        gather1.step(3)
        acc = stat0[...]
        for k, copy in enumerate(stats0):
            copy.wait_recv()
            acc = acc + stb0[k]
        s0o[...] = acc
        for b in range(4):
            for copy in saves(b, 0, proj0o, y0o, u0o):
                copy.wait()
        x1[h, s, c] = (x0[h, s, c].astype(F32) + own_scale(s0o) * ring.total()).astype(BF)
        spread.start()
        gather1.step(4)
        keep[2].start()

        def second(i, carry):
            when_each(i, 4, spread.ready)
            hi, mi = block_at(i, h, s, False)
            b = 2 * hi + mi
            forward_block(
                b, x1.at[hi, mi], w1, ng[1], cv.at[1], st,
                (part1.at[hi, mi], stat1, proj.at[b], yv.at[b], uv.at[b], dov.at[b], og),
                e1.at[hi, mi],
            )
            for copy in saves(b, 1, proj1o, y1o, u1o) + more(b, (hi, mi)):
                copy.start()
            return carry

        lax.fori_loop(0, 4, second, 0)
        s1o[...] = stat1[...]
        for copy in keep:
            copy.wait()
        for b in range(4):
            for copy in saves(b, 1, proj1o, y1o, u1o) + more(b, (b // 2, b % 2)):
                copy.wait()
        net.finish()

    blocks = lambda cols, t: jax.ShapeDtypeStruct((4, 256, cols), t)
    big = pltpu.VMEM((4, 2, 4, 48, D), BF)
    rows = pltpu.VMEM((2, 2, 2, 128, D), BF)
    return pl.pallas_call(
        kernel,
        name="forward",
        out_shape=(
            jax.ShapeDtypeStruct((2, 16, 640), F32),
            jax.ShapeDtypeStruct((2, 1, D), F32),
            jax.ShapeDtypeStruct((8, 128), jnp.int32),
            CHUNK,
            jax.ShapeDtypeStruct((8, 128), F32),
            jax.ShapeDtypeStruct((16, 128), F32),
            GATHERED,
            GATHERED,
            CHUNKS,
            CHUNKS,
            CHUNKS,
            blocks(CIN, F32),
            blocks(CIN, F32),
            blocks(HC, F32),
            blocks(HC, F32),
            blocks(D, BF),
            blocks(D, BF),
            blocks(HC, F32),
        ),
        in_specs=[VM] * 12,
        out_specs=(VM,) * 6 + (ANY,) * 12,
        scratch_shapes=[
            pltpu.VMEM((16, 128), F32),
            pltpu.VMEM((8, 16, 128), F32),
            pltpu.VMEM((4, 2, 32, 128), BF),
            pltpu.VMEM((4, 4, 2, 32, 128), BF),
            pltpu.VMEM((8, 48, HALF), BF),
            pltpu.VMEM((2, 4, 48, HALF), BF),
            pltpu.VMEM((2, 48, D), BF),
            pltpu.VMEM((2, 48, D), BF),
            pltpu.SMEM((8, 128), jnp.int32),
            big,
            big,
            rows,
            rows,
            rows,
            rows,
            rows,
            pltpu.VMEM((4, 256, CIN), F32),
            pltpu.VMEM((4, 256, HC), F32),
            pltpu.VMEM((4, 256, D), BF),
            pltpu.VMEM((4, 256, HC), F32),
            pltpu.VMEM((256, HC), BF),
            pltpu.VMEM((8, 128), F32),
            pltpu.VMEM((16, 128), F32),
            pltpu.VMEM((7, 8, 128), F32),
        ]
        + ring_scratch()
        + [
            pltpu.SemaphoreType.DMA((3,)),
            pltpu.SemaphoreType.DMA((3, 3, 4)),
            pltpu.SemaphoreType.DMA((4,)),
        ]
        + sems(100),
        compiler_params=params(1),
    )(starts, ngain, w_in, cw, cb, dtb, alog, skip, gate, w_out, tok, cot)


def results(rec, vec, heads, ig0, so1, got, eall, xall, w_in, ngain):
    def kernel(rec, vec, heads, ig0, so1, got, eall, xall, w_in, ngain, so, ig, gng, gwi, gcw, gcb, gdt, gal, gsk, ggg, gwo, buf, sem):
        s, z, h, x, c = place()
        dp = ((z * 2 + h) * 4 + x) * 2 + c
        copies = [
            pltpu.make_async_copy(src.at[h, :, c], buf.at[n], sem.at[n])
            for n, src in enumerate((eall, xall))
        ]
        for copy in copies:
            copy.start()
        tail = jnp.zeros((24, 256), F32)
        rate = jnp.zeros((24, 128), F32)
        lane = lax.broadcasted_iota(jnp.int32, (24, 128), 1)
        dots = jnp.zeros((24, 1), F32)

        def put(lanes, v):
            gwi[0, :, lanes] = v
            return jnp.sum(w_in[0, :, lanes].astype(F32) * v, axis=1, keepdims=True)

        for k in range(8):
            lanes = slice(k * HC, k * HC + HC)
            dots = dots + put(lanes, rec[k, 0:24, 0:HC].astype(F32))
            lanes = slice(3072 + k * HC, 3072 + k * HC + HC)
            dots = dots + put(lanes, rec[k, 0:24, HC:HALF].astype(F32))
            tail = tail + rec[k, 24:48, 0:256].astype(F32)
            part = jnp.where(lane < NH, rec[k, 24:48, 256:384].astype(F32), 0.0)
            rate = rate + (part if k == 0 else pltpu.roll(part, NH * k, axis=1))
            gwo[:, k * HC : k * HC + HC] = rec[k, 24:48, HC:HALF].astype(F32)
        dots = dots + put(slice(6144, 6400), tail)
        dots = dots + put(slice(6400, 6448), rate[:, 0:48])
        i = lax.broadcasted_iota(jnp.int32, (24, 24), 0)
        j = lax.broadcasted_iota(jnp.int32, (24, 24), 1)
        gng[...] = jnp.sum(jnp.where(i == j, dots, 0.0), axis=0, keepdims=True) / ngain[...].astype(F32)

        def exact(a, b):
            return jnp.dot(a, b, precision=HIGH, preferred_element_type=F32)

        high = vec[...].astype(BF).astype(F32)
        left = vec[...] - high
        middle = left.astype(BF).astype(F32)
        vec3 = jnp.concatenate([high, middle, left - middle], axis=0).astype(BF)

        def window(m):
            ch = lax.broadcasted_iota(jnp.int32, (3328, 128), 0)
            j = lax.broadcasted_iota(jnp.int32, (3328, 128), 1)
            pick = jnp.where(ch == m * dp + j, 1.0, 0.0).astype(BF)
            got3 = jnp.dot(vec3, pick, preferred_element_type=F32)
            return got3[0:8] + got3[8:16] + got3[16:24]

        conv = window(52)
        gcw[0] = conv[0:4, 0:52]
        gcb[...] = conv[4:5, 0:52]
        ggg[...] = window(48)[5:6, 0:48]
        ch = lax.broadcasted_iota(jnp.int32, (HC, 128), 0) >> 6
        j = lax.broadcasted_iota(jnp.int32, (HC, 128), 1)
        skip = exact(heads[:, 256:640], (ch == j).astype(F32))
        row = lax.broadcasted_iota(jnp.int32, (1, 128), 1)
        for out, v in ((gdt, heads[:, 0:128]), (gal, heads[:, 128:256]), (gsk, skip)):
            acc = jnp.zeros((1, 128), F32)
            for k in range(8):
                part = jnp.where(row < NH, v[k : k + 1], 0.0)
                acc = acc + (part if k == 0 else pltpu.roll(part, NH * k, axis=1))
            out[...] = acc[:, 0:48]
        for copy in copies:
            copy.wait()

        @pl.when(s == 0)
        def _():
            ig[0, 0] = ig0[...].astype(F32)
            ig[0, 1] = got[...].astype(F32)
            so[0] = buf[1]

        @pl.when(s == 1)
        def _():
            ig[0] = buf[0].astype(F32)
            so[0, 0] = got[...]
            so[0, 1] = so1[...]

    f = lambda *shape: jax.ShapeDtypeStruct(shape, F32)
    return pl.pallas_call(
        kernel,
        name="results",
        out_shape=(
            jax.ShapeDtypeStruct((1, 2, 128, D), BF),
            f(1, 2, 128, D),
            f(1, 24),
            f(1, 24, 6448),
            f(1, 4, 52),
            f(1, 52),
            f(1, 48),
            f(1, 48),
            f(1, 48),
            f(1, 48),
            f(24, 3072),
        ),
        in_specs=[VM] * 6 + [ANY] * 2 + [VM] * 2,
        out_specs=(VM,) * 11,
        scratch_shapes=[pltpu.VMEM((2, 2, 128, D), BF), pltpu.SemaphoreType.DMA((2,))],
        compiler_params=pltpu.CompilerParams(vmem_limit_bytes=VLIM),
    )(rec, vec, heads, ig0, so1, got, eall, xall, w_in, ngain)


def body(
    tokens,
    cotangent,
    starts,
    norm_gain,
    w_in,
    conv_weight,
    conv_bias,
    dt_bias,
    a_log,
    skip_d,
    gate_gain,
    w_out,
):
    cv, ng, st, x0own, stat0, stat1, w0, w1, call, xall, part1, proj0, proj1, y0, y1, u0, u1, do1 = forward(
        starts,
        norm_gain,
        w_in,
        conv_weight,
        conv_bias,
        dt_bias,
        a_log,
        skip_d,
        gate_gain,
        jnp.transpose(w_out[0]),
        tokens,
        cotangent,
    )
    eall, _, rec, vec, hd, ig0, so1, got = two_backward(
        st, w1, w0, ng, cv, call, xall, x0own, proj1, proj0, y1, y0, do1, u1, u0, part1, stat1, stat0
    )
    outs = results(rec, vec, hd, ig0, so1, got, eall, xall, w_in, norm_gain)
    return outs[:10] + (jnp.transpose(outs[10])[None],)


def solution(mesh):
    inner = Mesh(mesh.devices.reshape(2, 4, 2, 4, 2), ("s", "z", "h", "x", "c"))
    dp = ("z", "h", "x", "c")
    in_specs = (
        P(None, dp, None),
        P(None, dp, None),
        P(None, dp, None),
        P("s", dp),
        P("s", dp, None),
        P("s", None, dp),
        P("s", dp),
        P("s", None),
        P("s", None),
        P("s", None),
        P("s", dp),
        P("s", None, dp),
    )
    out_specs = (
        P("s", None, dp, None),
        P("s", None, dp, None),
        P("s", dp),
        P("s", dp, None),
        P("s", None, dp),
        P("s", dp),
        P("s", None),
        P("s", None),
        P("s", None),
        P("s", dp),
        P("s", None, dp),
    )
    return jax.shard_map(body, mesh=inner, in_specs=in_specs, out_specs=out_specs, check_vma=False)
```
